32 devices in a mesh: dp: 4 (over y, x), fsdp: 8 (over z, core).
Axes of the slice: x: 2, y: 2, z: 4, core: 2. Of those that a mesh axis runs over, the one named last changes fastest.
Arguments:
- byte_ids: int32 [2, 32, 1152], P(None, ('dp', 'fsdp')), may hold values from 0 to 255
- layouts: int32 [2, 32], P(None, ('dp', 'fsdp')), may hold values from 0 to 1
- weights: float32 [9728, 512], P(('dp', 'fsdp'))
- vectors: float32 [6, 512], P(None, ('dp', 'fsdp'))
- m_weights: float32 [9728, 512], P(('dp', 'fsdp')), may hold values from -0.002 to 0.002
- v_weights: float32 [9728, 512], P(('dp', 'fsdp')), may hold values from 2e-08 to 4e-07
- m_vectors: float32 [6, 512], P(None, ('dp', 'fsdp')), may hold values from -0.002 to 0.002
- v_vectors: float32 [6, 512], P(None, ('dp', 'fsdp')), may hold values from 2e-08 to 4e-07
Outputs:
- loss: float32 [], replicated
- grad_norm: float32 [], replicated
- m_weights_new: float32 [9728, 512], P(('dp', 'fsdp'))
- v_weights_new: float32 [9728, 512], P(('dp', 'fsdp'))
- weights_update: float32 [9728, 512], P(('dp', 'fsdp'))
- m_vectors_new: float32 [6, 512], P(None, ('dp', 'fsdp'))
- v_vectors_new: float32 [6, 512], P(None, ('dp', 'fsdp'))
- vectors_update: float32 [6, 512], P(None, ('dp', 'fsdp'))
The draws below stay inside these ranges and needn't reach their ends.
All inputs are finite; a program needn't handle non-finite values.
Results may differ from the reference program's by a relative error of at most 0.0052.
The reference program's roundings to bfloat16 on the way count: a program that leaves them out, or rounds other values in their place, can miss the bound.
Values may be sent and summed in bfloat16 or wider, within the bound.
No kernel may reach another device: no remote copies, remote signals or barrier semaphores. Data moves between devices by JAX's collectives and lax.ppermute only.
A program may use at most 192 MiB of HBM per device.

```python
import math
import jax
import jax.numpy as jnp
import numpy as np
from jax import lax

D = 512
HEADS = 8
HEAD = 64
FF = 2048
VOCAB = 256
POOL = 3
SLOT_LEN = 1152
MICRO = 2
SLOTS = 32
WROWS = 9728


def draw_weights(key, part):
    scales = jnp.concatenate([jnp.full((VOCAB,), 0.3, jnp.float32), jnp.full((POOL * D,), (POOL * D) ** (-0.5), jnp.float32), jnp.full((3 * D,), D ** (-0.5), jnp.float32), jnp.full((D,), 2.0 * D ** (-0.5), jnp.float32), jnp.full((FF,), D ** (-0.5), jnp.float32), jnp.full((FF,), FF ** (-0.5), jnp.float32), jnp.full((POOL * D,), D ** (-0.5), jnp.float32), jnp.full((VOCAB,), 2.0 * D ** (-0.5), jnp.float32)])
    noise = jax.random.normal(key, (WROWS, D), jnp.float32)
    return noise * scales[:, None]


def draw_vectors(key, part):
    noise = jax.random.normal(key, (6, D), jnp.float32)
    gains = (jnp.arange(6) % 2 == 0)[:, None]
    return jnp.where(gains, 1.0 + 0.15 * noise, 0.3 * noise)


def touch_ends(drawn, rng, smallest, largest):
    spot = [jax.random.randint(jax.random.fold_in(rng, axis), (), 0, length) for axis, length in enumerate(drawn.shape)]
    widest = drawn.shape.index(max(drawn.shape))
    beside = spot[:widest] + [(spot[widest] + 1) % drawn.shape[widest]] + spot[widest + 1:]
    return drawn.at[tuple(spot)].set(smallest).at[tuple(beside)].set(largest)


def block_scale(stream_key, shape, cuts, low, top_value):
    def one(dim, shards_of):
        draws = jax.random.uniform(jax.random.fold_in(jax.random.fold_in(stream_key, 6), dim), (shards_of,), jnp.float32, low / len(cuts), top_value / len(cuts))
        return jnp.repeat(jnp.exp(draws), shape[dim] // shards_of).reshape((-1,) + (1,) * (len(shape) - dim - 1))

    level = one(*cuts[0])
    for cut in cuts[1:]:
        level = level * one(*cut)
    return level


def cumulative_ranks(count, slope):
    portions = [(1 << 20) // math.isqrt(grade ** slope) + 1 for grade in range(1, count + 1)]
    scale = 1 + sum(portions) // (1 << 30)
    return np.cumsum(np.array([max(1, weight // scale) for weight in portions]))


def ranked_ids(stream_key, dims, number_of, lean):
    listing = cumulative_ranks(number_of, lean)
    lot = jax.random.randint(jax.random.fold_in(stream_key, 1), dims, 0, int(listing[number_of - 1]))
    standing = jnp.searchsorted(jnp.asarray(listing, jnp.int32), lot, side="right")
    return jax.random.permutation(jax.random.fold_in(stream_key, 2), number_of)[standing].astype(jnp.int32)


def centred(own_key, shape, deviation, most, cuts=(), kind=jnp.bfloat16):
    array = jax.random.normal(own_key, shape, jnp.float32) * deviation
    if len(cuts) > 0:
        array = block_scale(own_key, shape, cuts, -0.22, 0.18) * array
    return jnp.clip(array, min=-most, max=most).astype(kind)


def setup_inputs(seed: int = 0) -> dict:
    keys = jax.random.split(jax.random.key(seed), 9)
    return {
        "byte_ids": touch_ends(ranked_ids(keys[0], (MICRO, SLOTS, SLOT_LEN), VOCAB, 2), jax.random.fold_in(keys[0], 3), 0, VOCAB - 1).astype(jnp.int32),
        "layouts": touch_ends(jax.random.randint(keys[1], (MICRO, SLOTS), 0, 2), jax.random.fold_in(keys[1], 1), 0, 1).astype(jnp.int32),
        "weights": draw_weights(jax.random.fold_in(keys[8], 71), 0),
        "vectors": draw_vectors(jax.random.fold_in(keys[8], 71), 0),
        "m_weights": centred(keys[4], (WROWS, D), 0.0003, 0.002, ((0, 32),), jnp.float32),
        "v_weights": jnp.clip(jnp.exp(math.log(4.0000000467443897e-07) - 2.9957323 * jax.random.uniform(keys[5], (WROWS, D), jnp.float32) ** block_scale(keys[5], (WROWS, D), ((0, 32),), -0.2, 0.2)), 1.999999987845058e-08, 4.0000000467443897e-07),
        "m_vectors": centred(keys[6], (6, D), 0.0003, 0.002, ((1, 32),), jnp.float32),
        "v_vectors": jnp.clip(jnp.exp(math.log(4.0000000467443897e-07) - 2.9957323 * jax.random.uniform(keys[7], (6, D), jnp.float32) ** block_scale(keys[7], (6, D), ((1, 32),), -0.2, 0.2)), 1.999999987845058e-08, 4.0000000467443897e-07),
    }


@jax.custom_vjp
def low(v):
    return lax.optimization_barrier(v.astype(jnp.bfloat16)).astype(jnp.float32)

@jax.custom_vjp
def low_back(v):
    return v

def low_keep(v):
    return (low(v), None)

def low_pass(kept, grad):
    return (grad,)

def back_keep(v):
    return (v, None)

def back_low(kept, grad):
    return (low(grad),)
low.defvjp(low_keep, low_pass)
low_back.defvjp(back_keep, back_low)
EPS_NORM = 1e-05
EPS_ADAM = 1e-08
CLIP = 0.2
RATE = 0.03
DECAY = 0.1
BETA = 0.5
STEP = 3
NEGATIVE = -1000000000.0
HIGHEST = lax.Precision.HIGHEST

def product(left, right):
    return jnp.dot(left, right, precision=HIGHEST, preferred_element_type=jnp.float32)

def layer_norm(values, gain, offset):
    center = values - lax.optimization_barrier(jnp.mean(values, -1, keepdims=True))
    spread = lax.optimization_barrier(jnp.mean(center * center, -1, keepdims=True))
    return center * lax.rsqrt(spread + EPS_NORM) * gain + offset

def blocks(stacked):
    widths = [VOCAB, POOL * D, 3 * D, D, FF, FF, POOL * D, VOCAB]
    pieces = []
    offset = 0
    for width in widths:
        pieces.append(stacked[offset:offset + width])
        offset = offset + width
    return pieces

def row_bounds(layout, length):
    places = jnp.arange(length, dtype=jnp.int32)
    half = length // 2
    split = layout == 1
    first = jnp.where(split & (places >= half), half, 0).astype(jnp.int32)
    last = jnp.where(split & (places < half), half, length).astype(jnp.int32)
    return (places, first, last)

def attention_bias(layout, short_len):
    places = jnp.arange(short_len, dtype=jnp.int32)
    segment = ((layout == 1) & (places >= short_len // 2)).astype(jnp.int32)
    allowed = (places[None, :] <= places[:, None]) & (segment[None, :] == segment[:, None])
    slopes = 2.0 ** (-8.0 * (jnp.arange(HEADS, dtype=jnp.float32) + 1.0) / HEADS)
    distance = (places[:, None] - places[None, :]).astype(jnp.float32)
    return jnp.where(allowed[None], -slopes[:, None, None] * distance[None], NEGATIVE)

def to_heads(matrix):
    return matrix.reshape(matrix.shape[0], HEADS, HEAD).transpose(1, 0, 2)

def from_heads(tensor):
    return tensor.transpose(1, 0, 2).reshape(tensor.shape[1], HEADS * HEAD)

def slot_loss(stacked, vectors, byte_ids, layout):
    embed_table, pool_w, qkv_w, out_w, ffn_in, ffn_out, up_w, head_w = blocks(stacked)
    length = byte_ids.shape[0]
    short_len = length // POOL
    places, first, last = row_bounds(layout, length)
    vocab_ids = jnp.arange(VOCAB, dtype=jnp.int32)
    one_hot = (byte_ids[:, None] == vocab_ids[None, :]).astype(jnp.float32)
    embed = product(one_hot, embed_table)
    shifted = jnp.concatenate([jnp.zeros((2, D), jnp.float32), embed[:-2]], 0)
    shifted = jnp.where((places - 2 >= first)[:, None], shifted, 0.0)
    short = low_back(product(low(shifted).reshape(short_len, POOL * D), pool_w))
    normed = low(layer_norm(short, vectors[0], vectors[1]))
    qkv = low(low_back(product(normed, qkv_w.T)))
    queries = to_heads(qkv[:, :D])
    key_rows = to_heads(qkv[:, D:2 * D])
    val_rows = to_heads(qkv[:, 2 * D:])
    raw = low_back(jnp.einsum('hqd,hkd->hqk', queries, key_rows, precision=HIGHEST))
    scores = raw * 0.125 + attention_bias(layout, short_len)
    top = lax.optimization_barrier(jnp.max(scores, -1, keepdims=True))
    expo = jnp.exp(scores - top)
    probs = expo / lax.optimization_barrier(jnp.sum(expo, -1, keepdims=True))
    mixed = jnp.einsum('hqk,hkd->hqd', low(probs), val_rows, precision=HIGHEST)
    mixed = low(low_back(from_heads(mixed)))
    resid = short + low_back(product(mixed, out_w))
    normed2 = low(layer_norm(resid, vectors[2], vectors[3]))
    hidden = low_back(product(normed2, ffn_in.T))
    active = low(jax.nn.gelu(hidden, approximate=False))
    deep = resid + low_back(product(active, ffn_out))
    upward = low_back(product(low(deep), up_w.T)).reshape(length, D)
    joined = embed + upward
    final = low(layer_norm(joined, vectors[4], vectors[5]))
    logits = low_back(product(final, head_w.T))
    nexts = jnp.concatenate([byte_ids[1:], byte_ids[:1]])
    valid = (places + 1 < last).astype(jnp.float32)
    picked = lax.optimization_barrier(jnp.sum(logits * (nexts[:, None] == vocab_ids[None, :]).astype(jnp.float32), -1))
    peak = lax.optimization_barrier(jnp.max(logits, -1))
    total_lse = peak + jnp.log(lax.optimization_barrier(jnp.sum(jnp.exp(logits - peak[:, None]), -1)))
    return jnp.sum(valid * (total_lse - picked))

def adam(param, first_m, second_m, grad, decay):
    first_new = BETA * first_m + (1.0 - BETA) * grad
    second_new = BETA * second_m + (1.0 - BETA) * grad * grad
    correct = 1.0 - BETA ** STEP
    update = -RATE * (first_new / correct / (jnp.sqrt(second_new / correct) + EPS_ADAM) + decay * param)
    return (first_new, second_new, update)

def reference(byte_ids, layouts, weights, vectors, m_weights, v_weights, m_vectors, v_vectors):
    count = MICRO * SLOTS * SLOT_LEN
    flat_ids = byte_ids.reshape(MICRO * SLOTS, SLOT_LEN)
    flat_layouts = layouts.reshape(MICRO * SLOTS)

    def loss_of(stacked, vecs):
        stacked_low = low(stacked)
        vecs_low = low(vecs)
        checked = jax.checkpoint(slot_loss)

        def advance(carry, item):
            return (carry + checked(stacked_low, vecs_low, item[0], item[1]), None)
        summed, _ = lax.scan(advance, jnp.zeros((), jnp.float32), (flat_ids, flat_layouts))
        return summed / count
    loss, pull = jax.vjp(loss_of, weights, vectors)
    grad_w, grad_v = pull(jnp.ones((), jnp.float32))
    grad_norm = jnp.sqrt(jnp.sum(grad_w * grad_w) + jnp.sum(grad_v * grad_v))
    factor = CLIP / jnp.maximum(grad_norm, CLIP)
    first_w, second_w, update_w = adam(weights, m_weights, v_weights, grad_w * factor, DECAY)
    first_v, second_v, update_v = adam(vectors, m_vectors, v_vectors, grad_v * factor, 0.0)
    return (loss, grad_norm, first_w, second_w, update_w, first_v, second_v, update_v)
```

```python
from functools import partial

import jax
import jax.numpy as jnp
from jax import lax
from jax.experimental import pallas as pl
from jax.experimental.pallas import tpu as pltpu
from jax.sharding import PartitionSpec as P

D = 512
HEADS = 8
HEAD = 64
FF = 2048
VOCAB = 256
POOL = 3

EPS_NORM = 1e-05
EPS_ADAM = 1e-08
CLIP = 0.2
RATE = 0.03
DECAY = 0.1
BETA = 0.5
STEP = 3
NEGATIVE = -1000000000.0

F32 = jnp.float32
BF16 = jnp.bfloat16

ROW_E = 0
ROW_P = VOCAB
ROW_QKV = ROW_P + POOL * D
ROW_O = ROW_QKV + 3 * D
ROW_F1 = ROW_O + D
ROW_F2 = ROW_F1 + FF
ROW_U = ROW_F2 + FF
ROW_H = ROW_U + POOL * D
ROW_END = ROW_H + VOCAB

BLOCK = 256
AXES = ("dp", "fsdp")


def nn(left, right):
    return lax.dot_general(left, right, (((1,), (0,)), ((), ())), preferred_element_type=F32)


def nt(left, right):
    return lax.dot_general(left, right, (((1,), (1,)), ((), ())), preferred_element_type=F32)


def tn(left, right):
    return lax.dot_general(left, right, (((0,), (0,)), ((), ())), preferred_element_type=F32)


def norm_parts(values):
    center = values - jnp.mean(values, -1, keepdims=True)
    spread = jnp.mean(center * center, -1, keepdims=True)
    scale = lax.rsqrt(spread + EPS_NORM)
    return center * scale, scale


def norm_back(unit, scale, gain, grad):
    inner = grad * gain
    mean_inner = jnp.mean(inner, -1, keepdims=True)
    mean_cross = jnp.mean(inner * unit, -1, keepdims=True)
    return scale * (inner - mean_inner - unit * mean_cross)


def fold_rows(values):
    return jnp.sum(values.reshape(values.shape[0] // 8, 8, values.shape[1]), 0)


def one_hot_rows(ids):
    lanes = lax.broadcasted_iota(jnp.int32, (ids.shape[0], VOCAB), 1)
    return jnp.where(lanes == ids, 1.0, 0.0).astype(BF16)


def one_hot_cols(ids):
    lines = lax.broadcasted_iota(jnp.int32, (VOCAB, ids.shape[1]), 0)
    return jnp.where(lines == ids, 1.0, 0.0).astype(BF16)


def rows_of(index, size=BLOCK):
    return pl.ds(pl.multiple_of(index * size, size), size)


def attend_kernel(short_len, slots, lay_ref, slope_ref, cols_ref, vec_ref, w_hbm,
                  shifted_ref, short_ref, normed_ref, qkv_ref, lse_ref, mixed_ref, resid_ref,
                  w_ref, dist_ref, mask_ref, lse_cols, sems):
    rows = short_len * slots
    bounds = (ROW_E, ROW_QKV, ROW_O, ROW_F1)
    copies = [
        pltpu.make_async_copy(w_hbm.at[pl.ds(low, high - low)], w_ref.at[pl.ds(low, high - low)], sems.at[k])
        for k, (low, high) in enumerate(zip(bounds[:-1], bounds[1:]))
    ]
    for copy in copies:
        copy.start()
    copies[0].wait()
    gain, offset = vec_ref[0:1, :], vec_ref[1:2, :]

    def pool_step(block, carry):
        at = rows_of(block)
        for j in range(POOL):
            hot = one_hot_rows(cols_ref[at, POOL + j : POOL + j + 1])
            shifted_ref[at, j * D : (j + 1) * D] = nn(hot, w_ref[ROW_E:ROW_P, :]).astype(BF16)
        short = nn(shifted_ref[at, :], w_ref[ROW_P:ROW_QKV, :])
        short_ref[at, :] = short
        unit, _ = norm_parts(short)
        normed_ref[at, :] = (unit * gain + offset).astype(BF16)
        return carry

    lax.fori_loop(0, rows // BLOCK, pool_step, 0)
    copies[1].wait()

    def qkv_step(block, carry):
        at = rows_of(block)
        qkv_ref[at, :] = nt(normed_ref[at, :], w_ref[ROW_QKV:ROW_O, :]).astype(BF16)
        return carry

    lax.fori_loop(0, rows // BLOCK, qkv_step, 0)

    left_lanes = lax.broadcasted_iota(jnp.int32, (short_len, 2 * HEAD), 1) < HEAD
    tile = 128
    for slot in range(slots):
        at = pl.ds(slot * short_len, short_len)
        query = lax.broadcasted_iota(jnp.int32, (short_len, short_len), 0)
        key = lax.broadcasted_iota(jnp.int32, (short_len, short_len), 1)
        half = jnp.where(lay_ref[slot] == 1, short_len // 2, short_len)
        allowed = (key <= query) & ((key >= half) == (query >= half))
        dist_ref[...] = (key - query).astype(F32)
        mask_ref[...] = jnp.where(allowed, 0.0, NEGATIVE)

        def head_step(pair, carry):
            lanes = pl.ds(pl.multiple_of(pair * 2 * HEAD, 2 * HEAD), 2 * HEAD)
            lanes_k = pl.ds(pl.multiple_of(D + pair * 2 * HEAD, 2 * HEAD), 2 * HEAD)
            lanes_v = pl.ds(pl.multiple_of(2 * D + pair * 2 * HEAD, 2 * HEAD), 2 * HEAD)
            queries = qkv_ref[at, lanes] * jnp.asarray(0.125, BF16)
            keys = qkv_ref[at, lanes_k]
            values = qkv_ref[at, lanes_v]
            zero = jnp.zeros_like(values)
            vals = [jnp.where(left_lanes, values, zero), jnp.where(left_lanes, zero, values)]
            slots_q = [jnp.where(left_lanes, queries, zero), jnp.where(left_lanes, zero, queries)]
            for part in range(short_len // tile):
                low = part * tile
                mixed = jnp.zeros((tile, 2 * HEAD), F32)
                columns = lse_cols[low : low + tile, :]
                where = lax.broadcasted_iota(jnp.int32, (tile, 2 * HEAD), 1)
                for side in range(2):
                    head = pair * 2 + side
                    slope = slope_ref[head]
                    scores = nt(slots_q[side][low : low + tile], keys)
                    scores = scores + jnp.where(
                        mask_ref[low : low + tile, :] == 0.0, dist_ref[low : low + tile, :] * slope, NEGATIVE
                    )
                    top = jnp.max(scores, -1, keepdims=True)
                    expo = jnp.exp(scores - top)
                    total = jnp.sum(expo, -1, keepdims=True)
                    probs = (expo * (1.0 / total)).astype(BF16)
                    columns = jnp.where(where == head, top + jnp.log(total), columns)
                    mixed = mixed + nn(probs, vals[side])
                lse_cols[low : low + tile, :] = columns
                mixed_ref[pl.ds(slot * short_len + low, tile), lanes] = mixed.astype(BF16)
            return carry

        lse_cols[...] = jnp.zeros_like(lse_cols)
        lax.fori_loop(0, HEADS // 2, head_step, 0)
        turned = lse_cols[...].T
        for head in range(HEADS):
            lse_ref[slot, head] = turned[head : head + 1, :]

    copies[2].wait()

    def out_step(block, carry):
        at = rows_of(block)
        resid_ref[at, :] = short_ref[at, :] + nn(mixed_ref[at, :], w_ref[ROW_O:ROW_F1, :])
        return carry

    lax.fori_loop(0, rows // BLOCK, out_step, 0)


def gelu_parts(hidden):
    size = jnp.abs(hidden)
    near = 1.0 / (1.0 + (0.3275911 * 0.7071067811865476) * size)
    bell = jnp.exp(hidden * hidden * -0.5)
    tail = near * (0.127414796 + near * (-0.142248368 + near * (0.7107068705 + near * (-0.7265760135 + near * 0.5307027145))))
    tail = tail * bell
    cdf = jnp.where(hidden >= 0.0, 1.0 - tail, tail)
    return hidden * cdf, cdf + hidden * bell * 0.3989422804014327


def deep_kernel(count, cols_ref, lines_ref, vec_ref, resid_ref, w_hbm,
                grads_ref, table_ref, dresid_ref, small_ref,
                w_ref, normed_ref, act_ref, slope_ref, deep_ref, final_ref, dlog_ref, dup_ref, low_ref,
                ddeep_ref, dhid_ref, sems):
    rows = resid_ref.shape[0]
    blocks = rows // BLOCK
    base = ROW_F1 - VOCAB
    bounds = (ROW_F1, ROW_F2, ROW_U, ROW_END)
    copies = [
        pltpu.make_async_copy(w_hbm.at[pl.ds(low, high - low)], w_ref.at[pl.ds(low - base, high - low)], sems.at[k])
        for k, (low, high) in enumerate(zip(bounds[:-1], bounds[1:]))
    ]
    copies.append(pltpu.make_async_copy(w_hbm.at[pl.ds(0, VOCAB)], w_ref.at[pl.ds(0, VOCAB)], sems.at[3]))
    for copy in copies:
        copy.start()
    f1, f2, up, head = ROW_F1 - base, ROW_F2 - base, ROW_U - base, ROW_H - base
    gain2, offset2 = vec_ref[2:3, :], vec_ref[3:4, :]
    gain_f, offset_f = vec_ref[4:5, :], vec_ref[5:6, :]
    wide = 512

    def norm_step(block, carry):
        at = rows_of(block)
        unit, _ = norm_parts(resid_ref[at, :])
        normed_ref[at, :] = (unit * gain2 + offset2).astype(BF16)
        return carry

    lax.fori_loop(0, blocks, norm_step, 0)
    copies[0].wait()

    def hidden_step(index, carry):
        block, chunk = index // (FF // wide), index % (FF // wide)
        at = rows_of(block)
        lanes = rows_of(chunk, wide)
        hidden = nt(normed_ref[at, :], w_ref[pl.ds(pl.multiple_of(f1 + chunk * wide, VOCAB), wide), :])
        act, slope = gelu_parts(hidden)
        act_ref[at, lanes] = act.astype(BF16)
        slope_ref[at, lanes] = slope
        return carry

    lax.fori_loop(0, blocks * (FF // wide), hidden_step, 0)
    copies[1].wait()

    def deep_step(block, carry):
        at = rows_of(block)
        deep_ref[at, :] = (resid_ref[at, :] + nn(act_ref[at, :], w_ref[f2 : f2 + FF, :])).astype(BF16)
        return carry

    lax.fori_loop(0, blocks, deep_step, 0)
    copies[2].wait()
    copies[3].wait()

    small_ref[...] = jnp.zeros_like(small_ref)

    def head_step(index, carry):
        j, block = index // blocks, index % blocks
        at = rows_of(block)
        there = rows_of(index)
        up_rows = pl.ds(pl.multiple_of(up + j * D, VOCAB), D)
        columns = cols_ref[j, at, :]
        joined = nn(one_hot_rows(columns[:, 0:1]), w_ref[0:VOCAB, :]) + nt(deep_ref[at, :], w_ref[up_rows, :])
        unit, scale = norm_parts(joined)
        final = (unit * gain_f + offset_f).astype(BF16)
        final_ref[there, :] = final
        logits = nt(final, w_ref[head : head + VOCAB, :])
        nexts = columns[:, 2:3]
        lanes = lax.broadcasted_iota(jnp.int32, logits.shape, 1)
        target = jnp.where(lanes == nexts, 1.0, 0.0)
        valid = jnp.where(nexts >= 0, 1.0, 0.0)
        peak = jnp.max(logits, -1, keepdims=True)
        expo = jnp.exp(logits - peak)
        total = jnp.sum(expo, -1, keepdims=True)
        picked = jnp.sum(logits * target, -1, keepdims=True)
        losses = valid * (peak + jnp.log(total) - picked)
        dlogits = ((valid / count) * (expo * (1.0 / total) - target)).astype(BF16)
        dlog_ref[there, :] = dlogits
        dfinal = nn(dlogits, w_ref[head : head + VOCAB, :])
        djoined = norm_back(unit, scale, gain_f, dfinal)
        dup = djoined.astype(BF16)
        dup_ref[there, :] = dup
        low_ref[there, :] = (djoined - dup.astype(F32)).astype(BF16)
        back = nn(dup, w_ref[up_rows, :])

        @pl.when(j == 0)
        def _():
            ddeep_ref[at, :] = back

        @pl.when(j > 0)
        def _():
            ddeep_ref[at, :] += back

        small_ref[4, :, :] += fold_rows(dfinal * unit)
        small_ref[5, :, :] += fold_rows(dfinal)
        small_ref[6, :, :] += jnp.broadcast_to(fold_rows(losses), (8, D))
        return carry

    lax.fori_loop(0, POOL * blocks, head_step, 0)

    out_up, out_head = ROW_U - ROW_F1, ROW_H - ROW_F1
    grads_ref[out_head : out_head + VOCAB, :] = tn(dlog_ref[...], final_ref[...]).astype(BF16)
    for j in range(POOL):
        there = pl.ds(j * rows, rows)
        grads_ref[out_up + j * D : out_up + (j + 1) * D, :] = tn(dup_ref[there, :], deep_ref[...]).astype(BF16)
        hot = one_hot_cols(lines_ref[j : j + 1, :])
        part = nn(hot, dup_ref[there, :]) + nn(hot, low_ref[there, :])
        if j == 0:
            table_ref[...] = part
        else:
            table_ref[...] += part

    deep_ref[...] = ddeep_ref[...].astype(BF16)

    def dhid_step(index, carry):
        block, chunk = index // (FF // wide), index % (FF // wide)
        at = rows_of(block)
        lanes = rows_of(chunk, wide)
        dact = nt(deep_ref[at, :], w_ref[pl.ds(pl.multiple_of(f2 + chunk * wide, VOCAB), wide), :])
        dhid_ref[at, lanes] = (dact * slope_ref[at, lanes]).astype(BF16)
        return carry

    lax.fori_loop(0, blocks * (FF // wide), dhid_step, 0)

    def dff_step(chunk, carry):
        lanes = rows_of(chunk, wide)
        grads_ref[lanes, :] = tn(dhid_ref[:, lanes], normed_ref[...]).astype(BF16)
        grads_ref[pl.ds(pl.multiple_of(FF + chunk * wide, wide), wide), :] = tn(act_ref[:, lanes], deep_ref[...]).astype(BF16)
        return carry

    lax.fori_loop(0, FF // wide, dff_step, 0)

    def dnorm_step(block, carry):
        at = rows_of(block)
        dnormed = nn(dhid_ref[at, :], w_ref[f1 : f1 + FF, :])
        unit, scale = norm_parts(resid_ref[at, :])
        dresid_ref[at, :] = ddeep_ref[at, :] + norm_back(unit, scale, gain2, dnormed)
        small_ref[2, :, :] += fold_rows(dnormed * unit)
        small_ref[3, :, :] += fold_rows(dnormed)
        return carry

    lax.fori_loop(0, blocks, dnorm_step, 0)


def attend_back_kernel(short_len, slots, lay_ref, slope_ref, lines_ref, vec_ref, dresid_ref,
                       shifted_ref, short_ref, normed_ref, qkv_ref, lse_ref, mixed_ref, table_ref, w_hbm,
                       grads_ref, small_ref,
                       w_ref, dist_ref, mask_ref, dbranch_ref, dmix_ref, dqkv_ref, dshort_ref, sems):
    rows = short_len * slots
    blocks = rows // BLOCK
    base = ROW_P
    bounds = (ROW_O, ROW_QKV, ROW_P)
    ends = (ROW_F1, ROW_O, ROW_QKV)
    copies = [
        pltpu.make_async_copy(w_hbm.at[pl.ds(low, high - low)], w_ref.at[pl.ds(low - base, high - low)], sems.at[k])
        for k, (low, high) in enumerate(zip(bounds, ends))
    ]
    for copy in copies:
        copy.start()
    pool, proj, out = ROW_P - base, ROW_QKV - base, ROW_O - base
    small_ref[...] = jnp.zeros_like(small_ref)
    copies[0].wait()

    def dmix_step(block, carry):
        at = rows_of(block)
        dbranch = dresid_ref[at, :].astype(BF16)
        dbranch_ref[at, :] = dbranch
        dmix_ref[at, :] = nt(dbranch, w_ref[out : out + D, :]).astype(BF16)
        return carry

    lax.fori_loop(0, blocks, dmix_step, 0)
    grads_ref[ROW_O:ROW_F1, :] = tn(mixed_ref[...], dbranch_ref[...]).astype(BF16)

    left_lanes = lax.broadcasted_iota(jnp.int32, (short_len, 2 * HEAD), 1) < HEAD
    tile = 128
    for slot in range(slots):
        at = pl.ds(slot * short_len, short_len)
        key = lax.broadcasted_iota(jnp.int32, (short_len, short_len), 0)
        query = lax.broadcasted_iota(jnp.int32, (short_len, short_len), 1)
        half = jnp.where(lay_ref[slot] == 1, short_len // 2, short_len)
        allowed = (key <= query) & ((key >= half) == (query >= half))
        dist_ref[...] = (key - query).astype(F32)
        mask_ref[...] = jnp.where(allowed, 0.0, NEGATIVE)

        def head_step(pair, carry):
            lanes = pl.ds(pl.multiple_of(pair * 2 * HEAD, 2 * HEAD), 2 * HEAD)
            lanes_k = pl.ds(pl.multiple_of(D + pair * 2 * HEAD, 2 * HEAD), 2 * HEAD)
            lanes_v = pl.ds(pl.multiple_of(2 * D + pair * 2 * HEAD, 2 * HEAD), 2 * HEAD)
            queries = qkv_ref[at, lanes]
            keys = qkv_ref[at, lanes_k]
            values = qkv_ref[at, lanes_v]
            dmix = dmix_ref[at, lanes]
            zero = jnp.zeros_like(values)

            def one_side(side, array):
                return jnp.where(left_lanes, array, zero) if side == 0 else jnp.where(left_lanes, zero, array)

            scaled = queries * jnp.asarray(0.125, BF16)
            dkeys = jnp.zeros((short_len, 2 * HEAD), F32)
            dvalues = jnp.zeros((short_len, 2 * HEAD), F32)
            side_k = [one_side(side, keys) for side in range(2)]
            side_v = [one_side(side, values) for side in range(2)]
            side_q = [one_side(side, queries) for side in range(2)]
            side_m = [one_side(side, dmix) for side in range(2)]
            for part in range(short_len // tile):
                low = part * tile
                dqueries = jnp.zeros((tile, 2 * HEAD), F32)
                for side in range(2):
                    head = pair * 2 + side
                    slope = slope_ref[head]
                    scores = nt(side_k[side], scaled[low : low + tile])
                    scores = scores + jnp.where(
                        mask_ref[:, low : low + tile] == 0.0, dist_ref[:, low : low + tile] * slope, NEGATIVE
                    )
                    probs = jnp.exp(scores - lse_ref[slot, head, :, low : low + tile])
                    dprobs = nt(side_v[side], dmix[low : low + tile])
                    delta = jnp.sum(dprobs * probs, 0, keepdims=True)
                    dscores = (probs * (dprobs - delta) * 0.125).astype(BF16)
                    dvalues = dvalues + nn(probs.astype(BF16), side_m[side][low : low + tile])
                    dkeys = dkeys + nn(dscores, side_q[side][low : low + tile])
                    dqueries = dqueries + tn(dscores, side_k[side])
                dqkv_ref[pl.ds(slot * short_len + low, tile), lanes] = dqueries.astype(BF16)
            dqkv_ref[at, lanes_k] = dkeys.astype(BF16)
            dqkv_ref[at, lanes_v] = dvalues.astype(BF16)
            return carry

        lax.fori_loop(0, HEADS // 2, head_step, 0)

    copies[1].wait()
    gain = vec_ref[0:1, :]
    for part in range(3):
        grads_ref[ROW_QKV + part * D : ROW_QKV + (part + 1) * D, :] = tn(
            dqkv_ref[:, part * D : (part + 1) * D], normed_ref[...]
        ).astype(BF16)

    def dshort_step(block, carry):
        at = rows_of(block)
        dnormed = nn(dqkv_ref[at, :], w_ref[proj : proj + 3 * D, :])
        unit, scale = norm_parts(short_ref[at, :])
        dshort_ref[at, :] = (dresid_ref[at, :] + norm_back(unit, scale, gain, dnormed)).astype(BF16)
        small_ref[0, :, :] += fold_rows(dnormed * unit)
        small_ref[1, :, :] += fold_rows(dnormed)
        return carry

    lax.fori_loop(0, blocks, dshort_step, 0)
    copies[2].wait()
    table = table_ref[...]
    for j in range(POOL):
        cols = slice(j * D, (j + 1) * D)
        grads_ref[ROW_P + j * D : ROW_P + (j + 1) * D, :] = tn(shifted_ref[:, cols], dshort_ref[...]).astype(BF16)
        dshift = nt(dshort_ref[...], w_ref[pool + j * D : pool + (j + 1) * D, :])
        high = dshift.astype(BF16)
        low = (dshift - high.astype(F32)).astype(BF16)
        hot = one_hot_cols(lines_ref[POOL + j : POOL + j + 1, :])
        table = table + nn(hot, high) + nn(hot, low)
    grads_ref[ROW_E:ROW_P, :] = table.astype(BF16)


def step_inputs(byte_ids, layouts):
    slots, length = byte_ids.shape
    places = jnp.arange(length, dtype=jnp.int32)[None, :]
    half = length // 2
    split = (layouts == 1)[:, None]
    first = jnp.where(split & (places >= half), half, 0)
    last = jnp.where(split & (places < half), half, length)
    back = jnp.pad(byte_ids[:, :-2], ((0, 0), (2, 0)))
    back = jnp.where(places - 2 >= first, back, -1)
    ahead = jnp.pad(byte_ids[:, 1:], ((0, 0), (0, 1)))
    ahead = jnp.where(places + 1 < last, ahead, -1)
    kinds = jnp.stack([byte_ids, back, ahead], 0)
    kinds = kinds.reshape(3, slots, length // POOL, POOL).transpose(0, 3, 1, 2)
    kinds = kinds.reshape(3, POOL, slots * (length // POOL))
    lines = kinds.reshape(3 * POOL, -1)
    return lines


VMEM = pl.BlockSpec(memory_space=pltpu.VMEM)
SMEM = pl.BlockSpec(memory_space=pltpu.SMEM)
ANY = pl.BlockSpec(memory_space=pl.ANY)
LIMIT = 58 * 1024 * 1024


def device_grads(stacked, vecs, byte_ids, layouts, count):
    slots, length = byte_ids.shape
    short_len = length // POOL
    rows = slots * short_len
    lines = step_inputs(byte_ids, layouts)
    lines = jnp.pad(lines, ((0, 16 - lines.shape[0]), (0, 0)))
    cols = lines.T
    by_place = lines[: 3 * POOL].reshape(3, POOL, rows).transpose(1, 2, 0)
    slopes = 2.0 ** (-8.0 * (jnp.arange(HEADS, dtype=F32) + 1.0) / HEADS)
    vecs = jnp.pad(vecs.astype(F32), ((0, 2), (0, 0)))
    shape = jax.ShapeDtypeStruct
    params = pltpu.CompilerParams(vmem_limit_bytes=LIMIT)
    shifted, short, normed, qkv, lse, mixed, resid = pl.pallas_call(
        partial(attend_kernel, short_len, slots),
        out_shape=(
            shape((rows, POOL * D), BF16),
            shape((rows, D), F32),
            shape((rows, D), BF16),
            shape((rows, 3 * D), BF16),
            shape((slots, HEADS, 1, short_len), F32),
            shape((rows, D), BF16),
            shape((rows, D), F32),
        ),
        in_specs=[SMEM, SMEM, VMEM, VMEM, ANY],
        out_specs=(VMEM,) * 7,
        scratch_shapes=[
            pltpu.VMEM((ROW_F1, D), BF16),
            pltpu.VMEM((short_len, short_len), F32),
            pltpu.VMEM((short_len, short_len), F32),
            pltpu.VMEM((short_len, 2 * HEAD), F32),
            pltpu.SemaphoreType.DMA((3,)),
        ],
        compiler_params=params,
        name="attend",
    )(layouts, slopes, cols, vecs, stacked)
    grads_deep, table, dresid, small_deep = pl.pallas_call(
        partial(deep_kernel, count),
        out_shape=(
            shape((ROW_END - ROW_F1, D), BF16),
            shape((VOCAB, D), F32),
            shape((rows, D), F32),
            shape((8, 8, D), F32),
        ),
        in_specs=[VMEM, VMEM, VMEM, VMEM, ANY],
        out_specs=(VMEM,) * 4,
        scratch_shapes=[
            pltpu.VMEM((ROW_END - ROW_F1 + VOCAB, D), BF16),
            pltpu.VMEM((rows, D), BF16),
            pltpu.VMEM((rows, FF), BF16),
            pltpu.VMEM((rows, FF), F32),
            pltpu.VMEM((rows, D), BF16),
            pltpu.VMEM((POOL * rows, D), BF16),
            pltpu.VMEM((POOL * rows, VOCAB), BF16),
            pltpu.VMEM((POOL * rows, D), BF16),
            pltpu.VMEM((POOL * rows, D), BF16),
            pltpu.VMEM((rows, D), F32),
            pltpu.VMEM((rows, FF), BF16),
            pltpu.SemaphoreType.DMA((4,)),
        ],
        compiler_params=params,
        name="deep",
    )(by_place, lines, vecs, resid, stacked)
    grads_front, small_front = pl.pallas_call(
        partial(attend_back_kernel, short_len, slots),
        out_shape=(shape((ROW_F1, D), BF16), shape((8, 8, D), F32)),
        in_specs=[SMEM, SMEM] + [VMEM] * 10 + [ANY],
        out_specs=(VMEM,) * 2,
        scratch_shapes=[
            pltpu.VMEM((ROW_F1 - ROW_P, D), BF16),
            pltpu.VMEM((short_len, short_len), F32),
            pltpu.VMEM((short_len, short_len), F32),
            pltpu.VMEM((rows, D), BF16),
            pltpu.VMEM((rows, D), BF16),
            pltpu.VMEM((rows, 3 * D), BF16),
            pltpu.VMEM((rows, D), BF16),
            pltpu.SemaphoreType.DMA((3,)),
        ],
        compiler_params=params,
        name="attend_back",
    )(layouts, slopes, lines, vecs, dresid, shifted, short, normed, qkv, lse, mixed, table, stacked)
    small = jnp.sum(small_deep + small_front, 1)
    return grads_front, grads_deep, small


def adam(param, first_m, second_m, grad, decay):
    first_new = BETA * first_m + (1.0 - BETA) * grad
    second_new = BETA * second_m + (1.0 - BETA) * grad * grad
    correct = 1.0 - BETA**STEP
    update = -RATE * (
        first_new / correct / (jnp.sqrt(second_new / correct) + EPS_ADAM) + decay * param
    )
    return (first_new, second_new, update)


def shards(byte_ids, layouts, weights, vectors, m_weights, v_weights, m_vectors, v_vectors):
    devices = lax.axis_size(AXES)
    micro = byte_ids.shape[0]
    count = float(micro * layouts.shape[1] * devices * byte_ids.shape[2])
    stacked = lax.all_gather(weights.astype(BF16), AXES, axis=0, tiled=True)
    vecs = lax.all_gather(vectors.astype(BF16), AXES, axis=1, tiled=True)
    grads_front, grads_deep, small = device_grads(
        stacked, vecs, byte_ids.reshape(-1, byte_ids.shape[-1]), layouts.reshape(-1), count
    )
    local = jnp.concatenate([grads_front, grads_deep], 0)
    owned = lax.psum_scatter(local.astype(F32), AXES, scatter_dimension=0, tiled=True)
    small = lax.psum(small, AXES)
    loss = small[6, 0] / count
    vec_grads = small[:6]
    width = vectors.shape[1]
    owned_vecs = lax.dynamic_slice(vec_grads, (0, lax.axis_index(AXES) * width), (6, width))
    squares = lax.psum(jnp.sum(owned * owned), AXES) + jnp.sum(vec_grads * vec_grads)
    grad_norm = jnp.sqrt(squares)
    factor = CLIP / jnp.maximum(grad_norm, CLIP)
    first_w, second_w, update_w = adam(weights, m_weights, v_weights, owned * factor, DECAY)
    first_v, second_v, update_v = adam(vectors, m_vectors, v_vectors, owned_vecs * factor, 0.0)
    return (loss, grad_norm, first_w, second_w, update_w, first_v, second_v, update_v)


def solution(mesh):
    in_specs = (
        P(None, AXES, None),
        P(None, AXES),
        P(AXES, None),
        P(None, AXES),
        P(AXES, None),
        P(AXES, None),
        P(None, AXES),
        P(None, AXES),
    )
    out_specs = (
        P(),
        P(),
        P(AXES, None),
        P(AXES, None),
        P(AXES, None),
        P(None, AXES),
        P(None, AXES),
        P(None, AXES),
    )
    return jax.shard_map(shards, mesh=mesh, in_specs=in_specs, out_specs=out_specs, check_vma=False)
```

```python
from functools import partial

import jax
import jax.numpy as jnp
from jax import lax
from jax.experimental import pallas as pl
from jax.experimental.pallas import tpu as pltpu
from jax.sharding import PartitionSpec as P

D = 512
HEADS = 8
HEAD = 64
FF = 2048
VOCAB = 256
POOL = 3

EPS_NORM = 1e-05
EPS_ADAM = 1e-08
CLIP = 0.2
RATE = 0.03
DECAY = 0.1
BETA = 0.5
STEP = 3
NEGATIVE = -1000000000.0

F32 = jnp.float32
BF16 = jnp.bfloat16

ROW_E = 0
ROW_P = VOCAB
ROW_QKV = ROW_P + POOL * D
ROW_O = ROW_QKV + 3 * D
ROW_F1 = ROW_O + D
ROW_F2 = ROW_F1 + FF
ROW_U = ROW_F2 + FF
ROW_H = ROW_U + POOL * D
ROW_END = ROW_H + VOCAB

BLOCK = 256
AXES = ("dp", "fsdp")
SHARD = ROW_END // 32
GATHER_CUT = 208
SCATTER_CUT = 400


def nn(left, right):
    return lax.dot_general(left, right, (((1,), (0,)), ((), ())), preferred_element_type=F32)


def nt(left, right):
    return lax.dot_general(left, right, (((1,), (1,)), ((), ())), preferred_element_type=F32)


def tn(left, right):
    return lax.dot_general(left, right, (((0,), (0,)), ((), ())), preferred_element_type=F32)


def norm_parts(values):
    center = values - jnp.mean(values, -1, keepdims=True)
    spread = jnp.mean(center * center, -1, keepdims=True)
    scale = lax.rsqrt(spread + EPS_NORM)
    return center * scale, scale


def norm_back(unit, scale, gain, grad):
    inner = grad * gain
    mean_inner = jnp.mean(inner, -1, keepdims=True)
    mean_cross = jnp.mean(inner * unit, -1, keepdims=True)
    return scale * (inner - mean_inner - unit * mean_cross)


def fold_rows(values):
    return jnp.sum(values.reshape(values.shape[0] // 8, 8, values.shape[1]), 0)


def one_hot_rows(ids):
    lanes = lax.broadcasted_iota(jnp.int32, (ids.shape[0], VOCAB), 1)
    return jnp.where(lanes == ids, 1.0, 0.0).astype(BF16)


def one_hot_cols(ids):
    lines = lax.broadcasted_iota(jnp.int32, (VOCAB, ids.shape[1]), 0)
    return jnp.where(lines == ids, 1.0, 0.0).astype(BF16)


def rows_of(index, size=BLOCK):
    return pl.ds(pl.multiple_of(index * size, size), size)


class Fetch:
    def __init__(self, pieces, coords_ref, w_ref, sems, base, low, high):
        self.jobs = []
        if len(pieces) == 1:
            size = high - low
            copy = pltpu.make_async_copy(
                pieces[0].at[pl.ds(low, size)], w_ref.at[pl.ds(low - base, size)], sems.at[0]
            )
            self.jobs.append((None, copy))
            return
        dp, z, core = coords_ref[0], coords_ref[1], coords_ref[2]
        shard = SHARD
        first, last = low // shard, (high - 1) // shard
        number = 0
        for side in range(2):
            for k in range(4):
                for part in range(4):
                    for kind, (begin, size) in enumerate(((0, GATHER_CUT), (GATHER_CUT, shard - GATHER_CUT))):
                        d, e = (k, part) if kind == 0 else (part, k)
                        owner = (dp ^ d) * 8 + (z ^ e) * 2 + (core ^ side)
                        wanted = (owner >= first) & (owner <= last)
                        place = jnp.where(wanted, owner * shard - base + begin, 0)
                        copy = pltpu.make_async_copy(
                            pieces[side * 8 + kind * 4 + k].at[pl.ds(part * size, size)],
                            w_ref.at[pl.ds(pl.multiple_of(place, 16), size)],
                            sems.at[number],
                        )
                        self.jobs.append((wanted, copy))
                        number += 1

    def start(self):
        for wanted, copy in self.jobs:
            if wanted is None:
                copy.start()
            else:
                pl.when(wanted)(copy.start)

    def wait(self):
        for wanted, copy in self.jobs:
            if wanted is None:
                copy.wait()
            else:
                pl.when(wanted)(copy.wait)


def attend_kernel(short_len, slots, pieces, coords_ref, lay_ref, slope_ref, cols_ref, vec_ref, *refs):
    w_hbm, refs = refs[:pieces], refs[pieces:]
    (shifted_ref, short_ref, normed_ref, qkv_ref, lse_ref, mixed_ref, resid_ref,
     w_ref, dist_ref, mask_ref, lse_cols, sems) = refs
    rows = short_len * slots
    fetch = Fetch(w_hbm, coords_ref, w_ref, sems, 0, 0, ROW_F1)
    fetch.start()
    fetch.wait()
    gain, offset = vec_ref[0:1, :], vec_ref[1:2, :]

    def pool_step(block, carry):
        at = rows_of(block)
        for j in range(POOL):
            hot = one_hot_rows(cols_ref[at, POOL + j : POOL + j + 1])
            shifted_ref[at, j * D : (j + 1) * D] = nn(hot, w_ref[ROW_E:ROW_P, :]).astype(BF16)
        short = nn(shifted_ref[at, :], w_ref[ROW_P:ROW_QKV, :])
        short_ref[at, :] = short
        unit, _ = norm_parts(short)
        normed_ref[at, :] = (unit * gain + offset).astype(BF16)
        return carry

    lax.fori_loop(0, rows // BLOCK, pool_step, 0)

    def qkv_step(block, carry):
        at = rows_of(block)
        qkv_ref[at, :] = nt(normed_ref[at, :], w_ref[ROW_QKV:ROW_O, :]).astype(BF16)
        return carry

    lax.fori_loop(0, rows // BLOCK, qkv_step, 0)

    left_lanes = lax.broadcasted_iota(jnp.int32, (short_len, 2 * HEAD), 1) < HEAD
    tile = 128
    for slot in range(slots):
        at = pl.ds(slot * short_len, short_len)
        query = lax.broadcasted_iota(jnp.int32, (short_len, short_len), 0)
        key = lax.broadcasted_iota(jnp.int32, (short_len, short_len), 1)
        half = jnp.where(lay_ref[slot] == 1, short_len // 2, short_len)
        allowed = (key <= query) & ((key >= half) == (query >= half))
        dist_ref[...] = (key - query).astype(F32)
        mask_ref[...] = jnp.where(allowed, 0.0, NEGATIVE)

        def head_step(pair, carry):
            lanes = pl.ds(pl.multiple_of(pair * 2 * HEAD, 2 * HEAD), 2 * HEAD)
            lanes_k = pl.ds(pl.multiple_of(D + pair * 2 * HEAD, 2 * HEAD), 2 * HEAD)
            lanes_v = pl.ds(pl.multiple_of(2 * D + pair * 2 * HEAD, 2 * HEAD), 2 * HEAD)
            queries = qkv_ref[at, lanes] * jnp.asarray(0.125, BF16)
            keys = qkv_ref[at, lanes_k]
            values = qkv_ref[at, lanes_v]
            zero = jnp.zeros_like(values)
            vals = [jnp.where(left_lanes, values, zero), jnp.where(left_lanes, zero, values)]
            slots_q = [jnp.where(left_lanes, queries, zero), jnp.where(left_lanes, zero, queries)]
            for part in range(short_len // tile):
                low = part * tile
                mixed = jnp.zeros((tile, 2 * HEAD), F32)
                columns = lse_cols[low : low + tile, :]
                where = lax.broadcasted_iota(jnp.int32, (tile, 2 * HEAD), 1)
                for side in range(2):
                    head = pair * 2 + side
                    slope = slope_ref[head]
                    scores = nt(slots_q[side][low : low + tile], keys)
                    scores = scores + jnp.where(
                        mask_ref[low : low + tile, :] == 0.0, dist_ref[low : low + tile, :] * slope, NEGATIVE
                    )
                    top = jnp.max(scores, -1, keepdims=True)
                    expo = jnp.exp(scores - top)
                    total = jnp.sum(expo, -1, keepdims=True)
                    probs = (expo * (1.0 / total)).astype(BF16)
                    columns = jnp.where(where == head, top + jnp.log(total), columns)
                    mixed = mixed + nn(probs, vals[side])
                lse_cols[low : low + tile, :] = columns
                mixed_ref[pl.ds(slot * short_len + low, tile), lanes] = mixed.astype(BF16)
            return carry

        lse_cols[...] = jnp.zeros_like(lse_cols)
        lax.fori_loop(0, HEADS // 2, head_step, 0)
        turned = lse_cols[...].T
        for head in range(HEADS):
            lse_ref[slot, head] = turned[head : head + 1, :]

    def out_step(block, carry):
        at = rows_of(block)
        resid_ref[at, :] = short_ref[at, :] + nn(mixed_ref[at, :], w_ref[ROW_O:ROW_F1, :])
        return carry

    lax.fori_loop(0, rows // BLOCK, out_step, 0)


def gelu_parts(hidden):
    size = jnp.abs(hidden)
    near = 1.0 / (1.0 + (0.3275911 * 0.7071067811865476) * size)
    bell = jnp.exp(hidden * hidden * -0.5)
    tail = near * (0.127414796 + near * (-0.142248368 + near * (0.7107068705 + near * (-0.7265760135 + near * 0.5307027145))))
    tail = tail * bell
    cdf = jnp.where(hidden >= 0.0, 1.0 - tail, tail)
    return hidden * cdf, cdf + hidden * bell * 0.3989422804014327


def split_store(keep_ref, send_ref, core, rows, values):
    half = D // 2
    low, high = values[:, :half].astype(BF16), values[:, half:].astype(BF16)
    keep_ref[rows, :] = jnp.where(core == 0, low, high)
    send_ref[rows, :] = jnp.where(core == 0, high, low)


def deep_kernel(count, pieces, coords_ref, cols_ref, lines_ref, vec_ref, resid_ref, *refs):
    w_hbm, refs = refs[:pieces], refs[pieces:]
    (keep_ref, send_ref, table_ref, dresid_ref, small_ref,
     w_ref, e_ref, normed_ref, act_ref, slope_ref, deep_ref, final_ref, dlog_ref, dup_ref, low_ref,
     ddeep_ref, dhid_ref, sums_ref, sems, e_sems) = refs
    rows = resid_ref.shape[0]
    blocks = rows // BLOCK
    base = deep_base(pieces)
    core = coords_ref[2]
    fetch = Fetch(w_hbm, coords_ref, w_ref, sems, base, ROW_F1, ROW_END)
    fetch_e = Fetch(w_hbm, coords_ref, e_ref, e_sems, 0, 0, VOCAB)
    fetch.start()
    fetch_e.start()
    f1, f2, up, head = ROW_F1 - base, ROW_F2 - base, ROW_U - base, ROW_H - base
    gain2, offset2 = vec_ref[2:3, :], vec_ref[3:4, :]
    gain_f, offset_f = vec_ref[4:5, :], vec_ref[5:6, :]
    wide = 512

    def norm_step(block, carry):
        at = rows_of(block)
        unit, _ = norm_parts(resid_ref[at, :])
        normed_ref[at, :] = (unit * gain2 + offset2).astype(BF16)
        return carry

    lax.fori_loop(0, blocks, norm_step, 0)
    fetch.wait()
    fetch_e.wait()

    def hidden_step(index, carry):
        block, chunk = index // (FF // wide), index % (FF // wide)
        at = rows_of(block)
        lanes = rows_of(chunk, wide)
        hidden = nt(normed_ref[at, :], w_ref[pl.ds(pl.multiple_of(f1 + chunk * wide, 16), wide), :])
        act, slope = gelu_parts(hidden)
        act_ref[at, lanes] = act.astype(BF16)
        slope_ref[at, lanes] = slope
        return carry

    lax.fori_loop(0, blocks * (FF // wide), hidden_step, 0)

    def deep_step(block, carry):
        at = rows_of(block)
        deep_ref[at, :] = (resid_ref[at, :] + nn(act_ref[at, :], w_ref[f2 : f2 + FF, :])).astype(BF16)
        return carry

    lax.fori_loop(0, blocks, deep_step, 0)
    sums_ref[...] = jnp.zeros_like(sums_ref)

    def head_step(index, carry):
        j, block = index // blocks, index % blocks
        at = rows_of(block)
        there = rows_of(index)
        up_rows = pl.ds(pl.multiple_of(up + j * D, 16), D)
        columns = cols_ref[j, at, :]
        joined = nn(one_hot_rows(columns[:, 0:1]), e_ref[0:VOCAB, :]) + nt(deep_ref[at, :], w_ref[up_rows, :])
        unit, scale = norm_parts(joined)
        final = (unit * gain_f + offset_f).astype(BF16)
        final_ref[there, :] = final
        logits = nt(final, w_ref[head : head + VOCAB, :])
        nexts = columns[:, 2:3]
        lanes = lax.broadcasted_iota(jnp.int32, logits.shape, 1)
        target = jnp.where(lanes == nexts, 1.0, 0.0)
        valid = jnp.where(nexts >= 0, 1.0, 0.0)
        peak = jnp.max(logits, -1, keepdims=True)
        expo = jnp.exp(logits - peak)
        total = jnp.sum(expo, -1, keepdims=True)
        picked = jnp.sum(logits * target, -1, keepdims=True)
        losses = valid * (peak + jnp.log(total) - picked)
        dlogits = ((valid / count) * (expo * (1.0 / total) - target)).astype(BF16)
        dlog_ref[there, :] = dlogits
        dfinal = nn(dlogits, w_ref[head : head + VOCAB, :])
        djoined = norm_back(unit, scale, gain_f, dfinal)
        dup = djoined.astype(BF16)
        dup_ref[there, :] = dup
        low_ref[there, :] = (djoined - dup.astype(F32)).astype(BF16)
        back = nn(dup, w_ref[up_rows, :])

        @pl.when(j == 0)
        def _():
            ddeep_ref[at, :] = back

        @pl.when(j > 0)
        def _():
            ddeep_ref[at, :] += back

        sums_ref[4, :, :] += fold_rows(dfinal * unit)
        sums_ref[5, :, :] += fold_rows(dfinal)
        sums_ref[6, :, :] += jnp.broadcast_to(fold_rows(losses), (8, D))
        return carry

    lax.fori_loop(0, POOL * blocks, head_step, 0)

    out_up, out_head = ROW_U - ROW_F1, ROW_H - ROW_F1
    split_store(keep_ref, send_ref, core, pl.ds(out_head, VOCAB), tn(dlog_ref[...], final_ref[...]))
    for j in range(POOL):
        there = pl.ds(j * rows, rows)
        split_store(keep_ref, send_ref, core, pl.ds(out_up + j * D, D), tn(dup_ref[there, :], deep_ref[...]))
        hot = one_hot_cols(lines_ref[j : j + 1, :])
        part = nn(hot, dup_ref[there, :]) + nn(hot, low_ref[there, :])
        if j == 0:
            table_ref[...] = part
        else:
            table_ref[...] += part

    deep_ref[...] = ddeep_ref[...].astype(BF16)

    def dhid_step(index, carry):
        block, chunk = index // (FF // wide), index % (FF // wide)
        at = rows_of(block)
        lanes = rows_of(chunk, wide)
        dact = nt(deep_ref[at, :], w_ref[pl.ds(pl.multiple_of(f2 + chunk * wide, 16), wide), :])
        dhid_ref[at, lanes] = (dact * slope_ref[at, lanes]).astype(BF16)
        return carry

    lax.fori_loop(0, blocks * (FF // wide), dhid_step, 0)

    def dff_step(chunk, carry):
        lanes = rows_of(chunk, wide)
        split_store(keep_ref, send_ref, core, lanes, tn(dhid_ref[:, lanes], normed_ref[...]))
        there = pl.ds(pl.multiple_of(FF + chunk * wide, wide), wide)
        split_store(keep_ref, send_ref, core, there, tn(act_ref[:, lanes], deep_ref[...]))
        return carry

    lax.fori_loop(0, FF // wide, dff_step, 0)

    def dnorm_step(block, carry):
        at = rows_of(block)
        dnormed = nn(dhid_ref[at, :], w_ref[f1 : f1 + FF, :])
        unit, scale = norm_parts(resid_ref[at, :])
        dresid_ref[at, :] = ddeep_ref[at, :] + norm_back(unit, scale, gain2, dnormed)
        sums_ref[2, :, :] += fold_rows(dnormed * unit)
        sums_ref[3, :, :] += fold_rows(dnormed)
        return carry

    lax.fori_loop(0, blocks, dnorm_step, 0)
    for k in range(8):
        small_ref[k : k + 1, :] = jnp.sum(sums_ref[k], 0, keepdims=True)


def attend_back_kernel(short_len, slots, pieces, coords_ref, lay_ref, slope_ref, lines_ref, vec_ref, dresid_ref,
                       shifted_ref, short_ref, normed_ref, qkv_ref, lse_ref, mixed_ref, table_ref, deep_small_ref, *refs):
    w_hbm, refs = refs[:pieces], refs[pieces:]
    (keep_ref, send_ref, small_ref,
     w_ref, dist_ref, mask_ref, dbranch_ref, dmix_ref, dqkv_ref, dshort_ref, sums_ref, sems) = refs
    rows = short_len * slots
    blocks = rows // BLOCK
    base = 0
    core = coords_ref[2]
    fetch = Fetch(w_hbm, coords_ref, w_ref, sems, 0, 0, ROW_F1)
    fetch.start()
    pool, proj, out = ROW_P - base, ROW_QKV - base, ROW_O - base
    sums_ref[...] = jnp.zeros_like(sums_ref)
    fetch.wait()

    def dmix_step(block, carry):
        at = rows_of(block)
        dbranch = dresid_ref[at, :].astype(BF16)
        dbranch_ref[at, :] = dbranch
        dmix_ref[at, :] = nt(dbranch, w_ref[out : out + D, :]).astype(BF16)
        return carry

    lax.fori_loop(0, blocks, dmix_step, 0)
    split_store(keep_ref, send_ref, core, pl.ds(ROW_O, D), tn(mixed_ref[...], dbranch_ref[...]))

    left_lanes = lax.broadcasted_iota(jnp.int32, (short_len, 2 * HEAD), 1) < HEAD
    tile = 128
    for slot in range(slots):
        at = pl.ds(slot * short_len, short_len)
        key = lax.broadcasted_iota(jnp.int32, (short_len, short_len), 0)
        query = lax.broadcasted_iota(jnp.int32, (short_len, short_len), 1)
        half = jnp.where(lay_ref[slot] == 1, short_len // 2, short_len)
        allowed = (key <= query) & ((key >= half) == (query >= half))
        dist_ref[...] = (key - query).astype(F32)
        mask_ref[...] = jnp.where(allowed, 0.0, NEGATIVE)

        def head_step(pair, carry):
            lanes = pl.ds(pl.multiple_of(pair * 2 * HEAD, 2 * HEAD), 2 * HEAD)
            lanes_k = pl.ds(pl.multiple_of(D + pair * 2 * HEAD, 2 * HEAD), 2 * HEAD)
            lanes_v = pl.ds(pl.multiple_of(2 * D + pair * 2 * HEAD, 2 * HEAD), 2 * HEAD)
            queries = qkv_ref[at, lanes]
            keys = qkv_ref[at, lanes_k]
            values = qkv_ref[at, lanes_v]
            dmix = dmix_ref[at, lanes]
            zero = jnp.zeros_like(values)

            def one_side(side, array):
                return jnp.where(left_lanes, array, zero) if side == 0 else jnp.where(left_lanes, zero, array)

            scaled = queries * jnp.asarray(0.125, BF16)
            dkeys = jnp.zeros((short_len, 2 * HEAD), F32)
            dvalues = jnp.zeros((short_len, 2 * HEAD), F32)
            side_k = [one_side(side, keys) for side in range(2)]
            side_v = [one_side(side, values) for side in range(2)]
            side_q = [one_side(side, queries) for side in range(2)]
            side_m = [one_side(side, dmix) for side in range(2)]
            for part in range(short_len // tile):
                low = part * tile
                dqueries = jnp.zeros((tile, 2 * HEAD), F32)
                for side in range(2):
                    head = pair * 2 + side
                    slope = slope_ref[head]
                    scores = nt(side_k[side], scaled[low : low + tile])
                    scores = scores + jnp.where(
                        mask_ref[:, low : low + tile] == 0.0, dist_ref[:, low : low + tile] * slope, NEGATIVE
                    )
                    probs = jnp.exp(scores - lse_ref[slot, head, :, low : low + tile])
                    dprobs = nt(side_v[side], dmix[low : low + tile])
                    delta = jnp.sum(dprobs * probs, 0, keepdims=True)
                    dscores = (probs * (dprobs - delta) * 0.125).astype(BF16)
                    dvalues = dvalues + nn(probs.astype(BF16), side_m[side][low : low + tile])
                    dkeys = dkeys + nn(dscores, side_q[side][low : low + tile])
                    dqueries = dqueries + tn(dscores, side_k[side])
                dqkv_ref[pl.ds(slot * short_len + low, tile), lanes] = dqueries.astype(BF16)
            dqkv_ref[at, lanes_k] = dkeys.astype(BF16)
            dqkv_ref[at, lanes_v] = dvalues.astype(BF16)
            return carry

        lax.fori_loop(0, HEADS // 2, head_step, 0)

    gain = vec_ref[0:1, :]
    for part in range(3):
        grad = tn(dqkv_ref[:, part * D : (part + 1) * D], normed_ref[...])
        split_store(keep_ref, send_ref, core, pl.ds(ROW_QKV + part * D, D), grad)

    def dshort_step(block, carry):
        at = rows_of(block)
        dnormed = nn(dqkv_ref[at, :], w_ref[proj : proj + 3 * D, :])
        unit, scale = norm_parts(short_ref[at, :])
        dshort_ref[at, :] = (dresid_ref[at, :] + norm_back(unit, scale, gain, dnormed)).astype(BF16)
        sums_ref[0, :, :] += fold_rows(dnormed * unit)
        sums_ref[1, :, :] += fold_rows(dnormed)
        return carry

    lax.fori_loop(0, blocks, dshort_step, 0)
    table = table_ref[...]
    for j in range(POOL):
        cols = slice(j * D, (j + 1) * D)
        split_store(keep_ref, send_ref, core, pl.ds(ROW_P + j * D, D), tn(shifted_ref[:, cols], dshort_ref[...]))
        dshift = nt(dshort_ref[...], w_ref[pool + j * D : pool + (j + 1) * D, :])
        high = dshift.astype(BF16)
        low = (dshift - high.astype(F32)).astype(BF16)
        hot = one_hot_cols(lines_ref[POOL + j : POOL + j + 1, :])
        table = table + nn(hot, high) + nn(hot, low)
    split_store(keep_ref, send_ref, core, pl.ds(ROW_E, VOCAB), table)
    small_ref[...] = deep_small_ref[...]
    for k in range(2):
        small_ref[k : k + 1, :] = jnp.sum(sums_ref[k], 0, keepdims=True)
    half = D // 2
    for k in range(2):
        send_ref[ROW_F1 + 16 * k : ROW_F1 + 16 * (k + 1), :] = two_parts(small_ref[:, k * half : (k + 1) * half])


def two_parts(values):
    high = values.astype(BF16)
    low = (values - high.astype(F32)).astype(BF16)
    return jnp.concatenate([high.astype(F32), low.astype(F32)], 0).astype(BF16)


def one_value(parts):
    parts = parts.astype(F32)
    return parts[:8] + parts[8:]


def core_sum_kernel(coords_ref, keep_front, keep_deep, recv_front, recv_deep, small_ref,
                    p0, p1, p2, p3, q0, q1, q2, q3,
                    keep_ref, recv_ref, sems):
    copies = [
        pltpu.make_async_copy(source, target, sems.at[k])
        for k, (source, target) in enumerate((
            (keep_deep, keep_ref.at[pl.ds(ROW_F1, ROW_END - ROW_F1)]),
            (recv_deep, recv_ref.at[pl.ds(ROW_F1, ROW_END - ROW_F1)]),
            (keep_front, keep_ref.at[pl.ds(0, ROW_F1)]),
            (recv_front.at[pl.ds(0, ROW_F1)], recv_ref.at[pl.ds(0, ROW_F1)]),
            (recv_front.at[pl.ds(ROW_F1, 32)], recv_ref.at[pl.ds(ROW_END, 32)]),
        ))
    ]
    for copy in copies:
        copy.start()
    for copy in copies:
        copy.wait()
    dp, z = coords_ref[0], coords_ref[1]
    quarter = D // 4
    line = 2 * SHARD

    def total(half, column, x, zed, begin, size):
        row = half * (8 * line) + x * (4 * line) + zed * line + begin
        at = pl.ds(pl.multiple_of(row, 16), size)
        lanes = pl.ds(pl.multiple_of(column * quarter, quarter), quarter)
        return (keep_ref[at, lanes].astype(F32) + recv_ref[at, lanes].astype(F32)).astype(BF16)

    rest = line - SCATTER_CUT
    for k, p_ref in enumerate((p0, p1, p2, p3)):
        there = dp ^ k

        def p_step(index, carry):
            half, zed = index // 4, index % 4
            p_ref[pl.ds(pl.multiple_of(index * SCATTER_CUT, 16), SCATTER_CUT), :] = total(
                half, there // 2, there % 2, zed, 0, SCATTER_CUT
            )
            return carry

        lax.fori_loop(0, 8, p_step, 0)
    for k, q_ref in enumerate((q0, q1, q2, q3)):
        zed = z ^ k

        def q_step(index, carry):
            half, there = index // 4, index % 4
            q_ref[pl.ds(pl.multiple_of(index * rest, 16), rest), :] = total(
                half, there // 2, there % 2, zed, SCATTER_CUT, rest
            )
            return carry

        lax.fori_loop(0, 8, q_step, 0)
    for k in range(2):
        both = small_ref[:, 2 * k * quarter : 2 * (k + 1) * quarter] + one_value(
            recv_ref[ROW_END + 16 * k : ROW_END + 16 * (k + 1), :]
        )
        for side in range(2):
            parts = two_parts(both[:, side * quarter : (side + 1) * quarter])
            row = 8 * SCATTER_CUT + 16 * (2 * k + side)
            for p_ref in (p0, p1, p2, p3):
                p_ref[row : row + 16, :] = parts


def first_sum_kernel(coords_ref, p0, p1, p2, p3, q0, q1, q2, q3,
                     s0, s1, s2, s3, t0, t1, t2, t3):
    dp, z = coords_ref[0], coords_ref[1]
    rest = 2 * SHARD - SCATTER_CUT

    def total(refs, row, size):
        at = pl.ds(pl.multiple_of(row, 16), size)
        return (refs[0][at, :].astype(F32) + refs[1][at, :].astype(F32)) + (
            refs[2][at, :].astype(F32) + refs[3][at, :].astype(F32)
        )

    for k, s_ref in enumerate((s0, s1, s2, s3)):
        for half in range(2):
            s_ref[half * SCATTER_CUT : (half + 1) * SCATTER_CUT, :] = total(
                (p0, p1, p2, p3), (half * 4 + (z ^ k)) * SCATTER_CUT, SCATTER_CUT
            ).astype(BF16)
    for k, t_ref in enumerate((t0, t1, t2, t3)):
        for half in range(2):
            t_ref[half * rest : (half + 1) * rest, :] = total(
                (q0, q1, q2, q3), (half * 4 + (dp ^ k)) * rest, rest
            ).astype(BF16)
    for k in range(4):
        row = 8 * SCATTER_CUT + 16 * k
        value = sum(one_value(ref[row : row + 16, :]) for ref in (p0, p1, p2, p3))
        parts = two_parts(value)
        for s_ref in (s0, s1, s2, s3):
            s_ref[2 * SCATTER_CUT + 16 * k : 2 * SCATTER_CUT + 16 * (k + 1), :] = parts


def last_sum_kernel(coords_ref, s0, s1, s2, s3, t0, t1, t2, t3, mine_ref, other_ref, small_ref, square_ref):
    own = coords_ref[0] // 2
    line = 2 * SHARD
    rest = line - SCATTER_CUT

    def total(refs, half, size):
        at = pl.ds(pl.multiple_of(half * size, 16), size)
        return (refs[0][at, :].astype(F32) + refs[1][at, :].astype(F32)) + (
            refs[2][at, :].astype(F32) + refs[3][at, :].astype(F32)
        )

    squares = jnp.zeros((8, D // 4), F32)
    for half, out_ref in ((own, mine_ref), (1 - own, other_ref)):
        first = total((s0, s1, s2, s3), half, SCATTER_CUT)
        second = total((t0, t1, t2, t3), half, rest)
        out_ref[0:SCATTER_CUT, :] = first
        out_ref[SCATTER_CUT:line, :] = second
        squares = squares + fold_rows(first * first) + fold_rows(second * second)
    for k in range(4):
        row = 2 * SCATTER_CUT + 16 * k
        small_ref[:, k * (D // 4) : (k + 1) * (D // 4)] = sum(
            one_value(ref[row : row + 16, :]) for ref in (s0, s1, s2, s3)
        )
    square_ref[...] = squares


def step_inputs(byte_ids, layouts):
    slots, length = byte_ids.shape
    places = jnp.arange(length, dtype=jnp.int32)[None, :]
    half = length // 2
    split = (layouts == 1)[:, None]
    first = jnp.where(split & (places >= half), half, 0)
    last = jnp.where(split & (places < half), half, length)
    back = jnp.pad(byte_ids[:, :-2], ((0, 0), (2, 0)))
    back = jnp.where(places - 2 >= first, back, -1)
    ahead = jnp.pad(byte_ids[:, 1:], ((0, 0), (0, 1)))
    ahead = jnp.where(places + 1 < last, ahead, -1)
    kinds = jnp.stack([byte_ids, back, ahead], 0)
    kinds = kinds.reshape(3, slots, length // POOL, POOL).transpose(0, 3, 1, 2)
    kinds = kinds.reshape(3, POOL, slots * (length // POOL))
    lines = kinds.reshape(3 * POOL, -1)
    return lines


VMEM = pl.BlockSpec(memory_space=pltpu.VMEM)
SMEM = pl.BlockSpec(memory_space=pltpu.SMEM)
ANY = pl.BlockSpec(memory_space=pl.ANY)
LIMIT = 58 * 1024 * 1024


def deep_base(pieces):
    return ROW_F1 if pieces == 1 else ROW_F1 // SHARD * SHARD


def device_grads(pieces, coords, vecs, byte_ids, layouts, count, exchange):
    slots, length = byte_ids.shape
    short_len = length // POOL
    rows = slots * short_len
    lines = step_inputs(byte_ids, layouts)
    by_place = lines.reshape(3, POOL, rows).transpose(1, 2, 0)
    lines = jnp.pad(lines, ((0, 16 - lines.shape[0]), (0, 0)))
    cols = lines.T
    slopes = 2.0 ** (-8.0 * (jnp.arange(HEADS, dtype=F32) + 1.0) / HEADS)
    vecs = jnp.pad(vecs.astype(F32), ((0, 2), (0, 0)))
    shape = jax.ShapeDtypeStruct
    params = pltpu.CompilerParams(vmem_limit_bytes=LIMIT)
    number = len(pieces)
    whole_shards = number > 1
    front_rows = -(-ROW_F1 // SHARD) * SHARD if whole_shards else ROW_F1
    deep_rows = ROW_END - deep_base(number)
    table_rows = SHARD if whole_shards else VOCAB
    jobs = 64 if whole_shards else 1
    half = D // 2
    shifted, short, normed, qkv, lse, mixed, resid = pl.pallas_call(
        partial(attend_kernel, short_len, slots, number),
        out_shape=(
            shape((rows, POOL * D), BF16),
            shape((rows, D), F32),
            shape((rows, D), BF16),
            shape((rows, 3 * D), BF16),
            shape((slots, HEADS, 1, short_len), F32),
            shape((rows, D), BF16),
            shape((rows, D), F32),
        ),
        in_specs=[SMEM, SMEM, SMEM, VMEM, VMEM] + [ANY] * number,
        out_specs=(VMEM,) * 7,
        scratch_shapes=[
            pltpu.VMEM((front_rows, D), BF16),
            pltpu.VMEM((short_len, short_len), F32),
            pltpu.VMEM((short_len, short_len), F32),
            pltpu.VMEM((short_len, 2 * HEAD), F32),
            pltpu.SemaphoreType.DMA((jobs,)),
        ],
        compiler_params=params,
        name="attend",
    )(coords, layouts, slopes, cols, vecs, *pieces)
    keep_deep, send_deep, table, dresid, small_deep = pl.pallas_call(
        partial(deep_kernel, count, number),
        out_shape=(
            shape((ROW_END - ROW_F1, half), BF16),
            shape((ROW_END - ROW_F1, half), BF16),
            shape((VOCAB, D), F32),
            shape((rows, D), F32),
            shape((8, D), F32),
        ),
        in_specs=[SMEM] + [VMEM] * 4 + [ANY] * number,
        out_specs=(VMEM,) * 5,
        scratch_shapes=[
            pltpu.VMEM((deep_rows, D), BF16),
            pltpu.VMEM((table_rows, D), BF16),
            pltpu.VMEM((rows, D), BF16),
            pltpu.VMEM((rows, FF), BF16),
            pltpu.VMEM((rows, FF), F32),
            pltpu.VMEM((rows, D), BF16),
            pltpu.VMEM((POOL * rows, D), BF16),
            pltpu.VMEM((POOL * rows, VOCAB), BF16),
            pltpu.VMEM((POOL * rows, D), BF16),
            pltpu.VMEM((POOL * rows, D), BF16),
            pltpu.VMEM((rows, D), F32),
            pltpu.VMEM((rows, FF), BF16),
            pltpu.VMEM((8, 8, D), F32),
            pltpu.SemaphoreType.DMA((jobs,)),
            pltpu.SemaphoreType.DMA((jobs,)),
        ],
        compiler_params=params,
        name="deep",
    )(coords, by_place, lines, vecs, resid, *pieces)
    recv_deep = exchange(send_deep)
    keep_front, send_front, small = pl.pallas_call(
        partial(attend_back_kernel, short_len, slots, number),
        out_shape=(shape((ROW_F1, half), BF16), shape((ROW_F1 + 32, half), BF16), shape((8, D), F32)),
        in_specs=[SMEM, SMEM, SMEM] + [VMEM] * 11 + [ANY] * number,
        out_specs=(VMEM,) * 3,
        scratch_shapes=[
            pltpu.VMEM((front_rows, D), BF16),
            pltpu.VMEM((short_len, short_len), F32),
            pltpu.VMEM((short_len, short_len), F32),
            pltpu.VMEM((rows, D), BF16),
            pltpu.VMEM((rows, D), BF16),
            pltpu.VMEM((rows, 3 * D), BF16),
            pltpu.VMEM((rows, D), BF16),
            pltpu.VMEM((2, 8, D), F32),
            pltpu.SemaphoreType.DMA((jobs,)),
        ],
        compiler_params=params,
        cost_estimate=pl.CostEstimate(flops=13_000_000_000, bytes_accessed=20_000_000, transcendentals=2_400_000),
        name="attend_back",
    )(coords, layouts, slopes, lines, vecs, dresid, shifted, short, normed, qkv, lse, mixed, table, small_deep, *pieces)
    recv_front = exchange(send_front)
    return keep_front, recv_front, keep_deep, recv_deep, small


def swap_with(array, line=0, zed=0, core=0):
    lines, rest = lax.axis_size("dp"), lax.axis_size("fsdp")
    pairs = [
        (d * rest + f, (d ^ line) * rest + (f ^ (2 * zed + core)))
        for d in range(lines)
        for f in range(rest)
    ]
    return lax.ppermute(array, AXES, pairs)


def gather_pieces(shard):
    first, second = shard[:GATHER_CUT], shard[GATHER_CUT:]
    along = jnp.concatenate([first] + [swap_with(first, zed=k) for k in (1, 2, 3)], 0)
    across = jnp.concatenate([second] + [swap_with(second, line=k) for k in (1, 2, 3)], 0)
    pieces = [along] + [swap_with(along, line=k) for k in (1, 2, 3)]
    pieces += [across] + [swap_with(across, zed=k) for k in (1, 2, 3)]
    return pieces + [swap_with(piece, core=1) for piece in pieces]


def gather_vectors(vectors):
    width = vectors.shape[1]
    spread = jnp.zeros((8, lax.axis_size(AXES) * width), BF16)
    spread = lax.dynamic_update_slice(spread, jnp.pad(vectors, ((0, 2), (0, 0))), (0, lax.axis_index(AXES) * width))
    spread = spread + swap_with(spread, core=1)
    for k in (1, 2):
        spread = spread + swap_with(spread, line=k)
    for k in (1, 2):
        spread = spread + swap_with(spread, zed=k)
    return spread[:6]


def scatter_sum(coords, keep_front, recv_front, keep_deep, recv_deep, small):
    shape = jax.ShapeDtypeStruct
    params = pltpu.CompilerParams(vmem_limit_bytes=LIMIT)
    quarter = D // 4
    line = 2 * SHARD
    rest = line - SCATTER_CUT
    parts = pl.pallas_call(
        core_sum_kernel,
        out_shape=(shape((8 * SCATTER_CUT + 64, quarter), BF16),) * 4 + (shape((8 * rest, quarter), BF16),) * 4,
        in_specs=[SMEM] + [ANY] * 4 + [VMEM],
        out_specs=(VMEM,) * 8,
        scratch_shapes=[
            pltpu.VMEM((ROW_END, D // 2), BF16),
            pltpu.VMEM((ROW_END + 32, D // 2), BF16),
            pltpu.SemaphoreType.DMA((5,)),
        ],
        compiler_params=params,
        name="core_sum",
    )(coords, keep_front, keep_deep, recv_front, recv_deep, small)
    first = [parts[0]] + [swap_with(parts[k], line=k) for k in (1, 2, 3)]
    first += [parts[4]] + [swap_with(parts[4 + k], zed=k) for k in (1, 2, 3)]
    parts = pl.pallas_call(
        first_sum_kernel,
        out_shape=(shape((2 * SCATTER_CUT + 64, quarter), BF16),) * 4 + (shape((2 * rest, quarter), BF16),) * 4,
        in_specs=[SMEM] + [VMEM] * 8,
        out_specs=(VMEM,) * 8,
        compiler_params=params,
        name="first_sum",
    )(coords, *first)
    second = [parts[0]] + [swap_with(parts[k], zed=k) for k in (1, 2, 3)]
    second += [parts[4]] + [swap_with(parts[4 + k], line=k) for k in (1, 2, 3)]
    mine, other, small, squares = pl.pallas_call(
        last_sum_kernel,
        out_shape=(shape((line, quarter), F32),) * 2 + (shape((8, D), F32), shape((8, quarter), F32)),
        in_specs=[SMEM] + [VMEM] * 8,
        out_specs=(VMEM,) * 4,
        compiler_params=params,
        name="last_sum",
    )(coords, *second)
    row, core = coords[0] // 2, coords[2]
    theirs = swap_with(other, line=2)
    half = jnp.concatenate(
        [jnp.where(row == 0, mine, theirs), jnp.where(row == 0, theirs, mine)], 1
    )
    keep = jnp.where(core == 0, half[:SHARD], half[SHARD:])
    send = jnp.where(core == 0, half[SHARD:], half[:SHARD])
    back = swap_with(send, core=1)
    owned = jnp.concatenate([jnp.where(core == 0, keep, back), jnp.where(core == 0, back, keep)], 1)
    return owned, small, jnp.sum(squares)


def sum_all(value):
    value = jnp.broadcast_to(value, (8, 128))
    value = value + swap_with(value, core=1)
    for k in (1, 2):
        value = value + swap_with(value, line=k)
    for k in (1, 2):
        value = value + swap_with(value, zed=k)
    return value[0, 0]


def adam(param, first_m, second_m, grad, decay):
    first_new = BETA * first_m + (1.0 - BETA) * grad
    second_new = BETA * second_m + (1.0 - BETA) * grad * grad
    correct = 1.0 - BETA**STEP
    update = -RATE * (
        first_new / correct / (jnp.sqrt(second_new / correct) + EPS_ADAM) + decay * param
    )
    return (first_new, second_new, update)


def shards(byte_ids, layouts, weights, vectors, m_weights, v_weights, m_vectors, v_vectors):
    devices = lax.axis_size(AXES)
    micro = byte_ids.shape[0]
    count = float(micro * layouts.shape[1] * devices * byte_ids.shape[2])
    lines, rest = lax.axis_size("dp"), lax.axis_size("fsdp")
    place = lax.axis_index("fsdp")
    coords = jnp.stack([lax.axis_index("dp"), place // 2, place % 2, 0]).astype(jnp.int32)
    paired = lines == 4 and rest == 8 and weights.shape[0] == SHARD
    weights_low = weights.astype(BF16)
    vectors_low = vectors.astype(BF16)
    width = vectors.shape[1]
    mine = lax.axis_index(AXES) * width
    flat_ids, flat_layouts = byte_ids.reshape(-1, byte_ids.shape[-1]), layouts.reshape(-1)
    if paired:
        pieces = gather_pieces(weights_low)
        vecs = gather_vectors(vectors_low)
        parts = device_grads(pieces, coords, vecs, flat_ids, flat_layouts, count, partial(swap_with, core=1))
        owned, small, squares = scatter_sum(coords, *parts)
        squares = sum_all(squares)
    else:
        coords = coords * 0
        pieces = [lax.all_gather(weights_low, AXES, axis=0, tiled=True)]
        vecs = lax.all_gather(vectors_low, AXES, axis=1, tiled=True)
        parts = device_grads(pieces, coords, vecs, flat_ids, flat_layouts, count, lambda array: array)
        keep_front, send_front, keep_deep, send_deep, small = parts
        local = jnp.concatenate(
            [
                jnp.concatenate([keep_front, send_front[:ROW_F1]], 1),
                jnp.concatenate([keep_deep, send_deep], 1),
            ],
            0,
        )
        owned = lax.psum_scatter(local.astype(F32), AXES, scatter_dimension=0, tiled=True)
        small, squares = lax.psum((small, jnp.sum(owned * owned)), AXES)
    loss = small[6, 0] / count
    vec_grads = small[:6]
    owned_vecs = lax.dynamic_slice(vec_grads, (0, mine), (6, width))
    squares = squares + jnp.sum(vec_grads * vec_grads)
    grad_norm = jnp.sqrt(squares)
    factor = CLIP / jnp.maximum(grad_norm, CLIP)
    first_w, second_w, update_w = adam(weights, m_weights, v_weights, owned * factor, DECAY)
    first_v, second_v, update_v = adam(vectors, m_vectors, v_vectors, owned_vecs * factor, 0.0)
    return (loss, grad_norm, first_w, second_w, update_w, first_v, second_v, update_v)


def solution(mesh):
    in_specs = (
        P(None, AXES, None),
        P(None, AXES),
        P(AXES, None),
        P(None, AXES),
        P(AXES, None),
        P(AXES, None),
        P(None, AXES),
        P(None, AXES),
    )
    out_specs = (
        P(),
        P(),
        P(AXES, None),
        P(AXES, None),
        P(AXES, None),
        P(None, AXES),
        P(None, AXES),
        P(None, AXES),
    )
    return jax.shard_map(shards, mesh=mesh, in_specs=in_specs, out_specs=out_specs, check_vma=False)
```

```python
from functools import partial

import jax
import jax.numpy as jnp
import numpy as np
from jax import lax
from jax.experimental import pallas as pl
from jax.experimental.pallas import tpu as pltpu
from jax.sharding import PartitionSpec as P

D = 512
HEADS = 8
HEAD = 64
FF = 2048
VOCAB = 256
POOL = 3

EPS_NORM = 1e-05
EPS_ADAM = 1e-08
CLIP = 0.2
RATE = 0.03
DECAY = 0.1
BETA = 0.5
STEP = 3
NEGATIVE = -1000000000.0

F32 = jnp.float32
BF16 = jnp.bfloat16

ROW_E = 0
ROW_P = VOCAB
ROW_QKV = ROW_P + POOL * D
ROW_O = ROW_QKV + 3 * D
ROW_F1 = ROW_O + D
ROW_F2 = ROW_F1 + FF
ROW_U = ROW_F2 + FF
ROW_H = ROW_U + POOL * D
ROW_END = ROW_H + VOCAB

BLOCK = 256
AXES = ("dp", "fsdp")
SHARD = ROW_END // 32
GATHER_CUT = 208
SCATTER_CUT = 400


def nn(left, right):
    return lax.dot_general(left, right, (((1,), (0,)), ((), ())), preferred_element_type=F32)


def nt(left, right):
    return lax.dot_general(left, right, (((1,), (1,)), ((), ())), preferred_element_type=F32)


def tn(left, right):
    return lax.dot_general(left, right, (((0,), (0,)), ((), ())), preferred_element_type=F32)


def norm_parts(values):
    center = values - jnp.mean(values, -1, keepdims=True)
    spread = jnp.mean(center * center, -1, keepdims=True)
    scale = lax.rsqrt(spread + EPS_NORM)
    return center * scale, scale


def norm_back(unit, scale, gain, grad):
    inner = grad * gain
    mean_inner = jnp.mean(inner, -1, keepdims=True)
    mean_cross = jnp.mean(inner * unit, -1, keepdims=True)
    return scale * (inner - mean_inner - unit * mean_cross)


def fold_rows(values):
    return jnp.sum(values.reshape(values.shape[0] // 8, 8, values.shape[1]), 0)


def one_hot_rows(ids):
    lanes = lax.broadcasted_iota(jnp.int32, (ids.shape[0], VOCAB), 1)
    return jnp.where(lanes == ids, 1.0, 0.0).astype(BF16)


def one_hot_cols(ids):
    lines = lax.broadcasted_iota(jnp.int32, (VOCAB, ids.shape[1]), 0)
    return jnp.where(lines == ids, 1.0, 0.0).astype(BF16)


def rows_of(index, size=BLOCK):
    return pl.ds(pl.multiple_of(index * size, size), size)


def gathered_parts(coords_ref):
    dp, z, core = coords_ref[0], coords_ref[1], coords_ref[2]
    for side in range(2):
        for k in range(4):
            for part in range(4):
                for kind in range(2):
                    d, e = (k, part) if kind == 0 else (part, k)
                    line = dp ^ d
                    yield side * 8 + kind * 4 + k, part, kind, line // 2, (line % 2) * 8 + (z ^ e) * 2 + (core ^ side)


class Fetch:
    def __init__(self, pieces, coords_ref, w_ref, sems, base, low, high):
        self.jobs = []
        if len(pieces) == 1:
            size = high - low
            copy = pltpu.make_async_copy(
                pieces[0].at[pl.ds(low, size)], w_ref.at[pl.ds(low - base, size)], sems.at[0]
            )
            self.jobs.append((None, copy))
            return
        first, last = low // SHARD, (high - 1) // SHARD
        half = D // 2
        for number, (piece, part, kind, y, shard) in enumerate(gathered_parts(coords_ref)):
            begin, size, step = ((0, GATHER_CUT, GATHER_CUT + 16), (GATHER_CUT, SHARD - GATHER_CUT, SHARD - GATHER_CUT))[kind]
            wanted = (shard >= first) & (shard <= last)
            place = jnp.where(wanted, shard * SHARD - base + begin, 0)
            copy = pltpu.make_async_copy(
                pieces[piece].at[pl.ds(part * step, size)],
                w_ref.at[pl.ds(pl.multiple_of(place, 16), size), pl.ds(pl.multiple_of(y * half, half), half)],
                sems.at[number],
            )
            self.jobs.append((wanted, copy))

    def start(self):
        for wanted, copy in self.jobs:
            if wanted is None:
                copy.start()
            else:
                pl.when(wanted)(copy.start)

    def wait(self):
        for wanted, copy in self.jobs:
            if wanted is None:
                copy.wait()
            else:
                pl.when(wanted)(copy.wait)


def attend_kernel(short_len, slots, pieces, coords_ref, lay_ref, slope_ref, ids_ref, *refs):
    w_hbm, refs = refs[:pieces], refs[pieces:]
    if pieces == 1:
        vec_in_ref, refs = refs[0], refs[1:]
    (shifted_ref, short_ref, normed_ref, qkv_ref, lse_ref, mixed_ref, resid_ref, lines_ref, cols_ref, vec_ref,
     w_ref, dist_ref, mask_ref, lse_cols, part_ref, sems, part_sems) = refs
    rows = short_len * slots
    fetch = Fetch(w_hbm, coords_ref, w_ref, sems, 0, 0, ROW_F1)
    fetch.start()
    copies = []
    if pieces > 1:
        for piece, part, kind, _, _ in gathered_parts(coords_ref):
            if kind == 0:
                place = pl.ds(part * (GATHER_CUT + 16) + GATHER_CUT, 16)
                number = len(copies)
                copies.append(
                    pltpu.make_async_copy(w_hbm[piece].at[place], part_ref.at[number], part_sems.at[number])
                )
        for copy in copies:
            copy.start()

    ids = ids_ref[...]
    group = lax.broadcasted_iota(jnp.int32, (1, rows), 1)
    starts = group == 0
    for slot in range(slots):
        starts = starts | (group == slot * short_len)
        starts = starts | ((group == slot * short_len + short_len // 2) & (lay_ref[slot] == 1))
    ends = group == rows - 1
    for slot in range(slots):
        ends = ends | (group == (slot + 1) * short_len - 1)
        ends = ends | ((group == slot * short_len + short_len // 2 - 1) & (lay_ref[slot] == 1))
    before, after = pltpu.roll(ids, 1, 1), pltpu.roll(ids, rows - 1, 1)
    own = [ids[j : j + 1] for j in range(POOL)]
    back = [jnp.where(starts, -1, before[1:2]), jnp.where(starts, -1, before[2:3]), ids[0:1]]
    ahead = [ids[1:2], ids[2:3], jnp.where(ends, -1, after[0:1])]
    for j in range(POOL):
        lines_ref[j : j + 1, :] = own[j]
        lines_ref[POOL + j : POOL + j + 1, :] = back[j]
        lines_ref[2 * POOL + j : 2 * POOL + j + 1, :] = ahead[j]
    lines_ref[3 * POOL :, :] = jnp.zeros((16 - 3 * POOL, rows), jnp.int32)
    turned = jnp.concatenate([lines_ref[...].astype(F32), jnp.zeros((112, rows), F32)], 0).T.astype(jnp.int32)
    for j in range(POOL):
        cols_ref[j] = pltpu.roll(turned, 128 - j, 1)

    for copy in copies:
        copy.wait()
    if pieces > 1:
        both = part_ref[0].astype(F32)
        for k in range(1, len(copies)):
            both = both + part_ref[k].astype(F32)
        vec_ref[...] = jnp.concatenate([both[:8], both[8:]], 1)
    else:
        vec_ref[...] = vec_in_ref[...]
    fetch.wait()
    gain, offset = vec_ref[0:1, :], vec_ref[1:2, :]

    def pool_step(block, carry):
        at = rows_of(block)
        for j in range(POOL):
            hot = one_hot_rows(cols_ref[j, at, POOL : POOL + 1])
            shifted_ref[at, j * D : (j + 1) * D] = nn(hot, w_ref[ROW_E:ROW_P, :]).astype(BF16)
        short = nn(shifted_ref[at, :], w_ref[ROW_P:ROW_QKV, :])
        short_ref[at, :] = short
        unit, _ = norm_parts(short)
        normed_ref[at, :] = (unit * gain + offset).astype(BF16)
        return carry

    lax.fori_loop(0, rows // BLOCK, pool_step, 0)

    def qkv_step(block, carry):
        at = rows_of(block)
        qkv_ref[at, :] = nt(normed_ref[at, :], w_ref[ROW_QKV:ROW_O, :]).astype(BF16)
        return carry

    lax.fori_loop(0, rows // BLOCK, qkv_step, 0)

    left_lanes = lax.broadcasted_iota(jnp.int32, (short_len, 2 * HEAD), 1) < HEAD
    tile = 128
    for slot in range(slots):
        at = pl.ds(slot * short_len, short_len)
        query = lax.broadcasted_iota(jnp.int32, (short_len, short_len), 0)
        key = lax.broadcasted_iota(jnp.int32, (short_len, short_len), 1)
        half = jnp.where(lay_ref[slot] == 1, short_len // 2, short_len)
        allowed = (key <= query) & ((key >= half) == (query >= half))
        dist_ref[...] = (key - query).astype(F32)
        mask_ref[...] = jnp.where(allowed, 0.0, NEGATIVE)

        def head_step(pair, carry):
            lanes = pl.ds(pl.multiple_of(pair * 2 * HEAD, 2 * HEAD), 2 * HEAD)
            lanes_k = pl.ds(pl.multiple_of(D + pair * 2 * HEAD, 2 * HEAD), 2 * HEAD)
            lanes_v = pl.ds(pl.multiple_of(2 * D + pair * 2 * HEAD, 2 * HEAD), 2 * HEAD)
            queries = qkv_ref[at, lanes] * jnp.asarray(0.125, BF16)
            keys = qkv_ref[at, lanes_k]
            values = qkv_ref[at, lanes_v]
            zero = jnp.zeros_like(values)
            vals = [jnp.where(left_lanes, values, zero), jnp.where(left_lanes, zero, values)]
            slots_q = [jnp.where(left_lanes, queries, zero), jnp.where(left_lanes, zero, queries)]
            for part in range(short_len // tile):
                low = part * tile
                mixed = jnp.zeros((tile, 2 * HEAD), F32)
                columns = lse_cols[low : low + tile, :]
                where = lax.broadcasted_iota(jnp.int32, (tile, 2 * HEAD), 1)
                for side in range(2):
                    head = pair * 2 + side
                    slope = slope_ref[head]
                    scores = nt(slots_q[side][low : low + tile], keys)
                    scores = scores + jnp.where(
                        mask_ref[low : low + tile, :] == 0.0, dist_ref[low : low + tile, :] * slope, NEGATIVE
                    )
                    top = jnp.max(scores, -1, keepdims=True)
                    expo = jnp.exp(scores - top)
                    total = jnp.sum(expo, -1, keepdims=True)
                    probs = (expo * (1.0 / total)).astype(BF16)
                    columns = jnp.where(where == head, top + jnp.log(total), columns)
                    mixed = mixed + nn(probs, vals[side])
                lse_cols[low : low + tile, :] = columns
                mixed_ref[pl.ds(slot * short_len + low, tile), lanes] = mixed.astype(BF16)
            return carry

        lse_cols[...] = jnp.zeros_like(lse_cols)
        lax.fori_loop(0, HEADS // 2, head_step, 0)
        turned = lse_cols[...].T
        for head in range(HEADS):
            lse_ref[slot, head] = turned[head : head + 1, :]

    def out_step(block, carry):
        at = rows_of(block)
        resid_ref[at, :] = short_ref[at, :] + nn(mixed_ref[at, :], w_ref[ROW_O:ROW_F1, :])
        return carry

    lax.fori_loop(0, rows // BLOCK, out_step, 0)


def gelu_parts(hidden):
    size = jnp.abs(hidden)
    near = 1.0 / (1.0 + (0.3275911 * 0.7071067811865476) * size)
    bell = jnp.exp(hidden * hidden * -0.5)
    tail = near * (0.127414796 + near * (-0.142248368 + near * (0.7107068705 + near * (-0.7265760135 + near * 0.5307027145))))
    tail = tail * bell
    cdf = jnp.where(hidden >= 0.0, 1.0 - tail, tail)
    return hidden * cdf, cdf + hidden * bell * 0.3989422804014327


def split_store(keep_ref, send_ref, core, rows, values):
    half = D // 2
    low, high = values[:, :half].astype(BF16), values[:, half:].astype(BF16)
    keep_ref[rows, :] = jnp.where(core == 0, low, high)
    send_ref[rows, :] = jnp.where(core == 0, high, low)


def deep_kernel(count, pieces, coords_ref, cols_ref, lines_ref, vec_ref, resid_ref, *refs):
    w_hbm, refs = refs[:pieces], refs[pieces:]
    if pieces > 1:
        tail_hbm, refs = refs[0], refs[1:]
    (keep_ref, send_ref, table_ref, dresid_ref, small_ref,
     w_ref, e_ref, normed_ref, act_ref, slope_ref, deep_ref, final_ref, dlog_ref, dup_ref, low_ref,
     ddeep_ref, dhid_ref, sums_ref, sems, e_sems, tail_sems) = refs
    rows = resid_ref.shape[0]
    blocks = rows // BLOCK
    base = deep_base(pieces)
    core = coords_ref[2]
    fetches = [
        Fetch(w_hbm, coords_ref, w_ref, sems, base, ROW_F1, ROW_END if pieces == 1 else ROW_END // 2),
        Fetch(w_hbm, coords_ref, e_ref, e_sems, 0, 0, VOCAB),
    ]
    for fetch in fetches:
        fetch.start()
    copies = []
    if pieces > 1:
        half = ROW_END // 2
        for y in range(2):
            copies.append(
                pltpu.make_async_copy(
                    tail_hbm.at[pl.ds(y * half, half)],
                    w_ref.at[pl.ds(half - base, half), pl.ds(y * (D // 2), D // 2)],
                    tail_sems.at[y],
                )
            )
    for copy in copies:
        copy.start()
    f1, f2, up, head = ROW_F1 - base, ROW_F2 - base, ROW_U - base, ROW_H - base
    gain2, offset2 = vec_ref[2:3, :], vec_ref[3:4, :]
    gain_f, offset_f = vec_ref[4:5, :], vec_ref[5:6, :]
    wide = 512

    def norm_step(block, carry):
        at = rows_of(block)
        unit, _ = norm_parts(resid_ref[at, :])
        normed_ref[at, :] = (unit * gain2 + offset2).astype(BF16)
        return carry

    lax.fori_loop(0, blocks, norm_step, 0)
    for fetch in fetches:
        fetch.wait()
    for copy in copies:
        copy.wait()

    def hidden_step(index, carry):
        block, chunk = index // (FF // wide), index % (FF // wide)
        at = rows_of(block)
        lanes = rows_of(chunk, wide)
        hidden = nt(normed_ref[at, :], w_ref[pl.ds(pl.multiple_of(f1 + chunk * wide, 16), wide), :])
        act, slope = gelu_parts(hidden)
        act_ref[at, lanes] = act.astype(BF16)
        slope_ref[at, lanes] = slope
        return carry

    lax.fori_loop(0, blocks * (FF // wide), hidden_step, 0)

    def deep_step(block, carry):
        at = rows_of(block)
        deep_ref[at, :] = (resid_ref[at, :] + nn(act_ref[at, :], w_ref[f2 : f2 + FF, :])).astype(BF16)
        return carry

    lax.fori_loop(0, blocks, deep_step, 0)
    sums_ref[...] = jnp.zeros_like(sums_ref)

    def head_step(index, carry):
        j, block = index // blocks, index % blocks
        at = rows_of(block)
        there = rows_of(index)
        up_rows = pl.ds(pl.multiple_of(up + j * D, 16), D)
        columns = cols_ref[j, at, :]
        joined = nn(one_hot_rows(columns[:, 0:1]), e_ref[0:VOCAB, :]) + nt(deep_ref[at, :], w_ref[up_rows, :])
        unit, scale = norm_parts(joined)
        final = (unit * gain_f + offset_f).astype(BF16)
        final_ref[there, :] = final
        logits = nt(final, w_ref[head : head + VOCAB, :])
        nexts = columns[:, 2 * POOL : 2 * POOL + 1]
        lanes = lax.broadcasted_iota(jnp.int32, logits.shape, 1)
        target = jnp.where(lanes == nexts, 1.0, 0.0)
        valid = jnp.where(nexts >= 0, 1.0, 0.0)
        peak = jnp.max(logits, -1, keepdims=True)
        expo = jnp.exp(logits - peak)
        total = jnp.sum(expo, -1, keepdims=True)
        picked = jnp.sum(logits * target, -1, keepdims=True)
        losses = valid * (peak + jnp.log(total) - picked)
        dlogits = ((valid / count) * (expo * (1.0 / total) - target)).astype(BF16)
        dlog_ref[there, :] = dlogits
        dfinal = nn(dlogits, w_ref[head : head + VOCAB, :])
        djoined = norm_back(unit, scale, gain_f, dfinal)
        dup = djoined.astype(BF16)
        dup_ref[there, :] = dup
        low_ref[there, :] = (djoined - dup.astype(F32)).astype(BF16)
        back = nn(dup, w_ref[up_rows, :])

        @pl.when(j == 0)
        def _():
            ddeep_ref[at, :] = back

        @pl.when(j > 0)
        def _():
            ddeep_ref[at, :] += back

        sums_ref[4, :, :] += fold_rows(dfinal * unit)
        sums_ref[5, :, :] += fold_rows(dfinal)
        sums_ref[6, :, :] += jnp.broadcast_to(fold_rows(losses), (8, D))
        return carry

    lax.fori_loop(0, POOL * blocks, head_step, 0)

    out_up, out_head = ROW_U - ROW_F1, ROW_H - ROW_F1
    split_store(keep_ref, send_ref, core, pl.ds(out_head, VOCAB), tn(dlog_ref[...], final_ref[...]))
    for j in range(POOL):
        there = pl.ds(j * rows, rows)
        split_store(keep_ref, send_ref, core, pl.ds(out_up + j * D, D), tn(dup_ref[there, :], deep_ref[...]))
        hot = one_hot_cols(lines_ref[j : j + 1, :])
        part = nn(hot, dup_ref[there, :]) + nn(hot, low_ref[there, :])
        if j == 0:
            table_ref[...] = part
        else:
            table_ref[...] += part

    deep_ref[...] = ddeep_ref[...].astype(BF16)

    def dhid_step(index, carry):
        block, chunk = index // (FF // wide), index % (FF // wide)
        at = rows_of(block)
        lanes = rows_of(chunk, wide)
        dact = nt(deep_ref[at, :], w_ref[pl.ds(pl.multiple_of(f2 + chunk * wide, 16), wide), :])
        dhid_ref[at, lanes] = (dact * slope_ref[at, lanes]).astype(BF16)
        return carry

    lax.fori_loop(0, blocks * (FF // wide), dhid_step, 0)

    def dff_step(chunk, carry):
        lanes = rows_of(chunk, wide)
        split_store(keep_ref, send_ref, core, lanes, tn(dhid_ref[:, lanes], normed_ref[...]))
        there = pl.ds(pl.multiple_of(FF + chunk * wide, wide), wide)
        split_store(keep_ref, send_ref, core, there, tn(act_ref[:, lanes], deep_ref[...]))
        return carry

    lax.fori_loop(0, FF // wide, dff_step, 0)

    def dnorm_step(block, carry):
        at = rows_of(block)
        dnormed = nn(dhid_ref[at, :], w_ref[f1 : f1 + FF, :])
        unit, scale = norm_parts(resid_ref[at, :])
        dresid_ref[at, :] = ddeep_ref[at, :] + norm_back(unit, scale, gain2, dnormed)
        sums_ref[2, :, :] += fold_rows(dnormed * unit)
        sums_ref[3, :, :] += fold_rows(dnormed)
        return carry

    lax.fori_loop(0, blocks, dnorm_step, 0)
    for k in range(8):
        small_ref[k : k + 1, :] = jnp.sum(sums_ref[k], 0, keepdims=True)


def attend_back_kernel(short_len, slots, pieces, coords_ref, lay_ref, slope_ref, lines_ref, vec_ref, dresid_ref,
                       shifted_ref, short_ref, normed_ref, qkv_ref, lse_ref, mixed_ref, table_ref, deep_small_ref, *refs):
    w_hbm, refs = refs[:pieces], refs[pieces:]
    (keep_ref, send_ref, small_ref,
     w_ref, dist_ref, mask_ref, dbranch_ref, dmix_ref, dqkv_ref, dshort_ref, sums_ref, sems) = refs
    rows = short_len * slots
    blocks = rows // BLOCK
    base = 0
    core = coords_ref[2]
    fetch = Fetch(w_hbm, coords_ref, w_ref, sems, 0, 0, ROW_F1)
    fetch.start()
    pool, proj, out = ROW_P - base, ROW_QKV - base, ROW_O - base
    sums_ref[...] = jnp.zeros_like(sums_ref)
    fetch.wait()

    def dmix_step(block, carry):
        at = rows_of(block)
        dbranch = dresid_ref[at, :].astype(BF16)
        dbranch_ref[at, :] = dbranch
        dmix_ref[at, :] = nt(dbranch, w_ref[out : out + D, :]).astype(BF16)
        return carry

    lax.fori_loop(0, blocks, dmix_step, 0)
    split_store(keep_ref, send_ref, core, pl.ds(ROW_O, D), tn(mixed_ref[...], dbranch_ref[...]))

    left_lanes = lax.broadcasted_iota(jnp.int32, (short_len, 2 * HEAD), 1) < HEAD
    tile = 128
    for slot in range(slots):
        at = pl.ds(slot * short_len, short_len)
        key = lax.broadcasted_iota(jnp.int32, (short_len, short_len), 0)
        query = lax.broadcasted_iota(jnp.int32, (short_len, short_len), 1)
        half = jnp.where(lay_ref[slot] == 1, short_len // 2, short_len)
        allowed = (key <= query) & ((key >= half) == (query >= half))
        dist_ref[...] = (key - query).astype(F32)
        mask_ref[...] = jnp.where(allowed, 0.0, NEGATIVE)

        def head_step(pair, carry):
            lanes = pl.ds(pl.multiple_of(pair * 2 * HEAD, 2 * HEAD), 2 * HEAD)
            lanes_k = pl.ds(pl.multiple_of(D + pair * 2 * HEAD, 2 * HEAD), 2 * HEAD)
            lanes_v = pl.ds(pl.multiple_of(2 * D + pair * 2 * HEAD, 2 * HEAD), 2 * HEAD)
            queries = qkv_ref[at, lanes]
            keys = qkv_ref[at, lanes_k]
            values = qkv_ref[at, lanes_v]
            dmix = dmix_ref[at, lanes]
            zero = jnp.zeros_like(values)

            def one_side(side, array):
                return jnp.where(left_lanes, array, zero) if side == 0 else jnp.where(left_lanes, zero, array)

            scaled = queries * jnp.asarray(0.125, BF16)
            dkeys = jnp.zeros((short_len, 2 * HEAD), F32)
            dvalues = jnp.zeros((short_len, 2 * HEAD), F32)
            side_k = [one_side(side, keys) for side in range(2)]
            side_v = [one_side(side, values) for side in range(2)]
            side_q = [one_side(side, queries) for side in range(2)]
            side_m = [one_side(side, dmix) for side in range(2)]
            for part in range(short_len // tile):
                low = part * tile
                dqueries = jnp.zeros((tile, 2 * HEAD), F32)
                for side in range(2):
                    head = pair * 2 + side
                    slope = slope_ref[head]
                    scores = nt(side_k[side], scaled[low : low + tile])
                    scores = scores + jnp.where(
                        mask_ref[:, low : low + tile] == 0.0, dist_ref[:, low : low + tile] * slope, NEGATIVE
                    )
                    probs = jnp.exp(scores - lse_ref[slot, head, :, low : low + tile])
                    dprobs = nt(side_v[side], dmix[low : low + tile])
                    delta = jnp.sum(dprobs * probs, 0, keepdims=True)
                    dscores = (probs * (dprobs - delta) * 0.125).astype(BF16)
                    dvalues = dvalues + nn(probs.astype(BF16), side_m[side][low : low + tile])
                    dkeys = dkeys + nn(dscores, side_q[side][low : low + tile])
                    dqueries = dqueries + tn(dscores, side_k[side])
                dqkv_ref[pl.ds(slot * short_len + low, tile), lanes] = dqueries.astype(BF16)
            dqkv_ref[at, lanes_k] = dkeys.astype(BF16)
            dqkv_ref[at, lanes_v] = dvalues.astype(BF16)
            return carry

        lax.fori_loop(0, HEADS // 2, head_step, 0)

    gain = vec_ref[0:1, :]
    for part in range(3):
        grad = tn(dqkv_ref[:, part * D : (part + 1) * D], normed_ref[...])
        split_store(keep_ref, send_ref, core, pl.ds(ROW_QKV + part * D, D), grad)

    def dshort_step(block, carry):
        at = rows_of(block)
        dnormed = nn(dqkv_ref[at, :], w_ref[proj : proj + 3 * D, :])
        unit, scale = norm_parts(short_ref[at, :])
        dshort_ref[at, :] = (dresid_ref[at, :] + norm_back(unit, scale, gain, dnormed)).astype(BF16)
        sums_ref[0, :, :] += fold_rows(dnormed * unit)
        sums_ref[1, :, :] += fold_rows(dnormed)
        return carry

    lax.fori_loop(0, blocks, dshort_step, 0)
    table = table_ref[...]
    for j in range(POOL):
        cols = slice(j * D, (j + 1) * D)
        split_store(keep_ref, send_ref, core, pl.ds(ROW_P + j * D, D), tn(shifted_ref[:, cols], dshort_ref[...]))
        dshift = nt(dshort_ref[...], w_ref[pool + j * D : pool + (j + 1) * D, :])
        high = dshift.astype(BF16)
        low = (dshift - high.astype(F32)).astype(BF16)
        hot = one_hot_cols(lines_ref[POOL + j : POOL + j + 1, :])
        table = table + nn(hot, high) + nn(hot, low)
    split_store(keep_ref, send_ref, core, pl.ds(ROW_E, VOCAB), table)
    small_ref[...] = deep_small_ref[...]
    for k in range(2):
        small_ref[k : k + 1, :] = jnp.sum(sums_ref[k], 0, keepdims=True)
    half = D // 2
    for k in range(2):
        send_ref[ROW_F1 + 16 * k : ROW_F1 + 16 * (k + 1), :] = two_parts(small_ref[:, k * half : (k + 1) * half])


def two_parts(values):
    high = values.astype(BF16)
    low = (values - high.astype(F32)).astype(BF16)
    return jnp.concatenate([high.astype(F32), low.astype(F32)], 0).astype(BF16)


def one_value(parts):
    parts = parts.astype(F32)
    return parts[:8] + parts[8:]


def core_sum_kernel(coords_ref, keep_front, keep_deep, recv_front, recv_deep, small_ref,
                    p0, p1, p2, p3, q0, q1, q2, q3,
                    keep_ref, recv_ref, sems):
    copies = [
        pltpu.make_async_copy(source, target, sems.at[k])
        for k, (source, target) in enumerate((
            (keep_deep, keep_ref.at[pl.ds(ROW_F1, ROW_END - ROW_F1)]),
            (recv_deep, recv_ref.at[pl.ds(ROW_F1, ROW_END - ROW_F1)]),
            (keep_front, keep_ref.at[pl.ds(0, ROW_F1)]),
            (recv_front.at[pl.ds(0, ROW_F1)], recv_ref.at[pl.ds(0, ROW_F1)]),
            (recv_front.at[pl.ds(ROW_F1, 32)], recv_ref.at[pl.ds(ROW_END, 32)]),
        ))
    ]
    for copy in copies:
        copy.start()
    for copy in copies:
        copy.wait()
    dp, z = coords_ref[0], coords_ref[1]
    quarter = D // 4
    line = 2 * SHARD

    def total(half, column, x, zed, begin, size):
        row = half * (8 * line) + x * (4 * line) + zed * line + begin
        at = pl.ds(pl.multiple_of(row, 16), size)
        lanes = pl.ds(pl.multiple_of(column * quarter, quarter), quarter)
        return (keep_ref[at, lanes].astype(F32) + recv_ref[at, lanes].astype(F32)).astype(BF16)

    rest = line - SCATTER_CUT
    for k, p_ref in enumerate((p0, p1, p2, p3)):
        there = dp ^ k

        def p_step(index, carry):
            half, zed = index // 4, index % 4
            p_ref[pl.ds(pl.multiple_of(index * SCATTER_CUT, 16), SCATTER_CUT), :] = total(
                half, there // 2, there % 2, zed, 0, SCATTER_CUT
            )
            return carry

        lax.fori_loop(0, 8, p_step, 0)
    for k, q_ref in enumerate((q0, q1, q2, q3)):
        zed = z ^ k

        def q_step(index, carry):
            half, there = index // 4, index % 4
            q_ref[pl.ds(pl.multiple_of(index * rest, 16), rest), :] = total(
                half, there // 2, there % 2, zed, SCATTER_CUT, rest
            )
            return carry

        lax.fori_loop(0, 8, q_step, 0)
    for k in range(2):
        both = small_ref[:, 2 * k * quarter : 2 * (k + 1) * quarter] + one_value(
            recv_ref[ROW_END + 16 * k : ROW_END + 16 * (k + 1), :]
        )
        for side in range(2):
            parts = two_parts(both[:, side * quarter : (side + 1) * quarter])
            row = 8 * SCATTER_CUT + 16 * (2 * k + side)
            for p_ref in (p0, p1, p2, p3):
                p_ref[row : row + 16, :] = parts


def first_sum_kernel(coords_ref, p0, p1, p2, p3, q0, q1, q2, q3,
                     s0, s1, s2, s3, t0, t1, t2, t3):
    dp, z = coords_ref[0], coords_ref[1]
    rest = 2 * SHARD - SCATTER_CUT

    def total(refs, row, size):
        at = pl.ds(pl.multiple_of(row, 16), size)
        return (refs[0][at, :].astype(F32) + refs[1][at, :].astype(F32)) + (
            refs[2][at, :].astype(F32) + refs[3][at, :].astype(F32)
        )

    for k, s_ref in enumerate((s0, s1, s2, s3)):
        for half in range(2):
            s_ref[half * SCATTER_CUT : (half + 1) * SCATTER_CUT, :] = total(
                (p0, p1, p2, p3), (half * 4 + (z ^ k)) * SCATTER_CUT, SCATTER_CUT
            ).astype(BF16)
    for k, t_ref in enumerate((t0, t1, t2, t3)):
        for half in range(2):
            t_ref[half * rest : (half + 1) * rest, :] = total(
                (q0, q1, q2, q3), (half * 4 + (dp ^ k)) * rest, rest
            ).astype(BF16)
    for k in range(4):
        row = 8 * SCATTER_CUT + 16 * k
        value = sum(one_value(ref[row : row + 16, :]) for ref in (p0, p1, p2, p3))
        parts = two_parts(value)
        for s_ref in (s0, s1, s2, s3):
            s_ref[2 * SCATTER_CUT + 16 * k : 2 * SCATTER_CUT + 16 * (k + 1), :] = parts


def last_sum_kernel(coords_ref, s0, s1, s2, s3, t0, t1, t2, t3, mine_ref, other_ref, small_ref, square_ref):
    own = coords_ref[0] // 2
    line = 2 * SHARD
    rest = line - SCATTER_CUT

    def total(refs, half, size):
        at = pl.ds(pl.multiple_of(half * size, 16), size)
        return (refs[0][at, :].astype(F32) + refs[1][at, :].astype(F32)) + (
            refs[2][at, :].astype(F32) + refs[3][at, :].astype(F32)
        )

    squares = jnp.zeros((8, D // 4), F32)
    for half, out_ref in ((own, mine_ref), (1 - own, other_ref)):
        first = total((s0, s1, s2, s3), half, SCATTER_CUT)
        second = total((t0, t1, t2, t3), half, rest)
        out_ref[0:SCATTER_CUT, :] = first
        out_ref[SCATTER_CUT:line, :] = second
        squares = squares + fold_rows(first * first) + fold_rows(second * second)
    for k in range(4):
        row = 2 * SCATTER_CUT + 16 * k
        small_ref[:, k * (D // 4) : (k + 1) * (D // 4)] = sum(
            one_value(ref[row : row + 16, :]) for ref in (s0, s1, s2, s3)
        )
    square_ref[...] = squares


VMEM = pl.BlockSpec(memory_space=pltpu.VMEM)
SMEM = pl.BlockSpec(memory_space=pltpu.SMEM)
ANY = pl.BlockSpec(memory_space=pl.ANY)
LIMIT = 58 * 1024 * 1024


def deep_base(pieces):
    return ROW_F1 if pieces == 1 else ROW_F1 // SHARD * SHARD


def device_grads(pieces, tail, vecs, coords, ids, layouts, count, exchange):
    slots = layouts.shape[0]
    rows = ids.shape[1]
    short_len = rows // slots
    slopes = np.float32(2.0) ** (-8.0 * (np.arange(HEADS, dtype=np.float32) + 1.0) / HEADS)
    shape = jax.ShapeDtypeStruct
    params = pltpu.CompilerParams(vmem_limit_bytes=LIMIT)
    number = len(pieces)
    whole_shards = number > 1
    front_rows = -(-ROW_F1 // SHARD) * SHARD if whole_shards else ROW_F1
    deep_rows = ROW_END - deep_base(number)
    table_rows = SHARD if whole_shards else VOCAB
    jobs = 64 if whole_shards else 1
    more = [] if vecs is None else [vecs]
    rest = [] if tail is None else [tail]
    half = D // 2
    shifted, short, normed, qkv, lse, mixed, resid, lines, cols, vecs = pl.pallas_call(
        partial(attend_kernel, short_len, slots, number),
        out_shape=(
            shape((rows, POOL * D), BF16),
            shape((rows, D), F32),
            shape((rows, D), BF16),
            shape((rows, 3 * D), BF16),
            shape((slots, HEADS, 1, short_len), F32),
            shape((rows, D), BF16),
            shape((rows, D), F32),
            shape((16, rows), jnp.int32),
            shape((POOL, rows, 128), jnp.int32),
            shape((8, D), F32),
        ),
        in_specs=[SMEM, SMEM, SMEM, VMEM] + [ANY] * number + [VMEM] * len(more),
        out_specs=(VMEM,) * 10,
        scratch_shapes=[
            pltpu.VMEM((front_rows, D), BF16),
            pltpu.VMEM((short_len, short_len), F32),
            pltpu.VMEM((short_len, short_len), F32),
            pltpu.VMEM((short_len, 2 * HEAD), F32),
            pltpu.VMEM((32, 16, D // 2), BF16),
            pltpu.SemaphoreType.DMA((jobs,)),
            pltpu.SemaphoreType.DMA((32,)),
        ],
        compiler_params=params,
        cost_estimate=pl.CostEstimate(flops=9_000_000_000, bytes_accessed=20_000_000, transcendentals=2_400_000),
        name="attend",
    )(coords, layouts, slopes, ids, *pieces, *more)
    keep_deep, send_deep, table, dresid, small_deep = pl.pallas_call(
        partial(deep_kernel, count, number),
        out_shape=(
            shape((ROW_END - ROW_F1, half), BF16),
            shape((ROW_END - ROW_F1, half), BF16),
            shape((VOCAB, D), F32),
            shape((rows, D), F32),
            shape((8, D), F32),
        ),
        in_specs=[SMEM] + [VMEM] * 4 + [ANY] * (number + len(rest)),
        out_specs=(VMEM,) * 5,
        scratch_shapes=[
            pltpu.VMEM((deep_rows, D), BF16),
            pltpu.VMEM((table_rows, D), BF16),
            pltpu.VMEM((rows, D), BF16),
            pltpu.VMEM((rows, FF), BF16),
            pltpu.VMEM((rows, FF), F32),
            pltpu.VMEM((rows, D), BF16),
            pltpu.VMEM((POOL * rows, D), BF16),
            pltpu.VMEM((POOL * rows, VOCAB), BF16),
            pltpu.VMEM((POOL * rows, D), BF16),
            pltpu.VMEM((POOL * rows, D), BF16),
            pltpu.VMEM((rows, D), F32),
            pltpu.VMEM((rows, FF), BF16),
            pltpu.VMEM((8, 8, D), F32),
            pltpu.SemaphoreType.DMA((jobs,)),
            pltpu.SemaphoreType.DMA((jobs,)),
            pltpu.SemaphoreType.DMA((2,)),
        ],
        compiler_params=params,
        name="deep",
    )(coords, cols, lines, vecs, resid, *pieces, *rest)
    recv_deep = exchange(send_deep)
    keep_front, send_front, small = pl.pallas_call(
        partial(attend_back_kernel, short_len, slots, number),
        out_shape=(shape((ROW_F1, half), BF16), shape((ROW_F1 + 32, half), BF16), shape((8, D), F32)),
        in_specs=[SMEM, SMEM, SMEM] + [VMEM] * 11 + [ANY] * number,
        out_specs=(VMEM,) * 3,
        scratch_shapes=[
            pltpu.VMEM((front_rows, D), BF16),
            pltpu.VMEM((short_len, short_len), F32),
            pltpu.VMEM((short_len, short_len), F32),
            pltpu.VMEM((rows, D), BF16),
            pltpu.VMEM((rows, D), BF16),
            pltpu.VMEM((rows, 3 * D), BF16),
            pltpu.VMEM((rows, D), BF16),
            pltpu.VMEM((2, 8, D), F32),
            pltpu.SemaphoreType.DMA((jobs,)),
        ],
        compiler_params=params,
        cost_estimate=pl.CostEstimate(flops=13_000_000_000, bytes_accessed=20_000_000, transcendentals=2_400_000),
        name="attend_back",
    )(coords, layouts, slopes, lines, vecs, dresid, shifted, short, normed, qkv, lse, mixed, table, small_deep, *pieces)
    recv_front = exchange(send_front)
    return keep_front, recv_front, keep_deep, recv_deep, small


def swap_with(array, line=0, zed=0, core=0):
    lines, rest = lax.axis_size("dp"), lax.axis_size("fsdp")
    pairs = [
        (d * rest + f, (d ^ line) * rest + (f ^ (2 * zed + core)))
        for d in range(lines)
        for f in range(rest)
    ]
    return lax.ppermute(array, AXES, pairs)


def swap_halves(coords, shard):
    half = D // 2
    upper = coords[0] // 2 == 1
    left, right = shard[:, :half], shard[:, half:]
    keep, send = jnp.where(upper, right, left), jnp.where(upper, left, right)
    other = swap_with(send, line=2)
    return jnp.where(upper, other, keep), jnp.where(upper, keep, other)


def gather_pieces(block, vectors):
    half = D // 2
    width = vectors.shape[1]
    start = lax.axis_index(AXES) * width
    own = lax.dynamic_update_slice(
        jnp.zeros((16, half), BF16), vectors, (8 * (start // half), start % half)
    )
    first, second = jnp.concatenate([block[:GATHER_CUT], own], 0), block[GATHER_CUT:]
    along = jnp.concatenate([first] + [swap_with(first, zed=k) for k in (1, 2, 3)], 0)
    across = jnp.concatenate([second] + [swap_with(second, line=k) for k in (1, 2, 3)], 0)
    pieces = [along] + [swap_with(along, line=k) for k in (1, 2, 3)]
    pieces += [across] + [swap_with(across, zed=k) for k in (1, 2, 3)]
    return pieces + [swap_with(piece, core=1) for piece in pieces]


def scatter_sum(coords, keep_front, recv_front, keep_deep, recv_deep, small):
    shape = jax.ShapeDtypeStruct
    params = pltpu.CompilerParams(vmem_limit_bytes=LIMIT)
    quarter = D // 4
    line = 2 * SHARD
    rest = line - SCATTER_CUT
    parts = pl.pallas_call(
        core_sum_kernel,
        out_shape=(shape((8 * SCATTER_CUT + 64, quarter), BF16),) * 4 + (shape((8 * rest, quarter), BF16),) * 4,
        in_specs=[SMEM] + [ANY] * 4 + [VMEM],
        out_specs=(VMEM,) * 8,
        scratch_shapes=[
            pltpu.VMEM((ROW_END, D // 2), BF16),
            pltpu.VMEM((ROW_END + 32, D // 2), BF16),
            pltpu.SemaphoreType.DMA((5,)),
        ],
        compiler_params=params,
        name="core_sum",
    )(coords, keep_front, keep_deep, recv_front, recv_deep, small)
    first = [parts[0]] + [swap_with(parts[k], line=k) for k in (1, 2, 3)]
    first += [parts[4]] + [swap_with(parts[4 + k], zed=k) for k in (1, 2, 3)]
    parts = pl.pallas_call(
        first_sum_kernel,
        out_shape=(shape((2 * SCATTER_CUT + 64, quarter), BF16),) * 4 + (shape((2 * rest, quarter), BF16),) * 4,
        in_specs=[SMEM] + [VMEM] * 8,
        out_specs=(VMEM,) * 8,
        compiler_params=params,
        name="first_sum",
    )(coords, *first)
    second = [parts[0]] + [swap_with(parts[k], zed=k) for k in (1, 2, 3)]
    second += [parts[4]] + [swap_with(parts[4 + k], line=k) for k in (1, 2, 3)]
    mine, other, small, squares = pl.pallas_call(
        last_sum_kernel,
        out_shape=(shape((line, quarter), F32),) * 2 + (shape((8, D), F32), shape((8, quarter), F32)),
        in_specs=[SMEM] + [VMEM] * 8,
        out_specs=(VMEM,) * 4,
        compiler_params=params,
        name="last_sum",
    )(coords, *second)
    row, core = coords[0] // 2, coords[2]
    theirs = swap_with(other, line=2)
    half = jnp.concatenate(
        [jnp.where(row == 0, mine, theirs), jnp.where(row == 0, theirs, mine)], 1
    )
    keep = jnp.where(core == 0, half[:SHARD], half[SHARD:])
    send = jnp.where(core == 0, half[SHARD:], half[:SHARD])
    back = swap_with(send, core=1)
    owned = jnp.concatenate([jnp.where(core == 0, keep, back), jnp.where(core == 0, back, keep)], 1)
    return owned, small, jnp.sum(squares)


def sum_all(value):
    value = jnp.broadcast_to(value, (8, 128))
    value = value + swap_with(value, core=1)
    for k in (1, 2):
        value = value + swap_with(value, line=k)
    for k in (1, 2):
        value = value + swap_with(value, zed=k)
    return value[0, 0]


def adam(param, first_m, second_m, grad, decay):
    first_new = BETA * first_m + (1.0 - BETA) * grad
    second_new = BETA * second_m + (1.0 - BETA) * grad * grad
    correct = 1.0 - BETA**STEP
    update = -RATE * (
        first_new / correct / (jnp.sqrt(second_new / correct) + EPS_ADAM) + decay * param
    )
    return (first_new, second_new, update)


def shards(byte_ids, layouts, weights, vectors, m_weights, v_weights, m_vectors, v_vectors):
    devices = lax.axis_size(AXES)
    micro = byte_ids.shape[0]
    count = float(micro * layouts.shape[1] * devices * byte_ids.shape[2])
    lines, rest = lax.axis_size("dp"), lax.axis_size("fsdp")
    place = lax.axis_index("fsdp")
    coords = jnp.stack([lax.axis_index("dp"), place // 2, place % 2, 0]).astype(jnp.int32)
    paired = lines == 4 and rest == 8 and weights.shape[0] == SHARD
    weights_low = weights.astype(BF16)
    vectors_low = vectors.astype(BF16)
    width = vectors.shape[1]
    mine = lax.axis_index(AXES) * width
    flat_layouts = layouts.reshape(-1)
    ids = byte_ids.reshape(flat_layouts.shape[0], -1, POOL).transpose(2, 0, 1).reshape(POOL, -1)
    ids = jnp.pad(ids, ((0, 8 - POOL), (0, 0)))
    if paired:
        front, back = swap_halves(coords, weights_low)
        tail = lax.all_gather(back, AXES, axis=0, tiled=True)
        pieces = gather_pieces(front, vectors_low)
        parts = device_grads(pieces, tail, None, coords, ids, flat_layouts, count, partial(swap_with, core=1))
        owned, small, squares = scatter_sum(coords, *parts)
        squares = sum_all(squares)
    else:
        coords = coords * 0
        pieces = [lax.all_gather(weights_low, AXES, axis=0, tiled=True)]
        vecs = lax.all_gather(vectors_low, AXES, axis=1, tiled=True)
        vecs = jnp.pad(vecs.astype(F32), ((0, 2), (0, 0)))
        parts = device_grads(pieces, None, vecs, coords, ids, flat_layouts, count, lambda array: array)
        keep_front, send_front, keep_deep, send_deep, small = parts
        local = jnp.concatenate(
            [
                jnp.concatenate([keep_front, send_front[:ROW_F1]], 1),
                jnp.concatenate([keep_deep, send_deep], 1),
            ],
            0,
        )
        owned = lax.psum_scatter(local.astype(F32), AXES, scatter_dimension=0, tiled=True)
        small, squares = lax.psum((small, jnp.sum(owned * owned)), AXES)
    loss = small[6, 0] / count
    vec_grads = small[:6]
    owned_vecs = lax.dynamic_slice(vec_grads, (0, mine), (6, width))
    squares = squares + jnp.sum(vec_grads * vec_grads)
    grad_norm = jnp.sqrt(squares)
    factor = CLIP / jnp.maximum(grad_norm, CLIP)
    first_w, second_w, update_w = adam(weights, m_weights, v_weights, owned * factor, DECAY)
    first_v, second_v, update_v = adam(vectors, m_vectors, v_vectors, owned_vecs * factor, 0.0)
    return (loss, grad_norm, first_w, second_w, update_w, first_v, second_v, update_v)


def solution(mesh):
    in_specs = (
        P(None, AXES, None),
        P(None, AXES),
        P(AXES, None),
        P(None, AXES),
        P(AXES, None),
        P(AXES, None),
        P(None, AXES),
        P(None, AXES),
    )
    out_specs = (
        P(),
        P(),
        P(AXES, None),
        P(AXES, None),
        P(AXES, None),
        P(None, AXES),
        P(None, AXES),
        P(None, AXES),
    )
    return jax.shard_map(shards, mesh=mesh, in_specs=in_specs, out_specs=out_specs, check_vma=False)
```

```python
from functools import partial

import jax
import jax.numpy as jnp
import numpy as np
from jax import lax
from jax.experimental import pallas as pl
from jax.experimental.pallas import tpu as pltpu
from jax.sharding import PartitionSpec as P

D = 512
HEADS = 8
HEAD = 64
FF = 2048
VOCAB = 256
POOL = 3

EPS_NORM = 1e-05
EPS_ADAM = 1e-08
CLIP = 0.2
RATE = 0.03
DECAY = 0.1
BETA = 0.5
STEP = 3
NEGATIVE = -1000000000.0

F32 = jnp.float32
BF16 = jnp.bfloat16

ROW_E = 0
ROW_P = VOCAB
ROW_QKV = ROW_P + POOL * D
ROW_O = ROW_QKV + 3 * D
ROW_F1 = ROW_O + D
ROW_F2 = ROW_F1 + FF
ROW_U = ROW_F2 + FF
ROW_H = ROW_U + POOL * D
ROW_END = ROW_H + VOCAB
ROW_HALF = ROW_END // 2
assert ROW_HALF - ROW_F1 == FF // 2

BLOCK = 256
AXES = ("dp", "fsdp")
SHARD = ROW_END // 32
GATHER_CUT = 208
SCATTER_CUT = 400


def nn(left, right):
    return lax.dot_general(left, right, (((1,), (0,)), ((), ())), preferred_element_type=F32)


def nt(left, right):
    return lax.dot_general(left, right, (((1,), (1,)), ((), ())), preferred_element_type=F32)


def tn(left, right):
    return lax.dot_general(left, right, (((0,), (0,)), ((), ())), preferred_element_type=F32)


def norm_parts(values):
    center = values - jnp.mean(values, -1, keepdims=True)
    spread = jnp.mean(center * center, -1, keepdims=True)
    scale = lax.rsqrt(spread + EPS_NORM)
    return center * scale, scale


def norm_back(unit, scale, gain, grad):
    inner = grad * gain
    mean_inner = jnp.mean(inner, -1, keepdims=True)
    mean_cross = jnp.mean(inner * unit, -1, keepdims=True)
    return scale * (inner - mean_inner - unit * mean_cross)


def fold_rows(values):
    return jnp.sum(values.reshape(values.shape[0] // 8, 8, values.shape[1]), 0)


def one_hot_rows(ids):
    lanes = lax.broadcasted_iota(jnp.int32, (ids.shape[0], VOCAB), 1)
    return jnp.where(lanes == ids, 1.0, 0.0).astype(BF16)


def one_hot_cols(ids):
    lines = lax.broadcasted_iota(jnp.int32, (VOCAB, ids.shape[1]), 0)
    return jnp.where(lines == ids, 1.0, 0.0).astype(BF16)


def rows_of(index, size=BLOCK):
    return pl.ds(pl.multiple_of(index * size, size), size)


def gathered_parts(coords_ref):
    dp, z, core = coords_ref[0], coords_ref[1], coords_ref[2]
    for side in range(2):
        for k in range(4):
            for part in range(4):
                for kind in range(2):
                    d, e = (k, part) if kind == 0 else (part, k)
                    line = dp ^ d
                    yield side * 8 + kind * 4 + k, part, kind, line // 2, (line % 2) * 8 + (z ^ e) * 2 + (core ^ side)


class Fetch:
    def __init__(self, pieces, coords_ref, w_ref, sems, base, low, high):
        self.jobs = []
        if len(pieces) == 1:
            size = high - low
            copy = pltpu.make_async_copy(
                pieces[0].at[pl.ds(low, size)], w_ref.at[pl.ds(low - base, size)], sems.at[0]
            )
            self.jobs.append((None, copy))
            return
        first, last = low // SHARD, (high - 1) // SHARD
        half = D // 2
        for number, (piece, part, kind, y, shard) in enumerate(gathered_parts(coords_ref)):
            begin, size, step = ((0, GATHER_CUT, GATHER_CUT + 16), (GATHER_CUT, SHARD - GATHER_CUT, SHARD - GATHER_CUT))[kind]
            wanted = (shard >= first) & (shard <= last)
            place = jnp.where(wanted, shard * SHARD - base + begin, 0)
            copy = pltpu.make_async_copy(
                pieces[piece].at[pl.ds(part * step, size)],
                w_ref.at[pl.ds(pl.multiple_of(place, 16), size), pl.ds(pl.multiple_of(y * half, half), half)],
                sems.at[number],
            )
            self.jobs.append((wanted, copy))

    def start(self):
        for wanted, copy in self.jobs:
            if wanted is None:
                copy.start()
            else:
                pl.when(wanted)(copy.start)

    def wait(self):
        for wanted, copy in self.jobs:
            if wanted is None:
                copy.wait()
            else:
                pl.when(wanted)(copy.wait)


def attend_kernel(short_len, slots, pieces, coords_ref, lay_ref, slope_ref, ids_ref, *refs):
    w_hbm, refs = refs[:pieces], refs[pieces:]
    if pieces == 1:
        vec_in_ref, refs = refs[0], refs[1:]
    (shifted_ref, short_ref, normed_ref, qkv_ref, lse_ref, mixed_ref, resid_ref, lines_ref, cols_ref, vec_ref,
     w_ref, dist_ref, mask_ref, lse_cols, part_ref, sems, part_sems) = refs
    rows = short_len * slots
    fetch = Fetch(w_hbm, coords_ref, w_ref, sems, 0, 0, ROW_F1)
    fetch.start()
    copies = []
    if pieces > 1:
        for piece, part, kind, _, _ in gathered_parts(coords_ref):
            if kind == 0:
                place = pl.ds(part * (GATHER_CUT + 16) + GATHER_CUT, 16)
                number = len(copies)
                copies.append(
                    pltpu.make_async_copy(w_hbm[piece].at[place], part_ref.at[number], part_sems.at[number])
                )
        for copy in copies:
            copy.start()

    ids = ids_ref[...]
    group = lax.broadcasted_iota(jnp.int32, (1, rows), 1)
    starts = group == 0
    for slot in range(slots):
        starts = starts | (group == slot * short_len)
        starts = starts | ((group == slot * short_len + short_len // 2) & (lay_ref[slot] == 1))
    ends = group == rows - 1
    for slot in range(slots):
        ends = ends | (group == (slot + 1) * short_len - 1)
        ends = ends | ((group == slot * short_len + short_len // 2 - 1) & (lay_ref[slot] == 1))
    before, after = pltpu.roll(ids, 1, 1), pltpu.roll(ids, rows - 1, 1)
    own = [ids[j : j + 1] for j in range(POOL)]
    back = [jnp.where(starts, -1, before[1:2]), jnp.where(starts, -1, before[2:3]), ids[0:1]]
    ahead = [ids[1:2], ids[2:3], jnp.where(ends, -1, after[0:1])]
    for j in range(POOL):
        lines_ref[j : j + 1, :] = own[j]
        lines_ref[POOL + j : POOL + j + 1, :] = back[j]
        lines_ref[2 * POOL + j : 2 * POOL + j + 1, :] = ahead[j]
    lines_ref[3 * POOL :, :] = jnp.zeros((16 - 3 * POOL, rows), jnp.int32)
    turned = jnp.concatenate([lines_ref[...].astype(F32), jnp.zeros((112, rows), F32)], 0).T.astype(jnp.int32)
    for j in range(POOL):
        cols_ref[j] = pltpu.roll(turned, 128 - j, 1)

    for copy in copies:
        copy.wait()
    if pieces > 1:
        both = part_ref[0].astype(F32)
        for k in range(1, len(copies)):
            both = both + part_ref[k].astype(F32)
        vec_ref[...] = jnp.concatenate([both[:8], both[8:]], 1)
    else:
        vec_ref[...] = vec_in_ref[...]
    fetch.wait()
    gain, offset = vec_ref[0:1, :], vec_ref[1:2, :]

    def pool_step(block, carry):
        at = rows_of(block)
        for j in range(POOL):
            hot = one_hot_rows(cols_ref[j, at, POOL : POOL + 1])
            shifted_ref[at, j * D : (j + 1) * D] = nn(hot, w_ref[ROW_E:ROW_P, :]).astype(BF16)
        short = nn(shifted_ref[at, :], w_ref[ROW_P:ROW_QKV, :])
        short_ref[at, :] = short
        unit, _ = norm_parts(short)
        normed_ref[at, :] = (unit * gain + offset).astype(BF16)
        return carry

    lax.fori_loop(0, rows // BLOCK, pool_step, 0)

    def qkv_step(block, carry):
        at = rows_of(block)
        qkv_ref[at, :] = nt(normed_ref[at, :], w_ref[ROW_QKV:ROW_O, :]).astype(BF16)
        return carry

    lax.fori_loop(0, rows // BLOCK, qkv_step, 0)

    left_lanes = lax.broadcasted_iota(jnp.int32, (short_len, 2 * HEAD), 1) < HEAD
    tile = 128
    for slot in range(slots):
        at = pl.ds(slot * short_len, short_len)
        query = lax.broadcasted_iota(jnp.int32, (short_len, short_len), 0)
        key = lax.broadcasted_iota(jnp.int32, (short_len, short_len), 1)
        half = jnp.where(lay_ref[slot] == 1, short_len // 2, short_len)
        allowed = (key <= query) & ((key >= half) == (query >= half))
        dist_ref[...] = (key - query).astype(F32)
        mask_ref[...] = jnp.where(allowed, 0.0, NEGATIVE)

        def head_step(pair, carry):
            lanes = pl.ds(pl.multiple_of(pair * 2 * HEAD, 2 * HEAD), 2 * HEAD)
            lanes_k = pl.ds(pl.multiple_of(D + pair * 2 * HEAD, 2 * HEAD), 2 * HEAD)
            lanes_v = pl.ds(pl.multiple_of(2 * D + pair * 2 * HEAD, 2 * HEAD), 2 * HEAD)
            queries = qkv_ref[at, lanes] * jnp.asarray(0.125, BF16)
            keys = qkv_ref[at, lanes_k]
            values = qkv_ref[at, lanes_v]
            zero = jnp.zeros_like(values)
            vals = [jnp.where(left_lanes, values, zero), jnp.where(left_lanes, zero, values)]
            slots_q = [jnp.where(left_lanes, queries, zero), jnp.where(left_lanes, zero, queries)]
            for part in range(short_len // tile):
                low = part * tile
                mixed = jnp.zeros((tile, 2 * HEAD), F32)
                columns = lse_cols[low : low + tile, :]
                where = lax.broadcasted_iota(jnp.int32, (tile, 2 * HEAD), 1)
                for side in range(2):
                    head = pair * 2 + side
                    slope = slope_ref[head]
                    scores = nt(slots_q[side][low : low + tile], keys)
                    scores = scores + jnp.where(
                        mask_ref[low : low + tile, :] == 0.0, dist_ref[low : low + tile, :] * slope, NEGATIVE
                    )
                    top = jnp.max(scores, -1, keepdims=True)
                    expo = jnp.exp(scores - top)
                    total = jnp.sum(expo, -1, keepdims=True)
                    probs = (expo * (1.0 / total)).astype(BF16)
                    columns = jnp.where(where == head, top + jnp.log(total), columns)
                    mixed = mixed + nn(probs, vals[side])
                lse_cols[low : low + tile, :] = columns
                mixed_ref[pl.ds(slot * short_len + low, tile), lanes] = mixed.astype(BF16)
            return carry

        lse_cols[...] = jnp.zeros_like(lse_cols)
        lax.fori_loop(0, HEADS // 2, head_step, 0)
        turned = lse_cols[...].T
        for head in range(HEADS):
            lse_ref[slot, head] = turned[head : head + 1, :]

    def out_step(block, carry):
        at = rows_of(block)
        resid_ref[at, :] = short_ref[at, :] + nn(mixed_ref[at, :], w_ref[ROW_O:ROW_F1, :])
        return carry

    lax.fori_loop(0, rows // BLOCK, out_step, 0)


def gelu_parts(hidden):
    size = jnp.abs(hidden)
    near = 1.0 / (1.0 + (0.3275911 * 0.7071067811865476) * size)
    bell = jnp.exp(hidden * hidden * -0.5)
    tail = near * (0.127414796 + near * (-0.142248368 + near * (0.7107068705 + near * (-0.7265760135 + near * 0.5307027145))))
    tail = tail * bell
    cdf = jnp.where(hidden >= 0.0, 1.0 - tail, tail)
    return hidden * cdf, cdf + hidden * bell * 0.3989422804014327


def split_store(keep_ref, send_ref, core, rows, values):
    half = D // 2
    low, high = values[:, :half].astype(BF16), values[:, half:].astype(BF16)
    keep_ref[rows, :] = jnp.where(core == 0, low, high)
    send_ref[rows, :] = jnp.where(core == 0, high, low)


def deep_kernel(count, pieces, coords_ref, cols_ref, lines_ref, vec_ref, resid_ref, *refs):
    w_hbm, refs = refs[:pieces], refs[pieces:]
    if pieces > 1:
        tail_hbm, refs = refs[0], refs[1:]
    (keep_mid, send_mid, keep_ref, send_ref, table_ref, dresid_ref, small_ref,
     w_ref, e_ref, normed_ref, act_ref, slope_ref, deep_ref, final_ref, dlog_ref, dup_ref, low_ref,
     ddeep_ref, dhid_ref, sums_ref, sems, e_sems, tail_sems) = refs
    rows = resid_ref.shape[0]
    blocks = rows // BLOCK
    base = deep_base(pieces)
    core = coords_ref[2]
    fetches = [
        Fetch(w_hbm, coords_ref, w_ref, sems, base, ROW_F1, ROW_END if pieces == 1 else ROW_END // 2),
        Fetch(w_hbm, coords_ref, e_ref, e_sems, 0, 0, VOCAB),
    ]
    for fetch in fetches:
        fetch.start()
    copies = []
    if pieces > 1:
        half = ROW_END // 2
        for y in range(2):
            copies.append(
                pltpu.make_async_copy(
                    tail_hbm.at[pl.ds(y * half, half)],
                    w_ref.at[pl.ds(half - base, half), pl.ds(y * (D // 2), D // 2)],
                    tail_sems.at[y],
                )
            )
    for copy in copies:
        copy.start()
    f1, f2, up, head = ROW_F1 - base, ROW_F2 - base, ROW_U - base, ROW_H - base
    gain2, offset2 = vec_ref[2:3, :], vec_ref[3:4, :]
    gain_f, offset_f = vec_ref[4:5, :], vec_ref[5:6, :]
    wide = 512

    def norm_step(block, carry):
        at = rows_of(block)
        unit, _ = norm_parts(resid_ref[at, :])
        normed_ref[at, :] = (unit * gain2 + offset2).astype(BF16)
        return carry

    lax.fori_loop(0, blocks, norm_step, 0)
    for fetch in fetches:
        fetch.wait()
    for copy in copies:
        copy.wait()

    def hidden_step(index, carry):
        block, chunk = index // (FF // wide), index % (FF // wide)
        at = rows_of(block)
        lanes = rows_of(chunk, wide)
        hidden = nt(normed_ref[at, :], w_ref[pl.ds(pl.multiple_of(f1 + chunk * wide, 16), wide), :])
        act, slope = gelu_parts(hidden)
        act_ref[at, lanes] = act.astype(BF16)
        slope_ref[at, lanes] = slope
        return carry

    lax.fori_loop(0, blocks * (FF // wide), hidden_step, 0)

    def deep_step(block, carry):
        at = rows_of(block)
        deep_ref[at, :] = (resid_ref[at, :] + nn(act_ref[at, :], w_ref[f2 : f2 + FF, :])).astype(BF16)
        return carry

    lax.fori_loop(0, blocks, deep_step, 0)
    sums_ref[...] = jnp.zeros_like(sums_ref)

    def head_step(index, carry):
        j, block = index // blocks, index % blocks
        at = rows_of(block)
        there = rows_of(index)
        up_rows = pl.ds(pl.multiple_of(up + j * D, 16), D)
        columns = cols_ref[j, at, :]
        joined = nn(one_hot_rows(columns[:, 0:1]), e_ref[0:VOCAB, :]) + nt(deep_ref[at, :], w_ref[up_rows, :])
        unit, scale = norm_parts(joined)
        final = (unit * gain_f + offset_f).astype(BF16)
        final_ref[there, :] = final
        logits = nt(final, w_ref[head : head + VOCAB, :])
        nexts = columns[:, 2 * POOL : 2 * POOL + 1]
        lanes = lax.broadcasted_iota(jnp.int32, logits.shape, 1)
        target = jnp.where(lanes == nexts, 1.0, 0.0)
        valid = jnp.where(nexts >= 0, 1.0, 0.0)
        peak = jnp.max(logits, -1, keepdims=True)
        expo = jnp.exp(logits - peak)
        total = jnp.sum(expo, -1, keepdims=True)
        picked = jnp.sum(logits * target, -1, keepdims=True)
        losses = valid * (peak + jnp.log(total) - picked)
        dlogits = ((valid / count) * (expo * (1.0 / total) - target)).astype(BF16)
        dlog_ref[there, :] = dlogits
        dfinal = nn(dlogits, w_ref[head : head + VOCAB, :])
        djoined = norm_back(unit, scale, gain_f, dfinal)
        dup = djoined.astype(BF16)
        dup_ref[there, :] = dup
        low_ref[there, :] = (djoined - dup.astype(F32)).astype(BF16)
        back = nn(dup, w_ref[up_rows, :])

        @pl.when(j == 0)
        def _():
            ddeep_ref[at, :] = back

        @pl.when(j > 0)
        def _():
            ddeep_ref[at, :] += back

        sums_ref[4, :, :] += fold_rows(dfinal * unit)
        sums_ref[5, :, :] += fold_rows(dfinal)
        sums_ref[6, :, :] += jnp.broadcast_to(fold_rows(losses), (8, D))
        return carry

    lax.fori_loop(0, POOL * blocks, head_step, 0)

    out_up, out_head = ROW_U - ROW_HALF, ROW_H - ROW_HALF
    split_store(keep_ref, send_ref, core, pl.ds(out_head, VOCAB), tn(dlog_ref[...], final_ref[...]))
    for j in range(POOL):
        there = pl.ds(j * rows, rows)
        split_store(keep_ref, send_ref, core, pl.ds(out_up + j * D, D), tn(dup_ref[there, :], deep_ref[...]))
        hot = one_hot_cols(lines_ref[j : j + 1, :])
        part = nn(hot, dup_ref[there, :]) + nn(hot, low_ref[there, :])
        if j == 0:
            table_ref[...] = part
        else:
            table_ref[...] += part

    deep_ref[...] = ddeep_ref[...].astype(BF16)

    def dhid_step(index, carry):
        block, chunk = index // (FF // wide), index % (FF // wide)
        at = rows_of(block)
        lanes = rows_of(chunk, wide)
        dact = nt(deep_ref[at, :], w_ref[pl.ds(pl.multiple_of(f2 + chunk * wide, 16), wide), :])
        dhid_ref[at, lanes] = (dact * slope_ref[at, lanes]).astype(BF16)
        return carry

    lax.fori_loop(0, blocks * (FF // wide), dhid_step, 0)

    def dff_in(chunk, carry):
        here = rows_of(chunk, wide)
        split_store(keep_mid, send_mid, core, here, tn(dhid_ref[:, here], normed_ref[...]))
        lanes = pl.ds(pl.multiple_of(FF // 2 + chunk * wide, wide), wide)
        split_store(keep_ref, send_ref, core, here, tn(dhid_ref[:, lanes], normed_ref[...]))
        return carry

    lax.fori_loop(0, FF // wide // 2, dff_in, 0)

    def dff_out(chunk, carry):
        lanes = rows_of(chunk, wide)
        there = pl.ds(pl.multiple_of(FF // 2 + chunk * wide, wide), wide)
        split_store(keep_ref, send_ref, core, there, tn(act_ref[:, lanes], deep_ref[...]))
        return carry

    lax.fori_loop(0, FF // wide, dff_out, 0)

    def dnorm_step(block, carry):
        at = rows_of(block)
        dnormed = nn(dhid_ref[at, :], w_ref[f1 : f1 + FF, :])
        unit, scale = norm_parts(resid_ref[at, :])
        dresid_ref[at, :] = ddeep_ref[at, :] + norm_back(unit, scale, gain2, dnormed)
        sums_ref[2, :, :] += fold_rows(dnormed * unit)
        sums_ref[3, :, :] += fold_rows(dnormed)
        return carry

    lax.fori_loop(0, blocks, dnorm_step, 0)
    for k in range(8):
        small_ref[k : k + 1, :] = jnp.sum(sums_ref[k], 0, keepdims=True)


def shard_base(pieces, row):
    return row if pieces == 1 else row // SHARD * SHARD


def attend_back_kernel(short_len, slots, pieces, coords_ref, lay_ref, slope_ref, dresid_ref,
                       normed_ref, qkv_ref, lse_ref, mixed_ref, *refs):
    w_hbm, refs = refs[:pieces], refs[pieces:]
    (keep_ref, send_ref, dqkv_ref,
     w_ref, dist_ref, mask_ref, dbranch_ref, dmix_ref, sems) = refs
    rows = short_len * slots
    blocks = rows // BLOCK
    base = shard_base(pieces, ROW_O)
    core = coords_ref[2]
    fetch = Fetch(w_hbm, coords_ref, w_ref, sems, base, ROW_O, ROW_F1)
    fetch.start()
    out = ROW_O - base
    fetch.wait()

    def dmix_step(block, carry):
        at = rows_of(block)
        dbranch = dresid_ref[at, :].astype(BF16)
        dbranch_ref[at, :] = dbranch
        dmix_ref[at, :] = nt(dbranch, w_ref[out : out + D, :]).astype(BF16)
        return carry

    lax.fori_loop(0, blocks, dmix_step, 0)
    split_store(keep_ref, send_ref, core, pl.ds(3 * D, D), tn(mixed_ref[...], dbranch_ref[...]))

    left_lanes = lax.broadcasted_iota(jnp.int32, (short_len, 2 * HEAD), 1) < HEAD
    tile = 128
    for slot in range(slots):
        at = pl.ds(slot * short_len, short_len)
        key = lax.broadcasted_iota(jnp.int32, (short_len, short_len), 0)
        query = lax.broadcasted_iota(jnp.int32, (short_len, short_len), 1)
        half = jnp.where(lay_ref[slot] == 1, short_len // 2, short_len)
        allowed = (key <= query) & ((key >= half) == (query >= half))
        dist_ref[...] = (key - query).astype(F32)
        mask_ref[...] = jnp.where(allowed, 0.0, NEGATIVE)

        def head_step(pair, carry):
            lanes = pl.ds(pl.multiple_of(pair * 2 * HEAD, 2 * HEAD), 2 * HEAD)
            lanes_k = pl.ds(pl.multiple_of(D + pair * 2 * HEAD, 2 * HEAD), 2 * HEAD)
            lanes_v = pl.ds(pl.multiple_of(2 * D + pair * 2 * HEAD, 2 * HEAD), 2 * HEAD)
            queries = qkv_ref[at, lanes]
            keys = qkv_ref[at, lanes_k]
            values = qkv_ref[at, lanes_v]
            dmix = dmix_ref[at, lanes]
            zero = jnp.zeros_like(values)

            def one_side(side, array):
                return jnp.where(left_lanes, array, zero) if side == 0 else jnp.where(left_lanes, zero, array)

            scaled = queries * jnp.asarray(0.125, BF16)
            dkeys = jnp.zeros((short_len, 2 * HEAD), F32)
            dvalues = jnp.zeros((short_len, 2 * HEAD), F32)
            side_k = [one_side(side, keys) for side in range(2)]
            side_v = [one_side(side, values) for side in range(2)]
            side_q = [one_side(side, queries) for side in range(2)]
            side_m = [one_side(side, dmix) for side in range(2)]
            for part in range(short_len // tile):
                low = part * tile
                dqueries = jnp.zeros((tile, 2 * HEAD), F32)
                for side in range(2):
                    head = pair * 2 + side
                    slope = slope_ref[head]
                    scores = nt(side_k[side], scaled[low : low + tile])
                    scores = scores + jnp.where(
                        mask_ref[:, low : low + tile] == 0.0, dist_ref[:, low : low + tile] * slope, NEGATIVE
                    )
                    probs = jnp.exp(scores - lse_ref[slot, head, :, low : low + tile])
                    dprobs = nt(side_v[side], dmix[low : low + tile])
                    delta = jnp.sum(dprobs * probs, 0, keepdims=True)
                    dscores = (probs * (dprobs - delta) * 0.125).astype(BF16)
                    dvalues = dvalues + nn(probs.astype(BF16), side_m[side][low : low + tile])
                    dkeys = dkeys + nn(dscores, side_q[side][low : low + tile])
                    dqueries = dqueries + tn(dscores, side_k[side])
                dqkv_ref[pl.ds(slot * short_len + low, tile), lanes] = dqueries.astype(BF16)
            dqkv_ref[at, lanes_k] = dkeys.astype(BF16)
            dqkv_ref[at, lanes_v] = dvalues.astype(BF16)
            return carry

        lax.fori_loop(0, HEADS // 2, head_step, 0)

    for part in range(3):
        grad = tn(dqkv_ref[:, part * D : (part + 1) * D], normed_ref[...])
        split_store(keep_ref, send_ref, core, pl.ds(part * D, D), grad)


def front_back_kernel(pieces, coords_ref, lines_ref, vec_ref, dresid_ref, shifted_ref, short_ref, dqkv_ref, table_ref,
                      deep_small_ref, *refs):
    w_hbm, refs = refs[:pieces], refs[pieces:]
    keep_ref, send_ref, small_ref, w_ref, dshort_ref, sums_ref, sems = refs
    rows = dresid_ref.shape[0]
    blocks = rows // BLOCK
    core = coords_ref[2]
    fetch = Fetch(w_hbm, coords_ref, w_ref, sems, 0, 0 if pieces > 1 else ROW_E, ROW_O)
    fetch.start()
    pool, proj = ROW_P, ROW_QKV
    sums_ref[...] = jnp.zeros_like(sums_ref)
    gain = vec_ref[0:1, :]
    fetch.wait()

    def dshort_step(block, carry):
        at = rows_of(block)
        dnormed = nn(dqkv_ref[at, :], w_ref[proj : proj + 3 * D, :])
        unit, scale = norm_parts(short_ref[at, :])
        dshort_ref[at, :] = (dresid_ref[at, :] + norm_back(unit, scale, gain, dnormed)).astype(BF16)
        sums_ref[0, :, :] += fold_rows(dnormed * unit)
        sums_ref[1, :, :] += fold_rows(dnormed)
        return carry

    lax.fori_loop(0, blocks, dshort_step, 0)
    table = table_ref[...]
    for j in range(POOL):
        cols = slice(j * D, (j + 1) * D)
        split_store(keep_ref, send_ref, core, pl.ds(ROW_P + j * D, D), tn(shifted_ref[:, cols], dshort_ref[...]))
        dshift = nt(dshort_ref[...], w_ref[pool + j * D : pool + (j + 1) * D, :])
        high = dshift.astype(BF16)
        low = (dshift - high.astype(F32)).astype(BF16)
        hot = one_hot_cols(lines_ref[POOL + j : POOL + j + 1, :])
        table = table + nn(hot, high) + nn(hot, low)
    split_store(keep_ref, send_ref, core, pl.ds(ROW_E, VOCAB), table)
    small_ref[...] = deep_small_ref[...]
    for k in range(2):
        small_ref[k : k + 1, :] = jnp.sum(sums_ref[k], 0, keepdims=True)
    half = D // 2
    for k in range(2):
        send_ref[ROW_QKV + 16 * k : ROW_QKV + 16 * (k + 1), :] = two_parts(small_ref[:, k * half : (k + 1) * half])


def two_parts(values):
    high = values.astype(BF16)
    low = (values - high.astype(F32)).astype(BF16)
    return jnp.concatenate([high.astype(F32), low.astype(F32)], 0).astype(BF16)


def one_value(parts):
    parts = parts.astype(F32)
    return parts[:8] + parts[8:]


def lay_out(coords_ref, keep_ref, recv_ref, p_refs, q_refs):
    dp, z = coords_ref[0], coords_ref[1]
    quarter = D // 4
    line = 2 * SHARD
    rest = line - SCATTER_CUT

    def total(column, x, zed, begin, size):
        at = pl.ds(pl.multiple_of(x * (4 * line) + zed * line + begin, 16), size)
        lanes = pl.ds(pl.multiple_of(column * quarter, quarter), quarter)
        return (keep_ref[at, lanes].astype(F32) + recv_ref[at, lanes].astype(F32)).astype(BF16)

    for k in range(4):
        there = dp ^ k
        for zed in range(4):
            p_refs[k][zed * SCATTER_CUT : (zed + 1) * SCATTER_CUT, :] = total(
                there // 2, there % 2, zed, 0, SCATTER_CUT
            )
        for line_to in range(4):
            q_refs[k][line_to * rest : (line_to + 1) * rest, :] = total(
                line_to // 2, line_to % 2, z ^ k, SCATTER_CUT, rest
            )


def core_sum_kernel(coords_ref, keep_ref, recv_ref, *out_refs):
    lay_out(coords_ref, keep_ref, recv_ref, out_refs[:4], out_refs[4:])


def core_sum_front_kernel(coords_ref, keep_front, keep_att, keep_mid, recv_front, recv_att, recv_mid, small_ref, *refs):
    out_refs, (keep_ref, recv_ref, sems) = refs[:8], refs[8:]
    copies = [
        pltpu.make_async_copy(source, target, sems.at[k])
        for k, (source, target) in enumerate((
            (keep_att, keep_ref.at[pl.ds(ROW_QKV, ROW_F1 - ROW_QKV)]),
            (recv_att, recv_ref.at[pl.ds(ROW_QKV, ROW_F1 - ROW_QKV)]),
            (keep_mid, keep_ref.at[pl.ds(ROW_F1, ROW_HALF - ROW_F1)]),
            (recv_mid, recv_ref.at[pl.ds(ROW_F1, ROW_HALF - ROW_F1)]),
            (keep_front, keep_ref.at[pl.ds(0, ROW_QKV)]),
            (recv_front.at[pl.ds(0, ROW_QKV)], recv_ref.at[pl.ds(0, ROW_QKV)]),
            (recv_front.at[pl.ds(ROW_QKV, 32)], recv_ref.at[pl.ds(ROW_HALF, 32)]),
        ))
    ]
    for copy in copies:
        copy.start()
    for copy in copies:
        copy.wait()
    lay_out(coords_ref, keep_ref, recv_ref, out_refs[:4], out_refs[4:])
    quarter = D // 4
    for k in range(2):
        both = small_ref[:, 2 * k * quarter : 2 * (k + 1) * quarter] + one_value(
            recv_ref[ROW_HALF + 16 * k : ROW_HALF + 16 * (k + 1), :]
        )
        for side in range(2):
            parts = two_parts(both[:, side * quarter : (side + 1) * quarter])
            row = 4 * SCATTER_CUT + 16 * (2 * k + side)
            for p_ref in out_refs[:4]:
                p_ref[row : row + 16, :] = parts


def sum_of(refs, row, size):
    at = pl.ds(pl.multiple_of(row, 16), size)
    return (refs[0][at, :].astype(F32) + refs[1][at, :].astype(F32)) + (
        refs[2][at, :].astype(F32) + refs[3][at, :].astype(F32)
    )


def first_sum_kernel(coords_ref, *refs):
    sources = ((refs[0:4], refs[4:8]), (refs[8:12], refs[12:16]))
    s_refs, t_refs = refs[16:20], refs[20:24]
    dp, z = coords_ref[0], coords_ref[1]
    rest = 2 * SHARD - SCATTER_CUT
    for half, (p_refs, q_refs) in enumerate(sources):
        for k in range(4):
            s_refs[k][half * SCATTER_CUT : (half + 1) * SCATTER_CUT, :] = sum_of(
                p_refs, (z ^ k) * SCATTER_CUT, SCATTER_CUT
            ).astype(BF16)
            t_refs[k][half * rest : (half + 1) * rest, :] = sum_of(q_refs, (dp ^ k) * rest, rest).astype(BF16)
    for k in range(4):
        row = 4 * SCATTER_CUT + 16 * k
        value = sum(one_value(ref[row : row + 16, :]) for ref in sources[0][0])
        parts = two_parts(value)
        for s_ref in s_refs:
            s_ref[2 * SCATTER_CUT + 16 * k : 2 * SCATTER_CUT + 16 * (k + 1), :] = parts


def last_sum_kernel(coords_ref, *refs):
    s_refs, t_refs, out_refs, (small_ref, square_ref, sum_ref) = refs[:4], refs[4:8], refs[8:12], refs[12:]
    y, core = coords_ref[0] // 2, coords_ref[2]
    rest = 2 * SHARD - SCATTER_CUT
    squares = jnp.zeros((8, D // 4), F32)
    for k in range(2):
        half = y ^ k
        first = sum_of(s_refs, half * SCATTER_CUT, SCATTER_CUT)
        second = sum_of(t_refs, half * rest, rest)
        squares = squares + fold_rows(first * first) + fold_rows(second * second)
        sum_ref[0:SCATTER_CUT, :] = first
        sum_ref[SCATTER_CUT:, :] = second
        for other in range(2):
            out_refs[2 * other + k][...] = sum_ref[pl.ds(pl.multiple_of((core ^ other) * SHARD, 8), SHARD), :]
    for k in range(4):
        row = 2 * SCATTER_CUT + 16 * k
        small_ref[:, k * (D // 4) : (k + 1) * (D // 4)] = sum(
            one_value(ref[row : row + 16, :]) for ref in s_refs
        )
    square_ref[...] = squares


def adam(param, first_m, second_m, grad, decay):
    first_new = BETA * first_m + (1.0 - BETA) * grad
    second_new = BETA * second_m + (1.0 - BETA) * grad * grad
    correct = 1.0 - BETA**STEP
    update = -RATE * (
        first_new / correct / (jnp.sqrt(second_new / correct) + EPS_ADAM) + decay * param
    )
    return (first_new, second_new, update)


def update_kernel(count, coords_ref, g0, g1, g2, g3, q0, q1, q2, q3, small_ref, w_ref, mw_ref, vw_ref, w_vec, m_vec, v_vec,
                  loss_ref, norm_ref, mw_out, vw_out, uw_out, m_out, v_out, u_out):
    y, core, mine = coords_ref[0] // 2, coords_ref[2], coords_ref[3]
    small = small_ref[...]
    line = lax.broadcasted_iota(jnp.int32, small.shape, 0)
    gradient = jnp.where(line < 6, small, 0.0)
    squares = (q0[...] + q1[...]) + (q2[...] + q3[...])

    def whole(values):
        return jnp.sum(jnp.sum(values, 0, keepdims=True), 1, keepdims=True)

    norm = jnp.sqrt(whole(squares) + whole(gradient * gradient))
    factor = CLIP / jnp.maximum(norm, CLIP)
    norm_ref[...] = norm
    loss_ref[...] = small[6:7, 0:1] / count
    quarter = D // 4
    for k, grad_ref in enumerate((g0, g1, g2, g3)):
        place = (core ^ (k // 2)) * 2 + (y ^ (k % 2))
        lanes = pl.ds(pl.multiple_of(place * quarter, quarter), quarter)
        mw_out[:, lanes], vw_out[:, lanes], uw_out[:, lanes] = adam(
            w_ref[:, lanes], mw_ref[:, lanes], vw_ref[:, lanes], grad_ref[...] * factor, DECAY
        )
    width = w_vec.shape[1]
    owned = pltpu.roll(gradient, lax.rem(small.shape[1] - mine * width, small.shape[1]), 1)[:6, :width]
    m_out[...], v_out[...], u_out[...] = adam(w_vec[...], m_vec[...], v_vec[...], owned * factor, 0.0)


VMEM = pl.BlockSpec(memory_space=pltpu.VMEM)
SMEM = pl.BlockSpec(memory_space=pltpu.SMEM)
ANY = pl.BlockSpec(memory_space=pl.ANY)
LIMIT = 58 * 1024 * 1024


def deep_base(pieces):
    return shard_base(pieces, ROW_F1)


def device_grads(pieces, tail, vecs, coords, ids, layouts, count, paired):
    slots = layouts.shape[0]
    rows = ids.shape[1]
    short_len = rows // slots
    slopes = np.float32(2.0) ** (-8.0 * (np.arange(HEADS, dtype=np.float32) + 1.0) / HEADS)
    shape = jax.ShapeDtypeStruct
    params = pltpu.CompilerParams(vmem_limit_bytes=LIMIT)
    number = len(pieces)
    whole_shards = number > 1
    front_rows = -(-ROW_F1 // SHARD) * SHARD if whole_shards else ROW_F1
    deep_rows = ROW_END - deep_base(number)
    table_rows = SHARD if whole_shards else VOCAB
    jobs = 64 if whole_shards else 1
    more = [] if vecs is None else [vecs]
    rest = [] if tail is None else [tail]
    half = D // 2
    shifted, short, normed, qkv, lse, mixed, resid, lines, cols, vecs = pl.pallas_call(
        partial(attend_kernel, short_len, slots, number),
        out_shape=(
            shape((rows, POOL * D), BF16),
            shape((rows, D), F32),
            shape((rows, D), BF16),
            shape((rows, 3 * D), BF16),
            shape((slots, HEADS, 1, short_len), F32),
            shape((rows, D), BF16),
            shape((rows, D), F32),
            shape((16, rows), jnp.int32),
            shape((POOL, rows, 128), jnp.int32),
            shape((8, D), F32),
        ),
        in_specs=[SMEM, SMEM, SMEM, VMEM] + [ANY] * number + [VMEM] * len(more),
        out_specs=(VMEM,) * 10,
        scratch_shapes=[
            pltpu.VMEM((front_rows, D), BF16),
            pltpu.VMEM((short_len, short_len), F32),
            pltpu.VMEM((short_len, short_len), F32),
            pltpu.VMEM((short_len, 2 * HEAD), F32),
            pltpu.VMEM((32, 16, D // 2), BF16),
            pltpu.SemaphoreType.DMA((jobs,)),
            pltpu.SemaphoreType.DMA((32,)),
        ],
        compiler_params=params,
        cost_estimate=pl.CostEstimate(flops=9_000_000_000, bytes_accessed=20_000_000, transcendentals=2_400_000),
        name="attend",
    )(coords, layouts, slopes, ids, *pieces, *more)
    keep_mid, send_mid, keep_deep, send_deep, table, dresid, small_deep = pl.pallas_call(
        partial(deep_kernel, count, number),
        out_shape=(
            shape((ROW_HALF - ROW_F1, half), BF16),
            shape((ROW_HALF - ROW_F1, half), BF16),
            shape((ROW_END - ROW_HALF, half), BF16),
            shape((ROW_END - ROW_HALF, half), BF16),
            shape((VOCAB, D), F32),
            shape((rows, D), F32),
            shape((8, D), F32),
        ),
        in_specs=[SMEM] + [VMEM] * 4 + [ANY] * (number + len(rest)),
        out_specs=(VMEM,) * 7,
        scratch_shapes=[
            pltpu.VMEM((deep_rows, D), BF16),
            pltpu.VMEM((table_rows, D), BF16),
            pltpu.VMEM((rows, D), BF16),
            pltpu.VMEM((rows, FF), BF16),
            pltpu.VMEM((rows, FF), F32),
            pltpu.VMEM((rows, D), BF16),
            pltpu.VMEM((POOL * rows, D), BF16),
            pltpu.VMEM((POOL * rows, VOCAB), BF16),
            pltpu.VMEM((POOL * rows, D), BF16),
            pltpu.VMEM((POOL * rows, D), BF16),
            pltpu.VMEM((rows, D), F32),
            pltpu.VMEM((rows, FF), BF16),
            pltpu.VMEM((8, 8, D), F32),
            pltpu.SemaphoreType.DMA((jobs,)),
            pltpu.SemaphoreType.DMA((jobs,)),
            pltpu.SemaphoreType.DMA((2,)),
        ],
        compiler_params=params,
        name="deep",
    )(coords, cols, lines, vecs, resid, *pieces, *rest)
    out_base = shard_base(number, ROW_O)
    keep_att, send_att, dqkv = pl.pallas_call(
        partial(attend_back_kernel, short_len, slots, number),
        out_shape=(
            shape((ROW_F1 - ROW_QKV, half), BF16),
            shape((ROW_F1 - ROW_QKV, half), BF16),
            shape((rows, 3 * D), BF16),
        ),
        in_specs=[SMEM, SMEM, SMEM] + [VMEM] * 5 + [ANY] * number,
        out_specs=(VMEM,) * 3,
        scratch_shapes=[
            pltpu.VMEM((front_rows - out_base, D), BF16),
            pltpu.VMEM((short_len, short_len), F32),
            pltpu.VMEM((short_len, short_len), F32),
            pltpu.VMEM((rows, D), BF16),
            pltpu.VMEM((rows, D), BF16),
            pltpu.SemaphoreType.DMA((jobs,)),
        ],
        compiler_params=params,
        cost_estimate=pl.CostEstimate(flops=11_000_000_000, bytes_accessed=20_000_000, transcendentals=2_400_000),
        name="attend_back",
    )(coords, layouts, slopes, dresid, normed, qkv, lse, mixed, *pieces)
    if paired:
        recv_deep, recv_mid = swap_with(send_deep, core=1), swap_with(send_mid, core=1)
        recv_deep, recv_mid = lax.optimization_barrier((recv_deep, recv_mid))
        sent = core_sum(coords, keep_deep, recv_deep)
        recv_att = swap_with(send_att, core=1)
        sent, recv_att, dqkv = lax.optimization_barrier((sent, recv_att, dqkv))
        sent = first_exchange(sent)
    keep_front, send_front, small = pl.pallas_call(
        partial(front_back_kernel, number),
        out_shape=(shape((ROW_QKV, half), BF16), shape((ROW_QKV + 32, half), BF16), shape((8, D), F32)),
        in_specs=[SMEM] + [VMEM] * 8 + [ANY] * number,
        out_specs=(VMEM,) * 3,
        scratch_shapes=[
            pltpu.VMEM((front_rows, D), BF16),
            pltpu.VMEM((rows, D), BF16),
            pltpu.VMEM((2, 8, D), F32),
            pltpu.SemaphoreType.DMA((jobs,)),
        ],
        compiler_params=params,
        cost_estimate=pl.CostEstimate(flops=8_000_000_000, bytes_accessed=20_000_000, transcendentals=0),
        name="front_back",
    )(coords, lines, vecs, dresid, shifted, short, dqkv, table, small_deep, *pieces)
    if not paired:
        front = jnp.concatenate([keep_front, send_front[:ROW_QKV]], 1)
        others = [
            jnp.concatenate(pair, 1)
            for pair in ((keep_att, send_att), (keep_mid, send_mid), (keep_deep, send_deep))
        ]
        return jnp.concatenate([front] + others, 0), small
    late = 5
    early = [array for k, array in enumerate(sent) if k != late]
    early, keep_front, send_front, small = lax.optimization_barrier((early, keep_front, send_front, small))
    sent = early[:late] + [sent[late]] + early[late:]
    received = [swap_with(send_front, core=1), recv_att, recv_mid]
    out_p, out_q = exchange_shapes(64)
    parts = pl.pallas_call(
        core_sum_front_kernel,
        out_shape=(out_p,) * 4 + (out_q,) * 4,
        in_specs=[SMEM] + [ANY] * 6 + [VMEM],
        out_specs=(VMEM,) * 8,
        scratch_shapes=[
            pltpu.VMEM((ROW_HALF, half), BF16),
            pltpu.VMEM((ROW_HALF + 32, half), BF16),
            pltpu.SemaphoreType.DMA((7,)),
        ],
        compiler_params=params,
        name="core_sum_front",
    )(coords, keep_front, keep_att, keep_mid, *received, small)
    return first_exchange(parts), sent


def exchange_shapes(extra):
    quarter = D // 4
    return (
        jax.ShapeDtypeStruct((4 * SCATTER_CUT + extra, quarter), BF16),
        jax.ShapeDtypeStruct((4 * (2 * SHARD - SCATTER_CUT), quarter), BF16),
    )


def core_sum(coords, keep, received):
    out_p, out_q = exchange_shapes(0)
    return pl.pallas_call(
        core_sum_kernel,
        out_shape=(out_p,) * 4 + (out_q,) * 4,
        in_specs=[SMEM] + [VMEM] * 2,
        out_specs=(VMEM,) * 8,
        compiler_params=pltpu.CompilerParams(vmem_limit_bytes=LIMIT),
        name="core_sum",
    )(coords, keep, received)


def first_exchange(parts):
    over = [parts[0]] + [swap_with(parts[k], line=k) for k in (1, 2, 3)]
    return over + [parts[4]] + [swap_with(parts[4 + k], zed=k) for k in (1, 2, 3)]


def swap_with(array, line=0, zed=0, core=0):
    lines, rest = lax.axis_size("dp"), lax.axis_size("fsdp")
    pairs = [
        (d * rest + f, (d ^ line) * rest + (f ^ (2 * zed + core)))
        for d in range(lines)
        for f in range(rest)
    ]
    return lax.ppermute(array, AXES, pairs)


def swap_halves(coords, shard):
    half = D // 2
    upper = coords[0] // 2 == 1
    left, right = shard[:, :half], shard[:, half:]
    keep, send = jnp.where(upper, right, left), jnp.where(upper, left, right)
    other = swap_with(send, line=2)
    return jnp.where(upper, other, keep), jnp.where(upper, keep, other)


def gather_pieces(block, vectors):
    half = D // 2
    width = vectors.shape[1]
    start = lax.axis_index(AXES) * width
    own = lax.dynamic_update_slice(
        jnp.zeros((16, half), BF16), vectors, (8 * (start // half), start % half)
    )
    first, second = jnp.concatenate([block[:GATHER_CUT], own], 0), block[GATHER_CUT:]
    along = jnp.concatenate([first] + [swap_with(first, zed=k) for k in (1, 2, 3)], 0)
    across = jnp.concatenate([second] + [swap_with(second, line=k) for k in (1, 2, 3)], 0)
    pieces = [along] + [swap_with(along, line=k) for k in (1, 2, 3)]
    pieces += [across] + [swap_with(across, zed=k) for k in (1, 2, 3)]
    return pieces + [swap_with(piece, core=1) for piece in pieces]


def scatter_sum(coords, front, deep):
    shape = jax.ShapeDtypeStruct
    params = pltpu.CompilerParams(vmem_limit_bytes=LIMIT)
    quarter = D // 4
    rest = 2 * SHARD - SCATTER_CUT
    parts = pl.pallas_call(
        first_sum_kernel,
        out_shape=(shape((2 * SCATTER_CUT + 64, quarter), BF16),) * 4 + (shape((2 * rest, quarter), BF16),) * 4,
        in_specs=[SMEM] + [VMEM] * 16,
        out_specs=(VMEM,) * 8,
        compiler_params=params,
        name="first_sum",
    )(coords, *front, *deep)
    second = [parts[0]] + [swap_with(parts[k], zed=k) for k in (1, 2, 3)]
    second += [parts[4]] + [swap_with(parts[4 + k], line=k) for k in (1, 2, 3)]
    *outs, small, squares = pl.pallas_call(
        last_sum_kernel,
        out_shape=(shape((SHARD, quarter), F32),) * 4 + (shape((8, D), F32), shape((8, quarter), F32)),
        in_specs=[SMEM] + [VMEM] * 8,
        out_specs=(VMEM,) * 6,
        scratch_shapes=[pltpu.VMEM((2 * SHARD, quarter), F32)],
        compiler_params=params,
        name="last_sum",
    )(coords, *second)
    squares = squares + swap_with(squares, core=1)
    quarters = [outs[0], swap_with(outs[1], line=2), swap_with(outs[2], core=1), swap_with(outs[3], line=2, core=1)]
    squares = (squares + swap_with(squares, line=1)) + (swap_with(squares, line=2) + swap_with(squares, line=3))
    squares = [squares] + [swap_with(squares, zed=k) for k in (1, 2, 3)]
    return quarters, small, squares


def shards(byte_ids, layouts, weights, vectors, m_weights, v_weights, m_vectors, v_vectors):
    devices = lax.axis_size(AXES)
    micro = byte_ids.shape[0]
    count = float(micro * layouts.shape[1] * devices * byte_ids.shape[2])
    lines, rest = lax.axis_size("dp"), lax.axis_size("fsdp")
    place = lax.axis_index("fsdp")
    coords = jnp.stack([lax.axis_index("dp"), place // 2, place % 2, lax.axis_index(AXES)]).astype(jnp.int32)
    paired = lines == 4 and rest == 8 and weights.shape[0] == SHARD
    weights_low = weights.astype(BF16)
    vectors_low = vectors.astype(BF16)
    width = vectors.shape[1]
    mine = lax.axis_index(AXES) * width
    flat_layouts = layouts.reshape(-1)
    ids = byte_ids.reshape(flat_layouts.shape[0], -1, POOL).transpose(2, 0, 1).reshape(POOL, -1)
    ids = jnp.pad(ids, ((0, 8 - POOL), (0, 0)))
    if paired:
        front, back = swap_halves(coords, weights_low)
        tail = lax.all_gather(back, AXES, axis=0, tiled=True)
        pieces = gather_pieces(front, vectors_low)
        front, deep = device_grads(
            pieces, tail, None, coords, ids, flat_layouts, count, True
        )
        quarters, small, squares = scatter_sum(coords, front, deep)
        like = [jax.ShapeDtypeStruct((1, 1), F32)] * 2
        like += [jax.ShapeDtypeStruct(weights.shape, F32)] * 3 + [jax.ShapeDtypeStruct(vectors.shape, F32)] * 3
        loss, grad_norm, *updated = pl.pallas_call(
            partial(update_kernel, count),
            out_shape=like,
            in_specs=[SMEM] + [VMEM] * 15,
            out_specs=[VMEM] * 8,
            compiler_params=pltpu.CompilerParams(vmem_limit_bytes=LIMIT),
            name="update",
        )(coords, *quarters, *squares, small, weights, m_weights, v_weights, vectors, m_vectors, v_vectors)
        return (loss[0, 0], grad_norm[0, 0], *updated)
    coords = coords * 0
    pieces = [lax.all_gather(weights_low, AXES, axis=0, tiled=True)]
    vecs = lax.all_gather(vectors_low, AXES, axis=1, tiled=True)
    vecs = jnp.pad(vecs.astype(F32), ((0, 2), (0, 0)))
    local, small = device_grads(pieces, None, vecs, coords, ids, flat_layouts, count, False)
    owned = lax.psum_scatter(local.astype(F32), AXES, scatter_dimension=0, tiled=True)
    small, squares = lax.psum((small, jnp.sum(owned * owned)), AXES)
    loss = small[6, 0] / count
    vec_grads = small[:6]
    owned_vecs = lax.dynamic_slice(vec_grads, (0, mine), (6, width))
    squares = squares + jnp.sum(vec_grads * vec_grads)
    grad_norm = jnp.sqrt(squares)
    factor = CLIP / jnp.maximum(grad_norm, CLIP)
    first_w, second_w, update_w = adam(weights, m_weights, v_weights, owned * factor, DECAY)
    first_v, second_v, update_v = adam(vectors, m_vectors, v_vectors, owned_vecs * factor, 0.0)
    return (loss, grad_norm, first_w, second_w, update_w, first_v, second_v, update_v)


def solution(mesh):
    in_specs = (
        P(None, AXES, None),
        P(None, AXES),
        P(AXES, None),
        P(None, AXES),
        P(AXES, None),
        P(AXES, None),
        P(None, AXES),
        P(None, AXES),
    )
    out_specs = (
        P(),
        P(),
        P(AXES, None),
        P(AXES, None),
        P(AXES, None),
        P(None, AXES),
        P(None, AXES),
        P(None, AXES),
    )
    return jax.shard_map(shards, mesh=mesh, in_specs=in_specs, out_specs=out_specs, check_vma=False)
```

```python
from functools import partial

import jax
import jax.numpy as jnp
import numpy as np
from jax import lax
from jax.experimental import pallas as pl
from jax.experimental.pallas import tpu as pltpu
from jax.sharding import PartitionSpec as P

D = 512
HEADS = 8
HEAD = 64
FF = 2048
VOCAB = 256
POOL = 3

EPS_NORM = 1e-05
EPS_ADAM = 1e-08
CLIP = 0.2
RATE = 0.03
DECAY = 0.1
BETA = 0.5
STEP = 3
NEGATIVE = -1000000000.0

F32 = jnp.float32
BF16 = jnp.bfloat16

ROW_E = 0
ROW_P = VOCAB
ROW_QKV = ROW_P + POOL * D
ROW_O = ROW_QKV + 3 * D
ROW_F1 = ROW_O + D
ROW_F2 = ROW_F1 + FF
ROW_U = ROW_F2 + FF
ROW_H = ROW_U + POOL * D
ROW_END = ROW_H + VOCAB
ROW_HALF = ROW_END // 2
assert ROW_HALF - ROW_F1 == FF // 2

BLOCK = 768
AXES = ("dp", "fsdp")
SHARD = ROW_END // 32
GATHER_CUT = 208
SCATTER_CUT = 400


def nn(left, right):
    return lax.dot_general(left, right, (((1,), (0,)), ((), ())), preferred_element_type=F32)


def nt(left, right):
    return lax.dot_general(left, right, (((1,), (1,)), ((), ())), preferred_element_type=F32)


def tn(left, right):
    return lax.dot_general(left, right, (((0,), (0,)), ((), ())), preferred_element_type=F32)


def norm_parts(values):
    center = values - jnp.mean(values, -1, keepdims=True)
    spread = jnp.mean(center * center, -1, keepdims=True)
    scale = lax.rsqrt(spread + EPS_NORM)
    return center * scale, scale


def norm_back(unit, scale, gain, grad):
    inner = grad * gain
    mean_inner = jnp.mean(inner, -1, keepdims=True)
    mean_cross = jnp.mean(inner * unit, -1, keepdims=True)
    return scale * (inner - mean_inner - unit * mean_cross)


def fold_rows(values):
    return jnp.sum(values.reshape(values.shape[0] // 8, 8, values.shape[1]), 0)


def one_hot_rows(ids):
    lanes = lax.broadcasted_iota(jnp.int32, (ids.shape[0], VOCAB), 1)
    return jnp.where(lanes == ids, 1.0, 0.0).astype(BF16)


def one_hot_cols(ids):
    lines = lax.broadcasted_iota(jnp.int32, (VOCAB, ids.shape[1]), 0)
    return jnp.where(lines == ids, 1.0, 0.0).astype(BF16)


def rows_of(index, size=BLOCK):
    return pl.ds(pl.multiple_of(index * size, size), size)


def gathered_parts(coords_ref):
    dp, z, core = coords_ref[0], coords_ref[1], coords_ref[2]
    for side in range(2):
        for k in range(4):
            for part in range(4):
                for kind in range(2):
                    d, e = (k, part) if kind == 0 else (part, k)
                    line = dp ^ d
                    yield side * 8 + kind * 4 + k, part, kind, line // 2, (line % 2) * 8 + (z ^ e) * 2 + (core ^ side)


class Fetch:
    def __init__(self, pieces, coords_ref, w_ref, sems, base, low, high):
        self.jobs = []
        if len(pieces) == 1:
            size = high - low
            copy = pltpu.make_async_copy(
                pieces[0].at[pl.ds(low, size)], w_ref.at[pl.ds(low - base, size)], sems.at[0]
            )
            self.jobs.append((None, copy))
            return
        first, last = low // SHARD, (high - 1) // SHARD
        half = D // 2
        for number, (piece, part, kind, y, shard) in enumerate(gathered_parts(coords_ref)):
            begin, size, step = ((0, GATHER_CUT, GATHER_CUT + 16), (GATHER_CUT, SHARD - GATHER_CUT, SHARD - GATHER_CUT))[kind]
            wanted = (shard >= first) & (shard <= last)
            place = jnp.where(wanted, shard * SHARD - base + begin, 0)
            copy = pltpu.make_async_copy(
                pieces[piece].at[pl.ds(part * step, size)],
                w_ref.at[pl.ds(pl.multiple_of(place, 16), size), pl.ds(pl.multiple_of(y * half, half), half)],
                sems.at[number],
            )
            self.jobs.append((wanted, copy))

    def start(self):
        for wanted, copy in self.jobs:
            if wanted is None:
                copy.start()
            else:
                pl.when(wanted)(copy.start)

    def wait(self):
        for wanted, copy in self.jobs:
            if wanted is None:
                copy.wait()
            else:
                pl.when(wanted)(copy.wait)


def attend_kernel(short_len, slots, pieces, coords_ref, lay_ref, slope_ref, ids_ref, *refs):
    w_hbm, refs = refs[:pieces], refs[pieces:]
    if pieces == 1:
        vec_in_ref, refs = refs[0], refs[1:]
    (shifted_ref, short_ref, normed_ref, qkv_ref, lse_ref, mixed_ref, resid_ref, lines_ref, cols_ref, vec_ref,
     w_ref, dist_ref, mask_ref, lse_cols, part_ref, sems, part_sems) = refs
    rows = short_len * slots
    fetch = Fetch(w_hbm, coords_ref, w_ref, sems, 0, 0, ROW_F1)
    fetch.start()
    copies = []
    if pieces > 1:
        for piece, part, kind, _, _ in gathered_parts(coords_ref):
            if kind == 0:
                place = pl.ds(part * (GATHER_CUT + 16) + GATHER_CUT, 16)
                number = len(copies)
                copies.append(
                    pltpu.make_async_copy(w_hbm[piece].at[place], part_ref.at[number], part_sems.at[number])
                )
        for copy in copies:
            copy.start()

    ids = ids_ref[...]
    group = lax.broadcasted_iota(jnp.int32, (1, rows), 1)
    starts = group == 0
    for slot in range(slots):
        starts = starts | (group == slot * short_len)
        starts = starts | ((group == slot * short_len + short_len // 2) & (lay_ref[slot] == 1))
    ends = group == rows - 1
    for slot in range(slots):
        ends = ends | (group == (slot + 1) * short_len - 1)
        ends = ends | ((group == slot * short_len + short_len // 2 - 1) & (lay_ref[slot] == 1))
    before, after = pltpu.roll(ids, 1, 1), pltpu.roll(ids, rows - 1, 1)
    own = [ids[j : j + 1] for j in range(POOL)]
    back = [jnp.where(starts, -1, before[1:2]), jnp.where(starts, -1, before[2:3]), ids[0:1]]
    ahead = [ids[1:2], ids[2:3], jnp.where(ends, -1, after[0:1])]
    for j in range(POOL):
        lines_ref[j : j + 1, :] = own[j]
        lines_ref[POOL + j : POOL + j + 1, :] = back[j]
        lines_ref[2 * POOL + j : 2 * POOL + j + 1, :] = ahead[j]
    lines_ref[3 * POOL :, :] = jnp.zeros((16 - 3 * POOL, rows), jnp.int32)
    turned = jnp.concatenate([lines_ref[...].astype(F32), jnp.zeros((112, rows), F32)], 0).T.astype(jnp.int32)
    for j in range(POOL):
        cols_ref[j] = pltpu.roll(turned, 128 - j, 1)

    for copy in copies:
        copy.wait()
    if pieces > 1:
        both = part_ref[0].astype(F32)
        for k in range(1, len(copies)):
            both = both + part_ref[k].astype(F32)
        vec_ref[...] = jnp.concatenate([both[:8], both[8:]], 1)
    else:
        vec_ref[...] = vec_in_ref[...]
    fetch.wait()
    gain, offset = vec_ref[0:1, :], vec_ref[1:2, :]

    def pool_step(block, carry):
        at = rows_of(block)
        for j in range(POOL):
            hot = one_hot_rows(cols_ref[j, at, POOL : POOL + 1])
            shifted_ref[at, j * D : (j + 1) * D] = nn(hot, w_ref[ROW_E:ROW_P, :]).astype(BF16)
        short = nn(shifted_ref[at, :], w_ref[ROW_P:ROW_QKV, :])
        short_ref[at, :] = short
        unit, _ = norm_parts(short)
        normed_ref[at, :] = (unit * gain + offset).astype(BF16)
        return carry

    lax.fori_loop(0, rows // BLOCK, pool_step, 0)

    def qkv_step(block, carry):
        at = rows_of(block)
        qkv_ref[at, :] = nt(normed_ref[at, :], w_ref[ROW_QKV:ROW_O, :]).astype(BF16)
        return carry

    lax.fori_loop(0, rows // BLOCK, qkv_step, 0)

    left_lanes = lax.broadcasted_iota(jnp.int32, (short_len, 2 * HEAD), 1) < HEAD
    tile = short_len
    for slot in range(slots):
        at = pl.ds(slot * short_len, short_len)
        query = lax.broadcasted_iota(jnp.int32, (short_len, short_len), 0)
        key = lax.broadcasted_iota(jnp.int32, (short_len, short_len), 1)
        half = jnp.where(lay_ref[slot] == 1, short_len // 2, short_len)
        allowed = (key <= query) & ((key >= half) == (query >= half))
        dist_ref[...] = (key - query).astype(F32)
        mask_ref[...] = jnp.where(allowed, 0.0, NEGATIVE)

        def head_step(pair, carry):
            lanes = pl.ds(pl.multiple_of(pair * 2 * HEAD, 2 * HEAD), 2 * HEAD)
            lanes_k = pl.ds(pl.multiple_of(D + pair * 2 * HEAD, 2 * HEAD), 2 * HEAD)
            lanes_v = pl.ds(pl.multiple_of(2 * D + pair * 2 * HEAD, 2 * HEAD), 2 * HEAD)
            queries = qkv_ref[at, lanes] * jnp.asarray(0.125, BF16)
            keys = qkv_ref[at, lanes_k]
            values = qkv_ref[at, lanes_v]
            zero = jnp.zeros_like(values)
            vals = [jnp.where(left_lanes, values, zero), jnp.where(left_lanes, zero, values)]
            slots_q = [jnp.where(left_lanes, queries, zero), jnp.where(left_lanes, zero, queries)]
            for part in range(short_len // tile):
                low = part * tile
                mixed = jnp.zeros((tile, 2 * HEAD), F32)
                columns = lse_cols[low : low + tile, :]
                where = lax.broadcasted_iota(jnp.int32, (tile, 2 * HEAD), 1)
                for side in range(2):
                    head = pair * 2 + side
                    slope = slope_ref[head]
                    scores = nt(slots_q[side][low : low + tile], keys)
                    scores = scores + jnp.where(
                        mask_ref[low : low + tile, :] == 0.0, dist_ref[low : low + tile, :] * slope, NEGATIVE
                    )
                    top = jnp.max(scores, -1, keepdims=True)
                    expo = jnp.exp(scores - top)
                    total = jnp.sum(expo, -1, keepdims=True)
                    probs = (expo * (1.0 / total)).astype(BF16)
                    columns = jnp.where(where == head, top + jnp.log(total), columns)
                    mixed = mixed + nn(probs, vals[side])
                lse_cols[low : low + tile, :] = columns
                mixed_ref[pl.ds(slot * short_len + low, tile), lanes] = mixed.astype(BF16)
            return carry

        lse_cols[...] = jnp.zeros_like(lse_cols)
        lax.fori_loop(0, HEADS // 2, head_step, 0, unroll=True)
        turned = lse_cols[...].T
        for head in range(HEADS):
            lse_ref[slot, head] = turned[head : head + 1, :]

    def out_step(block, carry):
        at = rows_of(block)
        resid_ref[at, :] = short_ref[at, :] + nn(mixed_ref[at, :], w_ref[ROW_O:ROW_F1, :])
        return carry

    lax.fori_loop(0, rows // BLOCK, out_step, 0)


def gelu_parts(hidden):
    size = jnp.abs(hidden)
    near = 1.0 / (1.0 + (0.3275911 * 0.7071067811865476) * size)
    bell = jnp.exp(hidden * hidden * -0.5)
    tail = near * (0.127414796 + near * (-0.142248368 + near * (0.7107068705 + near * (-0.7265760135 + near * 0.5307027145))))
    tail = tail * bell
    cdf = jnp.where(hidden >= 0.0, 1.0 - tail, tail)
    return hidden * cdf, cdf + hidden * bell * 0.3989422804014327


def split_store(keep_ref, send_ref, core, rows, values):
    half = D // 2
    low, high = values[:, :half].astype(BF16), values[:, half:].astype(BF16)
    keep_ref[rows, :] = jnp.where(core == 0, low, high)
    send_ref[rows, :] = jnp.where(core == 0, high, low)


def deep_kernel(count, pieces, coords_ref, cols_ref, lines_ref, vec_ref, resid_ref, *refs):
    w_hbm, refs = refs[:pieces], refs[pieces:]
    if pieces > 1:
        tail_hbm, refs = refs[0], refs[1:]
    (keep_mid, send_mid, keep_ref, send_ref, table_ref, dresid_ref, small_ref,
     w_ref, e_ref, normed_ref, act_ref, slope_ref, deep_ref, final_ref, dlog_ref, dup_ref, low_ref,
     ddeep_ref, dhid_ref, sums_ref, sems, e_sems, tail_sems) = refs
    rows = resid_ref.shape[0]
    blocks = rows // BLOCK
    base = deep_base(pieces)
    core = coords_ref[2]
    fetches = [
        Fetch(w_hbm, coords_ref, w_ref, sems, base, ROW_F1, ROW_END if pieces == 1 else ROW_END // 2),
        Fetch(w_hbm, coords_ref, e_ref, e_sems, 0, 0, VOCAB),
    ]
    for fetch in fetches:
        fetch.start()
    copies = []
    if pieces > 1:
        half = ROW_END // 2
        for y in range(2):
            copies.append(
                pltpu.make_async_copy(
                    tail_hbm.at[pl.ds(y * half, half)],
                    w_ref.at[pl.ds(half - base, half), pl.ds(y * (D // 2), D // 2)],
                    tail_sems.at[y],
                )
            )
    for copy in copies:
        copy.start()
    f1, f2, up, head = ROW_F1 - base, ROW_F2 - base, ROW_U - base, ROW_H - base
    gain2, offset2 = vec_ref[2:3, :], vec_ref[3:4, :]
    gain_f, offset_f = vec_ref[4:5, :], vec_ref[5:6, :]
    wide = 1024

    def norm_step(block, carry):
        at = rows_of(block)
        unit, _ = norm_parts(resid_ref[at, :])
        normed_ref[at, :] = (unit * gain2 + offset2).astype(BF16)
        return carry

    lax.fori_loop(0, blocks, norm_step, 0)
    for fetch in fetches:
        fetch.wait()
    for copy in copies:
        copy.wait()

    def hidden_step(index, carry):
        block, chunk = index // (FF // wide), index % (FF // wide)
        at = rows_of(block)
        lanes = rows_of(chunk, wide)
        hidden = nt(normed_ref[at, :], w_ref[pl.ds(pl.multiple_of(f1 + chunk * wide, 16), wide), :])
        act, slope = gelu_parts(hidden)
        act_ref[at, lanes] = act.astype(BF16)
        slope_ref[at, lanes] = slope
        return carry

    lax.fori_loop(0, blocks * (FF // wide), hidden_step, 0)

    def deep_step(block, carry):
        at = rows_of(block)
        deep_ref[at, :] = (resid_ref[at, :] + nn(act_ref[at, :], w_ref[f2 : f2 + FF, :])).astype(BF16)
        return carry

    lax.fori_loop(0, blocks, deep_step, 0)
    sums_ref[...] = jnp.zeros_like(sums_ref)

    def head_step(index, carry):
        j, block = index // blocks, index % blocks
        at = rows_of(block)
        there = rows_of(index)
        up_rows = pl.ds(pl.multiple_of(up + j * D, 16), D)
        columns = cols_ref[j, at, :]
        joined = nn(one_hot_rows(columns[:, 0:1]), e_ref[0:VOCAB, :]) + nt(deep_ref[at, :], w_ref[up_rows, :])
        unit, scale = norm_parts(joined)
        final = (unit * gain_f + offset_f).astype(BF16)
        final_ref[there, :] = final
        logits = nt(final, w_ref[head : head + VOCAB, :])
        nexts = columns[:, 2 * POOL : 2 * POOL + 1]
        lanes = lax.broadcasted_iota(jnp.int32, logits.shape, 1)
        target = jnp.where(lanes == nexts, 1.0, 0.0)
        valid = jnp.where(nexts >= 0, 1.0, 0.0)
        peak = jnp.max(logits, -1, keepdims=True)
        expo = jnp.exp(logits - peak)
        total = jnp.sum(expo, -1, keepdims=True)
        picked = jnp.sum(logits * target, -1, keepdims=True)
        losses = valid * (peak + jnp.log(total) - picked)
        dlogits = ((valid / count) * (expo * (1.0 / total) - target)).astype(BF16)
        dlog_ref[there, :] = dlogits
        dfinal = nn(dlogits, w_ref[head : head + VOCAB, :])
        djoined = norm_back(unit, scale, gain_f, dfinal)
        dup = djoined.astype(BF16)
        dup_ref[there, :] = dup
        low_ref[there, :] = (djoined - dup.astype(F32)).astype(BF16)
        back = nn(dup, w_ref[up_rows, :])

        @pl.when(j == 0)
        def _():
            ddeep_ref[at, :] = back

        @pl.when(j > 0)
        def _():
            ddeep_ref[at, :] += back

        sums_ref[4, :, :] += fold_rows(dfinal * unit)
        sums_ref[5, :, :] += fold_rows(dfinal)
        sums_ref[6, :, :] += jnp.broadcast_to(fold_rows(losses), (8, D))
        return carry

    lax.fori_loop(0, POOL * blocks, head_step, 0)

    out_up, out_head = ROW_U - ROW_HALF, ROW_H - ROW_HALF
    split_store(keep_ref, send_ref, core, pl.ds(out_head, VOCAB), tn(dlog_ref[...], final_ref[...]))
    for j in range(POOL):
        there = pl.ds(j * rows, rows)
        split_store(keep_ref, send_ref, core, pl.ds(out_up + j * D, D), tn(dup_ref[there, :], deep_ref[...]))
        hot = one_hot_cols(lines_ref[j : j + 1, :])
        part = nn(hot, dup_ref[there, :]) + nn(hot, low_ref[there, :])
        if j == 0:
            table_ref[...] = part
        else:
            table_ref[...] += part

    deep_ref[...] = ddeep_ref[...].astype(BF16)

    def dhid_step(index, carry):
        block, chunk = index // (FF // wide), index % (FF // wide)
        at = rows_of(block)
        lanes = rows_of(chunk, wide)
        dact = nt(deep_ref[at, :], w_ref[pl.ds(pl.multiple_of(f2 + chunk * wide, 16), wide), :])
        dhid_ref[at, lanes] = (dact * slope_ref[at, lanes]).astype(BF16)
        return carry

    lax.fori_loop(0, blocks * (FF // wide), dhid_step, 0)

    def dff_in(chunk, carry):
        here = rows_of(chunk, wide)
        split_store(keep_mid, send_mid, core, here, tn(dhid_ref[:, here], normed_ref[...]))
        lanes = pl.ds(pl.multiple_of(FF // 2 + chunk * wide, wide), wide)
        split_store(keep_ref, send_ref, core, here, tn(dhid_ref[:, lanes], normed_ref[...]))
        return carry

    lax.fori_loop(0, FF // wide // 2, dff_in, 0)

    def dff_out(chunk, carry):
        lanes = rows_of(chunk, wide)
        there = pl.ds(pl.multiple_of(FF // 2 + chunk * wide, wide), wide)
        split_store(keep_ref, send_ref, core, there, tn(act_ref[:, lanes], deep_ref[...]))
        return carry

    lax.fori_loop(0, FF // wide, dff_out, 0)

    def dnorm_step(block, carry):
        at = rows_of(block)
        dnormed = nn(dhid_ref[at, :], w_ref[f1 : f1 + FF, :])
        unit, scale = norm_parts(resid_ref[at, :])
        dresid_ref[at, :] = ddeep_ref[at, :] + norm_back(unit, scale, gain2, dnormed)
        sums_ref[2, :, :] += fold_rows(dnormed * unit)
        sums_ref[3, :, :] += fold_rows(dnormed)
        return carry

    lax.fori_loop(0, blocks, dnorm_step, 0)
    for k in range(8):
        small_ref[k : k + 1, :] = jnp.sum(sums_ref[k], 0, keepdims=True)


def shard_base(pieces, row):
    return row if pieces == 1 else row // SHARD * SHARD


def attend_back_kernel(short_len, slots, pieces, coords_ref, lay_ref, slope_ref, dresid_ref,
                       normed_ref, qkv_ref, lse_ref, mixed_ref, *refs):
    w_hbm, refs = refs[:pieces], refs[pieces:]
    (keep_ref, send_ref, dqkv_ref,
     w_ref, dist_ref, mask_ref, dbranch_ref, dmix_ref, sems) = refs
    rows = short_len * slots
    blocks = rows // BLOCK
    base = shard_base(pieces, ROW_O)
    core = coords_ref[2]
    fetch = Fetch(w_hbm, coords_ref, w_ref, sems, base, ROW_O, ROW_F1)
    fetch.start()
    out = ROW_O - base
    fetch.wait()

    def dmix_step(block, carry):
        at = rows_of(block)
        dbranch = dresid_ref[at, :].astype(BF16)
        dbranch_ref[at, :] = dbranch
        dmix_ref[at, :] = nt(dbranch, w_ref[out : out + D, :]).astype(BF16)
        return carry

    lax.fori_loop(0, blocks, dmix_step, 0)
    split_store(keep_ref, send_ref, core, pl.ds(3 * D, D), tn(mixed_ref[...], dbranch_ref[...]))

    left_lanes = lax.broadcasted_iota(jnp.int32, (short_len, 2 * HEAD), 1) < HEAD
    tile = short_len
    for slot in range(slots):
        at = pl.ds(slot * short_len, short_len)
        key = lax.broadcasted_iota(jnp.int32, (short_len, short_len), 0)
        query = lax.broadcasted_iota(jnp.int32, (short_len, short_len), 1)
        half = jnp.where(lay_ref[slot] == 1, short_len // 2, short_len)
        allowed = (key <= query) & ((key >= half) == (query >= half))
        dist_ref[...] = (key - query).astype(F32)
        mask_ref[...] = jnp.where(allowed, 0.0, NEGATIVE)

        def head_step(pair, carry):
            lanes = pl.ds(pl.multiple_of(pair * 2 * HEAD, 2 * HEAD), 2 * HEAD)
            lanes_k = pl.ds(pl.multiple_of(D + pair * 2 * HEAD, 2 * HEAD), 2 * HEAD)
            lanes_v = pl.ds(pl.multiple_of(2 * D + pair * 2 * HEAD, 2 * HEAD), 2 * HEAD)
            queries = qkv_ref[at, lanes]
            keys = qkv_ref[at, lanes_k]
            values = qkv_ref[at, lanes_v]
            dmix = dmix_ref[at, lanes]
            zero = jnp.zeros_like(values)

            def one_side(side, array):
                return jnp.where(left_lanes, array, zero) if side == 0 else jnp.where(left_lanes, zero, array)

            scaled = queries * jnp.asarray(0.125, BF16)
            dkeys = jnp.zeros((short_len, 2 * HEAD), F32)
            dvalues = jnp.zeros((short_len, 2 * HEAD), F32)
            side_k = [one_side(side, keys) for side in range(2)]
            side_v = [one_side(side, values) for side in range(2)]
            side_q = [one_side(side, queries) for side in range(2)]
            side_m = [one_side(side, dmix) for side in range(2)]
            for part in range(short_len // tile):
                low = part * tile
                dqueries = jnp.zeros((tile, 2 * HEAD), F32)
                for side in range(2):
                    head = pair * 2 + side
                    slope = slope_ref[head]
                    scores = nt(side_k[side], scaled[low : low + tile])
                    scores = scores + jnp.where(
                        mask_ref[:, low : low + tile] == 0.0, dist_ref[:, low : low + tile] * slope, NEGATIVE
                    )
                    probs = jnp.exp(scores - lse_ref[slot, head, :, low : low + tile])
                    dprobs = nt(side_v[side], dmix[low : low + tile])
                    delta = jnp.sum(dprobs * probs, 0, keepdims=True)
                    dscores = (probs * (dprobs - delta) * 0.125).astype(BF16)
                    dvalues = dvalues + nn(probs.astype(BF16), side_m[side][low : low + tile])
                    dkeys = dkeys + nn(dscores, side_q[side][low : low + tile])
                    dqueries = dqueries + tn(dscores, side_k[side])
                dqkv_ref[pl.ds(slot * short_len + low, tile), lanes] = dqueries.astype(BF16)
            dqkv_ref[at, lanes_k] = dkeys.astype(BF16)
            dqkv_ref[at, lanes_v] = dvalues.astype(BF16)
            return carry

        lax.fori_loop(0, HEADS // 2, head_step, 0, unroll=True)

    for part in range(3):
        grad = tn(dqkv_ref[:, part * D : (part + 1) * D], normed_ref[...])
        split_store(keep_ref, send_ref, core, pl.ds(part * D, D), grad)


def front_back_kernel(pieces, coords_ref, lines_ref, vec_ref, dresid_ref, shifted_ref, short_ref, dqkv_ref, table_ref,
                      deep_small_ref, *refs):
    w_hbm, refs = refs[:pieces], refs[pieces:]
    keep_ref, send_ref, small_ref, w_ref, dshort_ref, sums_ref, sems = refs
    rows = dresid_ref.shape[0]
    blocks = rows // BLOCK
    core = coords_ref[2]
    fetch = Fetch(w_hbm, coords_ref, w_ref, sems, 0, 0 if pieces > 1 else ROW_E, ROW_O)
    fetch.start()
    pool, proj = ROW_P, ROW_QKV
    sums_ref[...] = jnp.zeros_like(sums_ref)
    gain = vec_ref[0:1, :]
    fetch.wait()

    def dshort_step(block, carry):
        at = rows_of(block)
        dnormed = nn(dqkv_ref[at, :], w_ref[proj : proj + 3 * D, :])
        unit, scale = norm_parts(short_ref[at, :])
        dshort_ref[at, :] = (dresid_ref[at, :] + norm_back(unit, scale, gain, dnormed)).astype(BF16)
        sums_ref[0, :, :] += fold_rows(dnormed * unit)
        sums_ref[1, :, :] += fold_rows(dnormed)
        return carry

    lax.fori_loop(0, blocks, dshort_step, 0)
    table = table_ref[...]
    for j in range(POOL):
        cols = slice(j * D, (j + 1) * D)
        split_store(keep_ref, send_ref, core, pl.ds(ROW_P + j * D, D), tn(shifted_ref[:, cols], dshort_ref[...]))
        dshift = nt(dshort_ref[...], w_ref[pool + j * D : pool + (j + 1) * D, :])
        high = dshift.astype(BF16)
        low = (dshift - high.astype(F32)).astype(BF16)
        hot = one_hot_cols(lines_ref[POOL + j : POOL + j + 1, :])
        table = table + nn(hot, high) + nn(hot, low)
    split_store(keep_ref, send_ref, core, pl.ds(ROW_E, VOCAB), table)
    small_ref[...] = deep_small_ref[...]
    for k in range(2):
        small_ref[k : k + 1, :] = jnp.sum(sums_ref[k], 0, keepdims=True)
    half = D // 2
    for k in range(2):
        send_ref[ROW_QKV + 16 * k : ROW_QKV + 16 * (k + 1), :] = two_parts(small_ref[:, k * half : (k + 1) * half])


def two_parts(values):
    high = values.astype(BF16)
    low = (values - high.astype(F32)).astype(BF16)
    return jnp.concatenate([high.astype(F32), low.astype(F32)], 0).astype(BF16)


def one_value(parts):
    parts = parts.astype(F32)
    return parts[:8] + parts[8:]


def lay_out(coords_ref, keep_ref, recv_ref, p_refs, q_refs):
    dp, z = coords_ref[0], coords_ref[1]
    quarter = D // 4
    line = 2 * SHARD
    rest = line - SCATTER_CUT

    def total(column, x, zed, begin, size):
        at = pl.ds(pl.multiple_of(x * (4 * line) + zed * line + begin, 16), size)
        lanes = pl.ds(pl.multiple_of(column * quarter, quarter), quarter)
        return (keep_ref[at, lanes].astype(F32) + recv_ref[at, lanes].astype(F32)).astype(BF16)

    for k in range(4):
        there = dp ^ k
        for zed in range(4):
            p_refs[k][zed * SCATTER_CUT : (zed + 1) * SCATTER_CUT, :] = total(
                there // 2, there % 2, zed, 0, SCATTER_CUT
            )
        for line_to in range(4):
            q_refs[k][line_to * rest : (line_to + 1) * rest, :] = total(
                line_to // 2, line_to % 2, z ^ k, SCATTER_CUT, rest
            )


def core_sum_kernel(coords_ref, keep_ref, recv_ref, *out_refs):
    lay_out(coords_ref, keep_ref, recv_ref, out_refs[:4], out_refs[4:])


def core_sum_front_kernel(coords_ref, keep_front, keep_att, keep_mid, recv_front, recv_att, recv_mid, small_ref, *refs):
    out_refs, (keep_ref, recv_ref, sems) = refs[:8], refs[8:]
    copies = [
        pltpu.make_async_copy(source, target, sems.at[k])
        for k, (source, target) in enumerate((
            (keep_att, keep_ref.at[pl.ds(ROW_QKV, ROW_F1 - ROW_QKV)]),
            (recv_att, recv_ref.at[pl.ds(ROW_QKV, ROW_F1 - ROW_QKV)]),
            (keep_mid, keep_ref.at[pl.ds(ROW_F1, ROW_HALF - ROW_F1)]),
            (recv_mid, recv_ref.at[pl.ds(ROW_F1, ROW_HALF - ROW_F1)]),
            (keep_front, keep_ref.at[pl.ds(0, ROW_QKV)]),
            (recv_front.at[pl.ds(0, ROW_QKV)], recv_ref.at[pl.ds(0, ROW_QKV)]),
            (recv_front.at[pl.ds(ROW_QKV, 32)], recv_ref.at[pl.ds(ROW_HALF, 32)]),
        ))
    ]
    for copy in copies:
        copy.start()
    for copy in copies:
        copy.wait()
    lay_out(coords_ref, keep_ref, recv_ref, out_refs[:4], out_refs[4:])
    quarter = D // 4
    for k in range(2):
        both = small_ref[:, 2 * k * quarter : 2 * (k + 1) * quarter] + one_value(
            recv_ref[ROW_HALF + 16 * k : ROW_HALF + 16 * (k + 1), :]
        )
        for side in range(2):
            parts = two_parts(both[:, side * quarter : (side + 1) * quarter])
            row = 4 * SCATTER_CUT + 16 * (2 * k + side)
            for p_ref in out_refs[:4]:
                p_ref[row : row + 16, :] = parts


def sum_of(refs, row, size):
    at = pl.ds(pl.multiple_of(row, 16), size)
    return (refs[0][at, :].astype(F32) + refs[1][at, :].astype(F32)) + (
        refs[2][at, :].astype(F32) + refs[3][at, :].astype(F32)
    )


def first_sum_kernel(coords_ref, *refs):
    sources = ((refs[0:4], refs[4:8]), (refs[8:12], refs[12:16]))
    s_refs, t_refs = refs[16:20], refs[20:24]
    dp, z = coords_ref[0], coords_ref[1]
    rest = 2 * SHARD - SCATTER_CUT
    for half, (p_refs, q_refs) in enumerate(sources):
        for k in range(4):
            s_refs[k][half * SCATTER_CUT : (half + 1) * SCATTER_CUT, :] = sum_of(
                p_refs, (z ^ k) * SCATTER_CUT, SCATTER_CUT
            ).astype(BF16)
            t_refs[k][half * rest : (half + 1) * rest, :] = sum_of(q_refs, (dp ^ k) * rest, rest).astype(BF16)
    for k in range(4):
        row = 4 * SCATTER_CUT + 16 * k
        value = sum(one_value(ref[row : row + 16, :]) for ref in sources[0][0])
        parts = two_parts(value)
        for s_ref in s_refs:
            s_ref[2 * SCATTER_CUT + 16 * k : 2 * SCATTER_CUT + 16 * (k + 1), :] = parts


def last_sum_kernel(coords_ref, *refs):
    s_refs, t_refs, out_refs, (small_ref, square_ref, sum_ref) = refs[:4], refs[4:8], refs[8:12], refs[12:]
    y, core = coords_ref[0] // 2, coords_ref[2]
    rest = 2 * SHARD - SCATTER_CUT
    squares = jnp.zeros((8, D // 4), F32)
    for k in range(2):
        half = y ^ k
        first = sum_of(s_refs, half * SCATTER_CUT, SCATTER_CUT)
        second = sum_of(t_refs, half * rest, rest)
        squares = squares + fold_rows(first * first) + fold_rows(second * second)
        sum_ref[0:SCATTER_CUT, :] = first
        sum_ref[SCATTER_CUT:, :] = second
        for other in range(2):
            out_refs[2 * other + k][...] = sum_ref[pl.ds(pl.multiple_of((core ^ other) * SHARD, 8), SHARD), :]
    for k in range(4):
        row = 2 * SCATTER_CUT + 16 * k
        small_ref[:, k * (D // 4) : (k + 1) * (D // 4)] = sum(
            one_value(ref[row : row + 16, :]) for ref in s_refs
        )
    square_ref[...] = squares


def adam(param, first_m, second_m, grad, decay):
    first_new = BETA * first_m + (1.0 - BETA) * grad
    second_new = BETA * second_m + (1.0 - BETA) * grad * grad
    correct = 1.0 - BETA**STEP
    update = -RATE * (
        first_new / correct / (jnp.sqrt(second_new / correct) + EPS_ADAM) + decay * param
    )
    return (first_new, second_new, update)


def update_kernel(count, coords_ref, g0, g1, g2, g3, q0, q1, q2, q3, small_ref, w_ref, mw_ref, vw_ref, w_vec, m_vec, v_vec,
                  loss_ref, norm_ref, mw_out, vw_out, uw_out, m_out, v_out, u_out):
    y, core, mine = coords_ref[0] // 2, coords_ref[2], coords_ref[3]
    small = small_ref[...]
    line = lax.broadcasted_iota(jnp.int32, small.shape, 0)
    gradient = jnp.where(line < 6, small, 0.0)
    squares = (q0[...] + q1[...]) + (q2[...] + q3[...])

    def whole(values):
        return jnp.sum(jnp.sum(values, 0, keepdims=True), 1, keepdims=True)

    norm = jnp.sqrt(whole(squares) + whole(gradient * gradient))
    factor = CLIP / jnp.maximum(norm, CLIP)
    norm_ref[...] = norm
    loss_ref[...] = small[6:7, 0:1] / count
    quarter = D // 4
    for k, grad_ref in enumerate((g0, g1, g2, g3)):
        place = (core ^ (k // 2)) * 2 + (y ^ (k % 2))
        lanes = pl.ds(pl.multiple_of(place * quarter, quarter), quarter)
        mw_out[:, lanes], vw_out[:, lanes], uw_out[:, lanes] = adam(
            w_ref[:, lanes], mw_ref[:, lanes], vw_ref[:, lanes], grad_ref[...] * factor, DECAY
        )
    width = w_vec.shape[1]
    owned = pltpu.roll(gradient, lax.rem(small.shape[1] - mine * width, small.shape[1]), 1)[:6, :width]
    m_out[...], v_out[...], u_out[...] = adam(w_vec[...], m_vec[...], v_vec[...], owned * factor, 0.0)


VMEM = pl.BlockSpec(memory_space=pltpu.VMEM)
SMEM = pl.BlockSpec(memory_space=pltpu.SMEM)
ANY = pl.BlockSpec(memory_space=pl.ANY)
LIMIT = 58 * 1024 * 1024


def deep_base(pieces):
    return shard_base(pieces, ROW_F1)


def device_grads(pieces, tail, vecs, coords, ids, layouts, count, paired):
    slots = layouts.shape[0]
    rows = ids.shape[1]
    short_len = rows // slots
    slopes = np.float32(2.0) ** (-8.0 * (np.arange(HEADS, dtype=np.float32) + 1.0) / HEADS)
    shape = jax.ShapeDtypeStruct
    params = pltpu.CompilerParams(vmem_limit_bytes=LIMIT)
    number = len(pieces)
    whole_shards = number > 1
    front_rows = -(-ROW_F1 // SHARD) * SHARD if whole_shards else ROW_F1
    deep_rows = ROW_END - deep_base(number)
    table_rows = SHARD if whole_shards else VOCAB
    jobs = 64 if whole_shards else 1
    more = [] if vecs is None else [vecs]
    rest = [] if tail is None else [tail]
    half = D // 2
    shifted, short, normed, qkv, lse, mixed, resid, lines, cols, vecs = pl.pallas_call(
        partial(attend_kernel, short_len, slots, number),
        out_shape=(
            shape((rows, POOL * D), BF16),
            shape((rows, D), F32),
            shape((rows, D), BF16),
            shape((rows, 3 * D), BF16),
            shape((slots, HEADS, 1, short_len), F32),
            shape((rows, D), BF16),
            shape((rows, D), F32),
            shape((16, rows), jnp.int32),
            shape((POOL, rows, 128), jnp.int32),
            shape((8, D), F32),
        ),
        in_specs=[SMEM, SMEM, SMEM, VMEM] + [ANY] * number + [VMEM] * len(more),
        out_specs=(VMEM,) * 10,
        scratch_shapes=[
            pltpu.VMEM((front_rows, D), BF16),
            pltpu.VMEM((short_len, short_len), F32),
            pltpu.VMEM((short_len, short_len), F32),
            pltpu.VMEM((short_len, 2 * HEAD), F32),
            pltpu.VMEM((32, 16, D // 2), BF16),
            pltpu.SemaphoreType.DMA((jobs,)),
            pltpu.SemaphoreType.DMA((32,)),
        ],
        compiler_params=params,
        cost_estimate=pl.CostEstimate(flops=9_000_000_000, bytes_accessed=20_000_000, transcendentals=2_400_000),
        name="attend",
    )(coords, layouts, slopes, ids, *pieces, *more)
    keep_mid, send_mid, keep_deep, send_deep, table, dresid, small_deep = pl.pallas_call(
        partial(deep_kernel, count, number),
        out_shape=(
            shape((ROW_HALF - ROW_F1, half), BF16),
            shape((ROW_HALF - ROW_F1, half), BF16),
            shape((ROW_END - ROW_HALF, half), BF16),
            shape((ROW_END - ROW_HALF, half), BF16),
            shape((VOCAB, D), F32),
            shape((rows, D), F32),
            shape((8, D), F32),
        ),
        in_specs=[SMEM] + [VMEM] * 4 + [ANY] * (number + len(rest)),
        out_specs=(VMEM,) * 7,
        scratch_shapes=[
            pltpu.VMEM((deep_rows, D), BF16),
            pltpu.VMEM((table_rows, D), BF16),
            pltpu.VMEM((rows, D), BF16),
            pltpu.VMEM((rows, FF), BF16),
            pltpu.VMEM((rows, FF), F32),
            pltpu.VMEM((rows, D), BF16),
            pltpu.VMEM((POOL * rows, D), BF16),
            pltpu.VMEM((POOL * rows, VOCAB), BF16),
            pltpu.VMEM((POOL * rows, D), BF16),
            pltpu.VMEM((POOL * rows, D), BF16),
            pltpu.VMEM((rows, D), F32),
            pltpu.VMEM((rows, FF), BF16),
            pltpu.VMEM((8, 8, D), F32),
            pltpu.SemaphoreType.DMA((jobs,)),
            pltpu.SemaphoreType.DMA((jobs,)),
            pltpu.SemaphoreType.DMA((2,)),
        ],
        compiler_params=params,
        name="deep",
    )(coords, cols, lines, vecs, resid, *pieces, *rest)
    out_base = shard_base(number, ROW_O)
    keep_att, send_att, dqkv = pl.pallas_call(
        partial(attend_back_kernel, short_len, slots, number),
        out_shape=(
            shape((ROW_F1 - ROW_QKV, half), BF16),
            shape((ROW_F1 - ROW_QKV, half), BF16),
            shape((rows, 3 * D), BF16),
        ),
        in_specs=[SMEM, SMEM, SMEM] + [VMEM] * 5 + [ANY] * number,
        out_specs=(VMEM,) * 3,
        scratch_shapes=[
            pltpu.VMEM((front_rows - out_base, D), BF16),
            pltpu.VMEM((short_len, short_len), F32),
            pltpu.VMEM((short_len, short_len), F32),
            pltpu.VMEM((rows, D), BF16),
            pltpu.VMEM((rows, D), BF16),
            pltpu.SemaphoreType.DMA((jobs,)),
        ],
        compiler_params=params,
        cost_estimate=pl.CostEstimate(flops=11_000_000_000, bytes_accessed=20_000_000, transcendentals=2_400_000),
        name="attend_back",
    )(coords, layouts, slopes, dresid, normed, qkv, lse, mixed, *pieces)
    if paired:
        recv_deep, recv_mid = swap_with(send_deep, core=1), swap_with(send_mid, core=1)
        recv_deep, recv_mid = lax.optimization_barrier((recv_deep, recv_mid))
        sent = core_sum(coords, keep_deep, recv_deep)
        recv_att = swap_with(send_att, core=1)
        sent, recv_att, dqkv = lax.optimization_barrier((sent, recv_att, dqkv))
        sent = first_exchange(sent)
    keep_front, send_front, small = pl.pallas_call(
        partial(front_back_kernel, number),
        out_shape=(shape((ROW_QKV, half), BF16), shape((ROW_QKV + 32, half), BF16), shape((8, D), F32)),
        in_specs=[SMEM] + [VMEM] * 8 + [ANY] * number,
        out_specs=(VMEM,) * 3,
        scratch_shapes=[
            pltpu.VMEM((front_rows, D), BF16),
            pltpu.VMEM((rows, D), BF16),
            pltpu.VMEM((2, 8, D), F32),
            pltpu.SemaphoreType.DMA((jobs,)),
        ],
        compiler_params=params,
        cost_estimate=pl.CostEstimate(flops=8_000_000_000, bytes_accessed=20_000_000, transcendentals=0),
        name="front_back",
    )(coords, lines, vecs, dresid, shifted, short, dqkv, table, small_deep, *pieces)
    if not paired:
        front = jnp.concatenate([keep_front, send_front[:ROW_QKV]], 1)
        others = [
            jnp.concatenate(pair, 1)
            for pair in ((keep_att, send_att), (keep_mid, send_mid), (keep_deep, send_deep))
        ]
        return jnp.concatenate([front] + others, 0), small
    late = 5
    early = [array for k, array in enumerate(sent) if k != late]
    early, keep_front, send_front, small = lax.optimization_barrier((early, keep_front, send_front, small))
    sent = early[:late] + [sent[late]] + early[late:]
    received = [swap_with(send_front, core=1), recv_att, recv_mid]
    out_p, out_q = exchange_shapes(64)
    parts = pl.pallas_call(
        core_sum_front_kernel,
        out_shape=(out_p,) * 4 + (out_q,) * 4,
        in_specs=[SMEM] + [ANY] * 6 + [VMEM],
        out_specs=(VMEM,) * 8,
        scratch_shapes=[
            pltpu.VMEM((ROW_HALF, half), BF16),
            pltpu.VMEM((ROW_HALF + 32, half), BF16),
            pltpu.SemaphoreType.DMA((7,)),
        ],
        compiler_params=params,
        name="core_sum_front",
    )(coords, keep_front, keep_att, keep_mid, *received, small)
    return first_exchange(parts), sent


def exchange_shapes(extra):
    quarter = D // 4
    return (
        jax.ShapeDtypeStruct((4 * SCATTER_CUT + extra, quarter), BF16),
        jax.ShapeDtypeStruct((4 * (2 * SHARD - SCATTER_CUT), quarter), BF16),
    )


def core_sum(coords, keep, received):
    out_p, out_q = exchange_shapes(0)
    return pl.pallas_call(
        core_sum_kernel,
        out_shape=(out_p,) * 4 + (out_q,) * 4,
        in_specs=[SMEM] + [VMEM] * 2,
        out_specs=(VMEM,) * 8,
        compiler_params=pltpu.CompilerParams(vmem_limit_bytes=LIMIT),
        name="core_sum",
    )(coords, keep, received)


def first_exchange(parts):
    over = [parts[0]] + [swap_with(parts[k], line=k) for k in (1, 2, 3)]
    return over + [parts[4]] + [swap_with(parts[4 + k], zed=k) for k in (1, 2, 3)]


def swap_with(array, line=0, zed=0, core=0):
    lines, rest = lax.axis_size("dp"), lax.axis_size("fsdp")
    pairs = [
        (d * rest + f, (d ^ line) * rest + (f ^ (2 * zed + core)))
        for d in range(lines)
        for f in range(rest)
    ]
    return lax.ppermute(array, AXES, pairs)


def swap_halves(coords, shard):
    half = D // 2
    upper = coords[0] // 2 == 1
    left, right = shard[:, :half], shard[:, half:]
    keep, send = jnp.where(upper, right, left), jnp.where(upper, left, right)
    other = swap_with(send, line=2)
    return jnp.where(upper, other, keep), jnp.where(upper, keep, other)


def gather_pieces(block, vectors):
    half = D // 2
    width = vectors.shape[1]
    start = lax.axis_index(AXES) * width
    own = lax.dynamic_update_slice(
        jnp.zeros((16, half), BF16), vectors, (8 * (start // half), start % half)
    )
    first, second = jnp.concatenate([block[:GATHER_CUT], own], 0), block[GATHER_CUT:]
    along = jnp.concatenate([first] + [swap_with(first, zed=k) for k in (1, 2, 3)], 0)
    across = jnp.concatenate([second] + [swap_with(second, line=k) for k in (1, 2, 3)], 0)
    pieces = [along] + [swap_with(along, line=k) for k in (1, 2, 3)]
    pieces += [across] + [swap_with(across, zed=k) for k in (1, 2, 3)]
    return pieces + [swap_with(piece, core=1) for piece in pieces]


def scatter_sum(coords, front, deep):
    shape = jax.ShapeDtypeStruct
    params = pltpu.CompilerParams(vmem_limit_bytes=LIMIT)
    quarter = D // 4
    rest = 2 * SHARD - SCATTER_CUT
    parts = pl.pallas_call(
        first_sum_kernel,
        out_shape=(shape((2 * SCATTER_CUT + 64, quarter), BF16),) * 4 + (shape((2 * rest, quarter), BF16),) * 4,
        in_specs=[SMEM] + [VMEM] * 16,
        out_specs=(VMEM,) * 8,
        compiler_params=params,
        name="first_sum",
    )(coords, *front, *deep)
    second = [parts[0]] + [swap_with(parts[k], zed=k) for k in (1, 2, 3)]
    second += [parts[4]] + [swap_with(parts[4 + k], line=k) for k in (1, 2, 3)]
    *outs, small, squares = pl.pallas_call(
        last_sum_kernel,
        out_shape=(shape((SHARD, quarter), F32),) * 4 + (shape((8, D), F32), shape((8, quarter), F32)),
        in_specs=[SMEM] + [VMEM] * 8,
        out_specs=(VMEM,) * 6,
        scratch_shapes=[pltpu.VMEM((2 * SHARD, quarter), F32)],
        compiler_params=params,
        name="last_sum",
    )(coords, *second)
    squares = squares + swap_with(squares, core=1)
    quarters = [outs[0], swap_with(outs[1], line=2), swap_with(outs[2], core=1), swap_with(outs[3], line=2, core=1)]
    squares = (squares + swap_with(squares, line=1)) + (swap_with(squares, line=2) + swap_with(squares, line=3))
    squares = [squares] + [swap_with(squares, zed=k) for k in (1, 2, 3)]
    return quarters, small, squares


def shards(byte_ids, layouts, weights, vectors, m_weights, v_weights, m_vectors, v_vectors):
    devices = lax.axis_size(AXES)
    micro = byte_ids.shape[0]
    count = float(micro * layouts.shape[1] * devices * byte_ids.shape[2])
    lines, rest = lax.axis_size("dp"), lax.axis_size("fsdp")
    place = lax.axis_index("fsdp")
    coords = jnp.stack([lax.axis_index("dp"), place // 2, place % 2, lax.axis_index(AXES)]).astype(jnp.int32)
    paired = lines == 4 and rest == 8 and weights.shape[0] == SHARD
    weights_low = weights.astype(BF16)
    vectors_low = vectors.astype(BF16)
    width = vectors.shape[1]
    mine = lax.axis_index(AXES) * width
    flat_layouts = layouts.reshape(-1)
    ids = byte_ids.reshape(flat_layouts.shape[0], -1, POOL).transpose(2, 0, 1).reshape(POOL, -1)
    ids = jnp.pad(ids, ((0, 8 - POOL), (0, 0)))
    if paired:
        front, back = swap_halves(coords, weights_low)
        tail = lax.all_gather(back, AXES, axis=0, tiled=True)
        pieces = gather_pieces(front, vectors_low)
        front, deep = device_grads(
            pieces, tail, None, coords, ids, flat_layouts, count, True
        )
        quarters, small, squares = scatter_sum(coords, front, deep)
        like = [jax.ShapeDtypeStruct((1, 1), F32)] * 2
        like += [jax.ShapeDtypeStruct(weights.shape, F32)] * 3 + [jax.ShapeDtypeStruct(vectors.shape, F32)] * 3
        loss, grad_norm, *updated = pl.pallas_call(
            partial(update_kernel, count),
            out_shape=like,
            in_specs=[SMEM] + [VMEM] * 15,
            out_specs=[VMEM] * 8,
            compiler_params=pltpu.CompilerParams(vmem_limit_bytes=LIMIT),
            name="update",
        )(coords, *quarters, *squares, small, weights, m_weights, v_weights, vectors, m_vectors, v_vectors)
        return (loss[0, 0], grad_norm[0, 0], *updated)
    coords = coords * 0
    pieces = [lax.all_gather(weights_low, AXES, axis=0, tiled=True)]
    vecs = lax.all_gather(vectors_low, AXES, axis=1, tiled=True)
    vecs = jnp.pad(vecs.astype(F32), ((0, 2), (0, 0)))
    local, small = device_grads(pieces, None, vecs, coords, ids, flat_layouts, count, False)
    owned = lax.psum_scatter(local.astype(F32), AXES, scatter_dimension=0, tiled=True)
    small, squares = lax.psum((small, jnp.sum(owned * owned)), AXES)
    loss = small[6, 0] / count
    vec_grads = small[:6]
    owned_vecs = lax.dynamic_slice(vec_grads, (0, mine), (6, width))
    squares = squares + jnp.sum(vec_grads * vec_grads)
    grad_norm = jnp.sqrt(squares)
    factor = CLIP / jnp.maximum(grad_norm, CLIP)
    first_w, second_w, update_w = adam(weights, m_weights, v_weights, owned * factor, DECAY)
    first_v, second_v, update_v = adam(vectors, m_vectors, v_vectors, owned_vecs * factor, 0.0)
    return (loss, grad_norm, first_w, second_w, update_w, first_v, second_v, update_v)


def solution(mesh):
    in_specs = (
        P(None, AXES, None),
        P(None, AXES),
        P(AXES, None),
        P(None, AXES),
        P(AXES, None),
        P(AXES, None),
        P(None, AXES),
        P(None, AXES),
    )
    out_specs = (
        P(),
        P(),
        P(AXES, None),
        P(AXES, None),
        P(AXES, None),
        P(None, AXES),
        P(None, AXES),
        P(None, AXES),
    )
    return jax.shard_map(shards, mesh=mesh, in_specs=in_specs, out_specs=out_specs, check_vma=False)
```

```python
from functools import partial

import jax
import jax.numpy as jnp
from jax import lax
from jax.experimental import pallas as pl
from jax.experimental.pallas import tpu as pltpu
from jax.sharding import PartitionSpec as P

D = 512
HEADS = 8
HEAD = 64
FF = 2048
VOCAB = 256
POOL = 3

EPS_NORM = 1e-05
EPS_ADAM = 1e-08
CLIP = 0.2
RATE = 0.03
DECAY = 0.1
BETA = 0.5
STEP = 3
NEGATIVE = -1000000000.0

F32 = jnp.float32
BF16 = jnp.bfloat16

ROW_E = 0
ROW_P = VOCAB
ROW_QKV = ROW_P + POOL * D
ROW_O = ROW_QKV + 3 * D
ROW_F1 = ROW_O + D
ROW_F2 = ROW_F1 + FF
ROW_U = ROW_F2 + FF
ROW_H = ROW_U + POOL * D
ROW_END = ROW_H + VOCAB
ROW_HALF = ROW_END // 2
assert ROW_HALF - ROW_F1 == FF // 2

AXES = ("dp", "fsdp")
SHARD = ROW_END // 32
GATHER_CUT = 208
SCATTER_CUT = 400


def nn(left, right):
    return lax.dot_general(left, right, (((1,), (0,)), ((), ())), preferred_element_type=F32)


def nt(left, right):
    return lax.dot_general(left, right, (((1,), (1,)), ((), ())), preferred_element_type=F32)


def tn(left, right):
    return lax.dot_general(left, right, (((0,), (0,)), ((), ())), preferred_element_type=F32)


def norm_parts(values):
    center = values - jnp.mean(values, -1, keepdims=True)
    spread = jnp.mean(center * center, -1, keepdims=True)
    scale = lax.rsqrt(spread + EPS_NORM)
    return center * scale, scale


def norm_back(unit, scale, gain, grad):
    inner = grad * gain
    mean_inner = jnp.mean(inner, -1, keepdims=True)
    mean_cross = jnp.mean(inner * unit, -1, keepdims=True)
    return scale * (inner - mean_inner - unit * mean_cross)


def fold_rows(values):
    return jnp.sum(values.reshape(values.shape[0] // 8, 8, values.shape[1]), 0)


def one_hot_rows(ids):
    lanes = lax.broadcasted_iota(jnp.int32, (ids.shape[0], VOCAB), 1)
    return jnp.where(lanes == ids, 1.0, 0.0).astype(BF16)


def one_hot_cols(ids):
    lines = lax.broadcasted_iota(jnp.int32, (VOCAB, ids.shape[1]), 0)
    return jnp.where(lines == ids, 1.0, 0.0).astype(BF16)


def rows_of(index, size):
    return pl.ds(pl.multiple_of(index * size, size), size)


def gathered_parts(coords_ref):
    dp, z, core = coords_ref[0], coords_ref[1], coords_ref[2]
    for side in range(2):
        for k in range(4):
            for part in range(4):
                for kind in range(2):
                    d, e = (k, part) if kind == 0 else (part, k)
                    line = dp ^ d
                    yield side * 8 + kind * 4 + k, part, kind, line // 2, (line % 2) * 8 + (z ^ e) * 2 + (core ^ side)


def fetch_gathered(pieces, coords_ref, w_ref, sems):
    half = D // 2
    copies = []
    for number, (piece, part, kind, y, shard) in enumerate(gathered_parts(coords_ref)):
        begin, size, step = ((0, GATHER_CUT, GATHER_CUT + 16), (GATHER_CUT, SHARD - GATHER_CUT, SHARD - GATHER_CUT))[kind]
        copy = pltpu.make_async_copy(
            pieces[piece].at[pl.ds(part * step, size)],
            w_ref.at[pl.ds(pl.multiple_of(shard * SHARD + begin, 16), size), pl.ds(pl.multiple_of(y * half, half), half)],
            sems.at[number],
        )
        copy.start()
        copies.append(copy)
    return copies


def fetch_rows(w_hbm, low, high, w_ref, sem):
    copy = pltpu.make_async_copy(w_hbm.at[pl.ds(low, high - low)], w_ref, sem)
    copy.start()
    return copy


def attend_kernel(short_len, slots, pieces, coords_ref, lay_ref, ids_ref, *refs):
    w_hbm, refs = refs[:pieces], refs[pieces:]
    if pieces == 1:
        vec_in_ref, refs = refs[0], refs[1:]
    if pieces > 1:
        w_out, refs = refs[0], refs[1:]
    (shifted_ref, short_ref, normed_ref, qkv_ref, lse_ref, mixed_ref, resid_ref, lines_ref, cols_ref, vec_ref,
     w_ref, dist_ref, mask_ref, part_ref, sems, part_sems) = refs
    rows = short_len * slots
    if pieces > 1:
        fetch = fetch_gathered(w_hbm, coords_ref, w_ref, sems)
    else:
        fetch = [fetch_rows(w_hbm[0], 0, ROW_HALF, w_ref, sems.at[0])]
    copies = []
    if pieces > 1:
        for piece, part, kind, _, _ in gathered_parts(coords_ref):
            if kind == 0:
                place = pl.ds(part * (GATHER_CUT + 16) + GATHER_CUT, 16)
                number = len(copies)
                copies.append(
                    pltpu.make_async_copy(w_hbm[piece].at[place], part_ref.at[number], part_sems.at[number])
                )
        for copy in copies:
            copy.start()

    ids = ids_ref[...]
    group = lax.broadcasted_iota(jnp.int32, (1, rows), 1)
    starts = group == 0
    for slot in range(slots):
        starts = starts | (group == slot * short_len)
        starts = starts | ((group == slot * short_len + short_len // 2) & (lay_ref[slot] == 1))
    ends = group == rows - 1
    for slot in range(slots):
        ends = ends | (group == (slot + 1) * short_len - 1)
        ends = ends | ((group == slot * short_len + short_len // 2 - 1) & (lay_ref[slot] == 1))
    before, after = pltpu.roll(ids, 1, 1), pltpu.roll(ids, rows - 1, 1)
    own = [ids[j : j + 1] for j in range(POOL)]
    back = [jnp.where(starts, -1, before[1:2]), jnp.where(starts, -1, before[2:3]), ids[0:1]]
    ahead = [ids[1:2], ids[2:3], jnp.where(ends, -1, after[0:1])]
    for j in range(POOL):
        for kind, line in enumerate((own[j], back[j], ahead[j])):
            lines_ref[j, kind : kind + 1, :] = line
        lines_ref[j, 3:, :] = jnp.zeros((5, rows), jnp.int32)
        padded = jnp.concatenate([lines_ref[j].astype(F32), jnp.zeros((120, rows), F32)], 0)
        cols_ref[j] = padded.T.astype(jnp.int32)

    for copy in copies:
        copy.wait()
    if pieces > 1:
        both = part_ref[0].astype(F32)
        for k in range(1, len(copies)):
            both = both + part_ref[k].astype(F32)
        vec_ref[...] = jnp.concatenate([both[:8], both[8:]], 1)
    else:
        vec_ref[...] = vec_in_ref[...]
    for copy in fetch:
        copy.wait()
    if pieces > 1:
        leave = pltpu.make_async_copy(w_ref, w_out, part_sems.at[len(copies)])
        leave.start()
    gain, offset = vec_ref[0:1, :], vec_ref[1:2, :]

    def shift_step(j, carry):
        lanes = rows_of(j, D)
        hot = one_hot_rows(cols_ref[j, :, 1:2])
        shifted_ref[:, lanes] = nn(hot, w_ref[ROW_E:ROW_P, :]).astype(BF16)
        return carry

    lax.fori_loop(0, POOL, shift_step, 0)
    short = nn(shifted_ref[...], w_ref[ROW_P:ROW_QKV, :])
    short_ref[...] = short
    unit, _ = norm_parts(short)
    normed_ref[...] = (unit * gain + offset).astype(BF16)
    qkv_ref[...] = nt(normed_ref[...], w_ref[ROW_QKV:ROW_O, :]).astype(BF16)

    left_lanes = lax.broadcasted_iota(jnp.int32, (short_len, 2 * HEAD), 1) < HEAD

    def slot_step(slot, carry):
        at = rows_of(slot, short_len)
        attention_bias(lay_ref[slot], short_len, dist_ref, mask_ref)
        for pair in range(HEADS // 2):
            lanes = slice(pair * 2 * HEAD, (pair + 1) * 2 * HEAD)
            queries = qkv_ref[at, lanes] * jnp.asarray(0.125, BF16)
            keys = qkv_ref[at, D + pair * 2 * HEAD : D + (pair + 1) * 2 * HEAD]
            values = qkv_ref[at, 2 * D + pair * 2 * HEAD : 2 * D + (pair + 1) * 2 * HEAD]
            mixed = jnp.zeros((short_len, 2 * HEAD), F32)
            for side in range(2):
                head = pair * 2 + side
                scores = nt(one_side(left_lanes, side, keys), queries)
                scores = scores + jnp.minimum(dist_ref[...] * head_slope(head), mask_ref[...])
                top = jnp.max(scores, 0, keepdims=True)
                expo = jnp.exp(scores - top)
                total = jnp.sum(expo, 0, keepdims=True)
                lse_ref[slot, head] = top + jnp.log(total)
                probs = (expo * (1.0 / total)).astype(BF16)
                mixed = mixed + tn(probs, one_side(left_lanes, side, values))
            mixed_ref[at, lanes] = mixed.astype(BF16)
        return carry

    lax.fori_loop(0, slots, slot_step, 0)
    resid_ref[...] = short_ref[...] + nn(mixed_ref[...], w_ref[ROW_O:ROW_F1, :])
    if pieces > 1:
        leave.wait()


def head_slope(head):
    return 2.0 ** (-8.0 * (head + 1.0) / HEADS)


def one_side(left_lanes, side, array):
    zero = jnp.zeros_like(array)
    return jnp.where(left_lanes, array, zero) if side == 0 else jnp.where(left_lanes, zero, array)


def attention_bias(layout, short_len, dist_ref, mask_ref):
    key = lax.broadcasted_iota(jnp.int32, (short_len, short_len), 0)
    query = lax.broadcasted_iota(jnp.int32, (short_len, short_len), 1)
    half = jnp.where(layout == 1, short_len // 2, short_len)
    allowed = (key <= query) & ((key >= half) == (query >= half))
    dist_ref[...] = (key - query).astype(F32)
    mask_ref[...] = jnp.where(allowed, 0.0, NEGATIVE)


def gelu_parts(hidden):
    size = jnp.abs(hidden)
    near = 1.0 / (1.0 + (0.3275911 * 0.7071067811865476) * size)
    bell = jnp.exp(hidden * hidden * -0.5)
    tail = near * (0.127414796 + near * (-0.142248368 + near * (0.7107068705 + near * (-0.7265760135 + near * 0.5307027145))))
    tail = tail * bell
    cdf = jnp.where(hidden >= 0.0, 1.0 - tail, tail)
    return hidden * cdf, cdf + hidden * bell * 0.3989422804014327


def split_store(keep_ref, send_ref, core, rows, values):
    half = D // 2
    low, high = values[:, :half].astype(BF16), values[:, half:].astype(BF16)
    keep_ref[rows, :] = jnp.where(core == 0, low, high)
    send_ref[rows, :] = jnp.where(core == 0, high, low)


def deep_kernel(count, split, coords_ref, vec_ref, cols_ref, lines_ref, resid_ref, w_hbm, *refs):
    if split:
        tail_hbm, refs = refs[0], refs[1:]
    (keep_mid, send_mid, keep_ref, send_ref, table_ref, dresid_ref, small_ref,
     w_ref, e_ref, normed_ref, act_ref, slope_ref, deep_ref, final_ref, dlog_ref, dup_ref,
     ddeep_ref, dhid_ref, sums_ref, sems) = refs
    rows = resid_ref.shape[0]
    base = ROW_F1
    core = coords_ref[2]
    first = [fetch_rows(w_hbm, ROW_F1, ROW_HALF, w_ref.at[pl.ds(0, ROW_HALF - base)], sems.at[0])]
    stages = [first, [], []]
    half = D // 2
    for k, (low, high) in enumerate(((ROW_HALF, ROW_F2), (ROW_F2, ROW_U), (ROW_U, ROW_END))):
        here = pl.ds(low - base, high - low)
        if split:
            for y in range(2):
                start = y * ROW_HALF + low - ROW_HALF
                target = w_ref.at[here, pl.ds(y * half, half)]
                stages[k].append(fetch_rows(tail_hbm, start, start + high - low, target, sems.at[1 + 2 * k + y]))
        else:
            stages[k].append(fetch_rows(w_hbm, low, high, w_ref.at[here], sems.at[1 + 2 * k]))
    stages[2].append(fetch_rows(w_hbm, 0, VOCAB, e_ref, sems.at[7]))
    f1, f2, up, head = ROW_F1 - base, ROW_F2 - base, ROW_U - base, ROW_H - base
    gain2, offset2 = vec_ref[2:3, :], vec_ref[3:4, :]
    gain_f, offset_f = vec_ref[4:5, :], vec_ref[5:6, :]
    wide = 1024
    sums_ref[...] = jnp.zeros_like(sums_ref)

    unit, _ = norm_parts(resid_ref[...])
    normed_ref[...] = (unit * gain2 + offset2).astype(BF16)
    for copy in stages[0]:
        copy.wait()

    def hidden_step(chunk, carry):
        lanes = rows_of(chunk, wide)
        hidden = nt(normed_ref[...], w_ref[pl.ds(pl.multiple_of(f1 + chunk * wide, 16), wide), :])
        act, slope = gelu_parts(hidden)
        act_ref[:, lanes] = act.astype(BF16)
        slope_ref[:, lanes] = slope
        return carry

    lax.fori_loop(0, FF // wide, hidden_step, 0)
    for copy in stages[1]:
        copy.wait()
    deep_ref[...] = (resid_ref[...] + nn(act_ref[...], w_ref[f2 : f2 + FF, :])).astype(BF16)
    for copy in stages[2]:
        copy.wait()
    ddeep_ref[...] = jnp.zeros_like(ddeep_ref)
    table_ref[...] = jnp.zeros_like(table_ref)

    def head_step(j, carry):
        there = rows_of(j, rows)
        up_rows = pl.ds(pl.multiple_of(up + j * D, 16), D)
        columns = cols_ref[j]
        joined = nn(one_hot_rows(columns[:, 0:1]), e_ref[0:VOCAB, :]) + nt(deep_ref[...], w_ref[up_rows, :])
        unit, scale = norm_parts(joined)
        final = (unit * gain_f + offset_f).astype(BF16)
        final_ref[there, :] = final
        logits = nt(final, w_ref[head : head + VOCAB, :])
        nexts = columns[:, 2:3]
        lanes = lax.broadcasted_iota(jnp.int32, logits.shape, 1)
        target = jnp.where(lanes == nexts, 1.0, 0.0)
        valid = jnp.where(nexts >= 0, 1.0, 0.0)
        peak = jnp.max(logits, -1, keepdims=True)
        expo = jnp.exp(logits - peak)
        total = jnp.sum(expo, -1, keepdims=True)
        picked = jnp.sum(logits * target, -1, keepdims=True)
        losses = valid * (peak + jnp.log(total) - picked)
        dlogits = ((valid / count) * (expo * (1.0 / total) - target)).astype(BF16)
        dlog_ref[there, :] = dlogits
        dfinal = nn(dlogits, w_ref[head : head + VOCAB, :])
        dup = norm_back(unit, scale, gain_f, dfinal).astype(BF16)
        dup_ref[there, :] = dup
        ddeep_ref[...] += nn(dup, w_ref[up_rows, :])
        sums_ref[4, :, :] += fold_rows(dfinal * unit)
        sums_ref[5, :, :] += fold_rows(dfinal)
        sums_ref[6, :, :] += jnp.broadcast_to(fold_rows(losses), (8, D))
        return carry

    lax.fori_loop(0, POOL, head_step, 0)

    out_f2, out_up, out_head = ROW_F2 - ROW_HALF, ROW_U - ROW_HALF, ROW_H - ROW_HALF
    split_store(keep_ref, send_ref, core, pl.ds(out_head, VOCAB), tn(dlog_ref[...], final_ref[...]))

    def dup_step(j, carry):
        there = rows_of(j, rows)
        dup = dup_ref[there, :]
        out = pl.ds(pl.multiple_of(out_up + j * D, D), D)
        split_store(keep_ref, send_ref, core, out, tn(dup, deep_ref[...]))
        table_ref[...] += nn(one_hot_cols(lines_ref[j, 0:1, :]), dup)
        return carry

    lax.fori_loop(0, POOL, dup_step, 0)

    deep_ref[...] = ddeep_ref[...].astype(BF16)

    def dff_step(chunk, carry):
        lanes = rows_of(chunk, wide)
        dact = nt(deep_ref[...], w_ref[pl.ds(pl.multiple_of(f2 + chunk * wide, 16), wide), :])
        dhid_ref[:, lanes] = (dact * slope_ref[:, lanes]).astype(BF16)
        grad = tn(dhid_ref[:, lanes], normed_ref[...])

        @pl.when(chunk == 0)
        def _():
            split_store(keep_mid, send_mid, core, slice(0, wide), grad)

        @pl.when(chunk > 0)
        def _():
            split_store(keep_ref, send_ref, core, slice(0, wide), grad)

        out = pl.ds(pl.multiple_of(out_f2 + chunk * wide, wide), wide)
        split_store(keep_ref, send_ref, core, out, tn(act_ref[:, lanes], deep_ref[...]))
        return carry

    lax.fori_loop(0, FF // wide, dff_step, 0)
    dnormed = nn(dhid_ref[...], w_ref[f1 : f1 + FF, :])
    unit, scale = norm_parts(resid_ref[...])
    dresid_ref[...] = ddeep_ref[...] + norm_back(unit, scale, gain2, dnormed)
    sums_ref[2, :, :] = fold_rows(dnormed * unit)
    sums_ref[3, :, :] = fold_rows(dnormed)
    for k in range(8):
        small_ref[k : k + 1, :] = jnp.sum(sums_ref[k], 0, keepdims=True)


def attend_back_kernel(short_len, coords_ref, lay_ref, dresid_ref, normed_ref, qkv_ref, lse_ref, mixed_ref,
                       w_hbm, *refs):
    (keep_ref, send_ref, dqkv_ref,
     w_ref, dist_ref, mask_ref, dbranch_ref, dmix_ref, sem) = refs
    core = coords_ref[2]
    fetch = fetch_rows(w_hbm, ROW_O, ROW_F1, w_ref, sem)
    dbranch_ref[...] = dresid_ref[...].astype(BF16)
    fetch.wait()
    dmix_ref[...] = nt(dbranch_ref[...], w_ref[...]).astype(BF16)

    left_lanes = lax.broadcasted_iota(jnp.int32, (short_len, 2 * HEAD), 1) < HEAD

    def slot_step(slot, carry):
        at = rows_of(slot, short_len)
        attention_bias(lay_ref[slot], short_len, dist_ref, mask_ref)
        for pair in range(HEADS // 2):
            lanes = slice(pair * 2 * HEAD, (pair + 1) * 2 * HEAD)
            lanes_k = slice(D + pair * 2 * HEAD, D + (pair + 1) * 2 * HEAD)
            lanes_v = slice(2 * D + pair * 2 * HEAD, 2 * D + (pair + 1) * 2 * HEAD)
            queries, keys, values = qkv_ref[at, lanes], qkv_ref[at, lanes_k], qkv_ref[at, lanes_v]
            dmix = dmix_ref[at, lanes]
            scaled = queries * jnp.asarray(0.125, BF16)
            dqueries, dkeys, dvalues = (jnp.zeros((short_len, 2 * HEAD), F32) for _ in range(3))
            for side in range(2):
                head = pair * 2 + side
                keys_here = one_side(left_lanes, side, keys)
                scores = nt(keys_here, scaled)
                scores = scores + jnp.minimum(dist_ref[...] * head_slope(head), mask_ref[...])
                probs = jnp.exp(scores - lse_ref[slot, head])
                dprobs = nt(one_side(left_lanes, side, values), dmix)
                delta = jnp.sum(dprobs * probs, 0, keepdims=True)
                dscores = (probs * (dprobs - delta) * 0.125).astype(BF16)
                dvalues = dvalues + nn(probs.astype(BF16), one_side(left_lanes, side, dmix))
                dkeys = dkeys + nn(dscores, one_side(left_lanes, side, queries))
                dqueries = dqueries + tn(dscores, keys_here)
            dqkv_ref[at, lanes] = dqueries.astype(BF16)
            dqkv_ref[at, lanes_k] = dkeys.astype(BF16)
            dqkv_ref[at, lanes_v] = dvalues.astype(BF16)
        return carry

    lax.fori_loop(0, lse_ref.shape[0], slot_step, 0)
    split_store(keep_ref, send_ref, core, pl.ds(3 * D, D), tn(mixed_ref[...], dbranch_ref[...]))

    def dproj_step(part, carry):
        grad = tn(dqkv_ref[:, rows_of(part, D)], normed_ref[...])
        split_store(keep_ref, send_ref, core, rows_of(part, D), grad)
        return carry

    lax.fori_loop(0, 3, dproj_step, 0)


def front_back_kernel(coords_ref, vec_ref, deep_small_ref, lines_ref, dresid_ref, shifted_ref, short_ref, dqkv_ref,
                      table_in, w_hbm, keep_ref, send_ref, small_ref, table_ref, w_ref, dshort_ref, sem):
    core = coords_ref[2]
    fetch = fetch_rows(w_hbm, ROW_P, ROW_O, w_ref, sem)
    gain = vec_ref[0:1, :]
    fetch.wait()
    dnormed = nn(dqkv_ref[...], w_ref[ROW_QKV - ROW_P :, :])
    unit, scale = norm_parts(short_ref[...])
    dshort_ref[...] = (dresid_ref[...] + norm_back(unit, scale, gain, dnormed)).astype(BF16)
    small_ref[...] = deep_small_ref[...]
    for k, values in enumerate((dnormed * unit, dnormed)):
        small_ref[k : k + 1, :] = jnp.sum(fold_rows(values), 0, keepdims=True)
    half = D // 2
    for k in range(2):
        send_ref[ROW_QKV + 16 * k : ROW_QKV + 16 * (k + 1), :] = two_parts(small_ref[:, k * half : (k + 1) * half])
    table_ref[...] = table_in[...]

    def pool_step(j, carry):
        dshift = nt(dshort_ref[...], w_ref[rows_of(j, D), :]).astype(BF16)
        table_ref[...] += nn(one_hot_cols(lines_ref[j, 1:2, :]), dshift)
        out = pl.ds(pl.multiple_of(ROW_P + j * D, 16), D)
        split_store(keep_ref, send_ref, core, out, tn(shifted_ref[:, rows_of(j, D)], dshort_ref[...]))
        return carry

    lax.fori_loop(0, POOL, pool_step, 0)
    split_store(keep_ref, send_ref, core, pl.ds(ROW_E, VOCAB), table_ref[...])


def two_parts(values):
    high = values.astype(BF16)
    low = (values - high.astype(F32)).astype(BF16)
    return jnp.concatenate([high.astype(F32), low.astype(F32)], 0).astype(BF16)


def one_value(parts):
    parts = parts.astype(F32)
    return parts[:8] + parts[8:]


def lay_out(coords_ref, keep_ref, recv_ref, p_refs, q_refs):
    dp, z = coords_ref[0], coords_ref[1]
    quarter = D // 4
    line = 2 * SHARD
    rest = line - SCATTER_CUT

    def total(column, x, zed, begin, size):
        at = pl.ds(pl.multiple_of(x * (4 * line) + zed * line + begin, 16), size)
        lanes = pl.ds(pl.multiple_of(column * quarter, quarter), quarter)
        return (keep_ref[at, lanes].astype(F32) + recv_ref[at, lanes].astype(F32)).astype(BF16)

    for k in range(4):
        there = dp ^ k
        for zed in range(4):
            p_refs[k][zed * SCATTER_CUT : (zed + 1) * SCATTER_CUT, :] = total(
                there // 2, there % 2, zed, 0, SCATTER_CUT
            )
        for line_to in range(4):
            q_refs[k][line_to * rest : (line_to + 1) * rest, :] = total(
                line_to // 2, line_to % 2, z ^ k, SCATTER_CUT, rest
            )


def core_sum_kernel(coords_ref, keep_ref, recv_ref, *out_refs):
    lay_out(coords_ref, keep_ref, recv_ref, out_refs[:4], out_refs[4:])


def core_sum_front_kernel(coords_ref, keep_front, keep_att, keep_mid, recv_front, recv_att, recv_mid, small_ref, *refs):
    out_refs, (keep_ref, recv_ref, sems) = refs[:8], refs[8:]
    copies = [
        pltpu.make_async_copy(source, target, sems.at[k])
        for k, (source, target) in enumerate((
            (keep_att, keep_ref.at[pl.ds(ROW_QKV, ROW_F1 - ROW_QKV)]),
            (recv_att, recv_ref.at[pl.ds(ROW_QKV, ROW_F1 - ROW_QKV)]),
            (keep_mid, keep_ref.at[pl.ds(ROW_F1, ROW_HALF - ROW_F1)]),
            (recv_mid, recv_ref.at[pl.ds(ROW_F1, ROW_HALF - ROW_F1)]),
            (keep_front, keep_ref.at[pl.ds(0, ROW_QKV)]),
            (recv_front.at[pl.ds(0, ROW_QKV)], recv_ref.at[pl.ds(0, ROW_QKV)]),
            (recv_front.at[pl.ds(ROW_QKV, 32)], recv_ref.at[pl.ds(ROW_HALF, 32)]),
        ))
    ]
    for copy in copies:
        copy.start()
    for copy in copies:
        copy.wait()
    lay_out(coords_ref, keep_ref, recv_ref, out_refs[:4], out_refs[4:])
    quarter = D // 4
    for k in range(2):
        both = small_ref[:, 2 * k * quarter : 2 * (k + 1) * quarter] + one_value(
            recv_ref[ROW_HALF + 16 * k : ROW_HALF + 16 * (k + 1), :]
        )
        for side in range(2):
            parts = two_parts(both[:, side * quarter : (side + 1) * quarter])
            row = 4 * SCATTER_CUT + 16 * (2 * k + side)
            for p_ref in out_refs[:4]:
                p_ref[row : row + 16, :] = parts


def sum_of(refs, row, size):
    at = pl.ds(pl.multiple_of(row, 16), size)
    return (refs[0][at, :].astype(F32) + refs[1][at, :].astype(F32)) + (
        refs[2][at, :].astype(F32) + refs[3][at, :].astype(F32)
    )


def first_sum_kernel(coords_ref, *refs):
    sources = ((refs[0:4], refs[4:8]), (refs[8:12], refs[12:16]))
    s_refs, t_refs = refs[16:20], refs[20:24]
    dp, z = coords_ref[0], coords_ref[1]
    rest = 2 * SHARD - SCATTER_CUT
    for half, (p_refs, q_refs) in enumerate(sources):
        for k in range(4):
            s_refs[k][half * SCATTER_CUT : (half + 1) * SCATTER_CUT, :] = sum_of(
                p_refs, (z ^ k) * SCATTER_CUT, SCATTER_CUT
            ).astype(BF16)
            t_refs[k][half * rest : (half + 1) * rest, :] = sum_of(q_refs, (dp ^ k) * rest, rest).astype(BF16)
    for k in range(4):
        row = 4 * SCATTER_CUT + 16 * k
        value = sum(one_value(ref[row : row + 16, :]) for ref in sources[0][0])
        parts = two_parts(value)
        for s_ref in s_refs:
            s_ref[2 * SCATTER_CUT + 16 * k : 2 * SCATTER_CUT + 16 * (k + 1), :] = parts


def last_sum_kernel(coords_ref, *refs):
    s_refs, t_refs, out_refs, (small_ref, square_ref, sum_ref) = refs[:4], refs[4:8], refs[8:12], refs[12:]
    y, core = coords_ref[0] // 2, coords_ref[2]
    rest = 2 * SHARD - SCATTER_CUT
    squares = jnp.zeros((8, D // 4), F32)
    for k in range(2):
        half = y ^ k
        first = sum_of(s_refs, half * SCATTER_CUT, SCATTER_CUT)
        second = sum_of(t_refs, half * rest, rest)
        squares = squares + fold_rows(first * first) + fold_rows(second * second)
        sum_ref[0:SCATTER_CUT, :] = first
        sum_ref[SCATTER_CUT:, :] = second
        for other in range(2):
            out_refs[2 * other + k][...] = sum_ref[pl.ds(pl.multiple_of((core ^ other) * SHARD, 8), SHARD), :]
    for k in range(4):
        row = 2 * SCATTER_CUT + 16 * k
        small_ref[:, k * (D // 4) : (k + 1) * (D // 4)] = sum(
            one_value(ref[row : row + 16, :]) for ref in s_refs
        )
    square_ref[...] = squares


def adam(param, first_m, second_m, grad, decay):
    first_new = BETA * first_m + (1.0 - BETA) * grad
    second_new = BETA * second_m + (1.0 - BETA) * grad * grad
    correct = 1.0 - BETA**STEP
    update = -RATE * (
        first_new / correct / (jnp.sqrt(second_new / correct) + EPS_ADAM) + decay * param
    )
    return (first_new, second_new, update)


def update_kernel(count, coords_ref, g0, g1, g2, g3, q0, q1, q2, q3, small_ref, w_ref, mw_ref, vw_ref, w_vec, m_vec, v_vec,
                  loss_ref, norm_ref, mw_out, vw_out, uw_out, m_out, v_out, u_out):
    y, core, mine = coords_ref[0] // 2, coords_ref[2], coords_ref[3]
    small = small_ref[...]
    line = lax.broadcasted_iota(jnp.int32, small.shape, 0)
    gradient = jnp.where(line < 6, small, 0.0)
    squares = (q0[...] + q1[...]) + (q2[...] + q3[...])

    def whole(values):
        return jnp.sum(jnp.sum(values, 0, keepdims=True), 1, keepdims=True)

    norm = jnp.sqrt(whole(squares) + whole(gradient * gradient))
    factor = CLIP / jnp.maximum(norm, CLIP)
    norm_ref[...] = norm
    loss_ref[...] = small[6:7, 0:1] / count
    quarter = D // 4
    for k, grad_ref in enumerate((g0, g1, g2, g3)):
        place = (core ^ (k // 2)) * 2 + (y ^ (k % 2))
        lanes = pl.ds(pl.multiple_of(place * quarter, quarter), quarter)
        mw_out[:, lanes], vw_out[:, lanes], uw_out[:, lanes] = adam(
            w_ref[:, lanes], mw_ref[:, lanes], vw_ref[:, lanes], grad_ref[...] * factor, DECAY
        )
    width = w_vec.shape[1]
    owned = pltpu.roll(gradient, lax.rem(small.shape[1] - mine * width, small.shape[1]), 1)[:6, :width]
    m_out[...], v_out[...], u_out[...] = adam(w_vec[...], m_vec[...], v_vec[...], owned * factor, 0.0)


VMEM = pl.BlockSpec(memory_space=pltpu.VMEM)
SMEM = pl.BlockSpec(memory_space=pltpu.SMEM)
ANY = pl.BlockSpec(memory_space=pl.ANY)
MIB = 1024 * 1024
LIMIT = 24 * MIB
LIMIT_ATTEND = 24 * MIB
LIMIT_DEEP = 40 * MIB
LIMIT_BACK = 24 * MIB


def device_grads(pieces, tail, vecs, coords, ids, layouts, count, paired):
    slots = layouts.shape[0]
    rows = ids.shape[1]
    short_len = rows // slots
    shape = jax.ShapeDtypeStruct
    params = pltpu.CompilerParams(vmem_limit_bytes=LIMIT)
    number = len(pieces)
    pieces = [pltpu.with_memory_space_constraint(piece, pltpu.HBM) for piece in pieces]
    tail = None if tail is None else pltpu.with_memory_space_constraint(tail, pltpu.HBM)
    jobs = 64 if number > 1 else 1
    more = [] if vecs is None else [vecs]
    rest = [] if tail is None else [tail]
    half = D // 2
    passed = (
        shape((rows, POOL * D), BF16),
        shape((rows, D), F32),
        shape((rows, D), BF16),
        shape((rows, 3 * D), BF16),
        shape((slots, HEADS, 1, short_len), F32),
        shape((rows, D), BF16),
        shape((rows, D), F32),
        shape((POOL, 8, rows), jnp.int32),
        shape((POOL, rows, 128), jnp.int32),
    )

    gathered = (pltpu.HBM((ROW_HALF, D), BF16),) if number > 1 else ()
    *gathered, shifted, short, normed, qkv, lse, mixed, resid, lines, cols, vecs = pl.pallas_call(
        partial(attend_kernel, short_len, slots, number),
        out_shape=gathered + passed + (shape((8, D), F32),),
        in_specs=[SMEM, SMEM, VMEM] + [ANY] * number + [VMEM] * len(more),
        out_specs=(ANY,) * len(gathered) + (VMEM,) * 10,
        scratch_shapes=[
            pltpu.VMEM((ROW_HALF, D), BF16),
            pltpu.VMEM((short_len, short_len), F32),
            pltpu.VMEM((short_len, short_len), F32),
            pltpu.VMEM((32, 16, D // 2), BF16),
            pltpu.SemaphoreType.DMA((jobs,)),
            pltpu.SemaphoreType.DMA((33,)),
        ],
        compiler_params=pltpu.CompilerParams(vmem_limit_bytes=LIMIT_ATTEND),
        cost_estimate=pl.CostEstimate(flops=9_000_000_000, bytes_accessed=20_000_000, transcendentals=2_400_000),
        name="attend",
    )(coords, layouts, ids, *pieces, *more)
    stacked = pltpu.with_memory_space_constraint(gathered[0], pltpu.HBM) if number > 1 else pieces[0]
    keep_mid, send_mid, keep_deep, send_deep, table, dresid, small_deep = pl.pallas_call(
        partial(deep_kernel, count, number > 1),
        out_shape=(
            shape((ROW_HALF - ROW_F1, half), BF16),
            shape((ROW_HALF - ROW_F1, half), BF16),
            shape((ROW_END - ROW_HALF, half), BF16),
            shape((ROW_END - ROW_HALF, half), BF16),
            shape((VOCAB, D), F32),
            shape((rows, D), F32),
            shape((8, D), F32),
        ),
        in_specs=[SMEM] + [VMEM] * 4 + [ANY] * (1 + len(rest)),
        out_specs=(VMEM,) * 7,
        scratch_shapes=[
            pltpu.VMEM((ROW_END - ROW_F1, D), BF16),
            pltpu.VMEM((VOCAB, D), BF16),
            pltpu.VMEM((rows, D), BF16),
            pltpu.VMEM((rows, FF), BF16),
            pltpu.VMEM((rows, FF), F32),
            pltpu.VMEM((rows, D), BF16),
            pltpu.VMEM((POOL * rows, D), BF16),
            pltpu.VMEM((POOL * rows, VOCAB), BF16),
            pltpu.VMEM((POOL * rows, D), BF16),
            pltpu.VMEM((rows, D), F32),
            pltpu.VMEM((rows, FF), BF16),
            pltpu.VMEM((8, 8, D), F32),
            pltpu.SemaphoreType.DMA((8,)),
        ],
        compiler_params=pltpu.CompilerParams(vmem_limit_bytes=LIMIT_DEEP),
        name="deep",
    )(coords, vecs, cols, lines, resid, stacked, *rest)
    keep_att, send_att, dqkv = pl.pallas_call(
        partial(attend_back_kernel, short_len),
        out_shape=(
            shape((ROW_F1 - ROW_QKV, half), BF16),
            shape((ROW_F1 - ROW_QKV, half), BF16),
            shape((rows, 3 * D), BF16),
        ),
        in_specs=[SMEM, SMEM] + [VMEM] * 5 + [ANY],
        out_specs=(VMEM,) * 3,
        scratch_shapes=[
            pltpu.VMEM((D, D), BF16),
            pltpu.VMEM((short_len, short_len), F32),
            pltpu.VMEM((short_len, short_len), F32),
            pltpu.VMEM((rows, D), BF16),
            pltpu.VMEM((rows, D), BF16),
            pltpu.SemaphoreType.DMA,
        ],
        compiler_params=pltpu.CompilerParams(vmem_limit_bytes=LIMIT_BACK),
        cost_estimate=pl.CostEstimate(flops=11_000_000_000, bytes_accessed=20_000_000, transcendentals=2_400_000),
        name="attend_back",
    )(coords, layouts, dresid, normed, qkv, lse, mixed, stacked)
    if paired:
        recv_deep, recv_mid = swap_with(send_deep, core=1), swap_with(send_mid, core=1)
        sent = core_sum(coords, keep_deep, recv_deep)
        recv_att = swap_with(send_att, core=1)
        sent, recv_att, recv_mid, dqkv = lax.optimization_barrier((sent, recv_att, recv_mid, dqkv))
        sent = first_exchange(sent)
    keep_front, send_front, small = pl.pallas_call(
        front_back_kernel,
        out_shape=(shape((ROW_QKV, half), BF16), shape((ROW_QKV + 32, half), BF16), shape((8, D), F32)),
        in_specs=[SMEM] + [VMEM] * 8 + [ANY],
        out_specs=(VMEM,) * 3,
        scratch_shapes=[
            pltpu.VMEM((VOCAB, D), F32),
            pltpu.VMEM((ROW_O - ROW_P, D), BF16),
            pltpu.VMEM((rows, D), BF16),
            pltpu.SemaphoreType.DMA,
        ],
        compiler_params=pltpu.CompilerParams(vmem_limit_bytes=LIMIT_BACK),
        cost_estimate=pl.CostEstimate(flops=8_000_000_000, bytes_accessed=20_000_000, transcendentals=0),
        name="front_back",
    )(coords, vecs, small_deep, lines, dresid, shifted, short, dqkv, table, stacked)
    if not paired:
        front = jnp.concatenate([keep_front, send_front[:ROW_QKV]], 1)
        others = [
            jnp.concatenate(pair, 1)
            for pair in ((keep_att, send_att), (keep_mid, send_mid), (keep_deep, send_deep))
        ]
        return jnp.concatenate([front] + others, 0), small
    late = 5
    early = [array for k, array in enumerate(sent) if k != late]
    early, keep_front, send_front, small = lax.optimization_barrier((early, keep_front, send_front, small))
    sent = early[:late] + [sent[late]] + early[late:]
    received = [swap_with(send_front, core=1), recv_att, recv_mid]
    out_p, out_q = exchange_shapes(64)
    parts = pl.pallas_call(
        core_sum_front_kernel,
        out_shape=(out_p,) * 4 + (out_q,) * 4,
        in_specs=[SMEM] + [ANY] * 6 + [VMEM],
        out_specs=(VMEM,) * 8,
        scratch_shapes=[
            pltpu.VMEM((ROW_HALF, half), BF16),
            pltpu.VMEM((ROW_HALF + 32, half), BF16),
            pltpu.SemaphoreType.DMA((7,)),
        ],
        compiler_params=params,
        name="core_sum_front",
    )(coords, keep_front, keep_att, keep_mid, *received, small)
    return first_exchange(parts), sent


def exchange_shapes(extra):
    quarter = D // 4
    return (
        jax.ShapeDtypeStruct((4 * SCATTER_CUT + extra, quarter), BF16),
        jax.ShapeDtypeStruct((4 * (2 * SHARD - SCATTER_CUT), quarter), BF16),
    )


def core_sum(coords, keep, received):
    out_p, out_q = exchange_shapes(0)
    return pl.pallas_call(
        core_sum_kernel,
        out_shape=(out_p,) * 4 + (out_q,) * 4,
        in_specs=[SMEM] + [VMEM] * 2,
        out_specs=(VMEM,) * 8,
        compiler_params=pltpu.CompilerParams(vmem_limit_bytes=LIMIT),
        name="core_sum",
    )(coords, keep, received)


def first_exchange(parts):
    over = [parts[0]] + [swap_with(parts[k], line=k) for k in (1, 2, 3)]
    return over + [parts[4]] + [swap_with(parts[4 + k], zed=k) for k in (1, 2, 3)]


def swap_with(array, line=0, zed=0, core=0):
    lines, rest = lax.axis_size("dp"), lax.axis_size("fsdp")
    pairs = [
        (d * rest + f, (d ^ line) * rest + (f ^ (2 * zed + core)))
        for d in range(lines)
        for f in range(rest)
    ]
    return lax.ppermute(array, AXES, pairs)


def swap_halves(coords, shard):
    half = D // 2
    upper = coords[0] // 2 == 1
    left, right = shard[:, :half], shard[:, half:]
    keep, send = jnp.where(upper, right, left), jnp.where(upper, left, right)
    other = swap_with(send, line=2)
    return jnp.where(upper, other, keep), jnp.where(upper, keep, other)


def gather_pieces(block, vectors):
    half = D // 2
    width = vectors.shape[1]
    start = lax.axis_index(AXES) * width
    own = lax.dynamic_update_slice(
        jnp.zeros((16, half), BF16), vectors, (8 * (start // half), start % half)
    )
    first, second = jnp.concatenate([block[:GATHER_CUT], own], 0), block[GATHER_CUT:]
    along = jnp.concatenate([first] + [swap_with(first, zed=k) for k in (1, 2, 3)], 0)
    across = jnp.concatenate([second] + [swap_with(second, line=k) for k in (1, 2, 3)], 0)
    pieces = [along] + [swap_with(along, line=k) for k in (1, 2, 3)]
    pieces += [across] + [swap_with(across, zed=k) for k in (1, 2, 3)]
    return pieces + [swap_with(piece, core=1) for piece in pieces]


def scatter_sum(coords, front, deep):
    shape = jax.ShapeDtypeStruct
    params = pltpu.CompilerParams(vmem_limit_bytes=LIMIT)
    quarter = D // 4
    rest = 2 * SHARD - SCATTER_CUT
    parts = pl.pallas_call(
        first_sum_kernel,
        out_shape=(shape((2 * SCATTER_CUT + 64, quarter), BF16),) * 4 + (shape((2 * rest, quarter), BF16),) * 4,
        in_specs=[SMEM] + [VMEM] * 16,
        out_specs=(VMEM,) * 8,
        compiler_params=params,
        name="first_sum",
    )(coords, *front, *deep)
    second = [parts[0]] + [swap_with(parts[k], zed=k) for k in (1, 2, 3)]
    second += [parts[4]] + [swap_with(parts[4 + k], line=k) for k in (1, 2, 3)]
    *outs, small, squares = pl.pallas_call(
        last_sum_kernel,
        out_shape=(shape((SHARD, quarter), F32),) * 4 + (shape((8, D), F32), shape((8, quarter), F32)),
        in_specs=[SMEM] + [VMEM] * 8,
        out_specs=(VMEM,) * 6,
        scratch_shapes=[pltpu.VMEM((2 * SHARD, quarter), F32)],
        compiler_params=params,
        name="last_sum",
    )(coords, *second)
    squares = squares + swap_with(squares, core=1)
    quarters = [outs[0], swap_with(outs[1], line=2), swap_with(outs[2], core=1), swap_with(outs[3], line=2, core=1)]
    squares = (squares + swap_with(squares, line=1)) + (swap_with(squares, line=2) + swap_with(squares, line=3))
    squares = [squares] + [swap_with(squares, zed=k) for k in (1, 2, 3)]
    return quarters, small, squares


def shards(byte_ids, layouts, weights, vectors, m_weights, v_weights, m_vectors, v_vectors):
    devices = lax.axis_size(AXES)
    micro = byte_ids.shape[0]
    count = float(micro * layouts.shape[1] * devices * byte_ids.shape[2])
    lines, rest = lax.axis_size("dp"), lax.axis_size("fsdp")
    place = lax.axis_index("fsdp")
    coords = jnp.stack([lax.axis_index("dp"), place // 2, place % 2, lax.axis_index(AXES)]).astype(jnp.int32)
    paired = lines == 4 and rest == 8 and weights.shape[0] == SHARD
    weights_low = weights.astype(BF16)
    vectors_low = vectors.astype(BF16)
    width = vectors.shape[1]
    mine = lax.axis_index(AXES) * width
    flat_layouts = layouts.reshape(-1)
    ids = byte_ids.reshape(flat_layouts.shape[0], -1, POOL).transpose(2, 0, 1).reshape(POOL, -1)
    ids = jnp.pad(ids, ((0, 8 - POOL), (0, 0)))
    if paired:
        front, back = swap_halves(coords, weights_low)
        tail = lax.all_gather(back, AXES, axis=0, tiled=True)
        pieces = gather_pieces(front, vectors_low)
        front, deep = device_grads(
            pieces, tail, None, coords, ids, flat_layouts, count, True
        )
        quarters, small, squares = scatter_sum(coords, front, deep)
        like = [jax.ShapeDtypeStruct((1, 1), F32)] * 2
        like += [jax.ShapeDtypeStruct(weights.shape, F32)] * 3 + [jax.ShapeDtypeStruct(vectors.shape, F32)] * 3
        loss, grad_norm, *updated = pl.pallas_call(
            partial(update_kernel, count),
            out_shape=like,
            in_specs=[SMEM] + [VMEM] * 15,
            out_specs=[VMEM] * 8,
            compiler_params=pltpu.CompilerParams(vmem_limit_bytes=LIMIT),
            name="update",
        )(coords, *quarters, *squares, small, weights, m_weights, v_weights, vectors, m_vectors, v_vectors)
        return (loss[0, 0], grad_norm[0, 0], *updated)
    coords = coords * 0
    pieces = [lax.all_gather(weights_low, AXES, axis=0, tiled=True)]
    vecs = lax.all_gather(vectors_low, AXES, axis=1, tiled=True)
    vecs = jnp.pad(vecs.astype(F32), ((0, 2), (0, 0)))
    local, small = device_grads(pieces, None, vecs, coords, ids, flat_layouts, count, False)
    owned = lax.psum_scatter(local.astype(F32), AXES, scatter_dimension=0, tiled=True)
    small, squares = lax.psum((small, jnp.sum(owned * owned)), AXES)
    loss = small[6, 0] / count
    vec_grads = small[:6]
    owned_vecs = lax.dynamic_slice(vec_grads, (0, mine), (6, width))
    squares = squares + jnp.sum(vec_grads * vec_grads)
    grad_norm = jnp.sqrt(squares)
    factor = CLIP / jnp.maximum(grad_norm, CLIP)
    first_w, second_w, update_w = adam(weights, m_weights, v_weights, owned * factor, DECAY)
    first_v, second_v, update_v = adam(vectors, m_vectors, v_vectors, owned_vecs * factor, 0.0)
    return (loss, grad_norm, first_w, second_w, update_w, first_v, second_v, update_v)


def solution(mesh):
    in_specs = (
        P(None, AXES, None),
        P(None, AXES),
        P(AXES, None),
        P(None, AXES),
        P(AXES, None),
        P(AXES, None),
        P(None, AXES),
        P(None, AXES),
    )
    out_specs = (
        P(),
        P(),
        P(AXES, None),
        P(AXES, None),
        P(AXES, None),
        P(None, AXES),
        P(None, AXES),
        P(None, AXES),
    )
    return jax.shard_map(shards, mesh=mesh, in_specs=in_specs, out_specs=out_specs, check_vma=False)
```

```python
from functools import partial

import jax
import jax.numpy as jnp
from jax import lax
from jax.experimental import pallas as pl
from jax.experimental.pallas import tpu as pltpu
from jax.sharding import PartitionSpec as P

D = 512
HEADS = 8
HEAD = 64
FF = 2048
VOCAB = 256
POOL = 3

EPS_NORM = 1e-05
EPS_ADAM = 1e-08
CLIP = 0.2
RATE = 0.03
DECAY = 0.1
BETA = 0.5
STEP = 3
NEGATIVE = -1000000000.0

F32 = jnp.float32
BF16 = jnp.bfloat16

ROW_E = 0
ROW_P = VOCAB
ROW_QKV = ROW_P + POOL * D
ROW_O = ROW_QKV + 3 * D
ROW_F1 = ROW_O + D
ROW_F2 = ROW_F1 + FF
ROW_U = ROW_F2 + FF
ROW_H = ROW_U + POOL * D
ROW_END = ROW_H + VOCAB
ROW_HALF = ROW_END // 2
assert ROW_HALF - ROW_F1 == FF // 2

AXES = ("dp", "fsdp")
SHARD = ROW_END // 32
GATHER_CUT = 208
SCATTER_CUT = 400


def nn(left, right):
    return lax.dot_general(left, right, (((1,), (0,)), ((), ())), preferred_element_type=F32)


def nt(left, right):
    return lax.dot_general(left, right, (((1,), (1,)), ((), ())), preferred_element_type=F32)


def tn(left, right):
    return lax.dot_general(left, right, (((0,), (0,)), ((), ())), preferred_element_type=F32)


def norm_parts(values):
    center = values - jnp.mean(values, -1, keepdims=True)
    spread = jnp.mean(center * center, -1, keepdims=True)
    scale = lax.rsqrt(spread + EPS_NORM)
    return center * scale, scale


def norm_back(unit, scale, gain, grad):
    inner = grad * gain
    mean_inner = jnp.mean(inner, -1, keepdims=True)
    mean_cross = jnp.mean(inner * unit, -1, keepdims=True)
    return scale * (inner - mean_inner - unit * mean_cross)


def fold_rows(values):
    return jnp.sum(values.reshape(values.shape[0] // 8, 8, values.shape[1]), 0)


def one_hot_rows(ids):
    lanes = lax.broadcasted_iota(jnp.int32, (ids.shape[0], VOCAB), 1)
    return jnp.where(lanes == ids, 1.0, 0.0).astype(BF16)


def one_hot_cols(ids):
    lines = lax.broadcasted_iota(jnp.int32, (VOCAB, ids.shape[1]), 0)
    return jnp.where(lines == ids, 1.0, 0.0).astype(BF16)


def rows_of(index, size):
    return pl.ds(pl.multiple_of(index * size, size), size)


def gathered_parts(coords_ref):
    dp, z, core = coords_ref[0], coords_ref[1], coords_ref[2]
    for side in range(2):
        for k in range(4):
            for part in range(4):
                for kind in range(2):
                    d, e = (k, part) if kind == 0 else (part, k)
                    yield side * 8 + kind * 4 + k, part, kind, (dp ^ d) * 8 + (z ^ e) * 2 + (core ^ side)


class FetchGathered:
    def __init__(self, pieces, coords_ref, w_ref, sems, high):
        self.jobs = []
        for number, (piece, part, kind, shard) in enumerate(gathered_parts(coords_ref)):
            begin, size, step = ((0, GATHER_CUT, GATHER_CUT + 16), (GATHER_CUT, SHARD - GATHER_CUT, SHARD - GATHER_CUT))[kind]
            copy = pltpu.make_async_copy(
                pieces[piece].at[pl.ds(part * step, size)],
                w_ref.at[pl.ds(pl.multiple_of(shard * SHARD + begin, 16), size)],
                sems.at[number],
            )
            self.jobs.append((shard * SHARD < high, copy))

    def start(self, first):
        for early, copy in self.jobs:
            pl.when(early if first else jnp.logical_not(early))(copy.start)

    def wait(self, first):
        for early, copy in self.jobs:
            pl.when(early if first else jnp.logical_not(early))(copy.wait)


def fetch_rows(w_hbm, low, high, w_ref, sem):
    copy = pltpu.make_async_copy(w_hbm.at[pl.ds(low, high - low)], w_ref, sem)
    copy.start()
    return copy


def attend_kernel(short_len, slots, pieces, coords_ref, lay_ref, ids_ref, *refs):
    w_hbm, refs = refs[:pieces], refs[pieces:]
    if pieces == 1:
        vec_in_ref, refs = refs[0], refs[1:]
    if pieces > 1:
        w_out, refs = refs[0], refs[1:]
    (shifted_ref, short_ref, normed_ref, qkv_ref, lse_ref, mixed_ref, resid_ref, lines_ref, cols_ref, vec_ref,
     w_ref, dist_ref, mask_ref, part_ref, sems, part_sems) = refs
    rows = short_len * slots
    if pieces > 1:
        fetch = FetchGathered(w_hbm, coords_ref, w_ref, sems, ROW_F1)
        fetch.start(True)
    else:
        fetch = fetch_rows(w_hbm[0], 0, ROW_F1, w_ref, sems.at[0])
    copies = []
    if pieces > 1:
        for piece, part, kind, _ in gathered_parts(coords_ref):
            if kind == 0:
                place = pl.ds(part * (GATHER_CUT + 16) + GATHER_CUT, 16)
                number = len(copies)
                copies.append(
                    pltpu.make_async_copy(w_hbm[piece].at[place], part_ref.at[number], part_sems.at[number])
                )
        for copy in copies:
            copy.start()

    ids = ids_ref[...]
    group = lax.broadcasted_iota(jnp.int32, (1, rows), 1)
    starts = group == 0
    for slot in range(slots):
        starts = starts | (group == slot * short_len)
        starts = starts | ((group == slot * short_len + short_len // 2) & (lay_ref[slot] == 1))
    ends = group == rows - 1
    for slot in range(slots):
        ends = ends | (group == (slot + 1) * short_len - 1)
        ends = ends | ((group == slot * short_len + short_len // 2 - 1) & (lay_ref[slot] == 1))
    before, after = pltpu.roll(ids, 1, 1), pltpu.roll(ids, rows - 1, 1)
    own = [ids[j : j + 1] for j in range(POOL)]
    back = [jnp.where(starts, -1, before[1:2]), jnp.where(starts, -1, before[2:3]), ids[0:1]]
    ahead = [ids[1:2], ids[2:3], jnp.where(ends, -1, after[0:1])]
    for j in range(POOL):
        for kind, line in enumerate((own[j], back[j], ahead[j])):
            lines_ref[j, kind : kind + 1, :] = line
        lines_ref[j, 3:, :] = jnp.zeros((5, rows), jnp.int32)
        padded = jnp.concatenate([lines_ref[j].astype(F32), jnp.zeros((120, rows), F32)], 0)
        cols_ref[j] = padded.T.astype(jnp.int32)

    for copy in copies:
        copy.wait()
    if pieces > 1:
        both = part_ref[0].astype(F32)
        for k in range(1, len(copies)):
            both = both + part_ref[k].astype(F32)
        vec_ref[...] = both[:8]
        fetch.wait(True)
        fetch.start(False)
    else:
        vec_ref[...] = vec_in_ref[...]
        fetch.wait()
    gain, offset = vec_ref[0:1, :], vec_ref[1:2, :]

    def shift_step(j, carry):
        lanes = rows_of(j, D)
        hot = one_hot_rows(cols_ref[j, :, 1:2])
        shifted_ref[:, lanes] = nn(hot, w_ref[ROW_E:ROW_P, :]).astype(BF16)
        return carry

    lax.fori_loop(0, POOL, shift_step, 0)

    def short_step(block, carry):
        at = rows_of(block, rows // 2)
        short = nn(shifted_ref[at, :], w_ref[ROW_P:ROW_QKV, :])
        short_ref[at, :] = short
        unit, _ = norm_parts(short)
        normed_ref[at, :] = (unit * gain + offset).astype(BF16)
        qkv_ref[at, :] = nt(normed_ref[at, :], w_ref[ROW_QKV:ROW_O, :]).astype(BF16)
        return carry

    lax.fori_loop(0, 2, short_step, 0)
    if pieces > 1:
        fetch.wait(False)
        leave = pltpu.make_async_copy(w_ref, w_out, part_sems.at[len(copies)])
        leave.start()

    left_lanes = lax.broadcasted_iota(jnp.int32, (short_len, 2 * HEAD), 1) < HEAD

    def slot_step(index, carry):
        slot, lower = index // 2, index % 2
        at = rows_of(slot, short_len)

        @pl.when(lower == 0)
        def _():
            attention_bias(lay_ref[slot], short_len, dist_ref, mask_ref)

        for pair in range(HEADS // 4):
            lanes, lanes_k, lanes_v = (pair_lanes(part, lower, pair) for part in range(3))
            queries = qkv_ref[at, lanes] * jnp.asarray(0.125, BF16)
            keys, values = qkv_ref[at, lanes_k], qkv_ref[at, lanes_v]
            mixed = jnp.zeros((short_len, 2 * HEAD), F32)
            for side in range(2):
                head = lower * (HEADS // 2) + pair * 2 + side
                slope = head_slope(lower, pair * 2 + side)
                scores = nt(one_side(left_lanes, side, keys), queries)
                scores = scores + jnp.minimum(dist_ref[...] * slope, mask_ref[...])
                top = jnp.max(scores, 0, keepdims=True)
                expo = jnp.exp(scores - top)
                total = jnp.sum(expo, 0, keepdims=True)
                lse_ref[slot, head] = top + jnp.log(total)
                probs = (expo * (1.0 / total)).astype(BF16)
                mixed = mixed + tn(probs, one_side(left_lanes, side, values))
            mixed_ref[at, lanes] = mixed.astype(BF16)
        return carry

    lax.fori_loop(0, 2 * slots, slot_step, 0)
    resid_ref[...] = short_ref[...] + nn(mixed_ref[...], w_ref[ROW_O:ROW_F1, :])
    if pieces > 1:
        leave.wait()


def head_slope(lower, head):
    return jnp.where(lower == 0, *(2.0 ** (-8.0 * (head + more + 1.0) / HEADS) for more in (0, HEADS // 2)))


def pair_lanes(part, lower, pair):
    return pl.ds(pl.multiple_of(part * D + lower * (D // 2) + pair * 2 * HEAD, 2 * HEAD), 2 * HEAD)


def one_side(left_lanes, side, array):
    zero = jnp.zeros_like(array)
    return jnp.where(left_lanes, array, zero) if side == 0 else jnp.where(left_lanes, zero, array)


def attention_bias(layout, short_len, dist_ref, mask_ref):
    key = lax.broadcasted_iota(jnp.int32, (short_len, short_len), 0)
    query = lax.broadcasted_iota(jnp.int32, (short_len, short_len), 1)
    half = jnp.where(layout == 1, short_len // 2, short_len)
    allowed = (key <= query) & ((key >= half) == (query >= half))
    dist_ref[...] = (key - query).astype(F32)
    mask_ref[...] = jnp.where(allowed, 0.0, NEGATIVE)


def gelu_parts(hidden):
    size = jnp.abs(hidden)
    near = 1.0 / (1.0 + (0.3275911 * 0.7071067811865476) * size)
    bell = jnp.exp(hidden * hidden * -0.5)
    tail = near * (0.127414796 + near * (-0.142248368 + near * (0.7107068705 + near * (-0.7265760135 + near * 0.5307027145))))
    tail = tail * bell
    cdf = jnp.where(hidden >= 0.0, 1.0 - tail, tail)
    return hidden * cdf, cdf + hidden * bell * 0.3989422804014327


def split_store(keep_ref, send_ref, core, rows, values):
    half = D // 2
    low, high = values[:, :half].astype(BF16), values[:, half:].astype(BF16)
    keep_ref[rows, :] = jnp.where(core == 0, low, high)
    send_ref[rows, :] = jnp.where(core == 0, high, low)


def deep_kernel(count, coords_ref, vec_ref, cols_ref, lines_ref, resid_ref, w_hbm, *refs):
    (keep_mid, send_mid, keep_ref, send_ref, table_ref, dresid_ref, small_ref,
     w_ref, e_ref, normed_ref, act_ref, slope_ref, deep_ref, final_ref, dlog_ref, dup_ref,
     ddeep_ref, dhid_ref, sums_ref, sems) = refs
    rows = resid_ref.shape[0]
    base = ROW_F1
    core = coords_ref[2]
    stages = []
    for k, (low, high) in enumerate(((ROW_F1, ROW_F2), (ROW_F2, ROW_U), (ROW_U, ROW_END))):
        stages.append([fetch_rows(w_hbm, low, high, w_ref.at[pl.ds(low - base, high - low)], sems.at[k])])
    stages[2].append(fetch_rows(w_hbm, 0, VOCAB, e_ref, sems.at[3]))
    f1, f2, up, head = ROW_F1 - base, ROW_F2 - base, ROW_U - base, ROW_H - base
    gain2, offset2 = vec_ref[2:3, :], vec_ref[3:4, :]
    gain_f, offset_f = vec_ref[4:5, :], vec_ref[5:6, :]
    wide = 1024
    sums_ref[...] = jnp.zeros_like(sums_ref)

    unit, _ = norm_parts(resid_ref[...])
    normed_ref[...] = (unit * gain2 + offset2).astype(BF16)
    for copy in stages[0]:
        copy.wait()

    def hidden_step(chunk, carry):
        lanes = rows_of(chunk, wide)
        hidden = nt(normed_ref[...], w_ref[pl.ds(pl.multiple_of(f1 + chunk * wide, 16), wide), :])
        act, slope = gelu_parts(hidden)
        act_ref[:, lanes] = act.astype(BF16)
        slope_ref[:, lanes] = slope
        return carry

    lax.fori_loop(0, FF // wide, hidden_step, 0)
    for copy in stages[1]:
        copy.wait()

    def deep_step(block, carry):
        at = rows_of(block, rows // 2)
        deep_ref[at, :] = (resid_ref[at, :] + nn(act_ref[at, :], w_ref[f2 : f2 + FF, :])).astype(BF16)
        return carry

    lax.fori_loop(0, 2, deep_step, 0)
    for copy in stages[2]:
        copy.wait()
    ddeep_ref[...] = jnp.zeros_like(ddeep_ref)
    table_ref[...] = jnp.zeros_like(table_ref)

    def head_step(j, carry):
        there = rows_of(j, rows)
        up_rows = pl.ds(pl.multiple_of(up + j * D, 16), D)
        columns = cols_ref[j]
        joined = nn(one_hot_rows(columns[:, 0:1]), e_ref[0:VOCAB, :]) + nt(deep_ref[...], w_ref[up_rows, :])
        unit, scale = norm_parts(joined)
        final = (unit * gain_f + offset_f).astype(BF16)
        final_ref[there, :] = final
        logits = nt(final, w_ref[head : head + VOCAB, :])
        nexts = columns[:, 2:3]
        lanes = lax.broadcasted_iota(jnp.int32, logits.shape, 1)
        target = jnp.where(lanes == nexts, 1.0, 0.0)
        valid = jnp.where(nexts >= 0, 1.0, 0.0)
        peak = jnp.max(logits, -1, keepdims=True)
        expo = jnp.exp(logits - peak)
        total = jnp.sum(expo, -1, keepdims=True)
        picked = jnp.sum(logits * target, -1, keepdims=True)
        losses = valid * (peak + jnp.log(total) - picked)
        dlogits = ((valid / count) * (expo * (1.0 / total) - target)).astype(BF16)
        dlog_ref[there, :] = dlogits
        dfinal = nn(dlogits, w_ref[head : head + VOCAB, :])
        dup = norm_back(unit, scale, gain_f, dfinal).astype(BF16)
        dup_ref[there, :] = dup
        ddeep_ref[...] += nn(dup, w_ref[up_rows, :])
        sums_ref[4, :, :] += fold_rows(dfinal * unit)
        sums_ref[5, :, :] += fold_rows(dfinal)
        sums_ref[6, :, :] += jnp.broadcast_to(fold_rows(losses), (8, D))
        return carry

    lax.fori_loop(0, POOL, head_step, 0)

    out_f2, out_up, out_head = ROW_F2 - ROW_HALF, ROW_U - ROW_HALF, ROW_H - ROW_HALF
    split_store(keep_ref, send_ref, core, pl.ds(out_head, VOCAB), tn(dlog_ref[...], final_ref[...]))

    def dup_step(j, carry):
        there = rows_of(j, rows)
        dup = dup_ref[there, :]
        out = pl.ds(pl.multiple_of(out_up + j * D, D), D)
        split_store(keep_ref, send_ref, core, out, tn(dup, deep_ref[...]))
        table_ref[...] += nn(one_hot_cols(lines_ref[j, 0:1, :]), dup)
        return carry

    lax.fori_loop(0, POOL, dup_step, 0)

    deep_ref[...] = ddeep_ref[...].astype(BF16)

    def dff_step(chunk, carry):
        lanes = rows_of(chunk, wide)
        dact = nt(deep_ref[...], w_ref[pl.ds(pl.multiple_of(f2 + chunk * wide, 16), wide), :])
        dhid_ref[:, lanes] = (dact * slope_ref[:, lanes]).astype(BF16)
        grad = tn(dhid_ref[:, lanes], normed_ref[...])

        @pl.when(chunk == 0)
        def _():
            split_store(keep_mid, send_mid, core, slice(0, wide), grad)

        @pl.when(chunk > 0)
        def _():
            split_store(keep_ref, send_ref, core, slice(0, wide), grad)

        out = pl.ds(pl.multiple_of(out_f2 + chunk * wide, wide), wide)
        split_store(keep_ref, send_ref, core, out, tn(act_ref[:, lanes], deep_ref[...]))
        return carry

    lax.fori_loop(0, FF // wide, dff_step, 0)
    def dnorm_step(block, carry):
        at = rows_of(block, rows // 2)
        dnormed = nn(dhid_ref[at, :], w_ref[f1 : f1 + FF, :])
        unit, scale = norm_parts(resid_ref[at, :])
        dresid_ref[at, :] = ddeep_ref[at, :] + norm_back(unit, scale, gain2, dnormed)
        sums_ref[2, :, :] += fold_rows(dnormed * unit)
        sums_ref[3, :, :] += fold_rows(dnormed)
        return carry

    lax.fori_loop(0, 2, dnorm_step, 0)
    for k in range(8):
        small_ref[k : k + 1, :] = jnp.sum(sums_ref[k], 0, keepdims=True)


def attend_back_kernel(short_len, coords_ref, lay_ref, dresid_ref, normed_ref, qkv_ref, lse_ref, mixed_ref,
                       w_hbm, *refs):
    (keep_ref, send_ref, dqkv_ref,
     w_ref, dist_ref, mask_ref, dbranch_ref, dmix_ref, sem) = refs
    core = coords_ref[2]
    fetch = fetch_rows(w_hbm, ROW_O, ROW_F1, w_ref, sem)
    dbranch_ref[...] = dresid_ref[...].astype(BF16)
    fetch.wait()
    dmix_ref[...] = nt(dbranch_ref[...], w_ref[...]).astype(BF16)

    left_lanes = lax.broadcasted_iota(jnp.int32, (short_len, 2 * HEAD), 1) < HEAD

    def slot_step(index, carry):
        slot, lower = index // 2, index % 2
        at = rows_of(slot, short_len)

        @pl.when(lower == 0)
        def _():
            attention_bias(lay_ref[slot], short_len, dist_ref, mask_ref)

        for pair in range(HEADS // 4):
            lanes, lanes_k, lanes_v = (pair_lanes(part, lower, pair) for part in range(3))
            queries, keys, values = qkv_ref[at, lanes], qkv_ref[at, lanes_k], qkv_ref[at, lanes_v]
            dmix = dmix_ref[at, lanes]
            scaled = queries * jnp.asarray(0.125, BF16)
            dqueries, dkeys, dvalues = (jnp.zeros((short_len, 2 * HEAD), F32) for _ in range(3))
            for side in range(2):
                head = lower * (HEADS // 2) + pair * 2 + side
                slope = head_slope(lower, pair * 2 + side)
                keys_here = one_side(left_lanes, side, keys)
                scores = nt(keys_here, scaled)
                scores = scores + jnp.minimum(dist_ref[...] * slope, mask_ref[...])
                probs = jnp.exp(scores - lse_ref[slot, head])
                dprobs = nt(one_side(left_lanes, side, values), dmix)
                delta = jnp.sum(dprobs * probs, 0, keepdims=True)
                dscores = (probs * (dprobs - delta) * 0.125).astype(BF16)
                dvalues = dvalues + nn(probs.astype(BF16), one_side(left_lanes, side, dmix))
                dkeys = dkeys + nn(dscores, one_side(left_lanes, side, queries))
                dqueries = dqueries + tn(dscores, keys_here)
            dqkv_ref[at, lanes] = dqueries.astype(BF16)
            dqkv_ref[at, lanes_k] = dkeys.astype(BF16)
            dqkv_ref[at, lanes_v] = dvalues.astype(BF16)
        return carry

    lax.fori_loop(0, 2 * lse_ref.shape[0], slot_step, 0)
    split_store(keep_ref, send_ref, core, pl.ds(3 * D, D), tn(mixed_ref[...], dbranch_ref[...]))

    def dproj_step(part, carry):
        grad = tn(dqkv_ref[:, rows_of(part, D)], normed_ref[...])
        split_store(keep_ref, send_ref, core, rows_of(part, D), grad)
        return carry

    lax.fori_loop(0, 3, dproj_step, 0)


def front_back_kernel(coords_ref, vec_ref, deep_small_ref, lines_ref, dresid_ref, shifted_ref, short_ref, dqkv_ref,
                      table_in, w_hbm, keep_ref, send_ref, small_ref, table_ref, w_ref, dshort_ref, sem):
    core = coords_ref[2]
    fetch = fetch_rows(w_hbm, ROW_P, ROW_O, w_ref, sem)
    gain = vec_ref[0:1, :]
    fetch.wait()
    dnormed = nn(dqkv_ref[...], w_ref[ROW_QKV - ROW_P :, :])
    unit, scale = norm_parts(short_ref[...])
    dshort_ref[...] = (dresid_ref[...] + norm_back(unit, scale, gain, dnormed)).astype(BF16)
    small_ref[...] = deep_small_ref[...]
    for k, values in enumerate((dnormed * unit, dnormed)):
        small_ref[k : k + 1, :] = jnp.sum(fold_rows(values), 0, keepdims=True)
    half = D // 2
    for k in range(2):
        send_ref[ROW_QKV + 16 * k : ROW_QKV + 16 * (k + 1), :] = two_parts(small_ref[:, k * half : (k + 1) * half])
    table_ref[...] = table_in[...]

    def pool_step(j, carry):
        dshift = nt(dshort_ref[...], w_ref[rows_of(j, D), :]).astype(BF16)
        table_ref[...] += nn(one_hot_cols(lines_ref[j, 1:2, :]), dshift)
        out = pl.ds(pl.multiple_of(ROW_P + j * D, 16), D)
        split_store(keep_ref, send_ref, core, out, tn(shifted_ref[:, rows_of(j, D)], dshort_ref[...]))
        return carry

    lax.fori_loop(0, POOL, pool_step, 0)
    split_store(keep_ref, send_ref, core, pl.ds(ROW_E, VOCAB), table_ref[...])


def two_parts(values):
    high = values.astype(BF16)
    low = (values - high.astype(F32)).astype(BF16)
    return jnp.concatenate([high.astype(F32), low.astype(F32)], 0).astype(BF16)


def one_value(parts):
    parts = parts.astype(F32)
    return parts[:8] + parts[8:]


def lay_out(coords_ref, keep_ref, recv_ref, p_refs, q_refs):
    dp, z = coords_ref[0], coords_ref[1]
    quarter = D // 4
    line = 2 * SHARD
    rest = line - SCATTER_CUT

    def total(column, x, zed, begin, size):
        at = pl.ds(pl.multiple_of(x * (4 * line) + zed * line + begin, 16), size)
        lanes = pl.ds(pl.multiple_of(column * quarter, quarter), quarter)
        return (keep_ref[at, lanes].astype(F32) + recv_ref[at, lanes].astype(F32)).astype(BF16)

    def part_step(part, carry):
        for k in range(4):
            there = dp ^ k
            out = pl.ds(pl.multiple_of(part * SCATTER_CUT, 16), SCATTER_CUT)
            p_refs[k][out, :] = total(there // 2, there % 2, part, 0, SCATTER_CUT)
            out = pl.ds(pl.multiple_of(part * rest, 16), rest)
            q_refs[k][out, :] = total(part // 2, part % 2, z ^ k, SCATTER_CUT, rest)
        return carry

    lax.fori_loop(0, 4, part_step, 0)


def core_sum_kernel(coords_ref, keep_ref, recv_ref, *out_refs):
    lay_out(coords_ref, keep_ref, recv_ref, out_refs[:4], out_refs[4:])


def core_sum_front_kernel(coords_ref, keep_front, keep_att, keep_mid, recv_front, recv_att, recv_mid, small_ref, *refs):
    out_refs, (keep_ref, recv_ref, sems) = refs[:8], refs[8:]
    copies = [
        pltpu.make_async_copy(source, target, sems.at[k])
        for k, (source, target) in enumerate((
            (keep_att, keep_ref.at[pl.ds(ROW_QKV, ROW_F1 - ROW_QKV)]),
            (recv_att, recv_ref.at[pl.ds(ROW_QKV, ROW_F1 - ROW_QKV)]),
            (keep_mid, keep_ref.at[pl.ds(ROW_F1, ROW_HALF - ROW_F1)]),
            (recv_mid, recv_ref.at[pl.ds(ROW_F1, ROW_HALF - ROW_F1)]),
            (keep_front, keep_ref.at[pl.ds(0, ROW_QKV)]),
            (recv_front.at[pl.ds(0, ROW_QKV)], recv_ref.at[pl.ds(0, ROW_QKV)]),
            (recv_front.at[pl.ds(ROW_QKV, 32)], recv_ref.at[pl.ds(ROW_HALF, 32)]),
        ))
    ]
    for copy in copies:
        copy.start()
    for copy in copies:
        copy.wait()
    lay_out(coords_ref, keep_ref, recv_ref, out_refs[:4], out_refs[4:])
    quarter = D // 4
    for k in range(2):
        both = small_ref[:, 2 * k * quarter : 2 * (k + 1) * quarter] + one_value(
            recv_ref[ROW_HALF + 16 * k : ROW_HALF + 16 * (k + 1), :]
        )
        for side in range(2):
            parts = two_parts(both[:, side * quarter : (side + 1) * quarter])
            row = 4 * SCATTER_CUT + 16 * (2 * k + side)
            for p_ref in out_refs[:4]:
                p_ref[row : row + 16, :] = parts


def sum_of(refs, row, size):
    at = pl.ds(pl.multiple_of(row, 16), size)
    return (refs[0][at, :].astype(F32) + refs[1][at, :].astype(F32)) + (
        refs[2][at, :].astype(F32) + refs[3][at, :].astype(F32)
    )


def first_sum_kernel(coords_ref, *refs):
    sources = ((refs[0:4], refs[4:8]), (refs[8:12], refs[12:16]))
    s_refs, t_refs = refs[16:20], refs[20:24]
    dp, z = coords_ref[0], coords_ref[1]
    rest = 2 * SHARD - SCATTER_CUT
    for half, (p_refs, q_refs) in enumerate(sources):
        for k in range(4):
            s_refs[k][half * SCATTER_CUT : (half + 1) * SCATTER_CUT, :] = sum_of(
                p_refs, (z ^ k) * SCATTER_CUT, SCATTER_CUT
            ).astype(BF16)
            t_refs[k][half * rest : (half + 1) * rest, :] = sum_of(q_refs, (dp ^ k) * rest, rest).astype(BF16)
    for k in range(4):
        row = 4 * SCATTER_CUT + 16 * k
        value = sum(one_value(ref[row : row + 16, :]) for ref in sources[0][0])
        parts = two_parts(value)
        for s_ref in s_refs:
            s_ref[2 * SCATTER_CUT + 16 * k : 2 * SCATTER_CUT + 16 * (k + 1), :] = parts


def last_sum_kernel(coords_ref, *refs):
    s_refs, t_refs, out_refs, (small_ref, square_ref, sum_ref) = refs[:4], refs[4:8], refs[8:12], refs[12:]
    y, core = coords_ref[0] // 2, coords_ref[2]
    rest = 2 * SHARD - SCATTER_CUT
    squares = jnp.zeros((8, D // 4), F32)
    for k in range(2):
        half = y ^ k
        first = sum_of(s_refs, half * SCATTER_CUT, SCATTER_CUT)
        second = sum_of(t_refs, half * rest, rest)
        squares = squares + fold_rows(first * first) + fold_rows(second * second)
        sum_ref[0:SCATTER_CUT, :] = first
        sum_ref[SCATTER_CUT:, :] = second
        for other in range(2):
            out_refs[2 * other + k][...] = sum_ref[pl.ds(pl.multiple_of((core ^ other) * SHARD, 8), SHARD), :]
    for k in range(4):
        row = 2 * SCATTER_CUT + 16 * k
        small_ref[:, k * (D // 4) : (k + 1) * (D // 4)] = sum(
            one_value(ref[row : row + 16, :]) for ref in s_refs
        )
    square_ref[...] = squares


def adam(param, first_m, second_m, grad, decay):
    first_new = BETA * first_m + (1.0 - BETA) * grad
    second_new = BETA * second_m + (1.0 - BETA) * grad * grad
    correct = 1.0 - BETA**STEP
    update = -RATE * (
        first_new / correct / (jnp.sqrt(second_new / correct) + EPS_ADAM) + decay * param
    )
    return (first_new, second_new, update)


def update_kernel(count, coords_ref, g0, g1, g2, g3, q0, q1, q2, q3, small_ref, w_ref, mw_ref, vw_ref, w_vec, m_vec, v_vec,
                  loss_ref, norm_ref, mw_out, vw_out, uw_out, m_out, v_out, u_out):
    y, core, mine = coords_ref[0] // 2, coords_ref[2], coords_ref[3]
    small = small_ref[...]
    line = lax.broadcasted_iota(jnp.int32, small.shape, 0)
    gradient = jnp.where(line < 6, small, 0.0)
    squares = (q0[...] + q1[...]) + (q2[...] + q3[...])

    def whole(values):
        return jnp.sum(jnp.sum(values, 0, keepdims=True), 1, keepdims=True)

    norm = jnp.sqrt(whole(squares) + whole(gradient * gradient))
    factor = CLIP / jnp.maximum(norm, CLIP)
    norm_ref[...] = norm
    loss_ref[...] = small[6:7, 0:1] / count
    quarter = D // 4
    for k, grad_ref in enumerate((g0, g1, g2, g3)):
        place = (core ^ (k // 2)) * 2 + (y ^ (k % 2))
        lanes = pl.ds(pl.multiple_of(place * quarter, quarter), quarter)
        mw_out[:, lanes], vw_out[:, lanes], uw_out[:, lanes] = adam(
            w_ref[:, lanes], mw_ref[:, lanes], vw_ref[:, lanes], grad_ref[...] * factor, DECAY
        )
    width = w_vec.shape[1]
    owned = pltpu.roll(gradient, lax.rem(small.shape[1] - mine * width, small.shape[1]), 1)[:6, :width]
    m_out[...], v_out[...], u_out[...] = adam(w_vec[...], m_vec[...], v_vec[...], owned * factor, 0.0)


VMEM = pl.BlockSpec(memory_space=pltpu.VMEM)
SMEM = pl.BlockSpec(memory_space=pltpu.SMEM)
ANY = pl.BlockSpec(memory_space=pl.ANY)
MIB = 1024 * 1024
LIMIT = 24 * MIB
LIMIT_ATTEND = 30 * MIB
LIMIT_DEEP = 40 * MIB
LIMIT_BACK = 24 * MIB


def device_grads(pieces, vecs, coords, ids, layouts, count, paired):
    slots = layouts.shape[0]
    rows = ids.shape[1]
    short_len = rows // slots
    shape = jax.ShapeDtypeStruct
    params = pltpu.CompilerParams(vmem_limit_bytes=LIMIT)
    number = len(pieces)
    pieces = [pltpu.with_memory_space_constraint(piece, pltpu.HBM) for piece in pieces]
    jobs = 64 if number > 1 else 1
    more = [] if vecs is None else [vecs]
    half = D // 2
    passed = (
        shape((rows, POOL * D), BF16),
        shape((rows, D), F32),
        shape((rows, D), BF16),
        shape((rows, 3 * D), BF16),
        shape((slots, HEADS, 1, short_len), F32),
        shape((rows, D), BF16),
        shape((rows, D), F32),
        shape((POOL, 8, rows), jnp.int32),
        shape((POOL, rows, 128), jnp.int32),
    )

    gathered = (pltpu.HBM((ROW_END, D), BF16),) if number > 1 else ()
    *gathered, shifted, short, normed, qkv, lse, mixed, resid, lines, cols, vecs = pl.pallas_call(
        partial(attend_kernel, short_len, slots, number),
        out_shape=gathered + passed + (shape((8, D), F32),),
        in_specs=[SMEM, SMEM, VMEM] + [ANY] * number + [VMEM] * len(more),
        out_specs=(ANY,) * len(gathered) + (VMEM,) * 10,
        scratch_shapes=[
            pltpu.VMEM((ROW_END if number > 1 else ROW_F1, D), BF16),
            pltpu.VMEM((short_len, short_len), F32),
            pltpu.VMEM((short_len, short_len), F32),
            pltpu.VMEM((32, 16, D), BF16),
            pltpu.SemaphoreType.DMA((jobs,)),
            pltpu.SemaphoreType.DMA((33,)),
        ],
        compiler_params=pltpu.CompilerParams(vmem_limit_bytes=LIMIT_ATTEND),
        cost_estimate=pl.CostEstimate(flops=9_000_000_000, bytes_accessed=20_000_000, transcendentals=2_400_000),
        name="attend",
    )(coords, layouts, ids, *pieces, *more)
    stacked = pltpu.with_memory_space_constraint(gathered[0], pltpu.HBM) if number > 1 else pieces[0]
    keep_mid, send_mid, keep_deep, send_deep, table, dresid, small_deep = pl.pallas_call(
        partial(deep_kernel, count),
        out_shape=(
            shape((ROW_HALF - ROW_F1, half), BF16),
            shape((ROW_HALF - ROW_F1, half), BF16),
            shape((ROW_END - ROW_HALF, half), BF16),
            shape((ROW_END - ROW_HALF, half), BF16),
            shape((VOCAB, D), F32),
            shape((rows, D), F32),
            shape((8, D), F32),
        ),
        in_specs=[SMEM] + [VMEM] * 4 + [ANY],
        out_specs=(VMEM,) * 7,
        scratch_shapes=[
            pltpu.VMEM((ROW_END - ROW_F1, D), BF16),
            pltpu.VMEM((VOCAB, D), BF16),
            pltpu.VMEM((rows, D), BF16),
            pltpu.VMEM((rows, FF), BF16),
            pltpu.VMEM((rows, FF), F32),
            pltpu.VMEM((rows, D), BF16),
            pltpu.VMEM((POOL * rows, D), BF16),
            pltpu.VMEM((POOL * rows, VOCAB), BF16),
            pltpu.VMEM((POOL * rows, D), BF16),
            pltpu.VMEM((rows, D), F32),
            pltpu.VMEM((rows, FF), BF16),
            pltpu.VMEM((8, 8, D), F32),
            pltpu.SemaphoreType.DMA((4,)),
        ],
        compiler_params=pltpu.CompilerParams(vmem_limit_bytes=LIMIT_DEEP),
        name="deep",
    )(coords, vecs, cols, lines, resid, stacked)
    keep_att, send_att, dqkv = pl.pallas_call(
        partial(attend_back_kernel, short_len),
        out_shape=(
            shape((ROW_F1 - ROW_QKV, half), BF16),
            shape((ROW_F1 - ROW_QKV, half), BF16),
            shape((rows, 3 * D), BF16),
        ),
        in_specs=[SMEM, SMEM] + [VMEM] * 5 + [ANY],
        out_specs=(VMEM,) * 3,
        scratch_shapes=[
            pltpu.VMEM((D, D), BF16),
            pltpu.VMEM((short_len, short_len), F32),
            pltpu.VMEM((short_len, short_len), F32),
            pltpu.VMEM((rows, D), BF16),
            pltpu.VMEM((rows, D), BF16),
            pltpu.SemaphoreType.DMA,
        ],
        compiler_params=pltpu.CompilerParams(vmem_limit_bytes=LIMIT_BACK),
        cost_estimate=pl.CostEstimate(flops=11_000_000_000, bytes_accessed=20_000_000, transcendentals=2_400_000),
        name="attend_back",
    )(coords, layouts, dresid, normed, qkv, lse, mixed, stacked)
    if paired:
        recv_deep, recv_mid = swap_with(send_deep, core=1), swap_with(send_mid, core=1)
        sent = core_sum(coords, keep_deep, recv_deep)
        recv_att = swap_with(send_att, core=1)
        sent, recv_att, recv_mid, dqkv = lax.optimization_barrier((sent, recv_att, recv_mid, dqkv))
        sent = first_exchange(sent)
    keep_front, send_front, small = pl.pallas_call(
        front_back_kernel,
        out_shape=(shape((ROW_QKV, half), BF16), shape((ROW_QKV + 32, half), BF16), shape((8, D), F32)),
        in_specs=[SMEM] + [VMEM] * 8 + [ANY],
        out_specs=(VMEM,) * 3,
        scratch_shapes=[
            pltpu.VMEM((VOCAB, D), F32),
            pltpu.VMEM((ROW_O - ROW_P, D), BF16),
            pltpu.VMEM((rows, D), BF16),
            pltpu.SemaphoreType.DMA,
        ],
        compiler_params=pltpu.CompilerParams(vmem_limit_bytes=LIMIT_BACK),
        cost_estimate=pl.CostEstimate(flops=8_000_000_000, bytes_accessed=20_000_000, transcendentals=0),
        name="front_back",
    )(coords, vecs, small_deep, lines, dresid, shifted, short, dqkv, table, stacked)
    if not paired:
        front = jnp.concatenate([keep_front, send_front[:ROW_QKV]], 1)
        others = [
            jnp.concatenate(pair, 1)
            for pair in ((keep_att, send_att), (keep_mid, send_mid), (keep_deep, send_deep))
        ]
        return jnp.concatenate([front] + others, 0), small
    late = 5
    early = [array for k, array in enumerate(sent) if k != late]
    early, keep_front, send_front, small = lax.optimization_barrier((early, keep_front, send_front, small))
    sent = early[:late] + [sent[late]] + early[late:]
    received = [swap_with(send_front, core=1), recv_att, recv_mid]
    out_p, out_q = exchange_shapes(64)
    parts = pl.pallas_call(
        core_sum_front_kernel,
        out_shape=(out_p,) * 4 + (out_q,) * 4,
        in_specs=[SMEM] + [ANY] * 6 + [VMEM],
        out_specs=(VMEM,) * 8,
        scratch_shapes=[
            pltpu.VMEM((ROW_HALF, half), BF16),
            pltpu.VMEM((ROW_HALF + 32, half), BF16),
            pltpu.SemaphoreType.DMA((7,)),
        ],
        compiler_params=params,
        name="core_sum_front",
    )(coords, keep_front, keep_att, keep_mid, *received, small)
    return first_exchange(parts), sent


def exchange_shapes(extra):
    quarter = D // 4
    return (
        jax.ShapeDtypeStruct((4 * SCATTER_CUT + extra, quarter), BF16),
        jax.ShapeDtypeStruct((4 * (2 * SHARD - SCATTER_CUT), quarter), BF16),
    )


def core_sum(coords, keep, received):
    out_p, out_q = exchange_shapes(0)
    return pl.pallas_call(
        core_sum_kernel,
        out_shape=(out_p,) * 4 + (out_q,) * 4,
        in_specs=[SMEM] + [VMEM] * 2,
        out_specs=(VMEM,) * 8,
        compiler_params=pltpu.CompilerParams(vmem_limit_bytes=LIMIT),
        name="core_sum",
    )(coords, keep, received)


def first_exchange(parts):
    over = [parts[0]] + [swap_with(parts[k], line=k) for k in (1, 2, 3)]
    return over + [parts[4]] + [swap_with(parts[4 + k], zed=k) for k in (1, 2, 3)]


def swap_with(array, line=0, zed=0, core=0):
    lines, rest = lax.axis_size("dp"), lax.axis_size("fsdp")
    pairs = [
        (d * rest + f, (d ^ line) * rest + (f ^ (2 * zed + core)))
        for d in range(lines)
        for f in range(rest)
    ]
    return lax.ppermute(array, AXES, pairs)


def gather_pieces(block, vectors):
    start = lax.axis_index(AXES) * vectors.shape[1]
    own = lax.dynamic_update_slice(jnp.zeros((16, D), BF16), vectors, (0, start))
    first, second = jnp.concatenate([block[:GATHER_CUT], own], 0), block[GATHER_CUT:]
    along = jnp.concatenate([first] + [swap_with(first, zed=k) for k in (1, 2, 3)], 0)
    across = jnp.concatenate([second] + [swap_with(second, line=k) for k in (1, 2, 3)], 0)
    pieces = [along] + [swap_with(along, line=k) for k in (1, 2, 3)]
    pieces += [across] + [swap_with(across, zed=k) for k in (1, 2, 3)]
    return pieces + [swap_with(piece, core=1) for piece in pieces]


def scatter_sum(coords, front, deep):
    shape = jax.ShapeDtypeStruct
    params = pltpu.CompilerParams(vmem_limit_bytes=LIMIT)
    quarter = D // 4
    rest = 2 * SHARD - SCATTER_CUT
    parts = pl.pallas_call(
        first_sum_kernel,
        out_shape=(shape((2 * SCATTER_CUT + 64, quarter), BF16),) * 4 + (shape((2 * rest, quarter), BF16),) * 4,
        in_specs=[SMEM] + [VMEM] * 16,
        out_specs=(VMEM,) * 8,
        compiler_params=params,
        name="first_sum",
    )(coords, *front, *deep)
    second = [parts[0]] + [swap_with(parts[k], zed=k) for k in (1, 2, 3)]
    second += [parts[4]] + [swap_with(parts[4 + k], line=k) for k in (1, 2, 3)]
    *outs, small, squares = pl.pallas_call(
        last_sum_kernel,
        out_shape=(shape((SHARD, quarter), F32),) * 4 + (shape((8, D), F32), shape((8, quarter), F32)),
        in_specs=[SMEM] + [VMEM] * 8,
        out_specs=(VMEM,) * 6,
        scratch_shapes=[pltpu.VMEM((2 * SHARD, quarter), F32)],
        compiler_params=params,
        name="last_sum",
    )(coords, *second)
    squares = squares + swap_with(squares, core=1)
    quarters = [outs[0], swap_with(outs[1], line=2), swap_with(outs[2], core=1), swap_with(outs[3], line=2, core=1)]
    squares = (squares + swap_with(squares, line=1)) + (swap_with(squares, line=2) + swap_with(squares, line=3))
    squares = [squares] + [swap_with(squares, zed=k) for k in (1, 2, 3)]
    return quarters, small, squares


def shards(byte_ids, layouts, weights, vectors, m_weights, v_weights, m_vectors, v_vectors):
    devices = lax.axis_size(AXES)
    micro = byte_ids.shape[0]
    count = float(micro * layouts.shape[1] * devices * byte_ids.shape[2])
    lines, rest = lax.axis_size("dp"), lax.axis_size("fsdp")
    place = lax.axis_index("fsdp")
    coords = jnp.stack([lax.axis_index("dp"), place // 2, place % 2, lax.axis_index(AXES)]).astype(jnp.int32)
    paired = lines == 4 and rest == 8 and weights.shape[0] == SHARD
    weights_low = weights.astype(BF16)
    vectors_low = vectors.astype(BF16)
    width = vectors.shape[1]
    mine = lax.axis_index(AXES) * width
    flat_layouts = layouts.reshape(-1)
    ids = byte_ids.reshape(flat_layouts.shape[0], -1, POOL).transpose(2, 0, 1).reshape(POOL, -1)
    ids = jnp.pad(ids, ((0, 8 - POOL), (0, 0)))
    if paired:
        pieces = gather_pieces(weights_low, vectors_low)
        front, deep = device_grads(
            pieces, None, coords, ids, flat_layouts, count, True
        )
        quarters, small, squares = scatter_sum(coords, front, deep)
        like = [jax.ShapeDtypeStruct((1, 1), F32)] * 2
        like += [jax.ShapeDtypeStruct(weights.shape, F32)] * 3 + [jax.ShapeDtypeStruct(vectors.shape, F32)] * 3
        loss, grad_norm, *updated = pl.pallas_call(
            partial(update_kernel, count),
            out_shape=like,
            in_specs=[SMEM] + [VMEM] * 15,
            out_specs=[VMEM] * 8,
            compiler_params=pltpu.CompilerParams(vmem_limit_bytes=LIMIT),
            name="update",
        )(coords, *quarters, *squares, small, weights, m_weights, v_weights, vectors, m_vectors, v_vectors)
        return (loss[0, 0], grad_norm[0, 0], *updated)
    coords = coords * 0
    pieces = [lax.all_gather(weights_low, AXES, axis=0, tiled=True)]
    vecs = lax.all_gather(vectors_low, AXES, axis=1, tiled=True)
    vecs = jnp.pad(vecs.astype(F32), ((0, 2), (0, 0)))
    local, small = device_grads(pieces, vecs, coords, ids, flat_layouts, count, False)
    owned = lax.psum_scatter(local.astype(F32), AXES, scatter_dimension=0, tiled=True)
    small, squares = lax.psum((small, jnp.sum(owned * owned)), AXES)
    loss = small[6, 0] / count
    vec_grads = small[:6]
    owned_vecs = lax.dynamic_slice(vec_grads, (0, mine), (6, width))
    squares = squares + jnp.sum(vec_grads * vec_grads)
    grad_norm = jnp.sqrt(squares)
    factor = CLIP / jnp.maximum(grad_norm, CLIP)
    first_w, second_w, update_w = adam(weights, m_weights, v_weights, owned * factor, DECAY)
    first_v, second_v, update_v = adam(vectors, m_vectors, v_vectors, owned_vecs * factor, 0.0)
    return (loss, grad_norm, first_w, second_w, update_w, first_v, second_v, update_v)


def solution(mesh):
    in_specs = (
        P(None, AXES, None),
        P(None, AXES),
        P(AXES, None),
        P(None, AXES),
        P(AXES, None),
        P(AXES, None),
        P(None, AXES),
        P(None, AXES),
    )
    out_specs = (
        P(),
        P(),
        P(AXES, None),
        P(AXES, None),
        P(AXES, None),
        P(None, AXES),
        P(None, AXES),
        P(None, AXES),
    )
    return jax.shard_map(shards, mesh=mesh, in_specs=in_specs, out_specs=out_specs, check_vma=False)
```

```python
from functools import partial

import jax
import jax.numpy as jnp
from jax import lax
from jax.experimental import pallas as pl
from jax.experimental.pallas import tpu as pltpu
from jax.sharding import PartitionSpec as P

D = 512
HEADS = 8
HEAD = 64
FF = 2048
VOCAB = 256
POOL = 3

EPS_NORM = 1e-05
EPS_ADAM = 1e-08
CLIP = 0.2
RATE = 0.03
DECAY = 0.1
BETA = 0.5
STEP = 3
NEGATIVE = -1000000000.0

F32 = jnp.float32
BF16 = jnp.bfloat16

ROW_E = 0
ROW_P = VOCAB
ROW_QKV = ROW_P + POOL * D
ROW_O = ROW_QKV + 3 * D
ROW_F1 = ROW_O + D
ROW_F2 = ROW_F1 + FF
ROW_U = ROW_F2 + FF
ROW_H = ROW_U + POOL * D
ROW_END = ROW_H + VOCAB
ROW_HALF = ROW_END // 2
assert ROW_HALF - ROW_F1 == FF // 2

AXES = ("dp", "fsdp")
SHARD = ROW_END // 32
GATHER_CUT = 208
SCATTER_CUT = 400


def nn(left, right):
    return lax.dot_general(left, right, (((1,), (0,)), ((), ())), preferred_element_type=F32)


def nt(left, right):
    return lax.dot_general(left, right, (((1,), (1,)), ((), ())), preferred_element_type=F32)


def tn(left, right):
    return lax.dot_general(left, right, (((0,), (0,)), ((), ())), preferred_element_type=F32)


def norm_parts(values):
    center = values - jnp.mean(values, -1, keepdims=True)
    spread = jnp.mean(center * center, -1, keepdims=True)
    scale = lax.rsqrt(spread + EPS_NORM)
    return center * scale, scale


def norm_back(unit, scale, gain, grad):
    inner = grad * gain
    mean_inner = jnp.mean(inner, -1, keepdims=True)
    mean_cross = jnp.mean(inner * unit, -1, keepdims=True)
    return scale * (inner - mean_inner - unit * mean_cross)


def fold_rows(values):
    return jnp.sum(values.reshape(values.shape[0] // 8, 8, values.shape[1]), 0)


def one_hot_rows(ids):
    lanes = lax.broadcasted_iota(jnp.int32, (ids.shape[0], VOCAB), 1)
    return jnp.where(lanes == ids, 1.0, 0.0).astype(BF16)


def one_hot_cols(ids):
    lines = lax.broadcasted_iota(jnp.int32, (VOCAB, ids.shape[1]), 0)
    return jnp.where(lines == ids, 1.0, 0.0).astype(BF16)


def rows_of(index, size):
    return pl.ds(pl.multiple_of(index * size, size), size)


def gathered_parts(coords_ref):
    dp, z, core = coords_ref[0], coords_ref[1], coords_ref[2]
    for side in range(2):
        for k in range(4):
            for part in range(4):
                for kind in range(2):
                    d, e = (k, part) if kind == 0 else (part, k)
                    yield side * 8 + kind * 4 + k, part, kind, (dp ^ d) * 8 + (z ^ e) * 2 + (core ^ side)


class FetchGathered:
    def __init__(self, pieces, coords_ref, w_ref, sems, high):
        self.jobs = []
        for number, (piece, part, kind, shard) in enumerate(gathered_parts(coords_ref)):
            begin, size, step = ((0, GATHER_CUT, GATHER_CUT + 16), (GATHER_CUT, SHARD - GATHER_CUT, SHARD - GATHER_CUT))[kind]
            copy = pltpu.make_async_copy(
                pieces[piece].at[pl.ds(part * step, size)],
                w_ref.at[pl.ds(pl.multiple_of(shard * SHARD + begin, 16), size)],
                sems.at[number],
            )
            self.jobs.append((shard * SHARD < high, copy))

    def start(self, first):
        for early, copy in self.jobs:
            pl.when(early if first else jnp.logical_not(early))(copy.start)

    def wait(self, first):
        for early, copy in self.jobs:
            pl.when(early if first else jnp.logical_not(early))(copy.wait)


def fetch_rows(w_hbm, low, high, w_ref, sem):
    copy = pltpu.make_async_copy(w_hbm.at[pl.ds(low, high - low)], w_ref, sem)
    copy.start()
    return copy


def attend_kernel(short_len, slots, pieces, coords_ref, lay_ref, ids_ref, *refs):
    w_hbm, refs = refs[:pieces], refs[pieces:]
    if pieces == 1:
        vec_in_ref, refs = refs[0], refs[1:]
    if pieces > 1:
        w_out, refs = refs[0], refs[1:]
    (shifted_ref, short_ref, normed_ref, qkv_ref, lse_ref, mixed_ref, resid_ref, lines_ref, cols_ref, vec_ref,
     w_ref, dist_ref, mask_ref, part_ref, sems, part_sems) = refs
    rows = short_len * slots
    if pieces > 1:
        fetch = FetchGathered(w_hbm, coords_ref, w_ref, sems, ROW_F1)
        fetch.start(True)
    else:
        fetch = fetch_rows(w_hbm[0], 0, ROW_F1, w_ref, sems.at[0])
    copies = []
    if pieces > 1:
        for piece, part, kind, _ in gathered_parts(coords_ref):
            if kind == 0:
                place = pl.ds(part * (GATHER_CUT + 16) + GATHER_CUT, 16)
                number = len(copies)
                copies.append(
                    pltpu.make_async_copy(w_hbm[piece].at[place], part_ref.at[number], part_sems.at[number])
                )
        for copy in copies:
            copy.start()

    ids = ids_ref[...]
    group = lax.broadcasted_iota(jnp.int32, (1, rows), 1)
    starts = group == 0
    for slot in range(slots):
        starts = starts | (group == slot * short_len)
        starts = starts | ((group == slot * short_len + short_len // 2) & (lay_ref[slot] == 1))
    ends = group == rows - 1
    for slot in range(slots):
        ends = ends | (group == (slot + 1) * short_len - 1)
        ends = ends | ((group == slot * short_len + short_len // 2 - 1) & (lay_ref[slot] == 1))
    before, after = pltpu.roll(ids, 1, 1), pltpu.roll(ids, rows - 1, 1)
    own = [ids[j : j + 1] for j in range(POOL)]
    back = [jnp.where(starts, -1, before[1:2]), jnp.where(starts, -1, before[2:3]), ids[0:1]]
    ahead = [ids[1:2], ids[2:3], jnp.where(ends, -1, after[0:1])]
    for j in range(POOL):
        for kind, line in enumerate((own[j], back[j], ahead[j])):
            lines_ref[j, kind : kind + 1, :] = line
        lines_ref[j, 3:, :] = jnp.zeros((5, rows), jnp.int32)
        padded = jnp.concatenate([lines_ref[j].astype(F32), jnp.zeros((120, rows), F32)], 0)
        cols_ref[j] = padded.T.astype(jnp.int32)

    for copy in copies:
        copy.wait()
    if pieces > 1:
        both = part_ref[0].astype(F32)
        for k in range(1, len(copies)):
            both = both + part_ref[k].astype(F32)
        vec_ref[...] = both[:8]
        fetch.wait(True)
        fetch.start(False)
    else:
        vec_ref[...] = vec_in_ref[...]
        fetch.wait()
    gain, offset = vec_ref[0:1, :], vec_ref[1:2, :]

    def shift_step(j, carry):
        lanes = rows_of(j, D)
        hot = one_hot_rows(cols_ref[j, :, 1:2])
        shifted_ref[:, lanes] = nn(hot, w_ref[ROW_E:ROW_P, :]).astype(BF16)
        return carry

    lax.fori_loop(0, POOL, shift_step, 0)

    def short_step(block, carry):
        at = rows_of(block, rows // 2)
        short = nn(shifted_ref[at, :], w_ref[ROW_P:ROW_QKV, :])
        short_ref[at, :] = short
        unit, _ = norm_parts(short)
        normed_ref[at, :] = (unit * gain + offset).astype(BF16)
        qkv_ref[at, :] = nt(normed_ref[at, :], w_ref[ROW_QKV:ROW_O, :]).astype(BF16)
        return carry

    lax.fori_loop(0, 2, short_step, 0)
    if pieces > 1:
        fetch.wait(False)
        leave = pltpu.make_async_copy(w_ref, w_out, part_sems.at[len(copies)])
        leave.start()

    left_lanes = lax.broadcasted_iota(jnp.int32, (short_len, 2 * HEAD), 1) < HEAD

    def slot_step(index, carry):
        slot, lower = index // 2, index % 2
        at = rows_of(slot, short_len)

        @pl.when(lower == 0)
        def _():
            attention_bias(lay_ref[slot], short_len, dist_ref, mask_ref)

        for pair in range(HEADS // 4):
            lanes, lanes_k, lanes_v = (pair_lanes(part, lower, pair) for part in range(3))
            queries = qkv_ref[at, lanes] * jnp.asarray(0.125, BF16)
            keys, values = qkv_ref[at, lanes_k], qkv_ref[at, lanes_v]
            mixed = jnp.zeros((short_len, 2 * HEAD), F32)
            for side in range(2):
                head = lower * (HEADS // 2) + pair * 2 + side
                slope = head_slope(lower, pair * 2 + side)
                scores = nt(one_side(left_lanes, side, keys), queries)
                scores = scores + jnp.minimum(dist_ref[...] * slope, mask_ref[...])
                top = jnp.max(scores, 0, keepdims=True)
                expo = jnp.exp(scores - top)
                total = jnp.sum(expo, 0, keepdims=True)
                lse_ref[slot, head] = top + jnp.log(total)
                probs = (expo * (1.0 / total)).astype(BF16)
                mixed = mixed + tn(probs, one_side(left_lanes, side, values))
            mixed_ref[at, lanes] = mixed.astype(BF16)
        return carry

    lax.fori_loop(0, 2 * slots, slot_step, 0)
    resid_ref[...] = short_ref[...] + nn(mixed_ref[...], w_ref[ROW_O:ROW_F1, :])
    if pieces > 1:
        leave.wait()


def head_slope(lower, head):
    return jnp.where(lower == 0, *(2.0 ** (-8.0 * (head + more + 1.0) / HEADS) for more in (0, HEADS // 2)))


def pair_lanes(part, lower, pair):
    return pl.ds(pl.multiple_of(part * D + lower * (D // 2) + pair * 2 * HEAD, 2 * HEAD), 2 * HEAD)


def one_side(left_lanes, side, array):
    zero = jnp.zeros_like(array)
    return jnp.where(left_lanes, array, zero) if side == 0 else jnp.where(left_lanes, zero, array)


def attention_bias(layout, short_len, dist_ref, mask_ref):
    key = lax.broadcasted_iota(jnp.int32, (short_len, short_len), 0)
    query = lax.broadcasted_iota(jnp.int32, (short_len, short_len), 1)
    half = jnp.where(layout == 1, short_len // 2, short_len)
    allowed = (key <= query) & ((key >= half) == (query >= half))
    dist_ref[...] = (key - query).astype(F32)
    mask_ref[...] = jnp.where(allowed, 0.0, NEGATIVE)


def gelu_parts(hidden):
    size = jnp.abs(hidden)
    near = 1.0 / (1.0 + (0.3275911 * 0.7071067811865476) * size)
    bell = jnp.exp(hidden * hidden * -0.5)
    tail = near * (0.127414796 + near * (-0.142248368 + near * (0.7107068705 + near * (-0.7265760135 + near * 0.5307027145))))
    tail = tail * bell
    cdf = jnp.where(hidden >= 0.0, 1.0 - tail, tail)
    return hidden * cdf, cdf + hidden * bell * 0.3989422804014327


def split_store(keep_ref, send_ref, core, rows, values):
    half = D // 2
    low, high = values[:, :half].astype(BF16), values[:, half:].astype(BF16)
    keep_ref[rows, :] = jnp.where(core == 0, low, high)
    send_ref[rows, :] = jnp.where(core == 0, high, low)


def deep_kernel(count, coords_ref, vec_ref, cols_ref, lines_ref, resid_ref, w_hbm, *refs):
    (keep_mid, send_mid, keep_ref, send_ref, table_ref, dresid_ref, small_ref,
     w_ref, e_ref, normed_ref, act_ref, slope_ref, deep_ref, final_ref, dlog_ref, dup_ref,
     ddeep_ref, dhid_ref, sums_ref, sems) = refs
    rows = resid_ref.shape[0]
    base = ROW_F1
    core = coords_ref[2]
    stages = []
    for k, (low, high) in enumerate(((ROW_F1, ROW_F2), (ROW_F2, ROW_U), (ROW_U, ROW_END))):
        stages.append([fetch_rows(w_hbm, low, high, w_ref.at[pl.ds(low - base, high - low)], sems.at[k])])
    stages[2].append(fetch_rows(w_hbm, 0, VOCAB, e_ref, sems.at[3]))
    f1, f2, up, head = ROW_F1 - base, ROW_F2 - base, ROW_U - base, ROW_H - base
    gain2, offset2 = vec_ref[2:3, :], vec_ref[3:4, :]
    gain_f, offset_f = vec_ref[4:5, :], vec_ref[5:6, :]
    wide = 1024
    sums_ref[...] = jnp.zeros_like(sums_ref)

    unit, _ = norm_parts(resid_ref[...])
    normed_ref[...] = (unit * gain2 + offset2).astype(BF16)
    for copy in stages[0]:
        copy.wait()

    def hidden_step(chunk, carry):
        lanes = rows_of(chunk, wide)
        hidden = nt(normed_ref[...], w_ref[pl.ds(pl.multiple_of(f1 + chunk * wide, 16), wide), :])
        act, slope = gelu_parts(hidden)
        act_ref[:, lanes] = act.astype(BF16)
        slope_ref[:, lanes] = slope
        return carry

    lax.fori_loop(0, FF // wide, hidden_step, 0)
    for copy in stages[1]:
        copy.wait()

    def deep_step(block, carry):
        at = rows_of(block, rows // 2)
        deep_ref[at, :] = (resid_ref[at, :] + nn(act_ref[at, :], w_ref[f2 : f2 + FF, :])).astype(BF16)
        return carry

    lax.fori_loop(0, 2, deep_step, 0)
    for copy in stages[2]:
        copy.wait()
    ddeep_ref[...] = jnp.zeros_like(ddeep_ref)
    table_ref[...] = jnp.zeros_like(table_ref)

    def head_step(j, carry):
        there = rows_of(j, rows)
        up_rows = pl.ds(pl.multiple_of(up + j * D, 16), D)
        columns = cols_ref[j]
        joined = nn(one_hot_rows(columns[:, 0:1]), e_ref[0:VOCAB, :]) + nt(deep_ref[...], w_ref[up_rows, :])
        unit, scale = norm_parts(joined)
        final = (unit * gain_f + offset_f).astype(BF16)
        final_ref[there, :] = final
        logits = nt(final, w_ref[head : head + VOCAB, :])
        nexts = columns[:, 2:3]
        lanes = lax.broadcasted_iota(jnp.int32, logits.shape, 1)
        target = jnp.where(lanes == nexts, 1.0, 0.0)
        valid = jnp.where(nexts >= 0, 1.0, 0.0)
        peak = jnp.max(logits, -1, keepdims=True)
        expo = jnp.exp(logits - peak)
        total = jnp.sum(expo, -1, keepdims=True)
        picked = jnp.sum(logits * target, -1, keepdims=True)
        losses = valid * (peak + jnp.log(total) - picked)
        dlogits = ((valid / count) * (expo * (1.0 / total) - target)).astype(BF16)
        dlog_ref[there, :] = dlogits
        dfinal = nn(dlogits, w_ref[head : head + VOCAB, :])
        dup = norm_back(unit, scale, gain_f, dfinal).astype(BF16)
        dup_ref[there, :] = dup
        ddeep_ref[...] += nn(dup, w_ref[up_rows, :])
        sums_ref[4, :, :] += fold_rows(dfinal * unit)
        sums_ref[5, :, :] += fold_rows(dfinal)
        sums_ref[6, :, :] += jnp.broadcast_to(fold_rows(losses), (8, D))
        return carry

    lax.fori_loop(0, POOL, head_step, 0)

    out_f2, out_up, out_head = ROW_F2 - ROW_HALF, ROW_U - ROW_HALF, ROW_H - ROW_HALF
    split_store(keep_ref, send_ref, core, pl.ds(out_head, VOCAB), tn(dlog_ref[...], final_ref[...]))

    def dup_step(j, carry):
        there = rows_of(j, rows)
        dup = dup_ref[there, :]
        out = pl.ds(pl.multiple_of(out_up + j * D, D), D)
        split_store(keep_ref, send_ref, core, out, tn(dup, deep_ref[...]))
        table_ref[...] += nn(one_hot_cols(lines_ref[j, 0:1, :]), dup)
        return carry

    lax.fori_loop(0, POOL, dup_step, 0)

    deep_ref[...] = ddeep_ref[...].astype(BF16)

    def dff_step(chunk, carry):
        lanes = rows_of(chunk, wide)
        dact = nt(deep_ref[...], w_ref[pl.ds(pl.multiple_of(f2 + chunk * wide, 16), wide), :])
        dhid_ref[:, lanes] = (dact * slope_ref[:, lanes]).astype(BF16)
        grad = tn(dhid_ref[:, lanes], normed_ref[...])

        @pl.when(chunk == 0)
        def _():
            split_store(keep_mid, send_mid, core, slice(0, wide), grad)

        @pl.when(chunk > 0)
        def _():
            split_store(keep_ref, send_ref, core, slice(0, wide), grad)

        out = pl.ds(pl.multiple_of(out_f2 + chunk * wide, wide), wide)
        split_store(keep_ref, send_ref, core, out, tn(act_ref[:, lanes], deep_ref[...]))
        return carry

    lax.fori_loop(0, FF // wide, dff_step, 0)
    def dnorm_step(block, carry):
        at = rows_of(block, rows // 2)
        dnormed = nn(dhid_ref[at, :], w_ref[f1 : f1 + FF, :])
        unit, scale = norm_parts(resid_ref[at, :])
        dresid_ref[at, :] = ddeep_ref[at, :] + norm_back(unit, scale, gain2, dnormed)
        sums_ref[2, :, :] += fold_rows(dnormed * unit)
        sums_ref[3, :, :] += fold_rows(dnormed)
        return carry

    lax.fori_loop(0, 2, dnorm_step, 0)
    for k in range(8):
        small_ref[k : k + 1, :] = jnp.sum(sums_ref[k], 0, keepdims=True)


def back_kernel(short_len, coords_ref, lay_ref, vec_ref, deep_small_ref, lines_ref, dresid_ref, normed_ref, qkv_ref, lse_ref,
                mixed_ref, shifted_ref, short_ref, table_in, w_hbm, *refs):
    (keep_ref, send_ref, small_ref,
     table_ref, w_ref, dist_ref, mask_ref, dbranch_ref, dmix_ref, dqkv_ref, dshort_ref, sem) = refs
    core = coords_ref[2]
    rows = dresid_ref.shape[0]
    fetch = fetch_rows(w_hbm, ROW_P, ROW_F1, w_ref, sem)
    dbranch_ref[...] = dresid_ref[...].astype(BF16)
    fetch.wait()
    dmix_ref[...] = nt(dbranch_ref[...], w_ref[ROW_O - ROW_P :, :]).astype(BF16)

    left_lanes = lax.broadcasted_iota(jnp.int32, (short_len, 2 * HEAD), 1) < HEAD

    def slot_step(index, carry):
        slot, lower = index // 2, index % 2
        at = rows_of(slot, short_len)

        @pl.when(lower == 0)
        def _():
            attention_bias(lay_ref[slot], short_len, dist_ref, mask_ref)

        for pair in range(HEADS // 4):
            lanes, lanes_k, lanes_v = (pair_lanes(part, lower, pair) for part in range(3))
            queries, keys, values = qkv_ref[at, lanes], qkv_ref[at, lanes_k], qkv_ref[at, lanes_v]
            dmix = dmix_ref[at, lanes]
            scaled = queries * jnp.asarray(0.125, BF16)
            dqueries, dkeys, dvalues = (jnp.zeros((short_len, 2 * HEAD), F32) for _ in range(3))
            for side in range(2):
                head = lower * (HEADS // 2) + pair * 2 + side
                slope = head_slope(lower, pair * 2 + side)
                keys_here = one_side(left_lanes, side, keys)
                scores = nt(keys_here, scaled)
                scores = scores + jnp.minimum(dist_ref[...] * slope, mask_ref[...])
                probs = jnp.exp(scores - lse_ref[slot, head])
                dprobs = nt(one_side(left_lanes, side, values), dmix)
                delta = jnp.sum(dprobs * probs, 0, keepdims=True)
                dscores = (probs * (dprobs - delta) * 0.125).astype(BF16)
                dvalues = dvalues + nn(probs.astype(BF16), one_side(left_lanes, side, dmix))
                dkeys = dkeys + nn(dscores, one_side(left_lanes, side, queries))
                dqueries = dqueries + tn(dscores, keys_here)
            dqkv_ref[at, lanes] = dqueries.astype(BF16)
            dqkv_ref[at, lanes_k] = dkeys.astype(BF16)
            dqkv_ref[at, lanes_v] = dvalues.astype(BF16)
        return carry

    lax.fori_loop(0, 2 * lse_ref.shape[0], slot_step, 0)
    split_store(keep_ref, send_ref, core, pl.ds(ROW_O, D), tn(mixed_ref[...], dbranch_ref[...]))

    def dproj_step(part, carry):
        grad = tn(dqkv_ref[:, rows_of(part, D)], normed_ref[...])
        split_store(keep_ref, send_ref, core, pl.ds(pl.multiple_of(ROW_QKV + part * D, 16), D), grad)
        return carry

    lax.fori_loop(0, 3, dproj_step, 0)

    gain = vec_ref[0:1, :]
    dnormed = nn(dqkv_ref[...], w_ref[ROW_QKV - ROW_P : ROW_O - ROW_P, :])
    unit, scale = norm_parts(short_ref[...])
    dshort_ref[...] = (dresid_ref[...] + norm_back(unit, scale, gain, dnormed)).astype(BF16)
    small_ref[...] = deep_small_ref[...]
    for k, values in enumerate((dnormed * unit, dnormed)):
        small_ref[k : k + 1, :] = jnp.sum(fold_rows(values), 0, keepdims=True)
    half = D // 2
    for k in range(2):
        send_ref[ROW_F1 + 16 * k : ROW_F1 + 16 * (k + 1), :] = two_parts(small_ref[:, k * half : (k + 1) * half])
    table_ref[...] = table_in[...]

    def pool_step(j, carry):
        dshift = nt(dshort_ref[...], w_ref[rows_of(j, D), :]).astype(BF16)
        table_ref[...] += nn(one_hot_cols(lines_ref[j, 1:2, :]), dshift)
        out = pl.ds(pl.multiple_of(ROW_P + j * D, 16), D)
        split_store(keep_ref, send_ref, core, out, tn(shifted_ref[:, rows_of(j, D)], dshort_ref[...]))
        return carry

    lax.fori_loop(0, POOL, pool_step, 0)
    split_store(keep_ref, send_ref, core, pl.ds(ROW_E, VOCAB), table_ref[...])


def two_parts(values):
    high = values.astype(BF16)
    low = (values - high.astype(F32)).astype(BF16)
    return jnp.concatenate([high.astype(F32), low.astype(F32)], 0).astype(BF16)


def one_value(parts):
    parts = parts.astype(F32)
    return parts[:8] + parts[8:]


def lay_out(coords_ref, keep_ref, recv_ref, p_refs, q_refs):
    dp, z = coords_ref[0], coords_ref[1]
    quarter = D // 4
    line = 2 * SHARD
    rest = line - SCATTER_CUT

    def total(column, x, zed, begin, size):
        at = pl.ds(pl.multiple_of(x * (4 * line) + zed * line + begin, 16), size)
        lanes = pl.ds(pl.multiple_of(column * quarter, quarter), quarter)
        return (keep_ref[at, lanes].astype(F32) + recv_ref[at, lanes].astype(F32)).astype(BF16)

    def part_step(part, carry):
        for k in range(4):
            there = dp ^ k
            out = pl.ds(pl.multiple_of(part * SCATTER_CUT, 16), SCATTER_CUT)
            p_refs[k][out, :] = total(there // 2, there % 2, part, 0, SCATTER_CUT)
            out = pl.ds(pl.multiple_of(part * rest, 16), rest)
            q_refs[k][out, :] = total(part // 2, part % 2, z ^ k, SCATTER_CUT, rest)
        return carry

    lax.fori_loop(0, 4, part_step, 0)


def core_sum_kernel(coords_ref, keep_ref, recv_ref, *out_refs):
    lay_out(coords_ref, keep_ref, recv_ref, out_refs[:4], out_refs[4:])


def core_sum_front_kernel(coords_ref, keep_front, keep_mid, recv_front, recv_mid, small_ref, *refs):
    out_refs, (keep_ref, recv_ref, sems) = refs[:8], refs[8:]
    copies = [
        pltpu.make_async_copy(source, target, sems.at[k])
        for k, (source, target) in enumerate((
            (keep_mid, keep_ref.at[pl.ds(ROW_F1, ROW_HALF - ROW_F1)]),
            (recv_mid, recv_ref.at[pl.ds(ROW_F1, ROW_HALF - ROW_F1)]),
            (keep_front, keep_ref.at[pl.ds(0, ROW_F1)]),
            (recv_front.at[pl.ds(0, ROW_F1)], recv_ref.at[pl.ds(0, ROW_F1)]),
            (recv_front.at[pl.ds(ROW_F1, 32)], recv_ref.at[pl.ds(ROW_HALF, 32)]),
        ))
    ]
    for copy in copies:
        copy.start()
    for copy in copies:
        copy.wait()
    lay_out(coords_ref, keep_ref, recv_ref, out_refs[:4], out_refs[4:])
    quarter = D // 4
    for k in range(2):
        both = small_ref[:, 2 * k * quarter : 2 * (k + 1) * quarter] + one_value(
            recv_ref[ROW_HALF + 16 * k : ROW_HALF + 16 * (k + 1), :]
        )
        for side in range(2):
            parts = two_parts(both[:, side * quarter : (side + 1) * quarter])
            row = 4 * SCATTER_CUT + 16 * (2 * k + side)
            for p_ref in out_refs[:4]:
                p_ref[row : row + 16, :] = parts


def sum_of(refs, row, size):
    at = pl.ds(pl.multiple_of(row, 16), size)
    return (refs[0][at, :].astype(F32) + refs[1][at, :].astype(F32)) + (
        refs[2][at, :].astype(F32) + refs[3][at, :].astype(F32)
    )


def first_sum_kernel(coords_ref, *refs):
    sources = ((refs[0:4], refs[4:8]), (refs[8:12], refs[12:16]))
    s_refs, t_refs = refs[16:20], refs[20:24]
    dp, z = coords_ref[0], coords_ref[1]
    rest = 2 * SHARD - SCATTER_CUT
    for half, (p_refs, q_refs) in enumerate(sources):
        for k in range(4):
            s_refs[k][half * SCATTER_CUT : (half + 1) * SCATTER_CUT, :] = sum_of(
                p_refs, (z ^ k) * SCATTER_CUT, SCATTER_CUT
            ).astype(BF16)
            t_refs[k][half * rest : (half + 1) * rest, :] = sum_of(q_refs, (dp ^ k) * rest, rest).astype(BF16)
    for k in range(4):
        row = 4 * SCATTER_CUT + 16 * k
        value = sum(one_value(ref[row : row + 16, :]) for ref in sources[0][0])
        parts = two_parts(value)
        for s_ref in s_refs:
            s_ref[2 * SCATTER_CUT + 16 * k : 2 * SCATTER_CUT + 16 * (k + 1), :] = parts


def last_sum_kernel(coords_ref, *refs):
    s_refs, t_refs, out_refs, (small_ref, square_ref, sum_ref) = refs[:4], refs[4:8], refs[8:12], refs[12:]
    y, core = coords_ref[0] // 2, coords_ref[2]
    rest = 2 * SHARD - SCATTER_CUT
    squares = jnp.zeros((8, D // 4), F32)
    for k in range(2):
        half = y ^ k
        first = sum_of(s_refs, half * SCATTER_CUT, SCATTER_CUT)
        second = sum_of(t_refs, half * rest, rest)
        squares = squares + fold_rows(first * first) + fold_rows(second * second)
        sum_ref[0:SCATTER_CUT, :] = first
        sum_ref[SCATTER_CUT:, :] = second
        for other in range(2):
            out_refs[2 * other + k][...] = sum_ref[pl.ds(pl.multiple_of((core ^ other) * SHARD, 8), SHARD), :]
    for k in range(4):
        row = 2 * SCATTER_CUT + 16 * k
        small_ref[:, k * (D // 4) : (k + 1) * (D // 4)] = sum(
            one_value(ref[row : row + 16, :]) for ref in s_refs
        )
    square_ref[...] = squares


def adam(param, first_m, second_m, grad, decay):
    first_new = BETA * first_m + (1.0 - BETA) * grad
    second_new = BETA * second_m + (1.0 - BETA) * grad * grad
    correct = 1.0 - BETA**STEP
    update = -RATE * (
        first_new / correct / (jnp.sqrt(second_new / correct) + EPS_ADAM) + decay * param
    )
    return (first_new, second_new, update)


def update_kernel(count, coords_ref, g0, g1, g2, g3, q0, q1, q2, q3, small_ref, w_ref, mw_ref, vw_ref, w_vec, m_vec, v_vec,
                  loss_ref, norm_ref, mw_out, vw_out, uw_out, m_out, v_out, u_out):
    y, core, mine = coords_ref[0] // 2, coords_ref[2], coords_ref[3]
    small = small_ref[...]
    line = lax.broadcasted_iota(jnp.int32, small.shape, 0)
    gradient = jnp.where(line < 6, small, 0.0)
    squares = (q0[...] + q1[...]) + (q2[...] + q3[...])

    def whole(values):
        return jnp.sum(jnp.sum(values, 0, keepdims=True), 1, keepdims=True)

    norm = jnp.sqrt(whole(squares) + whole(gradient * gradient))
    factor = CLIP / jnp.maximum(norm, CLIP)
    norm_ref[...] = norm
    loss_ref[...] = small[6:7, 0:1] / count
    quarter = D // 4
    for k, grad_ref in enumerate((g0, g1, g2, g3)):
        place = (core ^ (k // 2)) * 2 + (y ^ (k % 2))
        lanes = pl.ds(pl.multiple_of(place * quarter, quarter), quarter)
        mw_out[:, lanes], vw_out[:, lanes], uw_out[:, lanes] = adam(
            w_ref[:, lanes], mw_ref[:, lanes], vw_ref[:, lanes], grad_ref[...] * factor, DECAY
        )
    width = w_vec.shape[1]
    owned = pltpu.roll(gradient, lax.rem(small.shape[1] - mine * width, small.shape[1]), 1)[:6, :width]
    m_out[...], v_out[...], u_out[...] = adam(w_vec[...], m_vec[...], v_vec[...], owned * factor, 0.0)


VMEM = pl.BlockSpec(memory_space=pltpu.VMEM)
SMEM = pl.BlockSpec(memory_space=pltpu.SMEM)
ANY = pl.BlockSpec(memory_space=pl.ANY)
MIB = 1024 * 1024
LIMIT = 24 * MIB
LIMIT_ATTEND = 30 * MIB
LIMIT_DEEP = 40 * MIB
LIMIT_BACK = 24 * MIB


def device_grads(pieces, vecs, coords, ids, layouts, count, paired):
    slots = layouts.shape[0]
    rows = ids.shape[1]
    short_len = rows // slots
    shape = jax.ShapeDtypeStruct
    params = pltpu.CompilerParams(vmem_limit_bytes=LIMIT)
    number = len(pieces)
    pieces = [pltpu.with_memory_space_constraint(piece, pltpu.HBM) for piece in pieces]
    jobs = 64 if number > 1 else 1
    more = [] if vecs is None else [vecs]
    half = D // 2
    passed = (
        shape((rows, POOL * D), BF16),
        shape((rows, D), F32),
        shape((rows, D), BF16),
        shape((rows, 3 * D), BF16),
        shape((slots, HEADS, 1, short_len), F32),
        shape((rows, D), BF16),
        shape((rows, D), F32),
        shape((POOL, 8, rows), jnp.int32),
        shape((POOL, rows, 128), jnp.int32),
    )

    gathered = (pltpu.HBM((ROW_END, D), BF16),) if number > 1 else ()
    *gathered, shifted, short, normed, qkv, lse, mixed, resid, lines, cols, vecs = pl.pallas_call(
        partial(attend_kernel, short_len, slots, number),
        out_shape=gathered + passed + (shape((8, D), F32),),
        in_specs=[SMEM, SMEM, VMEM] + [ANY] * number + [VMEM] * len(more),
        out_specs=(ANY,) * len(gathered) + (VMEM,) * 10,
        scratch_shapes=[
            pltpu.VMEM((ROW_END if number > 1 else ROW_F1, D), BF16),
            pltpu.VMEM((short_len, short_len), F32),
            pltpu.VMEM((short_len, short_len), F32),
            pltpu.VMEM((32, 16, D), BF16),
            pltpu.SemaphoreType.DMA((jobs,)),
            pltpu.SemaphoreType.DMA((33,)),
        ],
        compiler_params=pltpu.CompilerParams(vmem_limit_bytes=LIMIT_ATTEND),
        cost_estimate=pl.CostEstimate(flops=9_000_000_000, bytes_accessed=20_000_000, transcendentals=2_400_000),
        name="attend",
    )(coords, layouts, ids, *pieces, *more)
    stacked = pltpu.with_memory_space_constraint(gathered[0], pltpu.HBM) if number > 1 else pieces[0]
    keep_mid, send_mid, keep_deep, send_deep, table, dresid, small_deep = pl.pallas_call(
        partial(deep_kernel, count),
        out_shape=(
            shape((ROW_HALF - ROW_F1, half), BF16),
            shape((ROW_HALF - ROW_F1, half), BF16),
            shape((ROW_END - ROW_HALF, half), BF16),
            shape((ROW_END - ROW_HALF, half), BF16),
            shape((VOCAB, D), F32),
            shape((rows, D), F32),
            shape((8, D), F32),
        ),
        in_specs=[SMEM] + [VMEM] * 4 + [ANY],
        out_specs=(VMEM,) * 7,
        scratch_shapes=[
            pltpu.VMEM((ROW_END - ROW_F1, D), BF16),
            pltpu.VMEM((VOCAB, D), BF16),
            pltpu.VMEM((rows, D), BF16),
            pltpu.VMEM((rows, FF), BF16),
            pltpu.VMEM((rows, FF), F32),
            pltpu.VMEM((rows, D), BF16),
            pltpu.VMEM((POOL * rows, D), BF16),
            pltpu.VMEM((POOL * rows, VOCAB), BF16),
            pltpu.VMEM((POOL * rows, D), BF16),
            pltpu.VMEM((rows, D), F32),
            pltpu.VMEM((rows, FF), BF16),
            pltpu.VMEM((8, 8, D), F32),
            pltpu.SemaphoreType.DMA((4,)),
        ],
        compiler_params=pltpu.CompilerParams(vmem_limit_bytes=LIMIT_DEEP),
        name="deep",
    )(coords, vecs, cols, lines, resid, stacked)
    if paired:
        recv_mid, recv_deep = swap_with(send_mid, core=1), swap_with(send_deep, core=1)
        sent = core_sum(coords, keep_deep, recv_deep)
        sent, recv_mid, dresid = lax.optimization_barrier((sent, recv_mid, dresid))
        sent = first_exchange(sent)
    keep_front, send_front, small = pl.pallas_call(
        partial(back_kernel, short_len),
        out_shape=(shape((ROW_F1, half), BF16), shape((ROW_F1 + 32, half), BF16), shape((8, D), F32)),
        in_specs=[SMEM, SMEM] + [VMEM] * 11 + [ANY],
        out_specs=(VMEM,) * 3,
        scratch_shapes=[
            pltpu.VMEM((VOCAB, D), F32),
            pltpu.VMEM((ROW_F1 - ROW_P, D), BF16),
            pltpu.VMEM((short_len, short_len), F32),
            pltpu.VMEM((short_len, short_len), F32),
            pltpu.VMEM((rows, D), BF16),
            pltpu.VMEM((rows, D), BF16),
            pltpu.VMEM((rows, 3 * D), BF16),
            pltpu.VMEM((rows, D), BF16),
            pltpu.SemaphoreType.DMA,
        ],
        compiler_params=pltpu.CompilerParams(vmem_limit_bytes=LIMIT_BACK),
        cost_estimate=pl.CostEstimate(flops=19_000_000_000, bytes_accessed=20_000_000, transcendentals=2_400_000),
        name="back",
    )(coords, layouts, vecs, small_deep, lines, dresid, normed, qkv, lse, mixed, shifted, short, table, stacked)
    if not paired:
        front = jnp.concatenate([keep_front, send_front[:ROW_F1]], 1)
        others = [
            jnp.concatenate(pair, 1)
            for pair in ((keep_mid, send_mid), (keep_deep, send_deep))
        ]
        return jnp.concatenate([front] + others, 0), small
    late = 5
    early = [array for k, array in enumerate(sent) if k != late]
    early, keep_front, send_front, small = lax.optimization_barrier((early, keep_front, send_front, small))
    sent = early[:late] + [sent[late]] + early[late:]
    received = [swap_with(send_front, core=1), recv_mid]
    out_p, out_q = exchange_shapes(64)
    parts = pl.pallas_call(
        core_sum_front_kernel,
        out_shape=(out_p,) * 4 + (out_q,) * 4,
        in_specs=[SMEM] + [ANY] * 4 + [VMEM],
        out_specs=(VMEM,) * 8,
        scratch_shapes=[
            pltpu.VMEM((ROW_HALF, half), BF16),
            pltpu.VMEM((ROW_HALF + 32, half), BF16),
            pltpu.SemaphoreType.DMA((5,)),
        ],
        compiler_params=params,
        name="core_sum_front",
    )(coords, keep_front, keep_mid, *received, small)
    return first_exchange(parts), sent


def exchange_shapes(extra):
    quarter = D // 4
    return (
        jax.ShapeDtypeStruct((4 * SCATTER_CUT + extra, quarter), BF16),
        jax.ShapeDtypeStruct((4 * (2 * SHARD - SCATTER_CUT), quarter), BF16),
    )


def core_sum(coords, keep, received):
    out_p, out_q = exchange_shapes(0)
    return pl.pallas_call(
        core_sum_kernel,
        out_shape=(out_p,) * 4 + (out_q,) * 4,
        in_specs=[SMEM] + [VMEM] * 2,
        out_specs=(VMEM,) * 8,
        compiler_params=pltpu.CompilerParams(vmem_limit_bytes=LIMIT),
        name="core_sum",
    )(coords, keep, received)


def first_exchange(parts):
    over = [parts[0]] + [swap_with(parts[k], line=k) for k in (1, 2, 3)]
    return over + [parts[4]] + [swap_with(parts[4 + k], zed=k) for k in (1, 2, 3)]


def swap_with(array, line=0, zed=0, core=0):
    lines, rest = lax.axis_size("dp"), lax.axis_size("fsdp")
    pairs = [
        (d * rest + f, (d ^ line) * rest + (f ^ (2 * zed + core)))
        for d in range(lines)
        for f in range(rest)
    ]
    return lax.ppermute(array, AXES, pairs)


def gather_pieces(block, vectors):
    start = lax.axis_index(AXES) * vectors.shape[1]
    own = lax.dynamic_update_slice(jnp.zeros((16, D), BF16), vectors, (0, start))
    first, second = jnp.concatenate([block[:GATHER_CUT], own], 0), block[GATHER_CUT:]
    along = jnp.concatenate([first] + [swap_with(first, zed=k) for k in (1, 2, 3)], 0)
    across = jnp.concatenate([second] + [swap_with(second, line=k) for k in (1, 2, 3)], 0)
    pieces = [along] + [swap_with(along, line=k) for k in (1, 2, 3)]
    pieces += [across] + [swap_with(across, zed=k) for k in (1, 2, 3)]
    return pieces + [swap_with(piece, core=1) for piece in pieces]


def scatter_sum(coords, front, deep):
    shape = jax.ShapeDtypeStruct
    params = pltpu.CompilerParams(vmem_limit_bytes=LIMIT)
    quarter = D // 4
    rest = 2 * SHARD - SCATTER_CUT
    parts = pl.pallas_call(
        first_sum_kernel,
        out_shape=(shape((2 * SCATTER_CUT + 64, quarter), BF16),) * 4 + (shape((2 * rest, quarter), BF16),) * 4,
        in_specs=[SMEM] + [VMEM] * 16,
        out_specs=(VMEM,) * 8,
        compiler_params=params,
        name="first_sum",
    )(coords, *front, *deep)
    second = [parts[0]] + [swap_with(parts[k], zed=k) for k in (1, 2, 3)]
    second += [parts[4]] + [swap_with(parts[4 + k], line=k) for k in (1, 2, 3)]
    *outs, small, squares = pl.pallas_call(
        last_sum_kernel,
        out_shape=(shape((SHARD, quarter), F32),) * 4 + (shape((8, D), F32), shape((8, quarter), F32)),
        in_specs=[SMEM] + [VMEM] * 8,
        out_specs=(VMEM,) * 6,
        scratch_shapes=[pltpu.VMEM((2 * SHARD, quarter), F32)],
        compiler_params=params,
        name="last_sum",
    )(coords, *second)
    squares = squares + swap_with(squares, core=1)
    quarters = [outs[0], swap_with(outs[1], line=2), swap_with(outs[2], core=1), swap_with(outs[3], line=2, core=1)]
    squares = (squares + swap_with(squares, line=1)) + (swap_with(squares, line=2) + swap_with(squares, line=3))
    squares = [squares] + [swap_with(squares, zed=k) for k in (1, 2, 3)]
    return quarters, small, squares


def shards(byte_ids, layouts, weights, vectors, m_weights, v_weights, m_vectors, v_vectors):
    devices = lax.axis_size(AXES)
    micro = byte_ids.shape[0]
    count = float(micro * layouts.shape[1] * devices * byte_ids.shape[2])
    lines, rest = lax.axis_size("dp"), lax.axis_size("fsdp")
    place = lax.axis_index("fsdp")
    coords = jnp.stack([lax.axis_index("dp"), place // 2, place % 2, lax.axis_index(AXES)]).astype(jnp.int32)
    paired = lines == 4 and rest == 8 and weights.shape[0] == SHARD
    weights_low = weights.astype(BF16)
    vectors_low = vectors.astype(BF16)
    width = vectors.shape[1]
    mine = lax.axis_index(AXES) * width
    flat_layouts = layouts.reshape(-1)
    ids = byte_ids.reshape(flat_layouts.shape[0], -1, POOL).transpose(2, 0, 1).reshape(POOL, -1)
    ids = jnp.pad(ids, ((0, 8 - POOL), (0, 0)))
    if paired:
        pieces = gather_pieces(weights_low, vectors_low)
        front, deep = device_grads(
            pieces, None, coords, ids, flat_layouts, count, True
        )
        quarters, small, squares = scatter_sum(coords, front, deep)
        like = [jax.ShapeDtypeStruct((1, 1), F32)] * 2
        like += [jax.ShapeDtypeStruct(weights.shape, F32)] * 3 + [jax.ShapeDtypeStruct(vectors.shape, F32)] * 3
        loss, grad_norm, *updated = pl.pallas_call(
            partial(update_kernel, count),
            out_shape=like,
            in_specs=[SMEM] + [VMEM] * 15,
            out_specs=[VMEM] * 8,
            compiler_params=pltpu.CompilerParams(vmem_limit_bytes=LIMIT),
            name="update",
        )(coords, *quarters, *squares, small, weights, m_weights, v_weights, vectors, m_vectors, v_vectors)
        return (loss[0, 0], grad_norm[0, 0], *updated)
    coords = coords * 0
    pieces = [lax.all_gather(weights_low, AXES, axis=0, tiled=True)]
    vecs = lax.all_gather(vectors_low, AXES, axis=1, tiled=True)
    vecs = jnp.pad(vecs.astype(F32), ((0, 2), (0, 0)))
    local, small = device_grads(pieces, vecs, coords, ids, flat_layouts, count, False)
    owned = lax.psum_scatter(local.astype(F32), AXES, scatter_dimension=0, tiled=True)
    small, squares = lax.psum((small, jnp.sum(owned * owned)), AXES)
    loss = small[6, 0] / count
    vec_grads = small[:6]
    owned_vecs = lax.dynamic_slice(vec_grads, (0, mine), (6, width))
    squares = squares + jnp.sum(vec_grads * vec_grads)
    grad_norm = jnp.sqrt(squares)
    factor = CLIP / jnp.maximum(grad_norm, CLIP)
    first_w, second_w, update_w = adam(weights, m_weights, v_weights, owned * factor, DECAY)
    first_v, second_v, update_v = adam(vectors, m_vectors, v_vectors, owned_vecs * factor, 0.0)
    return (loss, grad_norm, first_w, second_w, update_w, first_v, second_v, update_v)


def solution(mesh):
    in_specs = (
        P(None, AXES, None),
        P(None, AXES),
        P(AXES, None),
        P(None, AXES),
        P(AXES, None),
        P(AXES, None),
        P(None, AXES),
        P(None, AXES),
    )
    out_specs = (
        P(),
        P(),
        P(AXES, None),
        P(AXES, None),
        P(AXES, None),
        P(None, AXES),
        P(None, AXES),
        P(None, AXES),
    )
    return jax.shard_map(shards, mesh=mesh, in_specs=in_specs, out_specs=out_specs, check_vma=False)
```

```python
from functools import partial

import jax
import jax.numpy as jnp
from jax import lax
from jax.experimental import pallas as pl
from jax.experimental.pallas import tpu as pltpu
from jax.sharding import PartitionSpec as P

D = 512
HEADS = 8
HEAD = 64
FF = 2048
VOCAB = 256
POOL = 3

EPS_NORM = 1e-05
EPS_ADAM = 1e-08
CLIP = 0.2
RATE = 0.03
DECAY = 0.1
BETA = 0.5
STEP = 3
NEGATIVE = -1000000000.0

F32 = jnp.float32
BF16 = jnp.bfloat16

ROW_E = 0
ROW_P = VOCAB
ROW_QKV = ROW_P + POOL * D
ROW_O = ROW_QKV + 3 * D
ROW_F1 = ROW_O + D
ROW_F2 = ROW_F1 + FF
ROW_U = ROW_F2 + FF
ROW_H = ROW_U + POOL * D
ROW_END = ROW_H + VOCAB
ROW_HALF = ROW_END // 2
assert ROW_HALF - ROW_F1 == FF // 2

AXES = ("dp", "fsdp")
SHARD = ROW_END // 32
GATHER_CUT = 240
SCATTER_CUT = 400


def nn(left, right):
    return lax.dot_general(left, right, (((1,), (0,)), ((), ())), preferred_element_type=F32)


def nt(left, right):
    return lax.dot_general(left, right, (((1,), (1,)), ((), ())), preferred_element_type=F32)


def tn(left, right):
    return lax.dot_general(left, right, (((0,), (0,)), ((), ())), preferred_element_type=F32)


def norm_parts(values):
    center = values - jnp.mean(values, -1, keepdims=True)
    spread = jnp.mean(center * center, -1, keepdims=True)
    scale = lax.rsqrt(spread + EPS_NORM)
    return center * scale, scale


def norm_back(unit, scale, gain, grad):
    inner = grad * gain
    mean_inner = jnp.mean(inner, -1, keepdims=True)
    mean_cross = jnp.mean(inner * unit, -1, keepdims=True)
    return scale * (inner - mean_inner - unit * mean_cross)


def fold_rows(values):
    return jnp.sum(values.reshape(values.shape[0] // 8, 8, values.shape[1]), 0)


def one_hot_rows(ids):
    lanes = lax.broadcasted_iota(jnp.int32, (ids.shape[0], VOCAB), 1)
    return jnp.where(lanes == ids, 1.0, 0.0).astype(BF16)


def one_hot_cols(ids):
    lines = lax.broadcasted_iota(jnp.int32, (VOCAB, ids.shape[1]), 0)
    return jnp.where(lines == ids, 1.0, 0.0).astype(BF16)


def rows_of(index, size):
    return pl.ds(pl.multiple_of(index * size, size), size)


def gathered_parts(coords_ref):
    dp, z, core = coords_ref[0], coords_ref[1], coords_ref[2]
    for side in range(2):
        for d in range(4):
            for e in range(4):
                shard = (dp ^ d) * 8 + (z ^ e) * 2 + (core ^ side)
                yield side * 10 + e % 2 * 4 + d, e // 2, 0, shard
                yield side * 10 + 8 + e % 2, e // 2 * 4 + d, 1, shard


def place_vectors(part_ref, coords_ref):
    lines = lax.broadcasted_iota(jnp.int32, (8, D), 0)
    width = D // 32
    mine = lax.broadcasted_iota(jnp.int32, (8, D), 1) // width == lines
    total = jnp.zeros((8, D), F32)
    for piece, part, kind, shard in gathered_parts(coords_ref):
        if kind == 0:
            rows = part_ref[piece // 10 * 8 + piece % 10].astype(F32)
            line = jnp.where(mine, jnp.broadcast_to(rows[part : part + 1, :], (8, D)), 0.0)
            total = total + pltpu.roll(line, shard * width, 1)
    return jnp.concatenate(
        [pltpu.roll(total[k : k + 1, :], (D - k * width) % D, 1) for k in range(8)], 0
    )


class FetchGathered:
    def __init__(self, pieces, coords_ref, w_ref, sems, high):
        self.jobs = []
        for number, (piece, part, kind, shard) in enumerate(gathered_parts(coords_ref)):
            begin, size, step = ((0, GATHER_CUT, GATHER_CUT), (GATHER_CUT, SHARD - GATHER_CUT, SHARD - GATHER_CUT))[kind]
            copy = pltpu.make_async_copy(
                pieces[piece].at[pl.ds(part * step, size)],
                w_ref.at[pl.ds(pl.multiple_of(shard * SHARD + begin, 16), size)],
                sems.at[number],
            )
            self.jobs.append((shard * SHARD < high, copy))

    def start(self, first):
        for early, copy in self.jobs:
            pl.when(early if first else jnp.logical_not(early))(copy.start)

    def wait(self, first):
        for early, copy in self.jobs:
            pl.when(early if first else jnp.logical_not(early))(copy.wait)


def fetch_rows(w_hbm, low, high, w_ref, sem):
    copy = pltpu.make_async_copy(w_hbm.at[pl.ds(low, high - low)], w_ref, sem)
    copy.start()
    return copy


def attend_kernel(short_len, slots, pieces, coords_ref, lay_ref, ids_ref, *refs):
    w_hbm, refs = refs[:pieces], refs[pieces:]
    if pieces == 1:
        vec_in_ref, refs = refs[0], refs[1:]
    if pieces > 1:
        w_out, refs = refs[0], refs[1:]
    (shifted_ref, short_ref, normed_ref, qkv_ref, lse_ref, mixed_ref, resid_ref, lines_ref, cols_ref, vec_ref,
     w_ref, dist_ref, mask_ref, part_ref, sems, part_sems) = refs
    rows = short_len * slots
    if pieces > 1:
        fetch = FetchGathered(w_hbm, coords_ref, w_ref, sems, ROW_F1)
        fetch.start(True)
    else:
        fetch = fetch_rows(w_hbm[0], 0, ROW_F1, w_ref, sems.at[0])
    copies = []
    if pieces > 1:
        for number in range(16):
            piece = w_hbm[number // 8 * 10 + number % 8]
            place = pl.ds(2 * GATHER_CUT, 16)
            copies.append(pltpu.make_async_copy(piece.at[place], part_ref.at[number], part_sems.at[number]))
        for copy in copies:
            copy.start()

    ids = ids_ref[...]
    group = lax.broadcasted_iota(jnp.int32, (1, rows), 1)
    starts = group == 0
    for slot in range(slots):
        starts = starts | (group == slot * short_len)
        starts = starts | ((group == slot * short_len + short_len // 2) & (lay_ref[slot] == 1))
    ends = group == rows - 1
    for slot in range(slots):
        ends = ends | (group == (slot + 1) * short_len - 1)
        ends = ends | ((group == slot * short_len + short_len // 2 - 1) & (lay_ref[slot] == 1))
    before, after = pltpu.roll(ids, 1, 1), pltpu.roll(ids, rows - 1, 1)
    own = [ids[j : j + 1] for j in range(POOL)]
    back = [jnp.where(starts, -1, before[1:2]), jnp.where(starts, -1, before[2:3]), ids[0:1]]
    ahead = [ids[1:2], ids[2:3], jnp.where(ends, -1, after[0:1])]
    for j in range(POOL):
        for kind, line in enumerate((own[j], back[j], ahead[j])):
            lines_ref[j, kind : kind + 1, :] = line
        lines_ref[j, 3:, :] = jnp.zeros((5, rows), jnp.int32)
        padded = jnp.concatenate([lines_ref[j].astype(F32), jnp.zeros((120, rows), F32)], 0)
        cols_ref[j] = padded.T.astype(jnp.int32)

    for copy in copies:
        copy.wait()
    if pieces > 1:
        vec_ref[...] = place_vectors(part_ref, coords_ref)
        fetch.wait(True)
        fetch.start(False)
    else:
        vec_ref[...] = vec_in_ref[...]
        fetch.wait()
    gain, offset = vec_ref[0:1, :], vec_ref[1:2, :]

    def shift_step(j, carry):
        lanes = rows_of(j, D)
        hot = one_hot_rows(cols_ref[j, :, 1:2])
        shifted_ref[:, lanes] = nn(hot, w_ref[ROW_E:ROW_P, :]).astype(BF16)
        return carry

    lax.fori_loop(0, POOL, shift_step, 0)

    def short_step(block, carry):
        at = rows_of(block, rows // 2)
        short = nn(shifted_ref[at, :], w_ref[ROW_P:ROW_QKV, :])
        short_ref[at, :] = short
        unit, _ = norm_parts(short)
        normed_ref[at, :] = (unit * gain + offset).astype(BF16)
        qkv_ref[at, :] = nt(normed_ref[at, :], w_ref[ROW_QKV:ROW_O, :]).astype(BF16)
        return carry

    lax.fori_loop(0, 2, short_step, 0)
    if pieces > 1:
        fetch.wait(False)
        leave = pltpu.make_async_copy(w_ref, w_out, part_sems.at[len(copies)])
        leave.start()

    left_lanes = lax.broadcasted_iota(jnp.int32, (short_len, 2 * HEAD), 1) < HEAD

    def slot_step(index, carry):
        slot, lower = index // 2, index % 2
        at = rows_of(slot, short_len)

        @pl.when(lower == 0)
        def _():
            attention_bias(lay_ref[slot], short_len, dist_ref, mask_ref)

        for pair in range(HEADS // 4):
            lanes, lanes_k, lanes_v = (pair_lanes(part, lower, pair) for part in range(3))
            queries = qkv_ref[at, lanes] * jnp.asarray(0.125, BF16)
            keys, values = qkv_ref[at, lanes_k], qkv_ref[at, lanes_v]
            mixed = jnp.zeros((short_len, 2 * HEAD), F32)
            for side in range(2):
                head = lower * (HEADS // 2) + pair * 2 + side
                slope = head_slope(lower, pair * 2 + side)
                scores = nt(one_side(left_lanes, side, keys), queries)
                scores = scores + jnp.minimum(dist_ref[...] * slope, mask_ref[...])
                top = jnp.max(scores, 0, keepdims=True)
                expo = jnp.exp(scores - top)
                total = jnp.sum(expo, 0, keepdims=True)
                lse_ref[slot, head] = top + jnp.log(total)
                probs = (expo * (1.0 / total)).astype(BF16)
                mixed = mixed + tn(probs, one_side(left_lanes, side, values))
            mixed_ref[at, lanes] = mixed.astype(BF16)
        return carry

    lax.fori_loop(0, 2 * slots, slot_step, 0)
    resid_ref[...] = short_ref[...] + nn(mixed_ref[...], w_ref[ROW_O:ROW_F1, :])
    if pieces > 1:
        leave.wait()


def head_slope(lower, head):
    return jnp.where(lower == 0, *(2.0 ** (-8.0 * (head + more + 1.0) / HEADS) for more in (0, HEADS // 2)))


def pair_lanes(part, lower, pair):
    return pl.ds(pl.multiple_of(part * D + lower * (D // 2) + pair * 2 * HEAD, 2 * HEAD), 2 * HEAD)


def one_side(left_lanes, side, array):
    zero = jnp.zeros_like(array)
    return jnp.where(left_lanes, array, zero) if side == 0 else jnp.where(left_lanes, zero, array)


def attention_bias(layout, short_len, dist_ref, mask_ref):
    key = lax.broadcasted_iota(jnp.int32, (short_len, short_len), 0)
    query = lax.broadcasted_iota(jnp.int32, (short_len, short_len), 1)
    half = jnp.where(layout == 1, short_len // 2, short_len)
    allowed = (key <= query) & ((key >= half) == (query >= half))
    dist_ref[...] = (key - query).astype(F32)
    mask_ref[...] = jnp.where(allowed, 0.0, NEGATIVE)


def gelu_parts(hidden):
    size = jnp.abs(hidden)
    near = 1.0 / (1.0 + (0.3275911 * 0.7071067811865476) * size)
    bell = jnp.exp(hidden * hidden * -0.5)
    tail = near * (0.127414796 + near * (-0.142248368 + near * (0.7107068705 + near * (-0.7265760135 + near * 0.5307027145))))
    tail = tail * bell
    cdf = jnp.where(hidden >= 0.0, 1.0 - tail, tail)
    return hidden * cdf, cdf + hidden * bell * 0.3989422804014327


def split_store(keep_ref, send_ref, core, rows, values):
    half = D // 2
    low, high = values[:, :half].astype(BF16), values[:, half:].astype(BF16)
    keep_ref[rows, :] = jnp.where(core == 0, low, high)
    send_ref[rows, :] = jnp.where(core == 0, high, low)


def deep_kernel(count, coords_ref, vec_ref, cols_ref, lines_ref, resid_ref, w_hbm, *refs):
    (keep_mid, send_mid, keep_ref, send_ref, table_ref, dresid_ref, small_ref,
     w_ref, e_ref, normed_ref, act_ref, slope_ref, deep_ref, final_ref, dlog_ref, dup_ref,
     ddeep_ref, dhid_ref, sums_ref, sems) = refs
    rows = resid_ref.shape[0]
    base = ROW_F1
    core = coords_ref[2]
    stages = []
    for k, (low, high) in enumerate(((ROW_F1, ROW_F2), (ROW_F2, ROW_U), (ROW_U, ROW_END))):
        stages.append([fetch_rows(w_hbm, low, high, w_ref.at[pl.ds(low - base, high - low)], sems.at[k])])
    stages[2].append(fetch_rows(w_hbm, 0, VOCAB, e_ref, sems.at[3]))
    f1, f2, up, head = ROW_F1 - base, ROW_F2 - base, ROW_U - base, ROW_H - base
    gain2, offset2 = vec_ref[2:3, :], vec_ref[3:4, :]
    gain_f, offset_f = vec_ref[4:5, :], vec_ref[5:6, :]
    wide = 1024
    sums_ref[...] = jnp.zeros_like(sums_ref)

    unit, _ = norm_parts(resid_ref[...])
    normed_ref[...] = (unit * gain2 + offset2).astype(BF16)
    for copy in stages[0]:
        copy.wait()

    def hidden_step(chunk, carry):
        lanes = rows_of(chunk, wide)
        hidden = nt(normed_ref[...], w_ref[pl.ds(pl.multiple_of(f1 + chunk * wide, 16), wide), :])
        act, slope = gelu_parts(hidden)
        act_ref[:, lanes] = act.astype(BF16)
        slope_ref[:, lanes] = slope
        return carry

    lax.fori_loop(0, FF // wide, hidden_step, 0)
    for copy in stages[1]:
        copy.wait()

    def deep_step(block, carry):
        at = rows_of(block, rows // 2)
        deep_ref[at, :] = (resid_ref[at, :] + nn(act_ref[at, :], w_ref[f2 : f2 + FF, :])).astype(BF16)
        return carry

    lax.fori_loop(0, 2, deep_step, 0)
    for copy in stages[2]:
        copy.wait()
    ddeep_ref[...] = jnp.zeros_like(ddeep_ref)
    table_ref[...] = jnp.zeros_like(table_ref)

    def head_step(j, carry):
        there = rows_of(j, rows)
        up_rows = pl.ds(pl.multiple_of(up + j * D, 16), D)
        columns = cols_ref[j]
        joined = nn(one_hot_rows(columns[:, 0:1]), e_ref[0:VOCAB, :]) + nt(deep_ref[...], w_ref[up_rows, :])
        unit, scale = norm_parts(joined)
        final = (unit * gain_f + offset_f).astype(BF16)
        final_ref[there, :] = final
        logits = nt(final, w_ref[head : head + VOCAB, :])
        nexts = columns[:, 2:3]
        lanes = lax.broadcasted_iota(jnp.int32, logits.shape, 1)
        target = jnp.where(lanes == nexts, 1.0, 0.0)
        valid = jnp.where(nexts >= 0, 1.0, 0.0)
        peak = jnp.max(logits, -1, keepdims=True)
        expo = jnp.exp(logits - peak)
        total = jnp.sum(expo, -1, keepdims=True)
        picked = jnp.sum(logits * target, -1, keepdims=True)
        losses = valid * (peak + jnp.log(total) - picked)
        dlogits = ((valid / count) * (expo * (1.0 / total) - target)).astype(BF16)
        dlog_ref[there, :] = dlogits
        dfinal = nn(dlogits, w_ref[head : head + VOCAB, :])
        dup = norm_back(unit, scale, gain_f, dfinal).astype(BF16)
        dup_ref[there, :] = dup
        ddeep_ref[...] += nn(dup, w_ref[up_rows, :])
        sums_ref[4, :, :] += fold_rows(dfinal * unit)
        sums_ref[5, :, :] += fold_rows(dfinal)
        sums_ref[6, :, :] += jnp.broadcast_to(fold_rows(losses), (8, D))
        return carry

    lax.fori_loop(0, POOL, head_step, 0)

    out_f2, out_up, out_head = ROW_F2 - ROW_HALF, ROW_U - ROW_HALF, ROW_H - ROW_HALF
    split_store(keep_ref, send_ref, core, pl.ds(out_head, VOCAB), tn(dlog_ref[...], final_ref[...]))

    def dup_step(j, carry):
        there = rows_of(j, rows)
        dup = dup_ref[there, :]
        out = pl.ds(pl.multiple_of(out_up + j * D, D), D)
        split_store(keep_ref, send_ref, core, out, tn(dup, deep_ref[...]))
        table_ref[...] += nn(one_hot_cols(lines_ref[j, 0:1, :]), dup)
        return carry

    lax.fori_loop(0, POOL, dup_step, 0)

    deep_ref[...] = ddeep_ref[...].astype(BF16)

    def dff_step(chunk, carry):
        lanes = rows_of(chunk, wide)
        dact = nt(deep_ref[...], w_ref[pl.ds(pl.multiple_of(f2 + chunk * wide, 16), wide), :])
        dhid_ref[:, lanes] = (dact * slope_ref[:, lanes]).astype(BF16)
        grad = tn(dhid_ref[:, lanes], normed_ref[...])

        @pl.when(chunk == 0)
        def _():
            split_store(keep_mid, send_mid, core, slice(0, wide), grad)

        @pl.when(chunk > 0)
        def _():
            split_store(keep_ref, send_ref, core, slice(0, wide), grad)

        out = pl.ds(pl.multiple_of(out_f2 + chunk * wide, wide), wide)
        split_store(keep_ref, send_ref, core, out, tn(act_ref[:, lanes], deep_ref[...]))
        return carry

    lax.fori_loop(0, FF // wide, dff_step, 0)
    def dnorm_step(block, carry):
        at = rows_of(block, rows // 2)
        dnormed = nn(dhid_ref[at, :], w_ref[f1 : f1 + FF, :])
        unit, scale = norm_parts(resid_ref[at, :])
        dresid_ref[at, :] = ddeep_ref[at, :] + norm_back(unit, scale, gain2, dnormed)
        sums_ref[2, :, :] += fold_rows(dnormed * unit)
        sums_ref[3, :, :] += fold_rows(dnormed)
        return carry

    lax.fori_loop(0, 2, dnorm_step, 0)
    for k in range(8):
        small_ref[k : k + 1, :] = jnp.sum(sums_ref[k], 0, keepdims=True)


def back_kernel(short_len, coords_ref, lay_ref, vec_ref, deep_small_ref, lines_ref, dresid_ref, normed_ref, qkv_ref, lse_ref,
                mixed_ref, shifted_ref, short_ref, table_in, w_hbm, *refs):
    (keep_ref, send_ref, small_ref,
     table_ref, w_ref, dist_ref, mask_ref, dbranch_ref, dmix_ref, dqkv_ref, dshort_ref, sem) = refs
    core = coords_ref[2]
    rows = dresid_ref.shape[0]
    fetch = fetch_rows(w_hbm, ROW_P, ROW_F1, w_ref, sem)
    dbranch_ref[...] = dresid_ref[...].astype(BF16)
    fetch.wait()
    dmix_ref[...] = nt(dbranch_ref[...], w_ref[ROW_O - ROW_P :, :]).astype(BF16)

    left_lanes = lax.broadcasted_iota(jnp.int32, (short_len, 2 * HEAD), 1) < HEAD

    def slot_step(index, carry):
        slot, lower = index // 2, index % 2
        at = rows_of(slot, short_len)

        @pl.when(lower == 0)
        def _():
            attention_bias(lay_ref[slot], short_len, dist_ref, mask_ref)

        for pair in range(HEADS // 4):
            lanes, lanes_k, lanes_v = (pair_lanes(part, lower, pair) for part in range(3))
            queries, keys, values = qkv_ref[at, lanes], qkv_ref[at, lanes_k], qkv_ref[at, lanes_v]
            dmix = dmix_ref[at, lanes]
            scaled = queries * jnp.asarray(0.125, BF16)
            dqueries, dkeys, dvalues = (jnp.zeros((short_len, 2 * HEAD), F32) for _ in range(3))
            for side in range(2):
                head = lower * (HEADS // 2) + pair * 2 + side
                slope = head_slope(lower, pair * 2 + side)
                keys_here = one_side(left_lanes, side, keys)
                scores = nt(keys_here, scaled)
                scores = scores + jnp.minimum(dist_ref[...] * slope, mask_ref[...])
                probs = jnp.exp(scores - lse_ref[slot, head])
                dprobs = nt(one_side(left_lanes, side, values), dmix)
                delta = jnp.sum(dprobs * probs, 0, keepdims=True)
                dscores = (probs * (dprobs - delta) * 0.125).astype(BF16)
                dvalues = dvalues + nn(probs.astype(BF16), one_side(left_lanes, side, dmix))
                dkeys = dkeys + nn(dscores, one_side(left_lanes, side, queries))
                dqueries = dqueries + tn(dscores, keys_here)
            dqkv_ref[at, lanes] = dqueries.astype(BF16)
            dqkv_ref[at, lanes_k] = dkeys.astype(BF16)
            dqkv_ref[at, lanes_v] = dvalues.astype(BF16)
        return carry

    lax.fori_loop(0, 2 * lse_ref.shape[0], slot_step, 0)
    split_store(keep_ref, send_ref, core, pl.ds(ROW_O, D), tn(mixed_ref[...], dbranch_ref[...]))

    def dproj_step(part, carry):
        grad = tn(dqkv_ref[:, rows_of(part, D)], normed_ref[...])
        split_store(keep_ref, send_ref, core, pl.ds(pl.multiple_of(ROW_QKV + part * D, 16), D), grad)
        return carry

    lax.fori_loop(0, 3, dproj_step, 0)

    gain = vec_ref[0:1, :]
    dnormed = nn(dqkv_ref[...], w_ref[ROW_QKV - ROW_P : ROW_O - ROW_P, :])
    unit, scale = norm_parts(short_ref[...])
    dshort_ref[...] = (dresid_ref[...] + norm_back(unit, scale, gain, dnormed)).astype(BF16)
    small_ref[...] = deep_small_ref[...]
    for k, values in enumerate((dnormed * unit, dnormed)):
        small_ref[k : k + 1, :] = jnp.sum(fold_rows(values), 0, keepdims=True)
    half = D // 2
    for k in range(2):
        send_ref[ROW_F1 + 16 * k : ROW_F1 + 16 * (k + 1), :] = two_parts(small_ref[:, k * half : (k + 1) * half])
    table_ref[...] = table_in[...]

    def pool_step(j, carry):
        dshift = nt(dshort_ref[...], w_ref[rows_of(j, D), :]).astype(BF16)
        table_ref[...] += nn(one_hot_cols(lines_ref[j, 1:2, :]), dshift)
        out = pl.ds(pl.multiple_of(ROW_P + j * D, 16), D)
        split_store(keep_ref, send_ref, core, out, tn(shifted_ref[:, rows_of(j, D)], dshort_ref[...]))
        return carry

    lax.fori_loop(0, POOL, pool_step, 0)
    split_store(keep_ref, send_ref, core, pl.ds(ROW_E, VOCAB), table_ref[...])


def two_parts(values):
    high = values.astype(BF16)
    low = (values - high.astype(F32)).astype(BF16)
    return jnp.concatenate([high.astype(F32), low.astype(F32)], 0).astype(BF16)


def one_value(parts):
    parts = parts.astype(F32)
    return parts[:8] + parts[8:]


def lay_out(coords_ref, keep_ref, recv_ref, p_refs, q_refs):
    dp, z = coords_ref[0], coords_ref[1]
    quarter = D // 4
    line = 2 * SHARD
    rest = line - SCATTER_CUT

    def total(column, x, zed, begin, size):
        at = pl.ds(pl.multiple_of(x * (4 * line) + zed * line + begin, 16), size)
        lanes = pl.ds(pl.multiple_of(column * quarter, quarter), quarter)
        return (keep_ref[at, lanes].astype(F32) + recv_ref[at, lanes].astype(F32)).astype(BF16)

    def part_step(part, carry):
        for k in range(4):
            there = dp ^ k
            out = pl.ds(pl.multiple_of(part * SCATTER_CUT, 16), SCATTER_CUT)
            p_refs[k][out, :] = total(there // 2, there % 2, part, 0, SCATTER_CUT)
            out = pl.ds(pl.multiple_of(part * rest, 16), rest)
            q_refs[k][out, :] = total(part // 2, part % 2, z ^ k, SCATTER_CUT, rest)
        return carry

    lax.fori_loop(0, 4, part_step, 0)


def core_sum_kernel(coords_ref, keep_ref, recv_ref, *out_refs):
    lay_out(coords_ref, keep_ref, recv_ref, out_refs[:4], out_refs[4:])


def core_sum_front_kernel(coords_ref, keep_front, keep_mid, recv_front, recv_mid, small_ref, *refs):
    out_refs, (keep_ref, recv_ref, sems) = refs[:8], refs[8:]
    copies = [
        pltpu.make_async_copy(source, target, sems.at[k])
        for k, (source, target) in enumerate((
            (keep_mid, keep_ref.at[pl.ds(ROW_F1, ROW_HALF - ROW_F1)]),
            (recv_mid, recv_ref.at[pl.ds(ROW_F1, ROW_HALF - ROW_F1)]),
            (keep_front, keep_ref.at[pl.ds(0, ROW_F1)]),
            (recv_front.at[pl.ds(0, ROW_F1)], recv_ref.at[pl.ds(0, ROW_F1)]),
            (recv_front.at[pl.ds(ROW_F1, 32)], recv_ref.at[pl.ds(ROW_HALF, 32)]),
        ))
    ]
    for copy in copies:
        copy.start()
    for copy in copies:
        copy.wait()
    lay_out(coords_ref, keep_ref, recv_ref, out_refs[:4], out_refs[4:])
    quarter = D // 4
    for k in range(2):
        both = small_ref[:, 2 * k * quarter : 2 * (k + 1) * quarter] + one_value(
            recv_ref[ROW_HALF + 16 * k : ROW_HALF + 16 * (k + 1), :]
        )
        for side in range(2):
            parts = two_parts(both[:, side * quarter : (side + 1) * quarter])
            row = 4 * SCATTER_CUT + 16 * (2 * k + side)
            for p_ref in out_refs[:4]:
                p_ref[row : row + 16, :] = parts


def sum_of(refs, row, size):
    at = pl.ds(pl.multiple_of(row, 16), size)
    return (refs[0][at, :].astype(F32) + refs[1][at, :].astype(F32)) + (
        refs[2][at, :].astype(F32) + refs[3][at, :].astype(F32)
    )


def first_sum_kernel(coords_ref, *refs):
    sources = ((refs[0:4], refs[4:8]), (refs[8:12], refs[12:16]))
    s_refs, t_refs = refs[16:20], refs[20:24]
    dp, z = coords_ref[0], coords_ref[1]
    rest = 2 * SHARD - SCATTER_CUT
    for half, (p_refs, q_refs) in enumerate(sources):
        for k in range(4):
            s_refs[k][half * SCATTER_CUT : (half + 1) * SCATTER_CUT, :] = sum_of(
                p_refs, (z ^ k) * SCATTER_CUT, SCATTER_CUT
            ).astype(BF16)
            t_refs[k][half * rest : (half + 1) * rest, :] = sum_of(q_refs, (dp ^ k) * rest, rest).astype(BF16)
    for k in range(4):
        row = 4 * SCATTER_CUT + 16 * k
        value = sum(one_value(ref[row : row + 16, :]) for ref in sources[0][0])
        parts = two_parts(value)
        for s_ref in s_refs:
            s_ref[2 * SCATTER_CUT + 16 * k : 2 * SCATTER_CUT + 16 * (k + 1), :] = parts


def last_sum_kernel(coords_ref, *refs):
    s_refs, t_refs, out_refs, (small_ref, square_ref, sum_ref) = refs[:4], refs[4:8], refs[8:12], refs[12:]
    y, core = coords_ref[0] // 2, coords_ref[2]
    rest = 2 * SHARD - SCATTER_CUT
    squares = jnp.zeros((8, D // 4), F32)
    for k in range(2):
        half = y ^ k
        first = sum_of(s_refs, half * SCATTER_CUT, SCATTER_CUT)
        second = sum_of(t_refs, half * rest, rest)
        squares = squares + fold_rows(first * first) + fold_rows(second * second)
        sum_ref[0:SCATTER_CUT, :] = first
        sum_ref[SCATTER_CUT:, :] = second
        for other in range(2):
            out_refs[2 * other + k][...] = sum_ref[pl.ds(pl.multiple_of((core ^ other) * SHARD, 8), SHARD), :]
    for k in range(4):
        row = 2 * SCATTER_CUT + 16 * k
        small_ref[:, k * (D // 4) : (k + 1) * (D // 4)] = sum(
            one_value(ref[row : row + 16, :]) for ref in s_refs
        )
    square_ref[...] = squares


def adam(param, first_m, second_m, grad, decay):
    first_new = BETA * first_m + (1.0 - BETA) * grad
    second_new = BETA * second_m + (1.0 - BETA) * grad * grad
    correct = 1.0 - BETA**STEP
    update = -RATE * (
        first_new / correct / (jnp.sqrt(second_new / correct) + EPS_ADAM) + decay * param
    )
    return (first_new, second_new, update)


def update_kernel(count, coords_ref, g0, g1, g2, g3, q0, q1, q2, q3, small_ref, w_ref, mw_ref, vw_ref, w_vec, m_vec, v_vec,
                  loss_ref, norm_ref, mw_out, vw_out, uw_out, m_out, v_out, u_out):
    y, core, mine = coords_ref[0] // 2, coords_ref[2], coords_ref[3]
    small = small_ref[...]
    line = lax.broadcasted_iota(jnp.int32, small.shape, 0)
    gradient = jnp.where(line < 6, small, 0.0)
    squares = (q0[...] + q1[...]) + (q2[...] + q3[...])

    def whole(values):
        return jnp.sum(jnp.sum(values, 0, keepdims=True), 1, keepdims=True)

    norm = jnp.sqrt(whole(squares) + whole(gradient * gradient))
    factor = CLIP / jnp.maximum(norm, CLIP)
    norm_ref[...] = norm
    loss_ref[...] = small[6:7, 0:1] / count
    quarter = D // 4
    for k, grad_ref in enumerate((g0, g1, g2, g3)):
        place = (core ^ (k // 2)) * 2 + (y ^ (k % 2))
        lanes = pl.ds(pl.multiple_of(place * quarter, quarter), quarter)
        mw_out[:, lanes], vw_out[:, lanes], uw_out[:, lanes] = adam(
            w_ref[:, lanes], mw_ref[:, lanes], vw_ref[:, lanes], grad_ref[...] * factor, DECAY
        )
    width = w_vec.shape[1]
    owned = pltpu.roll(gradient, lax.rem(small.shape[1] - mine * width, small.shape[1]), 1)[:6, :width]
    m_out[...], v_out[...], u_out[...] = adam(w_vec[...], m_vec[...], v_vec[...], owned * factor, 0.0)


VMEM = pl.BlockSpec(memory_space=pltpu.VMEM)
SMEM = pl.BlockSpec(memory_space=pltpu.SMEM)
ANY = pl.BlockSpec(memory_space=pl.ANY)
MIB = 1024 * 1024
LIMIT = 24 * MIB
LIMIT_ATTEND = 30 * MIB
LIMIT_DEEP = 40 * MIB
LIMIT_BACK = 24 * MIB


def device_grads(pieces, vecs, coords, ids, layouts, count, paired):
    slots = layouts.shape[0]
    rows = ids.shape[1]
    short_len = rows // slots
    shape = jax.ShapeDtypeStruct
    params = pltpu.CompilerParams(vmem_limit_bytes=LIMIT)
    number = len(pieces)
    pieces = [pltpu.with_memory_space_constraint(piece, pltpu.HBM) for piece in pieces]
    jobs = 64 if number > 1 else 1
    more = [] if vecs is None else [vecs]
    half = D // 2
    passed = (
        shape((rows, POOL * D), BF16),
        shape((rows, D), F32),
        shape((rows, D), BF16),
        shape((rows, 3 * D), BF16),
        shape((slots, HEADS, 1, short_len), F32),
        shape((rows, D), BF16),
        shape((rows, D), F32),
        shape((POOL, 8, rows), jnp.int32),
        shape((POOL, rows, 128), jnp.int32),
    )

    gathered = (pltpu.HBM((ROW_END, D), BF16),) if number > 1 else ()
    *gathered, shifted, short, normed, qkv, lse, mixed, resid, lines, cols, vecs = pl.pallas_call(
        partial(attend_kernel, short_len, slots, number),
        out_shape=gathered + passed + (shape((8, D), F32),),
        in_specs=[SMEM, SMEM, VMEM] + [ANY] * number + [VMEM] * len(more),
        out_specs=(ANY,) * len(gathered) + (VMEM,) * 10,
        scratch_shapes=[
            pltpu.VMEM((ROW_END if number > 1 else ROW_F1, D), BF16),
            pltpu.VMEM((short_len, short_len), F32),
            pltpu.VMEM((short_len, short_len), F32),
            pltpu.VMEM((16, 16, D), BF16),
            pltpu.SemaphoreType.DMA((jobs,)),
            pltpu.SemaphoreType.DMA((17,)),
        ],
        compiler_params=pltpu.CompilerParams(vmem_limit_bytes=LIMIT_ATTEND),
        cost_estimate=pl.CostEstimate(flops=9_000_000_000, bytes_accessed=20_000_000, transcendentals=2_400_000),
        name="attend",
    )(coords, layouts, ids, *pieces, *more)
    stacked = pltpu.with_memory_space_constraint(gathered[0], pltpu.HBM) if number > 1 else pieces[0]
    keep_mid, send_mid, keep_deep, send_deep, table, dresid, small_deep = pl.pallas_call(
        partial(deep_kernel, count),
        out_shape=(
            shape((ROW_HALF - ROW_F1, half), BF16),
            shape((ROW_HALF - ROW_F1, half), BF16),
            shape((ROW_END - ROW_HALF, half), BF16),
            shape((ROW_END - ROW_HALF, half), BF16),
            shape((VOCAB, D), F32),
            shape((rows, D), F32),
            shape((8, D), F32),
        ),
        in_specs=[SMEM] + [VMEM] * 4 + [ANY],
        out_specs=(VMEM,) * 7,
        scratch_shapes=[
            pltpu.VMEM((ROW_END - ROW_F1, D), BF16),
            pltpu.VMEM((VOCAB, D), BF16),
            pltpu.VMEM((rows, D), BF16),
            pltpu.VMEM((rows, FF), BF16),
            pltpu.VMEM((rows, FF), F32),
            pltpu.VMEM((rows, D), BF16),
            pltpu.VMEM((POOL * rows, D), BF16),
            pltpu.VMEM((POOL * rows, VOCAB), BF16),
            pltpu.VMEM((POOL * rows, D), BF16),
            pltpu.VMEM((rows, D), F32),
            pltpu.VMEM((rows, FF), BF16),
            pltpu.VMEM((8, 8, D), F32),
            pltpu.SemaphoreType.DMA((4,)),
        ],
        compiler_params=pltpu.CompilerParams(vmem_limit_bytes=LIMIT_DEEP),
        name="deep",
    )(coords, vecs, cols, lines, resid, stacked)
    if paired:
        recv_mid, recv_deep = swap_with(send_mid, core=1), swap_with(send_deep, core=1)
        sent = core_sum(coords, keep_deep, recv_deep)
        sent, recv_mid, dresid = lax.optimization_barrier((sent, recv_mid, dresid))
        sent = first_exchange(sent)
    keep_front, send_front, small = pl.pallas_call(
        partial(back_kernel, short_len),
        out_shape=(shape((ROW_F1, half), BF16), shape((ROW_F1 + 32, half), BF16), shape((8, D), F32)),
        in_specs=[SMEM, SMEM] + [VMEM] * 11 + [ANY],
        out_specs=(VMEM,) * 3,
        scratch_shapes=[
            pltpu.VMEM((VOCAB, D), F32),
            pltpu.VMEM((ROW_F1 - ROW_P, D), BF16),
            pltpu.VMEM((short_len, short_len), F32),
            pltpu.VMEM((short_len, short_len), F32),
            pltpu.VMEM((rows, D), BF16),
            pltpu.VMEM((rows, D), BF16),
            pltpu.VMEM((rows, 3 * D), BF16),
            pltpu.VMEM((rows, D), BF16),
            pltpu.SemaphoreType.DMA,
        ],
        compiler_params=pltpu.CompilerParams(vmem_limit_bytes=LIMIT_BACK),
        cost_estimate=pl.CostEstimate(flops=19_000_000_000, bytes_accessed=20_000_000, transcendentals=2_400_000),
        name="back",
    )(coords, layouts, vecs, small_deep, lines, dresid, normed, qkv, lse, mixed, shifted, short, table, stacked)
    if not paired:
        front = jnp.concatenate([keep_front, send_front[:ROW_F1]], 1)
        others = [
            jnp.concatenate(pair, 1)
            for pair in ((keep_mid, send_mid), (keep_deep, send_deep))
        ]
        return jnp.concatenate([front] + others, 0), small
    late = 5
    early = [array for k, array in enumerate(sent) if k != late]
    early, keep_front, send_front, small = lax.optimization_barrier((early, keep_front, send_front, small))
    sent = early[:late] + [sent[late]] + early[late:]
    received = [swap_with(send_front, core=1), recv_mid]
    out_p, out_q = exchange_shapes(64)
    parts = pl.pallas_call(
        core_sum_front_kernel,
        out_shape=(out_p,) * 4 + (out_q,) * 4,
        in_specs=[SMEM] + [ANY] * 4 + [VMEM],
        out_specs=(VMEM,) * 8,
        scratch_shapes=[
            pltpu.VMEM((ROW_HALF, half), BF16),
            pltpu.VMEM((ROW_HALF + 32, half), BF16),
            pltpu.SemaphoreType.DMA((5,)),
        ],
        compiler_params=params,
        name="core_sum_front",
    )(coords, keep_front, keep_mid, *received, small)
    return first_exchange(parts), sent


def exchange_shapes(extra):
    quarter = D // 4
    return (
        jax.ShapeDtypeStruct((4 * SCATTER_CUT + extra, quarter), BF16),
        jax.ShapeDtypeStruct((4 * (2 * SHARD - SCATTER_CUT), quarter), BF16),
    )


def core_sum(coords, keep, received):
    out_p, out_q = exchange_shapes(0)
    return pl.pallas_call(
        core_sum_kernel,
        out_shape=(out_p,) * 4 + (out_q,) * 4,
        in_specs=[SMEM] + [VMEM] * 2,
        out_specs=(VMEM,) * 8,
        compiler_params=pltpu.CompilerParams(vmem_limit_bytes=LIMIT),
        name="core_sum",
    )(coords, keep, received)


def first_exchange(parts):
    over = [parts[0]] + [swap_with(parts[k], line=k) for k in (1, 2, 3)]
    return over + [parts[4]] + [swap_with(parts[4 + k], zed=k) for k in (1, 2, 3)]


def swap_with(array, line=0, zed=0, core=0):
    lines, rest = lax.axis_size("dp"), lax.axis_size("fsdp")
    pairs = [
        (d * rest + f, (d ^ line) * rest + (f ^ (2 * zed + core)))
        for d in range(lines)
        for f in range(rest)
    ]
    return lax.ppermute(array, AXES, pairs)


def gather_pieces(block, vectors):
    own = jnp.pad(vectors.reshape(1, -1), ((0, 0), (0, D - vectors.size)))
    first, second = jnp.concatenate([block[:GATHER_CUT], own], 0), block[GATHER_CUT:]
    parts = [first, swap_with(first, zed=2)]
    across = jnp.concatenate([second] + [swap_with(second, line=k) for k in (1, 2, 3)], 0)
    both = jnp.concatenate(
        [part[:GATHER_CUT] for part in parts] + [part[GATHER_CUT:] for part in parts] + [jnp.zeros((14, D), BF16)], 0
    )
    both, across = lax.optimization_barrier((both, across))
    other = swap_with(both, zed=1)
    by_x, by_y = swap_with(both, line=1), swap_with(both, line=2)
    other, by_x, by_y, across = lax.optimization_barrier((other, by_x, by_y, across))
    away = swap_with(across, zed=2)
    other_x, other_y = swap_with(other, line=1), swap_with(other, line=2)
    pieces = [both, by_x, by_y, swap_with(by_x, line=2)]
    other_x, other_y, away, across = lax.optimization_barrier((other_x, other_y, away, across))
    pieces += [other, other_x, other_y, swap_with(other_y, line=1)]
    across = jnp.concatenate([across, away], 0)
    pieces += [across, swap_with(across, zed=1)]
    return pieces + [swap_with(piece, core=1) for piece in pieces]


def scatter_sum(coords, front, deep):
    shape = jax.ShapeDtypeStruct
    params = pltpu.CompilerParams(vmem_limit_bytes=LIMIT)
    quarter = D // 4
    rest = 2 * SHARD - SCATTER_CUT
    parts = pl.pallas_call(
        first_sum_kernel,
        out_shape=(shape((2 * SCATTER_CUT + 64, quarter), BF16),) * 4 + (shape((2 * rest, quarter), BF16),) * 4,
        in_specs=[SMEM] + [VMEM] * 16,
        out_specs=(VMEM,) * 8,
        compiler_params=params,
        name="first_sum",
    )(coords, *front, *deep)
    second = [parts[0]] + [swap_with(parts[k], zed=k) for k in (1, 2, 3)]
    second += [parts[4]] + [swap_with(parts[4 + k], line=k) for k in (1, 2, 3)]
    *outs, small, squares = pl.pallas_call(
        last_sum_kernel,
        out_shape=(shape((SHARD, quarter), F32),) * 4 + (shape((8, D), F32), shape((8, quarter), F32)),
        in_specs=[SMEM] + [VMEM] * 8,
        out_specs=(VMEM,) * 6,
        scratch_shapes=[pltpu.VMEM((2 * SHARD, quarter), F32)],
        compiler_params=params,
        name="last_sum",
    )(coords, *second)
    squares = squares + swap_with(squares, core=1)
    quarters = [outs[0], swap_with(outs[1], line=2), swap_with(outs[2], core=1), swap_with(outs[3], line=2, core=1)]
    squares = (squares + swap_with(squares, line=1)) + (swap_with(squares, line=2) + swap_with(squares, line=3))
    squares = [squares] + [swap_with(squares, zed=k) for k in (1, 2, 3)]
    return quarters, small, squares


def shards(byte_ids, layouts, weights, vectors, m_weights, v_weights, m_vectors, v_vectors):
    devices = lax.axis_size(AXES)
    micro = byte_ids.shape[0]
    count = float(micro * layouts.shape[1] * devices * byte_ids.shape[2])
    lines, rest = lax.axis_size("dp"), lax.axis_size("fsdp")
    place = lax.axis_index("fsdp")
    coords = jnp.stack([lax.axis_index("dp"), place // 2, place % 2, lax.axis_index(AXES)]).astype(jnp.int32)
    paired = lines == 4 and rest == 8 and weights.shape[0] == SHARD
    weights_low = weights.astype(BF16)
    vectors_low = vectors.astype(BF16)
    width = vectors.shape[1]
    mine = lax.axis_index(AXES) * width
    flat_layouts = layouts.reshape(-1)
    ids = byte_ids.reshape(flat_layouts.shape[0], -1, POOL).transpose(2, 0, 1).reshape(POOL, -1)
    ids = jnp.pad(ids, ((0, 8 - POOL), (0, 0)))
    if paired:
        pieces = gather_pieces(weights_low, vectors_low)
        front, deep = device_grads(
            pieces, None, coords, ids, flat_layouts, count, True
        )
        quarters, small, squares = scatter_sum(coords, front, deep)
        like = [jax.ShapeDtypeStruct((1, 1), F32)] * 2
        like += [jax.ShapeDtypeStruct(weights.shape, F32)] * 3 + [jax.ShapeDtypeStruct(vectors.shape, F32)] * 3
        loss, grad_norm, *updated = pl.pallas_call(
            partial(update_kernel, count),
            out_shape=like,
            in_specs=[SMEM] + [VMEM] * 15,
            out_specs=[VMEM] * 8,
            compiler_params=pltpu.CompilerParams(vmem_limit_bytes=LIMIT),
            name="update",
        )(coords, *quarters, *squares, small, weights, m_weights, v_weights, vectors, m_vectors, v_vectors)
        return (loss[0, 0], grad_norm[0, 0], *updated)
    coords = coords * 0
    pieces = [lax.all_gather(weights_low, AXES, axis=0, tiled=True)]
    vecs = lax.all_gather(vectors_low, AXES, axis=1, tiled=True)
    vecs = jnp.pad(vecs.astype(F32), ((0, 2), (0, 0)))
    local, small = device_grads(pieces, vecs, coords, ids, flat_layouts, count, False)
    owned = lax.psum_scatter(local.astype(F32), AXES, scatter_dimension=0, tiled=True)
    small, squares = lax.psum((small, jnp.sum(owned * owned)), AXES)
    loss = small[6, 0] / count
    vec_grads = small[:6]
    owned_vecs = lax.dynamic_slice(vec_grads, (0, mine), (6, width))
    squares = squares + jnp.sum(vec_grads * vec_grads)
    grad_norm = jnp.sqrt(squares)
    factor = CLIP / jnp.maximum(grad_norm, CLIP)
    first_w, second_w, update_w = adam(weights, m_weights, v_weights, owned * factor, DECAY)
    first_v, second_v, update_v = adam(vectors, m_vectors, v_vectors, owned_vecs * factor, 0.0)
    return (loss, grad_norm, first_w, second_w, update_w, first_v, second_v, update_v)


def solution(mesh):
    in_specs = (
        P(None, AXES, None),
        P(None, AXES),
        P(AXES, None),
        P(None, AXES),
        P(AXES, None),
        P(AXES, None),
        P(None, AXES),
        P(None, AXES),
    )
    out_specs = (
        P(),
        P(),
        P(AXES, None),
        P(AXES, None),
        P(AXES, None),
        P(None, AXES),
        P(None, AXES),
        P(None, AXES),
    )
    return jax.shard_map(shards, mesh=mesh, in_specs=in_specs, out_specs=out_specs, check_vma=False)
```

```python
from functools import partial

import jax
import jax.numpy as jnp
from jax import lax
from jax.experimental import pallas as pl
from jax.experimental.pallas import tpu as pltpu
from jax.sharding import PartitionSpec as P

D = 512
HEADS = 8
HEAD = 64
FF = 2048
VOCAB = 256
POOL = 3

EPS_NORM = 1e-05
EPS_ADAM = 1e-08
CLIP = 0.2
RATE = 0.03
DECAY = 0.1
BETA = 0.5
STEP = 3
NEGATIVE = -1000000000.0

F32 = jnp.float32
BF16 = jnp.bfloat16

ROW_E = 0
ROW_P = VOCAB
ROW_QKV = ROW_P + POOL * D
ROW_O = ROW_QKV + 3 * D
ROW_F1 = ROW_O + D
ROW_F2 = ROW_F1 + FF
ROW_U = ROW_F2 + FF
ROW_H = ROW_U + POOL * D
ROW_END = ROW_H + VOCAB
ROW_HALF = ROW_END // 2
assert ROW_HALF - ROW_F1 == FF // 2

AXES = ("dp", "fsdp")
SHARD = ROW_END // 32
GATHER_CUT = 240
SCATTER_CUT = 400


def nn(left, right):
    return lax.dot_general(left, right, (((1,), (0,)), ((), ())), preferred_element_type=F32)


def nt(left, right):
    return lax.dot_general(left, right, (((1,), (1,)), ((), ())), preferred_element_type=F32)


def tn(left, right):
    return lax.dot_general(left, right, (((0,), (0,)), ((), ())), preferred_element_type=F32)


def norm_parts(values):
    center = values - jnp.mean(values, -1, keepdims=True)
    spread = jnp.mean(center * center, -1, keepdims=True)
    scale = lax.rsqrt(spread + EPS_NORM)
    return center * scale, scale


def norm_back(unit, scale, gain, grad):
    inner = grad * gain
    mean_inner = jnp.mean(inner, -1, keepdims=True)
    mean_cross = jnp.mean(inner * unit, -1, keepdims=True)
    return scale * (inner - mean_inner - unit * mean_cross)


def fold_rows(values):
    return jnp.sum(values.reshape(values.shape[0] // 8, 8, values.shape[1]), 0)


def one_hot_rows(ids):
    lanes = lax.broadcasted_iota(jnp.int32, (ids.shape[0], VOCAB), 1)
    return jnp.where(lanes == ids, 1.0, 0.0).astype(BF16)


def one_hot_cols(ids):
    lines = lax.broadcasted_iota(jnp.int32, (VOCAB, ids.shape[1]), 0)
    return jnp.where(lines == ids, 1.0, 0.0).astype(BF16)


def rows_of(index, size):
    return pl.ds(pl.multiple_of(index * size, size), size)


def gathered_parts(coords_ref):
    dp, z, core = coords_ref[0], coords_ref[1], coords_ref[2]
    for side in range(2):
        for d in range(4):
            for e in range(4):
                shard = (dp ^ d) * 8 + (z ^ e) * 2 + (core ^ side)
                yield side * 10 + e % 2 * 4 + d, e // 2, 0, shard
                yield side * 10 + 8 + e % 2, e // 2 * 4 + d, 1, shard


def place_vectors(part_ref, coords_ref):
    lines = lax.broadcasted_iota(jnp.int32, (8, D), 0)
    width = D // 32
    mine = lax.broadcasted_iota(jnp.int32, (8, D), 1) // width == lines
    total = jnp.zeros((8, D), F32)
    for piece, part, kind, shard in gathered_parts(coords_ref):
        if kind == 0:
            rows = part_ref[piece // 10 * 8 + piece % 10].astype(F32)
            line = jnp.where(mine, jnp.broadcast_to(rows[part : part + 1, :], (8, D)), 0.0)
            total = total + pltpu.roll(line, shard * width, 1)
    return jnp.concatenate(
        [pltpu.roll(total[k : k + 1, :], (D - k * width) % D, 1) for k in range(8)], 0
    )


class FetchGathered:
    def __init__(self, pieces, coords_ref, w_ref, sems, high):
        self.jobs = []
        for number, (piece, part, kind, shard) in enumerate(gathered_parts(coords_ref)):
            begin, size, step = ((0, GATHER_CUT, GATHER_CUT), (GATHER_CUT, SHARD - GATHER_CUT, SHARD - GATHER_CUT))[kind]
            copy = pltpu.make_async_copy(
                pieces[piece].at[pl.ds(part * step, size)],
                w_ref.at[pl.ds(pl.multiple_of(shard * SHARD + begin, 16), size)],
                sems.at[number],
            )
            self.jobs.append((shard * SHARD < high, copy))

    def start(self, first):
        for early, copy in self.jobs:
            pl.when(early if first else jnp.logical_not(early))(copy.start)

    def wait(self, first):
        for early, copy in self.jobs:
            pl.when(early if first else jnp.logical_not(early))(copy.wait)


def fetch_rows(w_hbm, low, high, w_ref, sem):
    copy = pltpu.make_async_copy(w_hbm.at[pl.ds(low, high - low)], w_ref, sem)
    copy.start()
    return copy


def attend_kernel(short_len, slots, pieces, coords_ref, lay_ref, ids_ref, *refs):
    w_hbm, refs = refs[:pieces], refs[pieces:]
    if pieces == 1:
        vec_in_ref, refs = refs[0], refs[1:]
    if pieces > 1:
        w_out, refs = refs[0], refs[1:]
    (shifted_ref, short_ref, normed_ref, qkv_ref, lse_ref, mixed_ref, resid_ref, lines_ref, cols_ref, vec_ref,
     w_ref, dist_ref, mask_ref, part_ref, sems, part_sems) = refs
    rows = short_len * slots
    if pieces > 1:
        fetch = FetchGathered(w_hbm, coords_ref, w_ref, sems, ROW_F1)
        fetch.start(True)
    else:
        fetch = fetch_rows(w_hbm[0], 0, ROW_F1, w_ref, sems.at[0])
    copies = []
    if pieces > 1:
        for number in range(16):
            piece = w_hbm[number // 8 * 10 + number % 8]
            place = pl.ds(2 * GATHER_CUT, 16)
            copies.append(pltpu.make_async_copy(piece.at[place], part_ref.at[number], part_sems.at[number]))
        for copy in copies:
            copy.start()

    ids = ids_ref[...]
    group = lax.broadcasted_iota(jnp.int32, (1, rows), 1)
    starts = group == 0
    for slot in range(slots):
        starts = starts | (group == slot * short_len)
        starts = starts | ((group == slot * short_len + short_len // 2) & (lay_ref[slot] == 1))
    ends = group == rows - 1
    for slot in range(slots):
        ends = ends | (group == (slot + 1) * short_len - 1)
        ends = ends | ((group == slot * short_len + short_len // 2 - 1) & (lay_ref[slot] == 1))
    before, after = pltpu.roll(ids, 1, 1), pltpu.roll(ids, rows - 1, 1)
    own = [ids[j : j + 1] for j in range(POOL)]
    back = [jnp.where(starts, -1, before[1:2]), jnp.where(starts, -1, before[2:3]), ids[0:1]]
    ahead = [ids[1:2], ids[2:3], jnp.where(ends, -1, after[0:1])]
    for j in range(POOL):
        for kind, line in enumerate((own[j], back[j], ahead[j])):
            lines_ref[j, kind : kind + 1, :] = line
        lines_ref[j, 3:, :] = jnp.zeros((5, rows), jnp.int32)
        padded = jnp.concatenate([lines_ref[j].astype(F32), jnp.zeros((120, rows), F32)], 0)
        cols_ref[j] = padded.T.astype(jnp.int32)

    for copy in copies:
        copy.wait()
    if pieces > 1:
        vec_ref[...] = place_vectors(part_ref, coords_ref)
        fetch.wait(True)
        fetch.start(False)
    else:
        vec_ref[...] = vec_in_ref[...]
        fetch.wait()
    gain, offset = vec_ref[0:1, :], vec_ref[1:2, :]

    def shift_step(j, carry):
        lanes = rows_of(j, D)
        hot = one_hot_rows(cols_ref[j, :, 1:2])
        shifted_ref[:, lanes] = nn(hot, w_ref[ROW_E:ROW_P, :]).astype(BF16)
        return carry

    lax.fori_loop(0, POOL, shift_step, 0)

    def short_step(block, carry):
        at = rows_of(block, rows // 2)
        short = nn(shifted_ref[at, :], w_ref[ROW_P:ROW_QKV, :])
        short_ref[at, :] = short
        unit, _ = norm_parts(short)
        normed_ref[at, :] = (unit * gain + offset).astype(BF16)
        qkv_ref[at, :] = nt(normed_ref[at, :], w_ref[ROW_QKV:ROW_O, :]).astype(BF16)
        return carry

    lax.fori_loop(0, 2, short_step, 0)
    if pieces > 1:
        fetch.wait(False)
        leave = pltpu.make_async_copy(w_ref, w_out, part_sems.at[len(copies)])
        leave.start()

    left_lanes = lax.broadcasted_iota(jnp.int32, (short_len, 2 * HEAD), 1) < HEAD

    def slot_step(slot, carry):
        at = rows_of(slot, short_len)
        attention_bias(lay_ref[slot], short_len, dist_ref, mask_ref)
        for pair in range(HEADS // 2):
            lanes, lanes_k, lanes_v = (pair_lanes(part, pair) for part in range(3))
            queries = qkv_ref[at, lanes] * jnp.asarray(0.125, BF16)
            keys, values = qkv_ref[at, lanes_k], qkv_ref[at, lanes_v]
            mixed = jnp.zeros((short_len, 2 * HEAD), F32)
            for side in range(2):
                head = pair * 2 + side
                slope = 2.0 ** (-8.0 * (head + 1.0) / HEADS)
                scores = nt(one_side(left_lanes, side, keys), queries)
                scores = scores + jnp.minimum(dist_ref[...] * slope, mask_ref[...])
                top = jnp.max(scores, 0, keepdims=True)
                expo = jnp.exp(scores - top)
                total = jnp.sum(expo, 0, keepdims=True)
                lse_ref[slot, head] = top + jnp.log(total)
                probs = (expo * (1.0 / total)).astype(BF16)
                mixed = mixed + tn(probs, one_side(left_lanes, side, values))
            mixed_ref[at, lanes] = mixed.astype(BF16)
        return carry

    lax.fori_loop(0, slots, slot_step, 0)
    resid_ref[...] = short_ref[...] + nn(mixed_ref[...], w_ref[ROW_O:ROW_F1, :])
    if pieces > 1:
        leave.wait()


def pair_lanes(part, pair):
    return slice(part * D + pair * 2 * HEAD, part * D + (pair + 1) * 2 * HEAD)


def one_side(left_lanes, side, array):
    zero = jnp.zeros_like(array)
    return jnp.where(left_lanes, array, zero) if side == 0 else jnp.where(left_lanes, zero, array)


def attention_bias(layout, short_len, dist_ref, mask_ref):
    key = lax.broadcasted_iota(jnp.int32, (short_len, short_len), 0)
    query = lax.broadcasted_iota(jnp.int32, (short_len, short_len), 1)
    half = jnp.where(layout == 1, short_len // 2, short_len)
    allowed = (key <= query) & ((key >= half) == (query >= half))
    dist_ref[...] = (key - query).astype(F32)
    mask_ref[...] = jnp.where(allowed, 0.0, NEGATIVE)


def gelu_parts(hidden):
    size = jnp.abs(hidden)
    near = 1.0 / (1.0 + (0.3275911 * 0.7071067811865476) * size)
    bell = jnp.exp(hidden * hidden * -0.5)
    tail = near * (0.127414796 + near * (-0.142248368 + near * (0.7107068705 + near * (-0.7265760135 + near * 0.5307027145))))
    tail = tail * bell
    cdf = jnp.where(hidden >= 0.0, 1.0 - tail, tail)
    return hidden * cdf, cdf + hidden * bell * 0.3989422804014327


def split_store(keep_ref, send_ref, core, rows, values):
    half = D // 2
    low, high = values[:, :half].astype(BF16), values[:, half:].astype(BF16)
    keep_ref[rows, :] = jnp.where(core == 0, low, high)
    send_ref[rows, :] = jnp.where(core == 0, high, low)


def deep_kernel(count, coords_ref, vec_ref, cols_ref, lines_ref, resid_ref, w_hbm, *refs):
    (keep_mid, send_mid, keep_ref, send_ref, table_ref, dresid_ref, small_ref,
     w_ref, e_ref, normed_ref, act_ref, slope_ref, deep_ref, final_ref, dlog_ref, dup_ref,
     ddeep_ref, dhid_ref, sums_ref, sems) = refs
    rows = resid_ref.shape[0]
    base = ROW_F1
    core = coords_ref[2]
    stages = []
    for k, (low, high) in enumerate(((ROW_F1, ROW_F2), (ROW_F2, ROW_U), (ROW_U, ROW_END))):
        stages.append([fetch_rows(w_hbm, low, high, w_ref.at[pl.ds(low - base, high - low)], sems.at[k])])
    stages[2].append(fetch_rows(w_hbm, 0, VOCAB, e_ref, sems.at[3]))
    f1, f2, up, head = ROW_F1 - base, ROW_F2 - base, ROW_U - base, ROW_H - base
    gain2, offset2 = vec_ref[2:3, :], vec_ref[3:4, :]
    gain_f, offset_f = vec_ref[4:5, :], vec_ref[5:6, :]
    wide = 1024
    sums_ref[...] = jnp.zeros_like(sums_ref)

    unit, _ = norm_parts(resid_ref[...])
    normed_ref[...] = (unit * gain2 + offset2).astype(BF16)
    for copy in stages[0]:
        copy.wait()

    def hidden_step(chunk, carry):
        lanes = rows_of(chunk, wide)
        hidden = nt(normed_ref[...], w_ref[pl.ds(pl.multiple_of(f1 + chunk * wide, 16), wide), :])
        act, slope = gelu_parts(hidden)
        act_ref[:, lanes] = act.astype(BF16)
        slope_ref[:, lanes] = slope
        return carry

    lax.fori_loop(0, FF // wide, hidden_step, 0)
    for copy in stages[1]:
        copy.wait()

    def deep_step(block, carry):
        at = rows_of(block, rows // 2)
        deep_ref[at, :] = (resid_ref[at, :] + nn(act_ref[at, :], w_ref[f2 : f2 + FF, :])).astype(BF16)
        return carry

    lax.fori_loop(0, 2, deep_step, 0)
    for copy in stages[2]:
        copy.wait()
    ddeep_ref[...] = jnp.zeros_like(ddeep_ref)
    table_ref[...] = jnp.zeros_like(table_ref)

    def head_step(j, carry):
        there = rows_of(j, rows)
        up_rows = pl.ds(pl.multiple_of(up + j * D, 16), D)
        columns = cols_ref[j]
        joined = nn(one_hot_rows(columns[:, 0:1]), e_ref[0:VOCAB, :]) + nt(deep_ref[...], w_ref[up_rows, :])
        unit, scale = norm_parts(joined)
        final = (unit * gain_f + offset_f).astype(BF16)
        final_ref[there, :] = final
        logits = nt(final, w_ref[head : head + VOCAB, :])
        nexts = columns[:, 2:3]
        lanes = lax.broadcasted_iota(jnp.int32, logits.shape, 1)
        target = jnp.where(lanes == nexts, 1.0, 0.0)
        valid = jnp.where(nexts >= 0, 1.0, 0.0)
        peak = jnp.max(logits, -1, keepdims=True)
        expo = jnp.exp(logits - peak)
        total = jnp.sum(expo, -1, keepdims=True)
        picked = jnp.sum(logits * target, -1, keepdims=True)
        losses = valid * (peak + jnp.log(total) - picked)
        dlogits = ((valid / count) * (expo * (1.0 / total) - target)).astype(BF16)
        dlog_ref[there, :] = dlogits
        dfinal = nn(dlogits, w_ref[head : head + VOCAB, :])
        dup = norm_back(unit, scale, gain_f, dfinal).astype(BF16)
        dup_ref[there, :] = dup
        ddeep_ref[...] += nn(dup, w_ref[up_rows, :])
        sums_ref[4, :, :] += fold_rows(dfinal * unit)
        sums_ref[5, :, :] += fold_rows(dfinal)
        sums_ref[6, :, :] += jnp.broadcast_to(fold_rows(losses), (8, D))
        return carry

    lax.fori_loop(0, POOL, head_step, 0)

    out_f2, out_up, out_head = ROW_F2 - ROW_HALF, ROW_U - ROW_HALF, ROW_H - ROW_HALF
    split_store(keep_ref, send_ref, core, pl.ds(out_head, VOCAB), tn(dlog_ref[...], final_ref[...]))

    def dup_step(j, carry):
        there = rows_of(j, rows)
        dup = dup_ref[there, :]
        out = pl.ds(pl.multiple_of(out_up + j * D, D), D)
        split_store(keep_ref, send_ref, core, out, tn(dup, deep_ref[...]))
        table_ref[...] += nn(one_hot_cols(lines_ref[j, 0:1, :]), dup)
        return carry

    lax.fori_loop(0, POOL, dup_step, 0)

    deep_ref[...] = ddeep_ref[...].astype(BF16)

    def dff_step(chunk, carry):
        lanes = rows_of(chunk, wide)
        dact = nt(deep_ref[...], w_ref[pl.ds(pl.multiple_of(f2 + chunk * wide, 16), wide), :])
        dhid_ref[:, lanes] = (dact * slope_ref[:, lanes]).astype(BF16)
        grad = tn(dhid_ref[:, lanes], normed_ref[...])

        @pl.when(chunk == 0)
        def _():
            split_store(keep_mid, send_mid, core, slice(0, wide), grad)

        @pl.when(chunk > 0)
        def _():
            split_store(keep_ref, send_ref, core, slice(0, wide), grad)

        out = pl.ds(pl.multiple_of(out_f2 + chunk * wide, wide), wide)
        split_store(keep_ref, send_ref, core, out, tn(act_ref[:, lanes], deep_ref[...]))
        return carry

    lax.fori_loop(0, FF // wide, dff_step, 0)
    def dnorm_step(block, carry):
        at = rows_of(block, rows // 2)
        dnormed = nn(dhid_ref[at, :], w_ref[f1 : f1 + FF, :])
        unit, scale = norm_parts(resid_ref[at, :])
        dresid_ref[at, :] = ddeep_ref[at, :] + norm_back(unit, scale, gain2, dnormed)
        sums_ref[2, :, :] += fold_rows(dnormed * unit)
        sums_ref[3, :, :] += fold_rows(dnormed)
        return carry

    lax.fori_loop(0, 2, dnorm_step, 0)
    for k in range(8):
        small_ref[k : k + 1, :] = jnp.sum(sums_ref[k], 0, keepdims=True)


def back_kernel(short_len, coords_ref, lay_ref, vec_ref, deep_small_ref, lines_ref, dresid_ref, normed_ref, qkv_ref, lse_ref,
                mixed_ref, shifted_ref, short_ref, table_in, w_hbm, *refs):
    (keep_ref, send_ref, small_ref,
     table_ref, w_ref, dist_ref, mask_ref, dbranch_ref, dmix_ref, dqkv_ref, dshort_ref, sem) = refs
    core = coords_ref[2]
    rows = dresid_ref.shape[0]
    fetch = fetch_rows(w_hbm, ROW_P, ROW_F1, w_ref, sem)
    dbranch_ref[...] = dresid_ref[...].astype(BF16)
    fetch.wait()
    dmix_ref[...] = nt(dbranch_ref[...], w_ref[ROW_O - ROW_P :, :]).astype(BF16)

    left_lanes = lax.broadcasted_iota(jnp.int32, (short_len, 2 * HEAD), 1) < HEAD

    def slot_step(slot, carry):
        at = rows_of(slot, short_len)
        attention_bias(lay_ref[slot], short_len, dist_ref, mask_ref)
        for pair in range(HEADS // 2):
            lanes, lanes_k, lanes_v = (pair_lanes(part, pair) for part in range(3))
            queries, keys, values = qkv_ref[at, lanes], qkv_ref[at, lanes_k], qkv_ref[at, lanes_v]
            dmix = dmix_ref[at, lanes]
            scaled = queries * jnp.asarray(0.125, BF16)
            dqueries, dkeys, dvalues = (jnp.zeros((short_len, 2 * HEAD), F32) for _ in range(3))
            for side in range(2):
                head = pair * 2 + side
                slope = 2.0 ** (-8.0 * (head + 1.0) / HEADS)
                keys_here = one_side(left_lanes, side, keys)
                scores = nt(keys_here, scaled)
                scores = scores + jnp.minimum(dist_ref[...] * slope, mask_ref[...])
                probs = jnp.exp(scores - lse_ref[slot, head])
                dprobs = nt(one_side(left_lanes, side, values), dmix)
                delta = jnp.sum(dprobs * probs, 0, keepdims=True)
                dscores = (probs * (dprobs - delta) * 0.125).astype(BF16)
                dvalues = dvalues + nn(probs.astype(BF16), one_side(left_lanes, side, dmix))
                dkeys = dkeys + nn(dscores, one_side(left_lanes, side, queries))
                dqueries = dqueries + tn(dscores, keys_here)
            dqkv_ref[at, lanes] = dqueries.astype(BF16)
            dqkv_ref[at, lanes_k] = dkeys.astype(BF16)
            dqkv_ref[at, lanes_v] = dvalues.astype(BF16)
        return carry

    lax.fori_loop(0, lse_ref.shape[0], slot_step, 0)
    split_store(keep_ref, send_ref, core, pl.ds(ROW_O, D), tn(mixed_ref[...], dbranch_ref[...]))

    def dproj_step(part, carry):
        grad = tn(dqkv_ref[:, rows_of(part, D)], normed_ref[...])
        split_store(keep_ref, send_ref, core, pl.ds(pl.multiple_of(ROW_QKV + part * D, 16), D), grad)
        return carry

    lax.fori_loop(0, 3, dproj_step, 0)

    gain = vec_ref[0:1, :]
    dnormed = nn(dqkv_ref[...], w_ref[ROW_QKV - ROW_P : ROW_O - ROW_P, :])
    unit, scale = norm_parts(short_ref[...])
    dshort_ref[...] = (dresid_ref[...] + norm_back(unit, scale, gain, dnormed)).astype(BF16)
    small_ref[...] = deep_small_ref[...]
    for k, values in enumerate((dnormed * unit, dnormed)):
        small_ref[k : k + 1, :] = jnp.sum(fold_rows(values), 0, keepdims=True)
    half = D // 2
    for k in range(2):
        send_ref[ROW_F1 + 16 * k : ROW_F1 + 16 * (k + 1), :] = two_parts(small_ref[:, k * half : (k + 1) * half])
    table_ref[...] = table_in[...]

    def pool_step(j, carry):
        dshift = nt(dshort_ref[...], w_ref[rows_of(j, D), :]).astype(BF16)
        table_ref[...] += nn(one_hot_cols(lines_ref[j, 1:2, :]), dshift)
        out = pl.ds(pl.multiple_of(ROW_P + j * D, 16), D)
        split_store(keep_ref, send_ref, core, out, tn(shifted_ref[:, rows_of(j, D)], dshort_ref[...]))
        return carry

    lax.fori_loop(0, POOL, pool_step, 0)
    split_store(keep_ref, send_ref, core, pl.ds(ROW_E, VOCAB), table_ref[...])


def two_parts(values):
    high = values.astype(BF16)
    low = (values - high.astype(F32)).astype(BF16)
    return jnp.concatenate([high.astype(F32), low.astype(F32)], 0).astype(BF16)


def one_value(parts):
    parts = parts.astype(F32)
    return parts[:8] + parts[8:]


def lay_out(coords_ref, keep_ref, recv_ref, p_refs, q_refs):
    dp, z = coords_ref[0], coords_ref[1]
    quarter = D // 4
    line = 2 * SHARD
    rest = line - SCATTER_CUT

    def total(column, x, zed, begin, size):
        at = pl.ds(pl.multiple_of(x * (4 * line) + zed * line + begin, 16), size)
        lanes = pl.ds(pl.multiple_of(column * quarter, quarter), quarter)
        return (keep_ref[at, lanes].astype(F32) + recv_ref[at, lanes].astype(F32)).astype(BF16)

    def part_step(part, carry):
        for k in range(4):
            there = dp ^ k
            out = pl.ds(pl.multiple_of(part * SCATTER_CUT, 16), SCATTER_CUT)
            p_refs[k][out, :] = total(there // 2, there % 2, part, 0, SCATTER_CUT)
            out = pl.ds(pl.multiple_of(part * rest, 16), rest)
            q_refs[k][out, :] = total(part // 2, part % 2, z ^ k, SCATTER_CUT, rest)
        return carry

    lax.fori_loop(0, 4, part_step, 0)


def core_sum_kernel(coords_ref, keep_ref, recv_ref, *out_refs):
    lay_out(coords_ref, keep_ref, recv_ref, out_refs[:4], out_refs[4:])


def core_sum_front_kernel(coords_ref, keep_front, keep_mid, recv_front, recv_mid, small_ref, *refs):
    out_refs, (keep_ref, recv_ref, sems) = refs[:8], refs[8:]
    copies = [
        pltpu.make_async_copy(source, target, sems.at[k])
        for k, (source, target) in enumerate((
            (keep_mid, keep_ref.at[pl.ds(ROW_F1, ROW_HALF - ROW_F1)]),
            (recv_mid, recv_ref.at[pl.ds(ROW_F1, ROW_HALF - ROW_F1)]),
            (keep_front, keep_ref.at[pl.ds(0, ROW_F1)]),
            (recv_front.at[pl.ds(0, ROW_F1)], recv_ref.at[pl.ds(0, ROW_F1)]),
            (recv_front.at[pl.ds(ROW_F1, 32)], recv_ref.at[pl.ds(ROW_HALF, 32)]),
        ))
    ]
    for copy in copies:
        copy.start()
    for copy in copies:
        copy.wait()
    lay_out(coords_ref, keep_ref, recv_ref, out_refs[:4], out_refs[4:])
    quarter = D // 4
    for k in range(2):
        both = small_ref[:, 2 * k * quarter : 2 * (k + 1) * quarter] + one_value(
            recv_ref[ROW_HALF + 16 * k : ROW_HALF + 16 * (k + 1), :]
        )
        for side in range(2):
            parts = two_parts(both[:, side * quarter : (side + 1) * quarter])
            row = 4 * SCATTER_CUT + 16 * (2 * k + side)
            for p_ref in out_refs[:4]:
                p_ref[row : row + 16, :] = parts


def sum_of(refs, row, size):
    at = pl.ds(pl.multiple_of(row, 16), size)
    return (refs[0][at, :].astype(F32) + refs[1][at, :].astype(F32)) + (
        refs[2][at, :].astype(F32) + refs[3][at, :].astype(F32)
    )


def first_sum_kernel(coords_ref, *refs):
    sources = ((refs[0:4], refs[4:8]), (refs[8:12], refs[12:16]))
    s_refs, t_refs = refs[16:20], refs[20:24]
    dp, z = coords_ref[0], coords_ref[1]
    rest = 2 * SHARD - SCATTER_CUT
    for half, (p_refs, q_refs) in enumerate(sources):
        for k in range(4):
            s_refs[k][half * SCATTER_CUT : (half + 1) * SCATTER_CUT, :] = sum_of(
                p_refs, (z ^ k) * SCATTER_CUT, SCATTER_CUT
            ).astype(BF16)
            t_refs[k][half * rest : (half + 1) * rest, :] = sum_of(q_refs, (dp ^ k) * rest, rest).astype(BF16)
    for k in range(4):
        row = 4 * SCATTER_CUT + 16 * k
        value = sum(one_value(ref[row : row + 16, :]) for ref in sources[0][0])
        parts = two_parts(value)
        for s_ref in s_refs:
            s_ref[2 * SCATTER_CUT + 16 * k : 2 * SCATTER_CUT + 16 * (k + 1), :] = parts


def last_sum_kernel(coords_ref, *refs):
    s_refs, t_refs, out_refs, (small_ref, square_ref, sum_ref) = refs[:4], refs[4:8], refs[8:12], refs[12:]
    y, core = coords_ref[0] // 2, coords_ref[2]
    rest = 2 * SHARD - SCATTER_CUT
    squares = jnp.zeros((8, D // 4), F32)
    for k in range(2):
        half = y ^ k
        first = sum_of(s_refs, half * SCATTER_CUT, SCATTER_CUT)
        second = sum_of(t_refs, half * rest, rest)
        squares = squares + fold_rows(first * first) + fold_rows(second * second)
        sum_ref[0:SCATTER_CUT, :] = first
        sum_ref[SCATTER_CUT:, :] = second
        for other in range(2):
            out_refs[2 * other + k][...] = sum_ref[pl.ds(pl.multiple_of((core ^ other) * SHARD, 8), SHARD), :]
    for k in range(4):
        row = 2 * SCATTER_CUT + 16 * k
        small_ref[:, k * (D // 4) : (k + 1) * (D // 4)] = sum(
            one_value(ref[row : row + 16, :]) for ref in s_refs
        )
    square_ref[...] = squares


def adam(param, first_m, second_m, grad, decay):
    first_new = BETA * first_m + (1.0 - BETA) * grad
    second_new = BETA * second_m + (1.0 - BETA) * grad * grad
    correct = 1.0 - BETA**STEP
    update = -RATE * (
        first_new / correct / (jnp.sqrt(second_new / correct) + EPS_ADAM) + decay * param
    )
    return (first_new, second_new, update)


def update_kernel(count, coords_ref, g0, g1, g2, g3, q0, q1, q2, q3, small_ref, w_ref, mw_ref, vw_ref, w_vec, m_vec, v_vec,
                  loss_ref, norm_ref, mw_out, vw_out, uw_out, m_out, v_out, u_out):
    y, core, mine = coords_ref[0] // 2, coords_ref[2], coords_ref[3]
    small = small_ref[...]
    line = lax.broadcasted_iota(jnp.int32, small.shape, 0)
    gradient = jnp.where(line < 6, small, 0.0)
    squares = (q0[...] + q1[...]) + (q2[...] + q3[...])

    def whole(values):
        return jnp.sum(jnp.sum(values, 0, keepdims=True), 1, keepdims=True)

    norm = jnp.sqrt(whole(squares) + whole(gradient * gradient))
    factor = CLIP / jnp.maximum(norm, CLIP)
    norm_ref[...] = norm
    loss_ref[...] = small[6:7, 0:1] / count
    quarter = D // 4
    for k, grad_ref in enumerate((g0, g1, g2, g3)):
        place = (core ^ (k // 2)) * 2 + (y ^ (k % 2))
        lanes = pl.ds(pl.multiple_of(place * quarter, quarter), quarter)
        mw_out[:, lanes], vw_out[:, lanes], uw_out[:, lanes] = adam(
            w_ref[:, lanes], mw_ref[:, lanes], vw_ref[:, lanes], grad_ref[...] * factor, DECAY
        )
    width = w_vec.shape[1]
    owned = pltpu.roll(gradient, lax.rem(small.shape[1] - mine * width, small.shape[1]), 1)[:6, :width]
    m_out[...], v_out[...], u_out[...] = adam(w_vec[...], m_vec[...], v_vec[...], owned * factor, 0.0)


VMEM = pl.BlockSpec(memory_space=pltpu.VMEM)
SMEM = pl.BlockSpec(memory_space=pltpu.SMEM)
ANY = pl.BlockSpec(memory_space=pl.ANY)
MIB = 1024 * 1024
LIMIT = 24 * MIB
LIMIT_ATTEND = 30 * MIB
LIMIT_DEEP = 40 * MIB
LIMIT_BACK = 24 * MIB


def device_grads(pieces, vecs, coords, ids, layouts, count, paired):
    slots = layouts.shape[0]
    rows = ids.shape[1]
    short_len = rows // slots
    shape = jax.ShapeDtypeStruct
    params = pltpu.CompilerParams(vmem_limit_bytes=LIMIT)
    number = len(pieces)
    pieces = [pltpu.with_memory_space_constraint(piece, pltpu.HBM) for piece in pieces]
    jobs = 64 if number > 1 else 1
    more = [] if vecs is None else [vecs]
    half = D // 2
    passed = (
        shape((rows, POOL * D), BF16),
        shape((rows, D), F32),
        shape((rows, D), BF16),
        shape((rows, 3 * D), BF16),
        shape((slots, HEADS, 1, short_len), F32),
        shape((rows, D), BF16),
        shape((rows, D), F32),
        shape((POOL, 8, rows), jnp.int32),
        shape((POOL, rows, 128), jnp.int32),
    )

    gathered = (pltpu.HBM((ROW_END, D), BF16),) if number > 1 else ()
    *gathered, shifted, short, normed, qkv, lse, mixed, resid, lines, cols, vecs = pl.pallas_call(
        partial(attend_kernel, short_len, slots, number),
        out_shape=gathered + passed + (shape((8, D), F32),),
        in_specs=[SMEM, SMEM, VMEM] + [ANY] * number + [VMEM] * len(more),
        out_specs=(ANY,) * len(gathered) + (VMEM,) * 10,
        scratch_shapes=[
            pltpu.VMEM((ROW_END if number > 1 else ROW_F1, D), BF16),
            pltpu.VMEM((short_len, short_len), F32),
            pltpu.VMEM((short_len, short_len), F32),
            pltpu.VMEM((16, 16, D), BF16),
            pltpu.SemaphoreType.DMA((jobs,)),
            pltpu.SemaphoreType.DMA((17,)),
        ],
        compiler_params=pltpu.CompilerParams(vmem_limit_bytes=LIMIT_ATTEND),
        cost_estimate=pl.CostEstimate(flops=9_000_000_000, bytes_accessed=20_000_000, transcendentals=2_400_000),
        name="attend",
    )(coords, layouts, ids, *pieces, *more)
    stacked = pltpu.with_memory_space_constraint(gathered[0], pltpu.HBM) if number > 1 else pieces[0]
    keep_mid, send_mid, keep_deep, send_deep, table, dresid, small_deep = pl.pallas_call(
        partial(deep_kernel, count),
        out_shape=(
            shape((ROW_HALF - ROW_F1, half), BF16),
            shape((ROW_HALF - ROW_F1, half), BF16),
            shape((ROW_END - ROW_HALF, half), BF16),
            shape((ROW_END - ROW_HALF, half), BF16),
            shape((VOCAB, D), F32),
            shape((rows, D), F32),
            shape((8, D), F32),
        ),
        in_specs=[SMEM] + [VMEM] * 4 + [ANY],
        out_specs=(VMEM,) * 7,
        scratch_shapes=[
            pltpu.VMEM((ROW_END - ROW_F1, D), BF16),
            pltpu.VMEM((VOCAB, D), BF16),
            pltpu.VMEM((rows, D), BF16),
            pltpu.VMEM((rows, FF), BF16),
            pltpu.VMEM((rows, FF), F32),
            pltpu.VMEM((rows, D), BF16),
            pltpu.VMEM((POOL * rows, D), BF16),
            pltpu.VMEM((POOL * rows, VOCAB), BF16),
            pltpu.VMEM((POOL * rows, D), BF16),
            pltpu.VMEM((rows, D), F32),
            pltpu.VMEM((rows, FF), BF16),
            pltpu.VMEM((8, 8, D), F32),
            pltpu.SemaphoreType.DMA((4,)),
        ],
        compiler_params=pltpu.CompilerParams(vmem_limit_bytes=LIMIT_DEEP),
        name="deep",
    )(coords, vecs, cols, lines, resid, stacked)
    if paired:
        recv_mid, recv_deep = swap_with(send_mid, core=1), swap_with(send_deep, core=1)
        sent = core_sum(coords, keep_deep, recv_deep)
        sent, recv_mid, dresid = lax.optimization_barrier((sent, recv_mid, dresid))
        sent = first_exchange(sent)
    keep_front, send_front, small = pl.pallas_call(
        partial(back_kernel, short_len),
        out_shape=(shape((ROW_F1, half), BF16), shape((ROW_F1 + 32, half), BF16), shape((8, D), F32)),
        in_specs=[SMEM, SMEM] + [VMEM] * 11 + [ANY],
        out_specs=(VMEM,) * 3,
        scratch_shapes=[
            pltpu.VMEM((VOCAB, D), F32),
            pltpu.VMEM((ROW_F1 - ROW_P, D), BF16),
            pltpu.VMEM((short_len, short_len), F32),
            pltpu.VMEM((short_len, short_len), F32),
            pltpu.VMEM((rows, D), BF16),
            pltpu.VMEM((rows, D), BF16),
            pltpu.VMEM((rows, 3 * D), BF16),
            pltpu.VMEM((rows, D), BF16),
            pltpu.SemaphoreType.DMA,
        ],
        compiler_params=pltpu.CompilerParams(vmem_limit_bytes=LIMIT_BACK),
        cost_estimate=pl.CostEstimate(flops=19_000_000_000, bytes_accessed=20_000_000, transcendentals=2_400_000),
        name="back",
    )(coords, layouts, vecs, small_deep, lines, dresid, normed, qkv, lse, mixed, shifted, short, table, stacked)
    if not paired:
        front = jnp.concatenate([keep_front, send_front[:ROW_F1]], 1)
        others = [
            jnp.concatenate(pair, 1)
            for pair in ((keep_mid, send_mid), (keep_deep, send_deep))
        ]
        return jnp.concatenate([front] + others, 0), small
    late = 5
    early = [array for k, array in enumerate(sent) if k != late]
    early, keep_front, send_front, small = lax.optimization_barrier((early, keep_front, send_front, small))
    sent = early[:late] + [sent[late]] + early[late:]
    received = [swap_with(send_front, core=1), recv_mid]
    out_p, out_q = exchange_shapes(64)
    parts = pl.pallas_call(
        core_sum_front_kernel,
        out_shape=(out_p,) * 4 + (out_q,) * 4,
        in_specs=[SMEM] + [ANY] * 4 + [VMEM],
        out_specs=(VMEM,) * 8,
        scratch_shapes=[
            pltpu.VMEM((ROW_HALF, half), BF16),
            pltpu.VMEM((ROW_HALF + 32, half), BF16),
            pltpu.SemaphoreType.DMA((5,)),
        ],
        compiler_params=params,
        name="core_sum_front",
    )(coords, keep_front, keep_mid, *received, small)
    return first_exchange(parts), sent


def exchange_shapes(extra):
    quarter = D // 4
    return (
        jax.ShapeDtypeStruct((4 * SCATTER_CUT + extra, quarter), BF16),
        jax.ShapeDtypeStruct((4 * (2 * SHARD - SCATTER_CUT), quarter), BF16),
    )


def core_sum(coords, keep, received):
    out_p, out_q = exchange_shapes(0)
    return pl.pallas_call(
        core_sum_kernel,
        out_shape=(out_p,) * 4 + (out_q,) * 4,
        in_specs=[SMEM] + [VMEM] * 2,
        out_specs=(VMEM,) * 8,
        compiler_params=pltpu.CompilerParams(vmem_limit_bytes=LIMIT),
        name="core_sum",
    )(coords, keep, received)


def first_exchange(parts):
    over = [parts[0]] + [swap_with(parts[k], line=k) for k in (1, 2, 3)]
    return over + [parts[4]] + [swap_with(parts[4 + k], zed=k) for k in (1, 2, 3)]


def swap_with(array, line=0, zed=0, core=0):
    lines, rest = lax.axis_size("dp"), lax.axis_size("fsdp")
    pairs = [
        (d * rest + f, (d ^ line) * rest + (f ^ (2 * zed + core)))
        for d in range(lines)
        for f in range(rest)
    ]
    return lax.ppermute(array, AXES, pairs)


def gather_pieces(block, vectors):
    own = jnp.pad(vectors.reshape(1, -1), ((0, 0), (0, D - vectors.size)))
    first, second = jnp.concatenate([block[:GATHER_CUT], own], 0), block[GATHER_CUT:]
    parts = [first, swap_with(first, zed=2)]
    across = jnp.concatenate([second] + [swap_with(second, line=k) for k in (1, 2, 3)], 0)
    both = jnp.concatenate(
        [part[:GATHER_CUT] for part in parts] + [part[GATHER_CUT:] for part in parts] + [jnp.zeros((14, D), BF16)], 0
    )
    both, across = lax.optimization_barrier((both, across))
    other = swap_with(both, zed=1)
    by_x, by_y = swap_with(both, line=1), swap_with(both, line=2)
    other, by_x, by_y, across = lax.optimization_barrier((other, by_x, by_y, across))
    away = swap_with(across, zed=2)
    other_x, other_y = swap_with(other, line=1), swap_with(other, line=2)
    pieces = [both, by_x, by_y, swap_with(by_x, line=2)]
    other_x, other_y, away, across = lax.optimization_barrier((other_x, other_y, away, across))
    pieces += [other, other_x, other_y, swap_with(other_y, line=1)]
    across = jnp.concatenate([across, away], 0)
    pieces += [across, swap_with(across, zed=1)]
    return pieces + [swap_with(piece, core=1) for piece in pieces]


def scatter_sum(coords, front, deep):
    shape = jax.ShapeDtypeStruct
    params = pltpu.CompilerParams(vmem_limit_bytes=LIMIT)
    quarter = D // 4
    rest = 2 * SHARD - SCATTER_CUT
    parts = pl.pallas_call(
        first_sum_kernel,
        out_shape=(shape((2 * SCATTER_CUT + 64, quarter), BF16),) * 4 + (shape((2 * rest, quarter), BF16),) * 4,
        in_specs=[SMEM] + [VMEM] * 16,
        out_specs=(VMEM,) * 8,
        compiler_params=params,
        name="first_sum",
    )(coords, *front, *deep)
    second = [parts[0]] + [swap_with(parts[k], zed=k) for k in (1, 2, 3)]
    second += [parts[4]] + [swap_with(parts[4 + k], line=k) for k in (1, 2, 3)]
    *outs, small, squares = pl.pallas_call(
        last_sum_kernel,
        out_shape=(shape((SHARD, quarter), F32),) * 4 + (shape((8, D), F32), shape((8, quarter), F32)),
        in_specs=[SMEM] + [VMEM] * 8,
        out_specs=(VMEM,) * 6,
        scratch_shapes=[pltpu.VMEM((2 * SHARD, quarter), F32)],
        compiler_params=params,
        name="last_sum",
    )(coords, *second)
    squares = squares + swap_with(squares, core=1)
    quarters = [outs[0], swap_with(outs[1], line=2), swap_with(outs[2], core=1), swap_with(outs[3], line=2, core=1)]
    squares = (squares + swap_with(squares, line=1)) + (swap_with(squares, line=2) + swap_with(squares, line=3))
    squares = [squares] + [swap_with(squares, zed=k) for k in (1, 2, 3)]
    return quarters, small, squares


def shards(byte_ids, layouts, weights, vectors, m_weights, v_weights, m_vectors, v_vectors):
    devices = lax.axis_size(AXES)
    micro = byte_ids.shape[0]
    count = float(micro * layouts.shape[1] * devices * byte_ids.shape[2])
    lines, rest = lax.axis_size("dp"), lax.axis_size("fsdp")
    place = lax.axis_index("fsdp")
    coords = jnp.stack([lax.axis_index("dp"), place // 2, place % 2, lax.axis_index(AXES)]).astype(jnp.int32)
    paired = lines == 4 and rest == 8 and weights.shape[0] == SHARD
    weights_low = weights.astype(BF16)
    vectors_low = vectors.astype(BF16)
    width = vectors.shape[1]
    mine = lax.axis_index(AXES) * width
    flat_layouts = layouts.reshape(-1)
    ids = byte_ids.reshape(flat_layouts.shape[0], -1, POOL).transpose(2, 0, 1).reshape(POOL, -1)
    ids = jnp.pad(ids, ((0, 8 - POOL), (0, 0)))
    if paired:
        pieces = gather_pieces(weights_low, vectors_low)
        front, deep = device_grads(
            pieces, None, coords, ids, flat_layouts, count, True
        )
        quarters, small, squares = scatter_sum(coords, front, deep)
        like = [jax.ShapeDtypeStruct((1, 1), F32)] * 2
        like += [jax.ShapeDtypeStruct(weights.shape, F32)] * 3 + [jax.ShapeDtypeStruct(vectors.shape, F32)] * 3
        loss, grad_norm, *updated = pl.pallas_call(
            partial(update_kernel, count),
            out_shape=like,
            in_specs=[SMEM] + [VMEM] * 15,
            out_specs=[VMEM] * 8,
            compiler_params=pltpu.CompilerParams(vmem_limit_bytes=LIMIT),
            name="update",
        )(coords, *quarters, *squares, small, weights, m_weights, v_weights, vectors, m_vectors, v_vectors)
        return (loss[0, 0], grad_norm[0, 0], *updated)
    coords = coords * 0
    pieces = [lax.all_gather(weights_low, AXES, axis=0, tiled=True)]
    vecs = lax.all_gather(vectors_low, AXES, axis=1, tiled=True)
    vecs = jnp.pad(vecs.astype(F32), ((0, 2), (0, 0)))
    local, small = device_grads(pieces, vecs, coords, ids, flat_layouts, count, False)
    owned = lax.psum_scatter(local.astype(F32), AXES, scatter_dimension=0, tiled=True)
    small, squares = lax.psum((small, jnp.sum(owned * owned)), AXES)
    loss = small[6, 0] / count
    vec_grads = small[:6]
    owned_vecs = lax.dynamic_slice(vec_grads, (0, mine), (6, width))
    squares = squares + jnp.sum(vec_grads * vec_grads)
    grad_norm = jnp.sqrt(squares)
    factor = CLIP / jnp.maximum(grad_norm, CLIP)
    first_w, second_w, update_w = adam(weights, m_weights, v_weights, owned * factor, DECAY)
    first_v, second_v, update_v = adam(vectors, m_vectors, v_vectors, owned_vecs * factor, 0.0)
    return (loss, grad_norm, first_w, second_w, update_w, first_v, second_v, update_v)


def solution(mesh):
    in_specs = (
        P(None, AXES, None),
        P(None, AXES),
        P(AXES, None),
        P(None, AXES),
        P(AXES, None),
        P(AXES, None),
        P(None, AXES),
        P(None, AXES),
    )
    out_specs = (
        P(),
        P(),
        P(AXES, None),
        P(AXES, None),
        P(AXES, None),
        P(None, AXES),
        P(None, AXES),
        P(None, AXES),
    )
    return jax.shard_map(shards, mesh=mesh, in_specs=in_specs, out_specs=out_specs, check_vma=False)
```

```python
from functools import partial

import jax
import jax.numpy as jnp
from jax import lax
from jax.experimental import pallas as pl
from jax.experimental.pallas import tpu as pltpu
from jax.sharding import PartitionSpec as P

D = 512
HEADS = 8
HEAD = 64
FF = 2048
VOCAB = 256
POOL = 3

EPS_NORM = 1e-05
EPS_ADAM = 1e-08
CLIP = 0.2
RATE = 0.03
DECAY = 0.1
BETA = 0.5
STEP = 3
NEGATIVE = -1000000000.0

F32 = jnp.float32
BF16 = jnp.bfloat16

ROW_E = 0
ROW_P = VOCAB
ROW_QKV = ROW_P + POOL * D
ROW_O = ROW_QKV + 3 * D
ROW_F1 = ROW_O + D
ROW_F2 = ROW_F1 + FF
ROW_U = ROW_F2 + FF
ROW_H = ROW_U + POOL * D
ROW_END = ROW_H + VOCAB
ROW_HALF = ROW_END // 2
assert ROW_HALF - ROW_F1 == FF // 2

AXES = ("dp", "fsdp")
SHARD = ROW_END // 32
GATHER_CUT = 240
SCATTER_CUT = 400


def nn(left, right):
    return lax.dot_general(left, right, (((1,), (0,)), ((), ())), preferred_element_type=F32)


def nt(left, right):
    return lax.dot_general(left, right, (((1,), (1,)), ((), ())), preferred_element_type=F32)


def tn(left, right):
    return lax.dot_general(left, right, (((0,), (0,)), ((), ())), preferred_element_type=F32)


def norm_parts(values):
    center = values - jnp.mean(values, -1, keepdims=True)
    spread = jnp.mean(center * center, -1, keepdims=True)
    scale = lax.rsqrt(spread + EPS_NORM)
    return center * scale, scale


def norm_back(unit, scale, gain, grad):
    inner = grad * gain
    mean_inner = jnp.mean(inner, -1, keepdims=True)
    mean_cross = jnp.mean(inner * unit, -1, keepdims=True)
    return scale * (inner - mean_inner - unit * mean_cross)


def fold_rows(values):
    return jnp.sum(values.reshape(values.shape[0] // 8, 8, values.shape[1]), 0)


def one_hot_rows(ids):
    lanes = lax.broadcasted_iota(jnp.int32, (ids.shape[0], VOCAB), 1)
    return jnp.where(lanes == ids, 1.0, 0.0).astype(BF16)


def one_hot_cols(ids):
    lines = lax.broadcasted_iota(jnp.int32, (VOCAB, ids.shape[1]), 0)
    return jnp.where(lines == ids, 1.0, 0.0).astype(BF16)


def rows_of(index, size):
    return pl.ds(pl.multiple_of(index * size, size), size)


def gathered_parts(coords_ref):
    dp, z, core = coords_ref[0], coords_ref[1], coords_ref[2]
    for side in range(2):
        for d in range(4):
            for e in range(4):
                shard = (dp ^ d) * 8 + (z ^ e) * 2 + (core ^ side)
                yield side * 10 + e % 2 * 4 + d, e // 2, 0, shard
                yield side * 10 + 8 + e % 2, e // 2 * 4 + d, 1, shard


def place_vectors(part_ref, coords_ref):
    lines = lax.broadcasted_iota(jnp.int32, (8, D), 0)
    width = D // 32
    mine = lax.broadcasted_iota(jnp.int32, (8, D), 1) // width == lines
    total = jnp.zeros((8, D), F32)
    for piece, part, kind, shard in gathered_parts(coords_ref):
        if kind == 0:
            rows = part_ref[piece // 10 * 8 + piece % 10].astype(F32)
            line = jnp.where(mine, jnp.broadcast_to(rows[part : part + 1, :], (8, D)), 0.0)
            total = total + pltpu.roll(line, shard * width, 1)
    return jnp.concatenate(
        [pltpu.roll(total[k : k + 1, :], (D - k * width) % D, 1) for k in range(8)], 0
    )


class FetchGathered:
    def __init__(self, pieces, coords_ref, w_ref, sems, high):
        self.jobs = []
        for number, (piece, part, kind, shard) in enumerate(gathered_parts(coords_ref)):
            begin, size, step = ((0, GATHER_CUT, GATHER_CUT), (GATHER_CUT, SHARD - GATHER_CUT, SHARD - GATHER_CUT))[kind]
            copy = pltpu.make_async_copy(
                pieces[piece].at[pl.ds(part * step, size)],
                w_ref.at[pl.ds(pl.multiple_of(shard * SHARD + begin, 16), size)],
                sems.at[number],
            )
            self.jobs.append((shard * SHARD < high, copy))

    def start(self, first):
        for early, copy in self.jobs:
            pl.when(early if first else jnp.logical_not(early))(copy.start)

    def wait(self, first):
        for early, copy in self.jobs:
            pl.when(early if first else jnp.logical_not(early))(copy.wait)


def fetch_rows(w_hbm, low, high, w_ref, sem):
    copy = pltpu.make_async_copy(w_hbm.at[pl.ds(low, high - low)], w_ref, sem)
    copy.start()
    return copy


def attend_kernel(short_len, slots, pieces, coords_ref, lay_ref, ids_ref, *refs):
    w_hbm, refs = refs[:pieces], refs[pieces:]
    if pieces == 1:
        vec_in_ref, refs = refs[0], refs[1:]
    if pieces > 1:
        w_out, refs = refs[0], refs[1:]
    (shifted_ref, short_ref, normed_ref, qkv_ref, lse_ref, mixed_ref, resid_ref, lines_ref, cols_ref, vec_ref,
     w_ref, dist_ref, mask_ref, part_ref, sems, part_sems) = refs
    rows = short_len * slots
    if pieces > 1:
        fetch = FetchGathered(w_hbm, coords_ref, w_ref, sems, ROW_F1)
        fetch.start(True)
    else:
        fetch = fetch_rows(w_hbm[0], 0, ROW_F1, w_ref, sems.at[0])
    copies = []
    if pieces > 1:
        for number in range(16):
            piece = w_hbm[number // 8 * 10 + number % 8]
            place = pl.ds(2 * GATHER_CUT, 16)
            copies.append(pltpu.make_async_copy(piece.at[place], part_ref.at[number], part_sems.at[number]))
        for copy in copies:
            copy.start()

    ids = ids_ref[...]
    group = lax.broadcasted_iota(jnp.int32, (1, rows), 1)
    starts = group == 0
    for slot in range(slots):
        starts = starts | (group == slot * short_len)
        starts = starts | ((group == slot * short_len + short_len // 2) & (lay_ref[slot] == 1))
    ends = group == rows - 1
    for slot in range(slots):
        ends = ends | (group == (slot + 1) * short_len - 1)
        ends = ends | ((group == slot * short_len + short_len // 2 - 1) & (lay_ref[slot] == 1))
    before, after = pltpu.roll(ids, 1, 1), pltpu.roll(ids, rows - 1, 1)
    own = [ids[j : j + 1] for j in range(POOL)]
    back = [jnp.where(starts, -1, before[1:2]), jnp.where(starts, -1, before[2:3]), ids[0:1]]
    ahead = [ids[1:2], ids[2:3], jnp.where(ends, -1, after[0:1])]
    for j in range(POOL):
        for kind, line in enumerate((own[j], back[j], ahead[j])):
            lines_ref[j, kind : kind + 1, :] = line
        lines_ref[j, 3:, :] = jnp.zeros((5, rows), jnp.int32)
        padded = jnp.concatenate([lines_ref[j].astype(F32), jnp.zeros((120, rows), F32)], 0)
        cols_ref[j] = padded.T.astype(jnp.int32)

    for copy in copies:
        copy.wait()
    if pieces > 1:
        vec_ref[...] = place_vectors(part_ref, coords_ref)
        fetch.wait(True)
        fetch.start(False)
    else:
        vec_ref[...] = vec_in_ref[...]
        fetch.wait()
    gain, offset = vec_ref[0:1, :], vec_ref[1:2, :]

    def shift_step(j, carry):
        lanes = rows_of(j, D)
        hot = one_hot_rows(cols_ref[j, :, 1:2])
        shifted_ref[:, lanes] = nn(hot, w_ref[ROW_E:ROW_P, :]).astype(BF16)
        return carry

    lax.fori_loop(0, POOL, shift_step, 0)

    def short_step(block, carry):
        at = rows_of(block, rows // 2)
        short = nn(shifted_ref[at, :], w_ref[ROW_P:ROW_QKV, :])
        short_ref[at, :] = short
        unit, _ = norm_parts(short)
        normed_ref[at, :] = (unit * gain + offset).astype(BF16)
        qkv_ref[at, :] = nt(normed_ref[at, :], w_ref[ROW_QKV:ROW_O, :]).astype(BF16)
        return carry

    lax.fori_loop(0, 2, short_step, 0, unroll=True)
    if pieces > 1:
        fetch.wait(False)
        leave = pltpu.make_async_copy(w_ref, w_out, part_sems.at[len(copies)])
        leave.start()

    left_lanes = lax.broadcasted_iota(jnp.int32, (short_len, 2 * HEAD), 1) < HEAD

    def slot_step(slot, carry):
        at = rows_of(slot, short_len)
        attention_bias(lay_ref[slot], short_len, dist_ref, mask_ref)
        for pair in range(HEADS // 2):
            lanes, lanes_k, lanes_v = (pair_lanes(part, pair) for part in range(3))
            queries = qkv_ref[at, lanes] * jnp.asarray(0.125, BF16)
            keys, values = qkv_ref[at, lanes_k], qkv_ref[at, lanes_v]
            mixed = jnp.zeros((short_len, 2 * HEAD), F32)
            for side in range(2):
                head = pair * 2 + side
                slope = 2.0 ** (-8.0 * (head + 1.0) / HEADS)
                scores = nt(one_side(left_lanes, side, keys), queries)
                scores = scores + jnp.minimum(dist_ref[...] * slope, mask_ref[...])
                top = jnp.max(scores, 0, keepdims=True)
                expo = jnp.exp(scores - top)
                total = jnp.sum(expo, 0, keepdims=True)
                lse_ref[slot, head] = top + jnp.log(total)
                probs = (expo * (1.0 / total)).astype(BF16)
                mixed = mixed + tn(probs, one_side(left_lanes, side, values))
            mixed_ref[at, lanes] = mixed.astype(BF16)
        return carry

    lax.fori_loop(0, slots, slot_step, 0)
    resid_ref[...] = short_ref[...] + nn(mixed_ref[...], w_ref[ROW_O:ROW_F1, :])
    if pieces > 1:
        leave.wait()


def pair_lanes(part, pair):
    return slice(part * D + pair * 2 * HEAD, part * D + (pair + 1) * 2 * HEAD)


def one_side(left_lanes, side, array):
    zero = jnp.zeros_like(array)
    return jnp.where(left_lanes, array, zero) if side == 0 else jnp.where(left_lanes, zero, array)


def attention_bias(layout, short_len, dist_ref, mask_ref):
    key = lax.broadcasted_iota(jnp.int32, (short_len, short_len), 0)
    query = lax.broadcasted_iota(jnp.int32, (short_len, short_len), 1)
    half = jnp.where(layout == 1, short_len // 2, short_len)
    allowed = (key <= query) & ((key >= half) == (query >= half))
    dist_ref[...] = (key - query).astype(F32)
    mask_ref[...] = jnp.where(allowed, 0.0, NEGATIVE)


def gelu_parts(hidden):
    size = jnp.abs(hidden)
    near = 1.0 / (1.0 + (0.3275911 * 0.7071067811865476) * size)
    bell = jnp.exp(hidden * hidden * -0.5)
    tail = near * (0.127414796 + near * (-0.142248368 + near * (0.7107068705 + near * (-0.7265760135 + near * 0.5307027145))))
    tail = tail * bell
    cdf = jnp.where(hidden >= 0.0, 1.0 - tail, tail)
    return hidden * cdf, cdf + hidden * bell * 0.3989422804014327


def split_store(keep_ref, send_ref, core, rows, values):
    half = D // 2
    low, high = values[:, :half].astype(BF16), values[:, half:].astype(BF16)
    keep_ref[rows, :] = jnp.where(core == 0, low, high)
    send_ref[rows, :] = jnp.where(core == 0, high, low)


def deep_kernel(count, coords_ref, vec_ref, cols_ref, lines_ref, resid_ref, w_hbm, *refs):
    (keep_mid, send_mid, keep_ref, send_ref, table_ref, dresid_ref, small_ref,
     w_ref, e_ref, normed_ref, act_ref, slope_ref, deep_ref, final_ref, dlog_ref, dup_ref,
     ddeep_ref, dhid_ref, sums_ref, sems) = refs
    rows = resid_ref.shape[0]
    base = ROW_F1
    core = coords_ref[2]
    stages = []
    for k, (low, high) in enumerate(((ROW_F1, ROW_F2), (ROW_F2, ROW_U), (ROW_U, ROW_END))):
        stages.append([fetch_rows(w_hbm, low, high, w_ref.at[pl.ds(low - base, high - low)], sems.at[k])])
    stages[2].append(fetch_rows(w_hbm, 0, VOCAB, e_ref, sems.at[3]))
    f1, f2, up, head = ROW_F1 - base, ROW_F2 - base, ROW_U - base, ROW_H - base
    gain2, offset2 = vec_ref[2:3, :], vec_ref[3:4, :]
    gain_f, offset_f = vec_ref[4:5, :], vec_ref[5:6, :]
    wide = 1024
    sums_ref[...] = jnp.zeros_like(sums_ref)

    unit, _ = norm_parts(resid_ref[...])
    normed_ref[...] = (unit * gain2 + offset2).astype(BF16)
    for copy in stages[0]:
        copy.wait()

    def hidden_step(chunk, carry):
        lanes = rows_of(chunk, wide)
        hidden = nt(normed_ref[...], w_ref[pl.ds(pl.multiple_of(f1 + chunk * wide, 16), wide), :])
        act, slope = gelu_parts(hidden)
        act_ref[:, lanes] = act.astype(BF16)
        slope_ref[:, lanes] = slope
        return carry

    lax.fori_loop(0, FF // wide, hidden_step, 0)
    for copy in stages[1]:
        copy.wait()

    def deep_step(block, carry):
        at = rows_of(block, rows // 2)
        deep_ref[at, :] = (resid_ref[at, :] + nn(act_ref[at, :], w_ref[f2 : f2 + FF, :])).astype(BF16)
        return carry

    lax.fori_loop(0, 2, deep_step, 0)
    for copy in stages[2]:
        copy.wait()
    ddeep_ref[...] = jnp.zeros_like(ddeep_ref)
    table_ref[...] = jnp.zeros_like(table_ref)

    def head_step(j, carry):
        there = rows_of(j, rows)
        up_rows = pl.ds(pl.multiple_of(up + j * D, 16), D)
        columns = cols_ref[j]
        joined = nn(one_hot_rows(columns[:, 0:1]), e_ref[0:VOCAB, :]) + nt(deep_ref[...], w_ref[up_rows, :])
        unit, scale = norm_parts(joined)
        final = (unit * gain_f + offset_f).astype(BF16)
        final_ref[there, :] = final
        logits = nt(final, w_ref[head : head + VOCAB, :])
        nexts = columns[:, 2:3]
        lanes = lax.broadcasted_iota(jnp.int32, logits.shape, 1)
        target = jnp.where(lanes == nexts, 1.0, 0.0)
        valid = jnp.where(nexts >= 0, 1.0, 0.0)
        peak = jnp.max(logits, -1, keepdims=True)
        expo = jnp.exp(logits - peak)
        total = jnp.sum(expo, -1, keepdims=True)
        picked = jnp.sum(logits * target, -1, keepdims=True)
        losses = valid * (peak + jnp.log(total) - picked)
        dlogits = ((valid / count) * (expo * (1.0 / total) - target)).astype(BF16)
        dlog_ref[there, :] = dlogits
        dfinal = nn(dlogits, w_ref[head : head + VOCAB, :])
        dup = norm_back(unit, scale, gain_f, dfinal).astype(BF16)
        dup_ref[there, :] = dup
        ddeep_ref[...] += nn(dup, w_ref[up_rows, :])
        sums_ref[4, :, :] += fold_rows(dfinal * unit)
        sums_ref[5, :, :] += fold_rows(dfinal)
        sums_ref[6, :, :] += jnp.broadcast_to(fold_rows(losses), (8, D))
        return carry

    lax.fori_loop(0, POOL, head_step, 0)

    out_f2, out_up, out_head = ROW_F2 - ROW_HALF, ROW_U - ROW_HALF, ROW_H - ROW_HALF
    split_store(keep_ref, send_ref, core, pl.ds(out_head, VOCAB), tn(dlog_ref[...], final_ref[...]))

    def dup_step(j, carry):
        there = rows_of(j, rows)
        dup = dup_ref[there, :]
        out = pl.ds(pl.multiple_of(out_up + j * D, D), D)
        split_store(keep_ref, send_ref, core, out, tn(dup, deep_ref[...]))
        table_ref[...] += nn(one_hot_cols(lines_ref[j, 0:1, :]), dup)
        return carry

    lax.fori_loop(0, POOL, dup_step, 0)

    deep_ref[...] = ddeep_ref[...].astype(BF16)

    def dff_step(chunk, carry):
        lanes = rows_of(chunk, wide)
        dact = nt(deep_ref[...], w_ref[pl.ds(pl.multiple_of(f2 + chunk * wide, 16), wide), :])
        dhid_ref[:, lanes] = (dact * slope_ref[:, lanes]).astype(BF16)
        grad = tn(dhid_ref[:, lanes], normed_ref[...])

        @pl.when(chunk == 0)
        def _():
            split_store(keep_mid, send_mid, core, slice(0, wide), grad)

        @pl.when(chunk > 0)
        def _():
            split_store(keep_ref, send_ref, core, slice(0, wide), grad)

        out = pl.ds(pl.multiple_of(out_f2 + chunk * wide, wide), wide)
        split_store(keep_ref, send_ref, core, out, tn(act_ref[:, lanes], deep_ref[...]))
        return carry

    lax.fori_loop(0, FF // wide, dff_step, 0)
    def dnorm_step(block, carry):
        at = rows_of(block, rows // 2)
        dnormed = nn(dhid_ref[at, :], w_ref[f1 : f1 + FF, :])
        unit, scale = norm_parts(resid_ref[at, :])
        dresid_ref[at, :] = ddeep_ref[at, :] + norm_back(unit, scale, gain2, dnormed)
        sums_ref[2, :, :] += fold_rows(dnormed * unit)
        sums_ref[3, :, :] += fold_rows(dnormed)
        return carry

    lax.fori_loop(0, 2, dnorm_step, 0, unroll=True)
    for k in range(8):
        small_ref[k : k + 1, :] = jnp.sum(sums_ref[k], 0, keepdims=True)


def back_kernel(short_len, coords_ref, lay_ref, vec_ref, deep_small_ref, lines_ref, dresid_ref, normed_ref, qkv_ref, lse_ref,
                mixed_ref, shifted_ref, short_ref, table_in, w_hbm, *refs):
    (keep_ref, send_ref, small_ref,
     table_ref, w_ref, dist_ref, mask_ref, dbranch_ref, dmix_ref, dqkv_ref, dshort_ref, sem) = refs
    core = coords_ref[2]
    rows = dresid_ref.shape[0]
    fetch = fetch_rows(w_hbm, ROW_P, ROW_F1, w_ref, sem)
    dbranch_ref[...] = dresid_ref[...].astype(BF16)
    fetch.wait()
    dmix_ref[...] = nt(dbranch_ref[...], w_ref[ROW_O - ROW_P :, :]).astype(BF16)

    left_lanes = lax.broadcasted_iota(jnp.int32, (short_len, 2 * HEAD), 1) < HEAD

    def slot_step(slot, carry):
        at = rows_of(slot, short_len)
        attention_bias(lay_ref[slot], short_len, dist_ref, mask_ref)
        for pair in range(HEADS // 2):
            lanes, lanes_k, lanes_v = (pair_lanes(part, pair) for part in range(3))
            queries, keys, values = qkv_ref[at, lanes], qkv_ref[at, lanes_k], qkv_ref[at, lanes_v]
            dmix = dmix_ref[at, lanes]
            scaled = queries * jnp.asarray(0.125, BF16)
            dqueries, dkeys, dvalues = (jnp.zeros((short_len, 2 * HEAD), F32) for _ in range(3))
            for side in range(2):
                head = pair * 2 + side
                slope = 2.0 ** (-8.0 * (head + 1.0) / HEADS)
                keys_here = one_side(left_lanes, side, keys)
                scores = nt(keys_here, scaled)
                scores = scores + jnp.minimum(dist_ref[...] * slope, mask_ref[...])
                probs = jnp.exp(scores - lse_ref[slot, head])
                dprobs = nt(one_side(left_lanes, side, values), dmix)
                delta = jnp.sum(dprobs * probs, 0, keepdims=True)
                dscores = (probs * (dprobs - delta) * 0.125).astype(BF16)
                dvalues = dvalues + nn(probs.astype(BF16), one_side(left_lanes, side, dmix))
                dkeys = dkeys + nn(dscores, one_side(left_lanes, side, queries))
                dqueries = dqueries + tn(dscores, keys_here)
            dqkv_ref[at, lanes] = dqueries.astype(BF16)
            dqkv_ref[at, lanes_k] = dkeys.astype(BF16)
            dqkv_ref[at, lanes_v] = dvalues.astype(BF16)
        return carry

    lax.fori_loop(0, lse_ref.shape[0], slot_step, 0)
    split_store(keep_ref, send_ref, core, pl.ds(ROW_O, D), tn(mixed_ref[...], dbranch_ref[...]))

    def dproj_step(part, carry):
        grad = tn(dqkv_ref[:, rows_of(part, D)], normed_ref[...])
        split_store(keep_ref, send_ref, core, pl.ds(pl.multiple_of(ROW_QKV + part * D, 16), D), grad)
        return carry

    lax.fori_loop(0, 3, dproj_step, 0)

    gain = vec_ref[0:1, :]
    dnormed = nn(dqkv_ref[...], w_ref[ROW_QKV - ROW_P : ROW_O - ROW_P, :])
    unit, scale = norm_parts(short_ref[...])
    dshort_ref[...] = (dresid_ref[...] + norm_back(unit, scale, gain, dnormed)).astype(BF16)
    small_ref[...] = deep_small_ref[...]
    for k, values in enumerate((dnormed * unit, dnormed)):
        small_ref[k : k + 1, :] = jnp.sum(fold_rows(values), 0, keepdims=True)
    half = D // 2
    for k in range(2):
        send_ref[ROW_F1 + 16 * k : ROW_F1 + 16 * (k + 1), :] = two_parts(small_ref[:, k * half : (k + 1) * half])
    table_ref[...] = table_in[...]

    def pool_step(j, carry):
        dshift = nt(dshort_ref[...], w_ref[rows_of(j, D), :]).astype(BF16)
        table_ref[...] += nn(one_hot_cols(lines_ref[j, 1:2, :]), dshift)
        out = pl.ds(pl.multiple_of(ROW_P + j * D, 16), D)
        split_store(keep_ref, send_ref, core, out, tn(shifted_ref[:, rows_of(j, D)], dshort_ref[...]))
        return carry

    lax.fori_loop(0, POOL, pool_step, 0)
    split_store(keep_ref, send_ref, core, pl.ds(ROW_E, VOCAB), table_ref[...])


def two_parts(values):
    high = values.astype(BF16)
    low = (values - high.astype(F32)).astype(BF16)
    return jnp.concatenate([high.astype(F32), low.astype(F32)], 0).astype(BF16)


def one_value(parts):
    parts = parts.astype(F32)
    return parts[:8] + parts[8:]


def lay_out(coords_ref, keep_ref, recv_ref, p_refs, q_refs):
    dp, z = coords_ref[0], coords_ref[1]
    quarter = D // 4
    line = 2 * SHARD
    rest = line - SCATTER_CUT

    def total(column, x, zed, begin, size):
        at = pl.ds(pl.multiple_of(x * (4 * line) + zed * line + begin, 16), size)
        lanes = pl.ds(pl.multiple_of(column * quarter, quarter), quarter)
        return (keep_ref[at, lanes].astype(F32) + recv_ref[at, lanes].astype(F32)).astype(BF16)

    def part_step(part, carry):
        for k in range(4):
            there = dp ^ k
            out = pl.ds(pl.multiple_of(part * SCATTER_CUT, 16), SCATTER_CUT)
            p_refs[k][out, :] = total(there // 2, there % 2, part, 0, SCATTER_CUT)
            out = pl.ds(pl.multiple_of(part * rest, 16), rest)
            q_refs[k][out, :] = total(part // 2, part % 2, z ^ k, SCATTER_CUT, rest)
        return carry

    lax.fori_loop(0, 4, part_step, 0)


def core_sum_kernel(coords_ref, keep_ref, recv_ref, *out_refs):
    lay_out(coords_ref, keep_ref, recv_ref, out_refs[:4], out_refs[4:])


def core_sum_front_kernel(coords_ref, keep_front, keep_mid, recv_front, recv_mid, small_ref, *refs):
    out_refs, (keep_ref, recv_ref, sems) = refs[:8], refs[8:]
    copies = [
        pltpu.make_async_copy(source, target, sems.at[k])
        for k, (source, target) in enumerate((
            (keep_mid, keep_ref.at[pl.ds(ROW_F1, ROW_HALF - ROW_F1)]),
            (recv_mid, recv_ref.at[pl.ds(ROW_F1, ROW_HALF - ROW_F1)]),
            (keep_front, keep_ref.at[pl.ds(0, ROW_F1)]),
            (recv_front.at[pl.ds(0, ROW_F1)], recv_ref.at[pl.ds(0, ROW_F1)]),
            (recv_front.at[pl.ds(ROW_F1, 32)], recv_ref.at[pl.ds(ROW_HALF, 32)]),
        ))
    ]
    for copy in copies:
        copy.start()
    for copy in copies:
        copy.wait()
    lay_out(coords_ref, keep_ref, recv_ref, out_refs[:4], out_refs[4:])
    quarter = D // 4
    for k in range(2):
        both = small_ref[:, 2 * k * quarter : 2 * (k + 1) * quarter] + one_value(
            recv_ref[ROW_HALF + 16 * k : ROW_HALF + 16 * (k + 1), :]
        )
        for side in range(2):
            parts = two_parts(both[:, side * quarter : (side + 1) * quarter])
            row = 4 * SCATTER_CUT + 16 * (2 * k + side)
            for p_ref in out_refs[:4]:
                p_ref[row : row + 16, :] = parts


def sum_of(refs, row, size):
    at = pl.ds(pl.multiple_of(row, 16), size)
    return (refs[0][at, :].astype(F32) + refs[1][at, :].astype(F32)) + (
        refs[2][at, :].astype(F32) + refs[3][at, :].astype(F32)
    )


def first_sum_kernel(coords_ref, *refs):
    sources = ((refs[0:4], refs[4:8]), (refs[8:12], refs[12:16]))
    s_refs, t_refs = refs[16:20], refs[20:24]
    dp, z = coords_ref[0], coords_ref[1]
    rest = 2 * SHARD - SCATTER_CUT
    for half, (p_refs, q_refs) in enumerate(sources):
        for k in range(4):
            s_refs[k][half * SCATTER_CUT : (half + 1) * SCATTER_CUT, :] = sum_of(
                p_refs, (z ^ k) * SCATTER_CUT, SCATTER_CUT
            ).astype(BF16)
            t_refs[k][half * rest : (half + 1) * rest, :] = sum_of(q_refs, (dp ^ k) * rest, rest).astype(BF16)
    for k in range(4):
        row = 4 * SCATTER_CUT + 16 * k
        value = sum(one_value(ref[row : row + 16, :]) for ref in sources[0][0])
        parts = two_parts(value)
        for s_ref in s_refs:
            s_ref[2 * SCATTER_CUT + 16 * k : 2 * SCATTER_CUT + 16 * (k + 1), :] = parts


def last_sum_kernel(coords_ref, *refs):
    s_refs, t_refs, out_refs, (small_ref, square_ref, sum_ref) = refs[:4], refs[4:8], refs[8:12], refs[12:]
    y, core = coords_ref[0] // 2, coords_ref[2]
    rest = 2 * SHARD - SCATTER_CUT
    squares = jnp.zeros((8, D // 4), F32)
    for k in range(2):
        half = y ^ k
        first = sum_of(s_refs, half * SCATTER_CUT, SCATTER_CUT)
        second = sum_of(t_refs, half * rest, rest)
        squares = squares + fold_rows(first * first) + fold_rows(second * second)
        sum_ref[0:SCATTER_CUT, :] = first
        sum_ref[SCATTER_CUT:, :] = second
        for other in range(2):
            out_refs[2 * other + k][...] = sum_ref[pl.ds(pl.multiple_of((core ^ other) * SHARD, 8), SHARD), :]
    for k in range(4):
        row = 2 * SCATTER_CUT + 16 * k
        small_ref[:, k * (D // 4) : (k + 1) * (D // 4)] = sum(
            one_value(ref[row : row + 16, :]) for ref in s_refs
        )
    square_ref[...] = squares


def adam(param, first_m, second_m, grad, decay):
    first_new = BETA * first_m + (1.0 - BETA) * grad
    second_new = BETA * second_m + (1.0 - BETA) * grad * grad
    correct = 1.0 - BETA**STEP
    update = -RATE * (
        first_new / correct / (jnp.sqrt(second_new / correct) + EPS_ADAM) + decay * param
    )
    return (first_new, second_new, update)


def update_kernel(count, coords_ref, g0, g1, g2, g3, q0, q1, q2, q3, small_ref, w_ref, mw_ref, vw_ref, w_vec, m_vec, v_vec,
                  loss_ref, norm_ref, mw_out, vw_out, uw_out, m_out, v_out, u_out):
    y, core, mine = coords_ref[0] // 2, coords_ref[2], coords_ref[3]
    small = small_ref[...]
    line = lax.broadcasted_iota(jnp.int32, small.shape, 0)
    gradient = jnp.where(line < 6, small, 0.0)
    squares = (q0[...] + q1[...]) + (q2[...] + q3[...])

    def whole(values):
        return jnp.sum(jnp.sum(values, 0, keepdims=True), 1, keepdims=True)

    norm = jnp.sqrt(whole(squares) + whole(gradient * gradient))
    factor = CLIP / jnp.maximum(norm, CLIP)
    norm_ref[...] = norm
    loss_ref[...] = small[6:7, 0:1] / count
    quarter = D // 4
    for k, grad_ref in enumerate((g0, g1, g2, g3)):
        place = (core ^ (k // 2)) * 2 + (y ^ (k % 2))
        lanes = pl.ds(pl.multiple_of(place * quarter, quarter), quarter)
        mw_out[:, lanes], vw_out[:, lanes], uw_out[:, lanes] = adam(
            w_ref[:, lanes], mw_ref[:, lanes], vw_ref[:, lanes], grad_ref[...] * factor, DECAY
        )
    width = w_vec.shape[1]
    owned = pltpu.roll(gradient, lax.rem(small.shape[1] - mine * width, small.shape[1]), 1)[:6, :width]
    m_out[...], v_out[...], u_out[...] = adam(w_vec[...], m_vec[...], v_vec[...], owned * factor, 0.0)


VMEM = pl.BlockSpec(memory_space=pltpu.VMEM)
SMEM = pl.BlockSpec(memory_space=pltpu.SMEM)
ANY = pl.BlockSpec(memory_space=pl.ANY)
MIB = 1024 * 1024
LIMIT = 24 * MIB
LIMIT_ATTEND = 30 * MIB
LIMIT_DEEP = 40 * MIB
LIMIT_BACK = 24 * MIB


def device_grads(pieces, vecs, coords, ids, layouts, count, paired):
    slots = layouts.shape[0]
    rows = ids.shape[1]
    short_len = rows // slots
    shape = jax.ShapeDtypeStruct
    params = pltpu.CompilerParams(vmem_limit_bytes=LIMIT)
    number = len(pieces)
    pieces = [pltpu.with_memory_space_constraint(piece, pltpu.HBM) for piece in pieces]
    jobs = 64 if number > 1 else 1
    more = [] if vecs is None else [vecs]
    half = D // 2
    passed = (
        shape((rows, POOL * D), BF16),
        shape((rows, D), F32),
        shape((rows, D), BF16),
        shape((rows, 3 * D), BF16),
        shape((slots, HEADS, 1, short_len), F32),
        shape((rows, D), BF16),
        shape((rows, D), F32),
        shape((POOL, 8, rows), jnp.int32),
        shape((POOL, rows, 128), jnp.int32),
    )

    gathered = (pltpu.HBM((ROW_END, D), BF16),) if number > 1 else ()
    *gathered, shifted, short, normed, qkv, lse, mixed, resid, lines, cols, vecs = pl.pallas_call(
        partial(attend_kernel, short_len, slots, number),
        out_shape=gathered + passed + (shape((8, D), F32),),
        in_specs=[SMEM, SMEM, VMEM] + [ANY] * number + [VMEM] * len(more),
        out_specs=(ANY,) * len(gathered) + (VMEM,) * 10,
        scratch_shapes=[
            pltpu.VMEM((ROW_END if number > 1 else ROW_F1, D), BF16),
            pltpu.VMEM((short_len, short_len), F32),
            pltpu.VMEM((short_len, short_len), F32),
            pltpu.VMEM((16, 16, D), BF16),
            pltpu.SemaphoreType.DMA((jobs,)),
            pltpu.SemaphoreType.DMA((17,)),
        ],
        compiler_params=pltpu.CompilerParams(vmem_limit_bytes=LIMIT_ATTEND),
        cost_estimate=pl.CostEstimate(flops=9_000_000_000, bytes_accessed=20_000_000, transcendentals=2_400_000),
        name="attend",
    )(coords, layouts, ids, *pieces, *more)
    stacked = pltpu.with_memory_space_constraint(gathered[0], pltpu.HBM) if number > 1 else pieces[0]
    keep_mid, send_mid, keep_deep, send_deep, table, dresid, small_deep = pl.pallas_call(
        partial(deep_kernel, count),
        out_shape=(
            shape((ROW_HALF - ROW_F1, half), BF16),
            shape((ROW_HALF - ROW_F1, half), BF16),
            shape((ROW_END - ROW_HALF, half), BF16),
            shape((ROW_END - ROW_HALF, half), BF16),
            shape((VOCAB, D), F32),
            shape((rows, D), F32),
            shape((8, D), F32),
        ),
        in_specs=[SMEM] + [VMEM] * 4 + [ANY],
        out_specs=(VMEM,) * 7,
        scratch_shapes=[
            pltpu.VMEM((ROW_END - ROW_F1, D), BF16),
            pltpu.VMEM((VOCAB, D), BF16),
            pltpu.VMEM((rows, D), BF16),
            pltpu.VMEM((rows, FF), BF16),
            pltpu.VMEM((rows, FF), F32),
            pltpu.VMEM((rows, D), BF16),
            pltpu.VMEM((POOL * rows, D), BF16),
            pltpu.VMEM((POOL * rows, VOCAB), BF16),
            pltpu.VMEM((POOL * rows, D), BF16),
            pltpu.VMEM((rows, D), F32),
            pltpu.VMEM((rows, FF), BF16),
            pltpu.VMEM((8, 8, D), F32),
            pltpu.SemaphoreType.DMA((4,)),
        ],
        compiler_params=pltpu.CompilerParams(vmem_limit_bytes=LIMIT_DEEP),
        name="deep",
    )(coords, vecs, cols, lines, resid, stacked)
    if paired:
        recv_mid, recv_deep = swap_with(send_mid, core=1), swap_with(send_deep, core=1)
        sent = core_sum(coords, keep_deep, recv_deep)
        sent, recv_mid, dresid = lax.optimization_barrier((sent, recv_mid, dresid))
        sent = first_exchange(sent)
    keep_front, send_front, small = pl.pallas_call(
        partial(back_kernel, short_len),
        out_shape=(shape((ROW_F1, half), BF16), shape((ROW_F1 + 32, half), BF16), shape((8, D), F32)),
        in_specs=[SMEM, SMEM] + [VMEM] * 11 + [ANY],
        out_specs=(VMEM,) * 3,
        scratch_shapes=[
            pltpu.VMEM((VOCAB, D), F32),
            pltpu.VMEM((ROW_F1 - ROW_P, D), BF16),
            pltpu.VMEM((short_len, short_len), F32),
            pltpu.VMEM((short_len, short_len), F32),
            pltpu.VMEM((rows, D), BF16),
            pltpu.VMEM((rows, D), BF16),
            pltpu.VMEM((rows, 3 * D), BF16),
            pltpu.VMEM((rows, D), BF16),
            pltpu.SemaphoreType.DMA,
        ],
        compiler_params=pltpu.CompilerParams(vmem_limit_bytes=LIMIT_BACK),
        cost_estimate=pl.CostEstimate(flops=19_000_000_000, bytes_accessed=20_000_000, transcendentals=2_400_000),
        name="back",
    )(coords, layouts, vecs, small_deep, lines, dresid, normed, qkv, lse, mixed, shifted, short, table, stacked)
    if not paired:
        front = jnp.concatenate([keep_front, send_front[:ROW_F1]], 1)
        others = [
            jnp.concatenate(pair, 1)
            for pair in ((keep_mid, send_mid), (keep_deep, send_deep))
        ]
        return jnp.concatenate([front] + others, 0), small
    late = 5
    early = [array for k, array in enumerate(sent) if k != late]
    early, keep_front, send_front, small = lax.optimization_barrier((early, keep_front, send_front, small))
    sent = early[:late] + [sent[late]] + early[late:]
    received = [swap_with(send_front, core=1), recv_mid]
    out_p, out_q = exchange_shapes(64)
    parts = pl.pallas_call(
        core_sum_front_kernel,
        out_shape=(out_p,) * 4 + (out_q,) * 4,
        in_specs=[SMEM] + [ANY] * 4 + [VMEM],
        out_specs=(VMEM,) * 8,
        scratch_shapes=[
            pltpu.VMEM((ROW_HALF, half), BF16),
            pltpu.VMEM((ROW_HALF + 32, half), BF16),
            pltpu.SemaphoreType.DMA((5,)),
        ],
        compiler_params=params,
        name="core_sum_front",
    )(coords, keep_front, keep_mid, *received, small)
    return first_exchange(parts), sent


def exchange_shapes(extra):
    quarter = D // 4
    return (
        jax.ShapeDtypeStruct((4 * SCATTER_CUT + extra, quarter), BF16),
        jax.ShapeDtypeStruct((4 * (2 * SHARD - SCATTER_CUT), quarter), BF16),
    )


def core_sum(coords, keep, received):
    out_p, out_q = exchange_shapes(0)
    return pl.pallas_call(
        core_sum_kernel,
        out_shape=(out_p,) * 4 + (out_q,) * 4,
        in_specs=[SMEM] + [VMEM] * 2,
        out_specs=(VMEM,) * 8,
        compiler_params=pltpu.CompilerParams(vmem_limit_bytes=LIMIT),
        name="core_sum",
    )(coords, keep, received)


def first_exchange(parts):
    over = [parts[0]] + [swap_with(parts[k], line=k) for k in (1, 2, 3)]
    return over + [parts[4]] + [swap_with(parts[4 + k], zed=k) for k in (1, 2, 3)]


def swap_with(array, line=0, zed=0, core=0):
    lines, rest = lax.axis_size("dp"), lax.axis_size("fsdp")
    pairs = [
        (d * rest + f, (d ^ line) * rest + (f ^ (2 * zed + core)))
        for d in range(lines)
        for f in range(rest)
    ]
    return lax.ppermute(array, AXES, pairs)


def gather_pieces(block, vectors):
    own = jnp.pad(vectors.reshape(1, -1), ((0, 0), (0, D - vectors.size)))
    first, second = jnp.concatenate([block[:GATHER_CUT], own], 0), block[GATHER_CUT:]
    parts = [first, swap_with(first, zed=2)]
    across = jnp.concatenate([second] + [swap_with(second, line=k) for k in (1, 2, 3)], 0)
    both = jnp.concatenate(
        [part[:GATHER_CUT] for part in parts] + [part[GATHER_CUT:] for part in parts] + [jnp.zeros((14, D), BF16)], 0
    )
    both, across = lax.optimization_barrier((both, across))
    other = swap_with(both, zed=1)
    by_x, by_y = swap_with(both, line=1), swap_with(both, line=2)
    other, by_x, by_y, across = lax.optimization_barrier((other, by_x, by_y, across))
    away = swap_with(across, zed=2)
    other_x, other_y = swap_with(other, line=1), swap_with(other, line=2)
    pieces = [both, by_x, by_y, swap_with(by_x, line=2)]
    other_x, other_y, away, across = lax.optimization_barrier((other_x, other_y, away, across))
    pieces += [other, other_x, other_y, swap_with(other_y, line=1)]
    across = jnp.concatenate([across, away], 0)
    pieces += [across, swap_with(across, zed=1)]
    return pieces + [swap_with(piece, core=1) for piece in pieces]


def scatter_sum(coords, front, deep):
    shape = jax.ShapeDtypeStruct
    params = pltpu.CompilerParams(vmem_limit_bytes=LIMIT)
    quarter = D // 4
    rest = 2 * SHARD - SCATTER_CUT
    parts = pl.pallas_call(
        first_sum_kernel,
        out_shape=(shape((2 * SCATTER_CUT + 64, quarter), BF16),) * 4 + (shape((2 * rest, quarter), BF16),) * 4,
        in_specs=[SMEM] + [VMEM] * 16,
        out_specs=(VMEM,) * 8,
        compiler_params=params,
        name="first_sum",
    )(coords, *front, *deep)
    second = [parts[0]] + [swap_with(parts[k], zed=k) for k in (1, 2, 3)]
    second += [parts[4]] + [swap_with(parts[4 + k], line=k) for k in (1, 2, 3)]
    *outs, small, squares = pl.pallas_call(
        last_sum_kernel,
        out_shape=(shape((SHARD, quarter), F32),) * 4 + (shape((8, D), F32), shape((8, quarter), F32)),
        in_specs=[SMEM] + [VMEM] * 8,
        out_specs=(VMEM,) * 6,
        scratch_shapes=[pltpu.VMEM((2 * SHARD, quarter), F32)],
        compiler_params=params,
        name="last_sum",
    )(coords, *second)
    squares = squares + swap_with(squares, core=1)
    quarters = [outs[0], swap_with(outs[1], line=2), swap_with(outs[2], core=1), swap_with(outs[3], line=2, core=1)]
    squares = (squares + swap_with(squares, line=1)) + (swap_with(squares, line=2) + swap_with(squares, line=3))
    squares = [squares] + [swap_with(squares, zed=k) for k in (1, 2, 3)]
    return quarters, small, squares


def shards(byte_ids, layouts, weights, vectors, m_weights, v_weights, m_vectors, v_vectors):
    devices = lax.axis_size(AXES)
    micro = byte_ids.shape[0]
    count = float(micro * layouts.shape[1] * devices * byte_ids.shape[2])
    lines, rest = lax.axis_size("dp"), lax.axis_size("fsdp")
    place = lax.axis_index("fsdp")
    coords = jnp.stack([lax.axis_index("dp"), place // 2, place % 2, lax.axis_index(AXES)]).astype(jnp.int32)
    paired = lines == 4 and rest == 8 and weights.shape[0] == SHARD
    weights_low = weights.astype(BF16)
    vectors_low = vectors.astype(BF16)
    width = vectors.shape[1]
    mine = lax.axis_index(AXES) * width
    flat_layouts = layouts.reshape(-1)
    ids = byte_ids.reshape(flat_layouts.shape[0], -1, POOL).transpose(2, 0, 1).reshape(POOL, -1)
    ids = jnp.pad(ids, ((0, 8 - POOL), (0, 0)))
    if paired:
        pieces = gather_pieces(weights_low, vectors_low)
        front, deep = device_grads(
            pieces, None, coords, ids, flat_layouts, count, True
        )
        quarters, small, squares = scatter_sum(coords, front, deep)
        like = [jax.ShapeDtypeStruct((1, 1), F32)] * 2
        like += [jax.ShapeDtypeStruct(weights.shape, F32)] * 3 + [jax.ShapeDtypeStruct(vectors.shape, F32)] * 3
        loss, grad_norm, *updated = pl.pallas_call(
            partial(update_kernel, count),
            out_shape=like,
            in_specs=[SMEM] + [VMEM] * 15,
            out_specs=[VMEM] * 8,
            compiler_params=pltpu.CompilerParams(vmem_limit_bytes=LIMIT),
            name="update",
        )(coords, *quarters, *squares, small, weights, m_weights, v_weights, vectors, m_vectors, v_vectors)
        return (loss[0, 0], grad_norm[0, 0], *updated)
    coords = coords * 0
    pieces = [lax.all_gather(weights_low, AXES, axis=0, tiled=True)]
    vecs = lax.all_gather(vectors_low, AXES, axis=1, tiled=True)
    vecs = jnp.pad(vecs.astype(F32), ((0, 2), (0, 0)))
    local, small = device_grads(pieces, vecs, coords, ids, flat_layouts, count, False)
    owned = lax.psum_scatter(local.astype(F32), AXES, scatter_dimension=0, tiled=True)
    small, squares = lax.psum((small, jnp.sum(owned * owned)), AXES)
    loss = small[6, 0] / count
    vec_grads = small[:6]
    owned_vecs = lax.dynamic_slice(vec_grads, (0, mine), (6, width))
    squares = squares + jnp.sum(vec_grads * vec_grads)
    grad_norm = jnp.sqrt(squares)
    factor = CLIP / jnp.maximum(grad_norm, CLIP)
    first_w, second_w, update_w = adam(weights, m_weights, v_weights, owned * factor, DECAY)
    first_v, second_v, update_v = adam(vectors, m_vectors, v_vectors, owned_vecs * factor, 0.0)
    return (loss, grad_norm, first_w, second_w, update_w, first_v, second_v, update_v)


def solution(mesh):
    in_specs = (
        P(None, AXES, None),
        P(None, AXES),
        P(AXES, None),
        P(None, AXES),
        P(AXES, None),
        P(AXES, None),
        P(None, AXES),
        P(None, AXES),
    )
    out_specs = (
        P(),
        P(),
        P(AXES, None),
        P(AXES, None),
        P(AXES, None),
        P(None, AXES),
        P(None, AXES),
        P(None, AXES),
    )
    return jax.shard_map(shards, mesh=mesh, in_specs=in_specs, out_specs=out_specs, check_vma=False)
```
